32 devices in a mesh: seq: 16 (over z, y, x), batch: 2 (over core).
Axes of the slice: x: 2, y: 2, z: 4, core: 2. Of those that a mesh axis runs over, the one named last changes fastest.
Arguments:
- tokens: bfloat16 [2, 2, 2048, 768], P('batch', None, 'seq'), may hold values from -6 to 6
- cotangent: bfloat16 [2, 2, 2048, 768], P('batch', None, 'seq'), may hold values from -6 to 6
- lengths: int32 [2, 2], P('batch'), may hold values from 256 to 2048, as said below
- norm_gain: float32 [4, 768], replicated, may hold values from 0.25 to 1.75
- norm_bias: float32 [4, 768], replicated, may hold values from -3 to 3
- w_qkv: bfloat16 [2, 768, 2304], replicated, may hold values from -0.21875 to 0.21875
- w_out: bfloat16 [2, 768, 768], replicated, may hold values from -0.4375 to 0.4375
- w_up: bfloat16 [2, 768, 3072], replicated, may hold values from -0.21875 to 0.21875
- w_down: bfloat16 [2, 3072, 768], replicated, may hold values from -0.109375 to 0.109375
- taps: float32 [4, 768], replicated, may hold values from -3 to 3
- skip: float32 [768], replicated, may hold values from -3 to 3
- ssm_rate: float32 [768, 64], replicated, may hold values from 0.00024414062 to 0.03
- ssm_out: float32 [768, 64], replicated, may hold values from -0.078125 to 0.078125
Outputs:
- mixed: bfloat16 [2, 2, 2048, 768], P('batch', None, 'seq')
- d_tokens: float32 [2, 2, 2048, 768], P('batch', None, 'seq')
- gain_grad: float32 [4, 768], P(None, 'seq')
- bias_grad: float32 [3, 768], P(None, 'seq')
- last_bias_grad: float32 [768], P('seq')
- w_qkv_grad: float32 [2, 768, 2304], P(None, 'seq')
- w_out_grad: float32 [2, 768, 768], P(None, 'seq')
- w_up_grad: float32 [2, 768, 3072], P(None, 'seq')
- w_down_grad: float32 [2, 3072, 768], P(None, 'seq')
- taps_grad: float32 [4, 768], P(None, 'seq')
- skip_grad: float32 [768], P('seq')
- rate_grad: float32 [768, 64], P('seq')
- ssm_out_grad: float32 [768, 64], P('seq')
The draws below stay inside these ranges and needn't reach their ends.
Inputs may be any that keep to these rules, and one draw needn't show every extreme that they name: `lengths`: in every row one sequence, drawn from the seed, has all 2048 positions valid.
All inputs are finite; a program needn't handle non-finite values.
Results may differ from the reference program's by a relative error of at most 0.022.
Values may be sent and summed in bfloat16 or wider, within the bound.
A program may use at most 448 MiB of HBM per device.

```python
import math
from functools import partial
import jax
import jax.numpy as jnp
from jax import lax

D = 768
HEADS = 12
HEAD = 64
FF = 3072
STATE = 64
TAPS = 4
SEQS = 2
LEN = 2048
GROUPS = 2


def draw_lengths(key, part):
    key = jax.random.fold_in(key, 11)
    pick_key, length_key = jax.random.split(key)
    full_index = jax.random.randint(pick_key, (GROUPS, 1), 0, SEQS)
    others = jax.random.randint(length_key, (GROUPS, SEQS), LEN // 8, LEN + 1)
    columns = jnp.arange(SEQS)[None, :]
    return jnp.where(columns == full_index, LEN, others).astype(jnp.int32)


def steps_of(rng, extent, cuts, smallest, high):
    level, own = 1.0, jax.random.fold_in(rng, 6)
    for dim, parts in cuts:
        heights = jnp.exp(jax.random.uniform(jax.random.fold_in(own, dim), (parts,), jnp.float32, smallest / len(cuts), high / len(cuts)))
        level = level * jnp.repeat(heights, extent[dim] // parts).reshape([-1 if axis == dim else 1 for axis in range(len(extent))])
    return level


def noise(key, extent, scale, bound, cuts=(), kind=jnp.bfloat16):
    drawn = jax.random.normal(key, extent, jnp.float32) * scale
    if len(cuts) > 0:
        drawn = steps_of(key, extent, cuts, -0.22, 0.18) * drawn
    return jnp.clip(drawn, min=-bound, max=bound).astype(kind)


def setup_inputs(seed: int = 0) -> dict:
    splits = jax.random.split(jax.random.key(seed), 14)
    return {
        "tokens": noise(splits[0], (GROUPS, SEQS, LEN, D), 1.0, 6.0, ((0, 2), (2, 16))),
        "cotangent": noise(splits[1], (GROUPS, SEQS, LEN, D), 1.0, 6.0, ((0, 2), (2, 16))),
        "lengths": draw_lengths(jax.random.fold_in(splits[13], 71), 0),
        "norm_gain": jnp.clip(1.0 + 0.15 * jax.random.normal(splits[3], (4, D), jnp.float32), 0.25, 1.75),
        "norm_bias": noise(splits[4], (4, D), 0.5, 3.0, (), jnp.float32),
        "w_qkv": noise(splits[5], (2, D, 3 * D), D ** -0.5, 0.21875),
        "w_out": noise(splits[6], (2, D, D), (D // 4) ** -0.5, 0.4375),
        "w_up": noise(splits[7], (2, D, FF), D ** -0.5, 0.21875),
        "w_down": noise(splits[8], (2, FF, D), FF ** -0.5, 0.109375),
        "taps": noise(splits[9], (TAPS, D), 0.5, 3.0, (), jnp.float32),
        "skip": noise(splits[10], (D,), 0.5, 3.0, (), jnp.float32),
        "ssm_rate": jnp.clip(jnp.exp(jax.random.uniform(splits[11], (D, STATE), jnp.float32, math.log(0.00024414062), math.log(0.03))), 0.00024414062, 0.03),
        "ssm_out": noise(splits[12], (D, STATE), ((STATE * LEN // 4) ** -0.5), 0.078125, (), jnp.float32),
    }


@jax.custom_vjp
def low(v):
    return lax.optimization_barrier(v.astype(jnp.bfloat16)).astype(jnp.float32)

@jax.custom_vjp
def low_back(v):
    return v

def low_keep(v):
    return (low(v), None)

def low_pass(kept, grad):
    return (grad,)

def back_keep(v):
    return (v, None)

def back_low(kept, grad):
    return (low(grad),)
low.defvjp(low_keep, low_pass)
low_back.defvjp(back_keep, back_low)
norm_eps = 1e-05
masked_score = -1e+30

def product_high(operand_a, operand_b):
    return jnp.dot(operand_a, operand_b, precision=lax.Precision.HIGHEST)

def layer_norm(inputs, scale_row, shift_row):
    center = inputs - lax.optimization_barrier(jnp.mean(inputs, -1, keepdims=True))
    spread = lax.optimization_barrier(jnp.mean(center * center, -1, keepdims=True))
    return center * lax.rsqrt(spread + norm_eps) * scale_row + shift_row

def kernel_spectrum(ssm_rate, ssm_out):
    fft_length = 2 * LEN
    frequency = jnp.arange(LEN + 1, dtype=jnp.int32)
    angles = (frequency.astype(jnp.float32) * (2.0 * math.pi / fft_length))[:, None, None]
    odd_mask = (frequency % 2 == 1)[:, None, None]
    blocks = STATE // 8
    rate_blocks = ssm_rate.reshape(D, blocks, 8).transpose(1, 0, 2)
    weight_blocks = ssm_out.reshape(D, blocks, 8).transpose(1, 0, 2)

    def add_block(running, piece_pair):
        rate_part, weight_part = piece_pair
        decays = jnp.exp(-rate_part)
        half_sine = jnp.sin(angles / 2.0)
        real_den = -jnp.expm1(-rate_part) + decays * 2.0 * half_sine * half_sine
        imag_den = decays * jnp.sin(angles)
        numerator = jnp.where(odd_mask, 1.0 + jnp.exp(-rate_part * LEN), -jnp.expm1(-rate_part * LEN))
        factor = weight_part * numerator / (real_den * real_den + imag_den * imag_den)
        return ((running[0] + lax.optimization_barrier(jnp.sum(factor * real_den, -1)), running[1] - lax.optimization_barrier(jnp.sum(factor * imag_den, -1))), None)
    zeros_init = jnp.zeros((LEN + 1, D), jnp.float32)
    return lax.scan(jax.checkpoint(add_block), (zeros_init, zeros_init), (rate_blocks, weight_blocks))[0]

def attention(queries, key_rows, value_rows, length_value):
    heads_query = queries.reshape(LEN, HEADS, HEAD).transpose(1, 0, 2)
    heads_key = key_rows.reshape(LEN, HEADS, HEAD).transpose(1, 0, 2)
    heads_value = value_rows.reshape(LEN, HEADS, HEAD).transpose(1, 0, 2)
    block_rows = min(512, LEN)
    count_blocks = LEN // block_rows
    query_blocks = heads_query.reshape(HEADS, count_blocks, block_rows, HEAD).transpose(1, 0, 2, 3)
    key_positions = jnp.arange(LEN, dtype=jnp.int32)

    def attend_block(block_pair):
        query_block, block_index = block_pair
        query_positions = block_index * block_rows + jnp.arange(block_rows, dtype=jnp.int32)
        scores = low_back(jnp.einsum('hqe,hke->hqk', query_block, heads_key, precision=lax.Precision.HIGHEST) * HEAD ** (-0.5))
        allowed = (key_positions[None, :] <= query_positions[:, None]) & (key_positions[None, :] < length_value)
        masked = jnp.where(allowed[None], scores, masked_score)
        probs = low(jax.nn.softmax(masked, axis=-1))
        return jnp.einsum('hqk,hke->hqe', probs, heads_value, precision=lax.Precision.HIGHEST)
    outputs = lax.map(jax.checkpoint(attend_block), (query_blocks, jnp.arange(count_blocks, dtype=jnp.int32)))
    return outputs.transpose(0, 2, 1, 3).reshape(LEN, D)

def feed_forward(inputs, scale_row, shift_row, weight_up, weight_down):
    normed = low(layer_norm(inputs, scale_row, shift_row))
    upper_part = low_back(product_high(normed, weight_up))
    active = low(jax.nn.gelu(upper_part))
    return inputs + low_back(product_high(active, weight_down))

def sequence_forward(inputs, length_value, kernel, params):
    norm_gain, norm_bias, w_qkv, w_out, w_up, w_down, taps, skip = params
    positions = jnp.arange(LEN, dtype=jnp.int32)
    validity = (positions < length_value).astype(jnp.float32)[:, None]
    masked_in = inputs * validity
    normed = low(layer_norm(masked_in, norm_gain[0], norm_bias[0]))
    mixed_qkv = product_high(normed, w_qkv[0])
    queries = low_back(mixed_qkv[:, :D])
    key_rows = low(low_back(mixed_qkv[:, D:2 * D]))
    value_rows = low_back(mixed_qkv[:, 2 * D:])
    padded = jnp.pad(key_rows, ((TAPS - 1, 0), (0, 0)))
    shifted = sum((taps[offset] * padded[TAPS - 1 - offset:TAPS - 1 - offset + LEN] for offset in range(TAPS)))
    carried = low(shifted * value_rows * validity)
    spectrum = jnp.fft.rfft(carried, n=2 * LEN, axis=0)
    convolved = low_back(jnp.fft.irfft(spectrum * kernel, n=2 * LEN, axis=0)[:LEN])
    gated_rows = low(queries * (convolved + skip * carried))
    hidden = masked_in + low_back(product_high(gated_rows, w_out[0]))
    hidden = feed_forward(hidden, norm_gain[1], norm_bias[1], w_up[0], w_down[0])
    normed = low(layer_norm(hidden, norm_gain[2], norm_bias[2]))
    mixed_qkv = low(low_back(product_high(normed, w_qkv[1])))
    attended = attention(mixed_qkv[:, :D], mixed_qkv[:, D:2 * D], mixed_qkv[:, 2 * D:], length_value)
    attended = low(low_back(attended))
    hidden = hidden + low_back(product_high(attended, w_out[1]))
    hidden = feed_forward(hidden, norm_gain[3], norm_bias[3], w_up[1], w_down[1])
    return hidden * validity

def forward_all(lengths, tokens, norm_gain, norm_bias, w_qkv, w_out, w_up, w_down, taps, skip, ssm_rate, ssm_out):
    kernel_real, kernel_imag = kernel_spectrum(ssm_rate, ssm_out)
    kernel = lax.complex(kernel_real, kernel_imag)
    params = (norm_gain, norm_bias, w_qkv, w_out, w_up, w_down, taps, skip)
    flat_tokens = tokens.reshape(GROUPS * SEQS, LEN, D)
    flat_lengths = lengths.reshape(GROUPS * SEQS)

    def one_sequence(running, seq_pair):
        return (running, sequence_forward(seq_pair[0], seq_pair[1], kernel, params))
    outputs = lax.scan(one_sequence, jnp.zeros((), jnp.float32), (flat_tokens, flat_lengths))[1]
    return outputs.reshape(GROUPS, SEQS, LEN, D)

def reference(tokens, cotangent, lengths, norm_gain, norm_bias, w_qkv, w_out, w_up, w_down, taps, skip, ssm_rate, ssm_out):
    outputs, pullback = jax.vjp(partial(forward_all, lengths), tokens.astype(jnp.float32), norm_gain.astype(jnp.float32), norm_bias.astype(jnp.float32), w_qkv.astype(jnp.float32), w_out.astype(jnp.float32), w_up.astype(jnp.float32), w_down.astype(jnp.float32), taps.astype(jnp.float32), skip.astype(jnp.float32), ssm_rate.astype(jnp.float32), ssm_out.astype(jnp.float32))
    grads = pullback(cotangent.astype(jnp.float32))
    return (outputs.astype(jnp.bfloat16), grads[0], grads[1], grads[2][:3], grads[2][3], grads[3], grads[4], grads[5], grads[6], grads[7], grads[8], grads[9], grads[10])
```

```python
import functools
import math

import jax
import jax.numpy as jnp
from jax import lax
from jax.experimental import pallas as pl
from jax.experimental.pallas import tpu as pltpu
from jax.sharding import PartitionSpec as P

HEADS = 12
HEAD = 64
TAPS = 4
STATES = 64
MESH = pl.DeviceIdType.MESH
VMEM_BYTES = 60 * 2**20


norm_eps = 1e-05
highest = lax.Precision.HIGHEST
masked_score = -1e30


def for_sending(array):
    return jax.tree.map(lambda a: a.astype(jnp.bfloat16) if a.dtype == jnp.float32 else a, array)


def passed_along(value, axis, steps):
    count = lax.axis_size(axis)
    initial, last = (max(0, -steps), min(count, count - steps))
    return lax.ppermute(value, axis, [(source, source + steps) for source in range(initial, last)])


def layer_norm(inputs, scale_row, shift_row):
    center = inputs - jnp.mean(inputs, -1, keepdims=True)
    spread = jnp.mean(center * center, -1, keepdims=True)
    return center * lax.rsqrt(spread + norm_eps) * scale_row + shift_row


def dense_product(operand_a, operand_b):
    return jnp.dot(operand_a, operand_b, preferred_element_type=jnp.float32)


def product_left(operand_a, operand_b):
    return lax.dot_general(
        operand_a, operand_b, (((0,), (0,)), ((), ())), preferred_element_type=jnp.float32
    )


def product_right(operand_a, operand_b):
    return lax.dot_general(
        operand_a, operand_b, (((1,), (1,)), ((), ())), preferred_element_type=jnp.float32
    )


def angle_table(count_rows, count_cols, period):
    product_index = (
        jnp.arange(count_rows, dtype=jnp.int32)[:, None]
        * jnp.arange(count_cols, dtype=jnp.int32)[None, :]
        % period
    )
    angles = product_index.astype(jnp.float32) * (2.0 * math.pi / period)
    return (jnp.cos(angles), jnp.sin(angles))


def table_einsum(form, table, data):
    return jnp.einsum(form, table, data, precision=highest)


def forward_spectrum(time_parts):
    count_parts = time_parts.shape[0]
    span_rows = time_parts.shape[2]
    count_freq = 2 * count_parts
    cos_parts, sin_parts = angle_table(count_freq, count_parts, count_freq)
    first_real = table_einsum("fp,pjsc->fjsc", cos_parts, time_parts)
    first_imag = -table_einsum("fp,pjsc->fjsc", sin_parts, time_parts)
    cos_twist, sin_twist = angle_table(count_freq, span_rows, count_freq * span_rows)
    cos_twist = cos_twist[:, None, :, None]
    sin_twist = sin_twist[:, None, :, None]
    twist_real = first_real * cos_twist + first_imag * sin_twist
    twist_imag = first_imag * cos_twist - first_real * sin_twist
    cos_span, sin_span = angle_table(span_rows, span_rows, span_rows)
    out_real = table_einsum("ts,fjsc->fjtc", cos_span, twist_real) + table_einsum(
        "ts,fjsc->fjtc", sin_span, twist_imag
    )
    out_imag = table_einsum("ts,fjsc->fjtc", cos_span, twist_imag) - table_einsum(
        "ts,fjsc->fjtc", sin_span, twist_real
    )
    return (out_real, out_imag)


def inverse_spectrum(freq_real, freq_imag):
    count_freq = freq_real.shape[0]
    span_rows = freq_real.shape[2]
    count_parts = count_freq // 2
    fft_length = count_freq * span_rows
    cos_span, sin_span = angle_table(span_rows, span_rows, span_rows)
    first_real = table_einsum("st,fjtc->fjsc", cos_span, freq_real) - table_einsum(
        "st,fjtc->fjsc", sin_span, freq_imag
    )
    first_imag = table_einsum("st,fjtc->fjsc", cos_span, freq_imag) + table_einsum(
        "st,fjtc->fjsc", sin_span, freq_real
    )
    cos_twist, sin_twist = angle_table(count_freq, span_rows, fft_length)
    cos_twist = cos_twist[:, None, :, None]
    sin_twist = sin_twist[:, None, :, None]
    twist_real = first_real * cos_twist - first_imag * sin_twist
    twist_imag = first_imag * cos_twist + first_real * sin_twist
    cos_parts, sin_parts = angle_table(count_parts, count_freq, count_freq)
    summed = table_einsum("pf,fjsc->pjsc", cos_parts, twist_real) - table_einsum(
        "pf,fjsc->pjsc", sin_parts, twist_imag
    )
    return summed / fft_length


def to_frequency(data_low):
    parts = lax.all_to_all(data_low[None], "seq", split_axis=3, concat_axis=0, tiled=True)
    return forward_spectrum(parts.astype(jnp.float32))


def from_frequency(freq_real, freq_imag):
    time_parts = inverse_spectrum(freq_real, freq_imag)
    joined = lax.all_to_all(
        for_sending(time_parts), "seq", split_axis=0, concat_axis=3, tiled=True
    ).astype(time_parts.dtype)
    return joined[0]


def kernel_parts(rate_slice, weight_slice, count_freq, span_rows):
    fft_length = count_freq * span_rows
    length_full = fft_length // 2
    frequency = (
        jnp.arange(count_freq, dtype=jnp.int32)[:, None]
        + count_freq * jnp.arange(span_rows, dtype=jnp.int32)[None, :]
    )
    angles = (frequency.astype(jnp.float32) * (2.0 * math.pi / fft_length))[:, None, :, None, None]
    odd_mask = (frequency % 2 == 1)[:, None, :, None, None]
    channels = rate_slice.shape[0]
    blocks = rate_slice.shape[1] // 8
    rate_blocks = rate_slice.reshape(channels, blocks, 8).transpose(1, 0, 2)
    weight_blocks = weight_slice.reshape(channels, blocks, 8).transpose(1, 0, 2)

    def add_block(running, piece_pair):
        rate_part, weight_part = piece_pair
        decays = jnp.exp(-rate_part)
        half_sine = jnp.sin(angles / 2.0)
        real_den = -jnp.expm1(-rate_part) + decays * 2.0 * half_sine * half_sine
        imag_den = decays * jnp.sin(angles)
        numerator = jnp.where(
            odd_mask, 1.0 + jnp.exp(-rate_part * length_full), -jnp.expm1(-rate_part * length_full)
        )
        factor = weight_part * numerator / (real_den * real_den + imag_den * imag_den)
        return (
            (
                running[0] + jnp.sum(factor * real_den, -1),
                running[1] - jnp.sum(factor * imag_den, -1),
            ),
            None,
        )

    zeros_init = jnp.zeros((count_freq, 1, span_rows, channels), jnp.float32)
    return lax.scan(
        jax.checkpoint(add_block), (zeros_init, zeros_init), (rate_blocks, weight_blocks)
    )[0]


def attention_mask(query_positions, key_count, length_value):
    key_positions = jnp.arange(key_count, dtype=jnp.int32)
    return (key_positions[None, :] <= query_positions[:, None]) & (
        key_positions[None, :] < length_value
    )


def head_slice(matrix, head_index):
    return lax.dynamic_slice_in_dim(matrix, head_index * HEAD, HEAD, 1)


def attend_forward(query_low, keys_low, values_low, length_value, query_positions):
    whole_keys, whole_values = (
        lax.all_gather(keys_low, "seq", axis=0, tiled=True),
        lax.all_gather(values_low, "seq", axis=0, tiled=True),
    )
    allowed = attention_mask(query_positions, whole_keys.shape[0], length_value)
    score_scale = HEAD ** (-0.5)

    def head_forward(head_index):
        scores = jnp.where(
            allowed,
            score_scale
            * product_right(head_slice(query_low, head_index), head_slice(whole_keys, head_index)),
            masked_score,
        )
        top_score = jnp.max(scores, -1, keepdims=True)
        expos = jnp.exp(scores - top_score)
        totals = jnp.sum(expos, -1, keepdims=True)
        probs_low = (expos / totals).astype(jnp.bfloat16)
        return (
            dense_product(probs_low, head_slice(whole_values, head_index)),
            (top_score + jnp.log(totals))[:, 0],
        )

    head_outputs, log_totals = lax.map(head_forward, jnp.arange(HEADS, dtype=jnp.int32))
    attended = head_outputs.transpose(1, 0, 2).reshape(query_low.shape[0], HEADS * HEAD)
    return (attended, log_totals, whole_keys, whole_values)


def join_heads(head_rows):
    return head_rows.transpose(1, 0, 2).reshape(head_rows.shape[1], HEADS * HEAD)


def attend_backward(
    query_low, whole_keys, whole_values, log_totals, grad_low, length_value, query_positions
):
    allowed = attention_mask(query_positions, whole_keys.shape[0], length_value)
    score_scale = HEAD ** (-0.5)
    span_rows = query_low.shape[0]

    def query_side(head_index):
        head_query = head_slice(query_low, head_index)
        head_keys = head_slice(whole_keys, head_index)
        head_grad = head_slice(grad_low, head_index)
        scores = jnp.where(
            allowed, score_scale * product_right(head_query, head_keys), masked_score
        )
        weights = jnp.exp(scores - log_totals[head_index][:, None])
        d_weights = product_right(head_grad, head_slice(whole_values, head_index))
        row_term = jnp.sum(weights * d_weights, -1, keepdims=True)
        d_scores = (weights * (d_weights - row_term)).astype(jnp.bfloat16)
        d_query = score_scale * dense_product(d_scores, head_keys)
        return (d_query, row_term[:, 0], d_scores, weights)

    def head_backward(head_index):
        d_query, row_term, d_scores, weights = query_side(head_index)
        head_query = head_slice(query_low, head_index)
        head_grad = head_slice(grad_low, head_index)
        d_keys = score_scale * product_left(d_scores, head_query)
        d_values = product_left(weights.astype(jnp.bfloat16), head_grad)
        return (d_query, d_keys, d_values)

    query_grads, key_grads, value_grads = lax.map(head_backward, jnp.arange(HEADS, dtype=jnp.int32))
    count_rows = span_rows * lax.axis_size("seq")
    key_part = (
        lax.slice_in_dim(key_grads, 0, count_rows, axis=1)
        .transpose(1, 0, 2)
        .reshape(count_rows, HEADS * HEAD)
    )
    value_part = (
        lax.slice_in_dim(value_grads, 0, count_rows, axis=1)
        .transpose(1, 0, 2)
        .reshape(count_rows, HEADS * HEAD)
    )
    key_value = lax.psum_scatter(
        jnp.stack([key_part, value_part], 1), "seq", scatter_dimension=0, tiled=True
    )
    return (join_heads(query_grads), key_value[:, 0], key_value[:, 1])


def per_device(
    tokens,
    cotangent,
    lengths,
    norm_gain,
    norm_bias,
    w_qkv,
    w_out,
    w_up,
    w_down,
    taps,
    skip,
    ssm_rate,
    ssm_out,
):
    seq_count = tokens.shape[1]
    span_rows = tokens.shape[2]
    width = tokens.shape[3]
    devices = lax.axis_size("seq")
    place = lax.axis_index("seq")
    channels = width // devices
    count_freq = 2 * devices
    fft_length = count_freq * span_rows
    rim = TAPS - 1
    row_count = seq_count * span_rows
    query_positions = place * span_rows + jnp.arange(span_rows, dtype=jnp.int32)
    validity = (query_positions[None, :] < lengths[0][:, None]).astype(jnp.float32)[:, :, None]
    rate_slice = lax.dynamic_slice_in_dim(ssm_rate, place * channels, channels, 0)
    weight_slice = lax.dynamic_slice_in_dim(ssm_out, place * channels, channels, 0)

    def spectrum_of(rate_in, weight_in):
        return kernel_parts(rate_in, weight_in, count_freq, span_rows)

    def feed_forward(inputs, norm_row, layer):
        normed_low = layer_norm(inputs, norm_gain[norm_row], norm_bias[norm_row]).astype(
            jnp.bfloat16
        )
        raised = dense_product(normed_low, w_up[layer])
        active_low = jax.nn.gelu(raised).astype(jnp.bfloat16)
        return (normed_low, raised, active_low, inputs + dense_product(active_low, w_down[layer]))

    def norm_backward(inputs, norm_row, d_normed):
        norm_pull = jax.vjp(layer_norm, inputs, norm_gain[norm_row], norm_bias[norm_row])[1]
        return norm_pull(d_normed)

    def feed_backward(grad_rows, inputs, normed_low, raised, active_low, norm_row, layer):
        branch_low = grad_rows.astype(jnp.bfloat16)
        down_grad = product_left(active_low, branch_low)
        d_active = product_right(branch_low, w_down[layer])
        gelu_pull = jax.vjp(jax.nn.gelu, raised)[1]
        d_raised = gelu_pull(d_active)[0].astype(jnp.bfloat16)
        up_grad = product_left(normed_low, d_raised)
        d_inputs, gain_part, bias_part = norm_backward(
            inputs, norm_row, product_right(d_raised, w_up[layer])
        )
        return (grad_rows + d_inputs, down_grad, up_grad, gain_part, bias_part)

    def forward_pass(token_block):
        masked_in = token_block[0].astype(jnp.float32) * validity
        flat_in = masked_in.reshape(row_count, width)
        normed_one = layer_norm(flat_in, norm_gain[0], norm_bias[0]).astype(jnp.bfloat16)
        qkv_one = dense_product(normed_one, w_qkv[0]).reshape(seq_count, span_rows, 3 * width)
        queries_one = qkv_one[:, :, :width]
        keys_one = qkv_one[:, :, width : 2 * width].astype(jnp.bfloat16)
        values_one = qkv_one[:, :, 2 * width :]
        earlier = passed_along(keys_one[:, span_rows - rim :], "seq", 1)
        extended = jnp.concatenate([earlier, keys_one], 1)
        shifted = sum(
            (
                taps[offset]
                * extended[:, rim - offset : rim - offset + span_rows].astype(jnp.float32)
                for offset in range(TAPS)
            )
        )
        carried_low = (shifted * values_one * validity).astype(jnp.bfloat16)
        carried_real, carried_imag = to_frequency(carried_low)
        kernel_both, kernel_pull = jax.vjp(spectrum_of, rate_slice, weight_slice)
        kernel_real, kernel_imag = kernel_both
        convolved = from_frequency(
            carried_real * kernel_real - carried_imag * kernel_imag,
            carried_real * kernel_imag + carried_imag * kernel_real,
        )
        carried = carried_low.astype(jnp.float32)
        mixer = convolved + skip * carried
        gated_low = (queries_one * mixer).reshape(row_count, width).astype(jnp.bfloat16)
        hidden_one = flat_in + dense_product(gated_low, w_out[0])
        normed_two, raised_one, active_one, hidden_two = feed_forward(hidden_one, 1, 0)
        normed_three = layer_norm(hidden_two, norm_gain[2], norm_bias[2]).astype(jnp.bfloat16)
        qkv_two = (
            dense_product(normed_three, w_qkv[1])
            .astype(jnp.bfloat16)
            .reshape(seq_count, span_rows, 3 * width)
        )
        attended_list = []
        totals_list = []
        keys_list = []
        values_list = []
        for seq_index in range(seq_count):
            attended, log_totals, whole_keys, whole_values = attend_forward(
                qkv_two[seq_index, :, :width],
                qkv_two[seq_index, :, width : 2 * width],
                qkv_two[seq_index, :, 2 * width :],
                lengths[0, seq_index],
                query_positions,
            )
            attended_list.append(attended)
            totals_list.append(log_totals)
            keys_list.append(whole_keys)
            values_list.append(whole_values)
        attended_low = jnp.concatenate(attended_list, 0).astype(jnp.bfloat16)
        hidden_three = hidden_two + dense_product(attended_low, w_out[1])
        normed_four, raised_two, active_two, hidden_four = feed_forward(hidden_three, 3, 1)
        output = hidden_four.reshape(seq_count, span_rows, width) * validity
        saved = dict(
            flat_in=flat_in,
            normed_one=normed_one,
            queries_one=queries_one,
            values_one=values_one,
            extended=extended,
            shifted=shifted,
            carried=carried,
            carried_real=carried_real,
            carried_imag=carried_imag,
            kernel_real=kernel_real,
            kernel_imag=kernel_imag,
            kernel_pull=kernel_pull,
            mixer=mixer,
            gated_low=gated_low,
            hidden_one=hidden_one,
            normed_two=normed_two,
            raised_one=raised_one,
            active_one=active_one,
            hidden_two=hidden_two,
            normed_three=normed_three,
            qkv_two=qkv_two,
            totals_list=totals_list,
            keys_list=keys_list,
            values_list=values_list,
            attended_low=attended_low,
            hidden_three=hidden_three,
            normed_four=normed_four,
            raised_two=raised_two,
            active_two=active_two,
        )
        return (output, saved)

    output = forward_pass(tokens)[0]
    saved = forward_pass(lax.optimization_barrier(tokens))[1]
    grad_rows = (cotangent[0].astype(jnp.float32) * validity).reshape(row_count, width)
    grad_rows, down_two, up_two, gain_four, bias_four = feed_backward(
        grad_rows,
        saved["hidden_three"],
        saved["normed_four"],
        saved["raised_two"],
        saved["active_two"],
        3,
        1,
    )
    branch_low = grad_rows.astype(jnp.bfloat16)
    out_two = product_left(saved["attended_low"], branch_low)
    d_attended = (
        product_right(branch_low, w_out[1])
        .astype(jnp.bfloat16)
        .reshape(seq_count, span_rows, width)
    )
    qkv_two = saved["qkv_two"]
    grad_parts = []
    for seq_index in range(seq_count):
        d_query_rows, d_key_rows, d_value_rows = attend_backward(
            qkv_two[seq_index, :, :width],
            saved["keys_list"][seq_index],
            saved["values_list"][seq_index],
            saved["totals_list"][seq_index],
            d_attended[seq_index],
            lengths[0, seq_index],
            query_positions,
        )
        grad_parts.append(jnp.concatenate([d_query_rows, d_key_rows, d_value_rows], -1))
    d_qkv_two = jnp.concatenate(grad_parts, 0).astype(jnp.bfloat16)
    qkv_grad_two = product_left(saved["normed_three"], d_qkv_two)
    d_inputs, gain_three, bias_three = norm_backward(
        saved["hidden_two"], 2, product_right(d_qkv_two, w_qkv[1])
    )
    grad_rows = grad_rows + d_inputs
    grad_rows, down_one, up_one, gain_two, bias_two = feed_backward(
        grad_rows,
        saved["hidden_one"],
        saved["normed_two"],
        saved["raised_one"],
        saved["active_one"],
        1,
        0,
    )
    branch_low = grad_rows.astype(jnp.bfloat16)
    out_one = product_left(saved["gated_low"], branch_low)
    d_gated = product_right(branch_low, w_out[0]).reshape(seq_count, span_rows, width)
    d_queries = d_gated * saved["mixer"]
    d_mixer = d_gated * saved["queries_one"]
    skip_grad = jnp.sum(d_mixer * saved["carried"], (0, 1))
    conv_real, conv_imag = to_frequency(d_mixer.astype(jnp.bfloat16))
    kernel_real = saved["kernel_real"]
    kernel_imag = saved["kernel_imag"]
    from_conv = from_frequency(
        kernel_real * conv_real + kernel_imag * conv_imag,
        kernel_real * conv_imag - kernel_imag * conv_real,
    )
    d_carried = d_mixer * skip + from_conv
    carried_real = saved["carried_real"]
    carried_imag = saved["carried_imag"]
    cot_real = (
        jnp.sum(carried_real * conv_real + carried_imag * conv_imag, 1, keepdims=True) / fft_length
    )
    cot_imag = (
        jnp.sum(carried_real * conv_imag - carried_imag * conv_real, 1, keepdims=True) / fft_length
    )
    rate_grad, weight_grad = saved["kernel_pull"]((cot_real, cot_imag))
    d_shifted = d_carried * saved["values_one"] * validity
    d_values = d_carried * saved["shifted"] * validity
    extended = saved["extended"]
    grads_extended = sum(
        (
            jnp.pad(taps[offset] * d_shifted, ((0, 0), (rim - offset, offset), (0, 0)))
            for offset in range(TAPS)
        )
    )
    taps_grad = jnp.stack(
        [
            jnp.sum(
                d_shifted
                * extended[:, rim - offset : rim - offset + span_rows].astype(jnp.float32),
                (0, 1),
            )
            for offset in range(TAPS)
        ]
    )
    later = passed_along(grads_extended[:, :rim], "seq", -1)
    d_keys = grads_extended[:, rim:] + jnp.pad(later, ((0, 0), (span_rows - rim, 0), (0, 0)))
    d_qkv_one = (
        jnp.concatenate([d_queries, d_keys, d_values], -1)
        .reshape(row_count, 3 * width)
        .astype(jnp.bfloat16)
    )
    qkv_grad_one = product_left(saved["normed_one"], d_qkv_one)
    d_inputs, gain_one, bias_one = norm_backward(
        saved["flat_in"], 0, product_right(d_qkv_one, w_qkv[0])
    )
    d_tokens = ((grad_rows + d_inputs).reshape(seq_count, span_rows, width) * validity)[None]
    gain_sum, bias_sum, qkv_sum, out_sum, up_sum, down_sum, taps_sum, skip_sum = (
        lax.psum_scatter(
            jnp.stack([gain_one, gain_two, gain_three, gain_four]),
            "seq",
            scatter_dimension=1,
            tiled=True,
        ),
        lax.psum_scatter(
            jnp.stack([bias_one, bias_two, bias_three, bias_four]),
            "seq",
            scatter_dimension=1,
            tiled=True,
        ),
        lax.psum_scatter(
            jnp.stack([qkv_grad_one, qkv_grad_two]), "seq", scatter_dimension=1, tiled=True
        ),
        lax.psum_scatter(jnp.stack([out_one, out_two]), "seq", scatter_dimension=1, tiled=True),
        lax.psum_scatter(jnp.stack([up_one, up_two]), "seq", scatter_dimension=1, tiled=True),
        lax.psum_scatter(jnp.stack([down_one, down_two]), "seq", scatter_dimension=1, tiled=True),
        lax.psum_scatter(taps_grad, "seq", scatter_dimension=1, tiled=True),
        lax.psum_scatter(skip_grad[None], "seq", scatter_dimension=1, tiled=True),
    )
    totals = (
        lax.psum(gain_sum.astype(jnp.bfloat16), "batch").astype(jnp.float32),
        lax.psum(bias_sum.astype(jnp.bfloat16), "batch").astype(jnp.float32),
        lax.psum(qkv_sum.astype(jnp.bfloat16), "batch").astype(jnp.float32),
        lax.psum(out_sum.astype(jnp.bfloat16), "batch").astype(jnp.float32),
        lax.psum(up_sum.astype(jnp.bfloat16), "batch").astype(jnp.float32),
        lax.psum(down_sum.astype(jnp.bfloat16), "batch").astype(jnp.float32),
        lax.psum(taps_sum.astype(jnp.bfloat16), "batch").astype(jnp.float32),
        lax.psum(skip_sum.astype(jnp.bfloat16), "batch").astype(jnp.float32),
        lax.psum(rate_grad.astype(jnp.bfloat16), "batch").astype(jnp.float32),
        lax.psum(weight_grad.astype(jnp.bfloat16), "batch").astype(jnp.float32),
    )
    return (
        output[None].astype(jnp.bfloat16),
        d_tokens,
        totals[0],
        totals[1][:3],
        totals[1][3],
        totals[2],
        totals[3],
        totals[4],
        totals[5],
        totals[6],
        totals[7][0],
        totals[8],
        totals[9],
    )


def other_device(place, core, to_place, to_core):
    return jnp.logical_or(place != to_place, core != to_core)


def greet(devices):
    barrier = pltpu.get_barrier_semaphore()
    for device in devices:
        pl.semaphore_signal(barrier, inc=1, device_id=device, device_id_type=MESH)
    pl.semaphore_wait(barrier, len(devices))


def remote(source, target, send_sem, recv_sem, device):
    return pltpu.make_async_remote_copy(
        src_ref=source,
        dst_ref=target,
        send_sem=send_sem,
        recv_sem=recv_sem,
        device_id=device,
        device_id_type=MESH,
    )


def split_low(value):
    upper = value.astype(jnp.bfloat16)
    return upper, (value - upper.astype(jnp.float32)).astype(jnp.bfloat16)


NN = (((1,), (0,)), ((), ()))
NT = (((1,), (1,)), ((), ()))
TN = (((0,), (0,)), ((), ()))


def dot(left, right, form=NN):
    return lax.dot_general(left, right, form, preferred_element_type=jnp.float32)


def dot_fine(left, right, form=NN):
    left_up, left_low = left
    right_up, right_low = right
    total = dot(left_up, right_up, form) + dot(left_up, right_low, form)
    if left_low is not None:
        total = total + dot(left_low, right_up, form)
    return total


def state_tables(rate_row, weight_row, span):
    row = lax.broadcasted_iota(jnp.int32, (span, 2 * STATES), 0)
    lane = lax.broadcasted_iota(jnp.int32, (span, 2 * STATES), 1)
    steps = jnp.where(lane < STATES, span - 1 - row, row + 1).astype(jnp.float32)
    table = jnp.exp(-rate_row * steps)
    lane_row = lax.broadcasted_iota(jnp.int32, (8, 2 * STATES), 1)
    lead = jnp.where(lane_row < STATES, 0.0, weight_row * jnp.exp(rate_row))
    response = lax.dot_general(
        lead, table, NT, precision=highest, preferred_element_type=jnp.float32
    )[:1]
    spread = pltpu.roll(
        jnp.broadcast_to(response, (span, span)), 0, 1, stride=1, stride_axis=0
    )
    later = lax.broadcasted_iota(jnp.int32, (span, span), 1)
    earlier = lax.broadcasted_iota(jnp.int32, (span, span), 0)
    toeplitz = jnp.where(later >= earlier, spread, 0.0)
    return table, steps, toeplitz


def shift_rows(value, count):
    if count > 0:
        return jnp.concatenate([jnp.zeros_like(value[:count]), value[:-count]], 0)
    return jnp.concatenate([value[-count:], jnp.zeros_like(value[:-count])], 0)


def scan_states(value, decay, seqs, blocks, direction):
    step = 1
    while step < blocks:
        value = value + shift_rows(value, direction * step * seqs) * jnp.exp(decay * step)
        step *= 2
    return shift_rows(value, direction * seqs)


def mixer_forward_kernel(
    n, seqs, span, channels, unroll,
    x_ref, rate_ref, weight_ref, y_ref, held_ref,
    flat, flat_out, answer, send, recv, back_send, back_recv, own_sem,
):
    me, core = lax.axis_index("seq"), lax.axis_index("batch")
    peers = [lax.rem(me + step, n) for step in range(1, n)]
    greet([(peer, core) for peer in peers])
    outgoing = []
    for step, peer in enumerate(peers):
        rows = pl.ds(pl.multiple_of(peer * channels, 16), channels)
        copy = remote(
            x_ref.at[:, rows, :], held_ref.at[me], send.at[step], recv.at[step], (peer, core)
        )
        copy.start()
        outgoing.append(copy)
    own_rows = pl.ds(pl.multiple_of(me * channels, 16), channels)
    own = pltpu.make_async_copy(x_ref.at[:, own_rows, :], held_ref.at[me], own_sem.at[0])
    own.start()
    own.wait()
    for copy in outgoing:
        copy.wait()
    total_rows = n * seqs * channels
    flat[...] = held_ref[...].astype(jnp.float32).reshape(total_rows, span)

    def one_channel(channel, carry):
        rate_row = rate_ref[pl.ds(channel, 1), :]
        weight_row = weight_ref[pl.ds(channel, 1), :]
        table, _, toeplitz = state_tables(rate_row, weight_row, span)
        rows = pl.ds(channel, n * seqs, stride=channels)
        data = (flat[rows, :].astype(jnp.bfloat16), None)
        table_parts = split_low(table)
        inner = dot_fine(data, split_low(toeplitz))
        states = dot_fine(data, table_parts)
        states = scan_states(states, -span * rate_row, seqs, n, 1)
        lane = lax.broadcasted_iota(jnp.int32, states.shape, 1)
        weighted = jnp.where(lane < STATES, 0.0, pltpu.roll(states, STATES, 1) * weight_row)
        flat_out[rows, :] = inner + dot_fine(split_low(weighted), table_parts, NT)
        return carry

    lax.fori_loop(0, channels, one_channel, 0, unroll=unroll)
    answer[...] = flat_out[...].reshape(n, seqs, channels, span).astype(jnp.bfloat16)
    outgoing = []
    for step, peer in enumerate(peers):
        copy = remote(
            answer.at[peer], y_ref.at[:, own_rows, :], back_send.at[step], back_recv.at[step],
            (peer, core),
        )
        copy.start()
        outgoing.append(copy)
    own = pltpu.make_async_copy(answer.at[me], y_ref.at[:, own_rows, :], own_sem.at[1])
    own.start()
    own.wait()
    for copy in outgoing:
        copy.wait()


def mixer_forward(x, rates, weights, n, collective):
    seqs, width, span = x.shape
    channels = width // n
    total_rows = n * seqs * channels
    vmem = pl.BlockSpec(memory_space=pltpu.VMEM)
    return pl.pallas_call(
        functools.partial(mixer_forward_kernel, n, seqs, span, channels, 4),
        out_shape=(
            jax.ShapeDtypeStruct(x.shape, jnp.bfloat16),
            jax.ShapeDtypeStruct((n, seqs, channels, span), jnp.bfloat16),
        ),
        in_specs=[vmem] * 3,
        out_specs=(vmem, vmem),
        scratch_shapes=[
            pltpu.VMEM((total_rows, span), jnp.float32),
            pltpu.VMEM((total_rows, span), jnp.float32),
            pltpu.VMEM((n, seqs, channels, span), jnp.bfloat16),
            pltpu.SemaphoreType.DMA((n - 1,)),
            pltpu.SemaphoreType.DMA((n - 1,)),
            pltpu.SemaphoreType.DMA((n - 1,)),
            pltpu.SemaphoreType.DMA((n - 1,)),
            pltpu.SemaphoreType.DMA((2,)),
        ],
        compiler_params=pltpu.CompilerParams(
            collective_id=collective, has_side_effects=True, vmem_limit_bytes=VMEM_BYTES
        ),
    )(x, rates, weights)


def mixer_backward_kernel(
    n, seqs, span, channels, unroll,
    d_ref, held_ref, rate_ref, weight_ref, dx_ref, rate_grad_ref, weight_grad_ref,
    landing, flat_x, flat_d, flat_out, answer,
    send, recv, back_send, back_recv, own_sem,
):
    me, core = lax.axis_index("seq"), lax.axis_index("batch")
    peers = [lax.rem(me + step, n) for step in range(1, n)]
    greet([(peer, core) for peer in peers])
    outgoing = []
    for step, peer in enumerate(peers):
        rows = pl.ds(pl.multiple_of(peer * channels, 16), channels)
        copy = remote(
            d_ref.at[:, rows, :], landing.at[me], send.at[step], recv.at[step], (peer, core)
        )
        copy.start()
        outgoing.append(copy)
    own_rows = pl.ds(pl.multiple_of(me * channels, 16), channels)
    own = pltpu.make_async_copy(d_ref.at[:, own_rows, :], landing.at[me], own_sem.at[0])
    own.start()
    total_rows = n * seqs * channels
    flat_x[...] = held_ref[...].astype(jnp.float32).reshape(total_rows, span)
    own.wait()
    for copy in outgoing:
        copy.wait()
    flat_d[...] = landing[...].astype(jnp.float32).reshape(total_rows, span)

    def one_channel(channel, carry):
        rate_row = rate_ref[pl.ds(channel, 1), :]
        weight_row = weight_ref[pl.ds(channel, 1), :]
        table, steps, toeplitz = state_tables(rate_row, weight_row, span)
        rows = pl.ds(channel, n * seqs, stride=channels)
        data = flat_x[rows, :].astype(jnp.bfloat16)
        grad = flat_d[rows, :].astype(jnp.bfloat16)
        table_parts = split_low(table)
        both_parts = split_low(jnp.concatenate([table, table * steps], 1))
        count = n * seqs
        sides = dot_fine((jnp.concatenate([data, grad], 0), None), both_parts)
        lane = lax.broadcasted_iota(jnp.int32, (count, 2 * STATES), 1)
        low_lanes = lane < STATES

        def aligned(value):
            return jnp.where(low_lanes, pltpu.roll(value, STATES, 1), 0.0)

        entering = jnp.where(low_lanes, sides[:count, : 2 * STATES], 0.0)
        entering_steps = jnp.where(low_lanes, sides[:count, 2 * STATES :], 0.0)
        leaving = aligned(sides[count:, : 2 * STATES])
        leaving_steps = aligned(sides[count:, 2 * STATES :])
        decay = -span * rate_row
        states = scan_states(entering, decay, seqs, n, 1)
        states_steps = scan_states(states * jnp.exp(decay), decay, seqs, n, 1)
        returned = scan_states(leaving, decay, seqs, n, -1)
        far_weight = jnp.sum(leaving * states, 0, keepdims=True)
        far_rate = jnp.sum(
            leaving_steps * states + returned * entering_steps + span * (leaving * states_steps),
            0, keepdims=True,
        )
        cross = dot(data, grad, TN)
        later = lax.broadcasted_iota(jnp.int32, (span, span), 1)
        earlier = lax.broadcasted_iota(jnp.int32, (span, span), 0)
        cross = jnp.where(later >= earlier, cross, 0.0)
        met = dot_fine(split_low(cross), both_parts, TN)
        met_plain = pltpu.roll(met[:, : 2 * STATES], STATES, 1)
        met_steps = pltpu.roll(met[:, 2 * STATES :], STATES, 1)
        rise = jnp.exp(span * rate_row)
        near_weight = rise * jnp.sum(table * met_plain, 0, keepdims=True)
        near_rate = rise * jnp.sum(
            table * ((steps - span) * met_plain + met_steps), 0, keepdims=True
        )
        lane_row = lane[:1]
        near_weight = jnp.where(lane_row < STATES, pltpu.roll(near_weight, STATES, 1), 0.0)
        near_rate = jnp.where(lane_row < STATES, pltpu.roll(near_rate, STATES, 1), 0.0)
        weight_grad_ref[pl.ds(channel, 1), :] = near_weight + far_weight
        rate_grad_ref[pl.ds(channel, 1), :] = -weight_row * (near_rate + far_rate)
        inner = dot_fine((grad, None), split_low(toeplitz), NT)
        weighted = returned * weight_row
        flat_out[rows, :] = inner + dot_fine(split_low(weighted), table_parts, NT)
        return carry

    lax.fori_loop(0, channels, one_channel, 0, unroll=unroll)
    answer[...] = flat_out[...].reshape(n, seqs, channels, span).astype(jnp.bfloat16)
    outgoing = []
    for step, peer in enumerate(peers):
        copy = remote(
            answer.at[peer], dx_ref.at[:, own_rows, :], back_send.at[step], back_recv.at[step],
            (peer, core),
        )
        copy.start()
        outgoing.append(copy)
    own = pltpu.make_async_copy(answer.at[me], dx_ref.at[:, own_rows, :], own_sem.at[1])
    own.start()
    own.wait()
    for copy in outgoing:
        copy.wait()


def mixer_backward(d, held, rates, weights, n, collective):
    seqs, width, span = d.shape
    channels = width // n
    total_rows = n * seqs * channels
    vmem = pl.BlockSpec(memory_space=pltpu.VMEM)
    return pl.pallas_call(
        functools.partial(mixer_backward_kernel, n, seqs, span, channels, 2),
        out_shape=(
            jax.ShapeDtypeStruct(d.shape, jnp.bfloat16),
            jax.ShapeDtypeStruct((channels, 2 * STATES), jnp.float32),
            jax.ShapeDtypeStruct((channels, 2 * STATES), jnp.float32),
        ),
        in_specs=[vmem] * 4,
        out_specs=(vmem, vmem, vmem),
        scratch_shapes=[
            pltpu.VMEM((n, seqs, channels, span), jnp.bfloat16),
            pltpu.VMEM((total_rows, span), jnp.float32),
            pltpu.VMEM((total_rows, span), jnp.float32),
            pltpu.VMEM((total_rows, span), jnp.float32),
            pltpu.VMEM((n, seqs, channels, span), jnp.bfloat16),
            pltpu.SemaphoreType.DMA((n - 1,)),
            pltpu.SemaphoreType.DMA((n - 1,)),
            pltpu.SemaphoreType.DMA((n - 1,)),
            pltpu.SemaphoreType.DMA((n - 1,)),
            pltpu.SemaphoreType.DMA((2,)),
        ],
        compiler_params=pltpu.CompilerParams(
            collective_id=collective, has_side_effects=True, vmem_limit_bytes=VMEM_BYTES
        ),
    )(d, held, rates, weights)


def block_of(index, core):
    return 2 * index + lax.rem(index + core, 2)


def keeper_of(block):
    return lax.rem((block + 1) // 2, 2)


class HeadPlaces:
    def __init__(self, n, seqs, groups):
        self.n, self.seqs, self.groups = n, seqs, groups
        self.me, self.core = lax.axis_index("seq"), lax.axis_index("batch")
        self.group = self.me // (2 * seqs)
        self.seq = lax.rem(self.me // 2, seqs)
        self.batch = lax.rem(self.me, 2)
        self.keeper = keeper_of(self.me)
        self.sibling = (self.me, 1 - self.core)
        self.targets = [
            ((group * 2 * seqs + seq * 2 + self.core, self.keeper), seq, group)
            for seq in range(seqs)
            for group in range(groups)
        ]
        self.blocks = [block_of(index, self.core) for index in range(n // 2)]
        self.sources = [(block, self.batch) for block in self.blocks]

    def is_other(self, device):
        return jnp.logical_or(device[0] != self.me, device[1] != self.core)

    def greet(self):
        barrier = pltpu.get_barrier_semaphore()
        others = [target for target, _, _ in self.targets] + self.sources
        for device in others:

            @pl.when(self.is_other(device))
            def _():
                pl.semaphore_signal(barrier, inc=1, device_id=device, device_id_type=MESH)

        pl.semaphore_signal(barrier, inc=1, device_id=self.sibling, device_id_type=MESH)
        kept = jnp.logical_and(self.batch == self.core, self.is_kept_here())
        pl.semaphore_wait(barrier, len(others) + 1 - 2 * kept.astype(jnp.int32))

    def is_kept_here(self):
        return self.keeper == self.core

    def send(self, source, target, send_sem, recv_sem, device):
        @pl.when(self.is_other(device))
        def _():
            remote(source, target, send_sem, recv_sem, device).start()

        @pl.when(jnp.logical_not(self.is_other(device)))
        def _():
            pltpu.make_async_copy(source, target, recv_sem).start()

    def wait_sent(self, source, target, send_sem, recv_sem, device):
        @pl.when(self.is_other(device))
        def _():
            remote(source, target, send_sem, recv_sem, device).wait_send()


def fill_heads(held, head, first, n, span, rows_out, columns_out):
    start = pl.multiple_of(first + head * HEAD, HEAD)
    for block in range(n):
        part = held[block, pl.ds(start, HEAD), :]
        if rows_out is not None:
            rows_out[block * span : (block + 1) * span, :] = part.T
        if columns_out is not None:
            columns_out[:, block * span : (block + 1) * span] = part


def causal(first_key, rows, first_query, span):
    key = first_key + lax.broadcasted_iota(jnp.int32, (rows, span), 0)
    query = first_query + lax.broadcasted_iota(jnp.int32, (rows, span), 1)
    return key <= query


def attention_forward_kernel(
    n, seqs, groups, span, group_rows,
    qkv_ref, out_ref, held, lse_ref,
    outputs, key_rows, value_columns,
    send, recv, pass_send, pass_recv, back_send, back_recv,
):
    at = HeadPlaces(n, seqs, groups)
    half = n // 2
    at.greet()
    for count, (device, seq, group) in enumerate(at.targets):
        at.send(qkv_ref.at[seq, group], held.at[at.me], send.at[count], recv.at[at.me // 2], device)
    passed = []
    for index, block in enumerate(at.blocks):
        remote(held.at[block], held.at[block], send.at[0], recv.at[index], at.sibling).wait_recv()
        part = held.at[block, group_rows : 3 * group_rows, :]
        copy = remote(part, part, pass_send.at[index], pass_recv.at[index], at.sibling)
        copy.start()
        passed.append(copy)
    for copy in passed:
        copy.wait()
    for count, (device, seq, group) in enumerate(at.targets):
        at.wait_sent(
            qkv_ref.at[seq, group], held.at[at.me], send.at[count], recv.at[at.me // 2], device
        )

    def one_head(head, carry):
        fill_heads(held, head, group_rows, n, span, key_rows, None)
        fill_heads(held, head, 2 * group_rows, n, span, None, value_columns)
        query_rows = pl.ds(pl.multiple_of(head * HEAD, HEAD), HEAD)
        for index, block in enumerate(at.blocks):
            query = held[block, query_rows, :] * jnp.bfloat16(HEAD**-0.5)
            clear, reach = 2 * index * span, 2 * (index + 1) * span
            edge = dot(key_rows[clear:reach, :], query)
            edge = jnp.where(causal(clear, reach - clear, block * span, span), edge, masked_score)
            top = jnp.max(edge, 0, keepdims=True)
            if index > 0:
                body = dot(key_rows[:clear, :], query)
                top = jnp.maximum(top, jnp.max(body, 0, keepdims=True))
            edge = jnp.exp(edge - top)
            total = jnp.sum(edge, 0, keepdims=True)
            result = dot(value_columns[:, clear:reach], edge.astype(jnp.bfloat16))
            if index > 0:
                body = jnp.exp(body - top)
                total = total + jnp.sum(body, 0, keepdims=True)
                result = result + dot(value_columns[:, :clear], body.astype(jnp.bfloat16))
            outputs[index, query_rows, :] = (result / total).astype(jnp.bfloat16)
            lse_ref[index, pl.ds(head, 1), :] = top + jnp.log(total)
        return carry

    lax.fori_loop(0, group_rows // HEAD, one_head, 0)
    into = pl.ds(pl.multiple_of(at.group * group_rows, 16), group_rows)
    slot = at.seq * groups + at.group
    for index, device in enumerate(at.sources):
        at.send(
            outputs.at[index], out_ref.at[at.seq, into, :], back_send.at[index],
            back_recv.at[slot], device,
        )
    for count, (device, seq, group) in enumerate(at.targets):
        landed = out_ref.at[seq, group * group_rows : (group + 1) * group_rows, :]
        remote(landed, landed, back_send.at[0], back_recv.at[count], at.sibling).wait_recv()
    for index, device in enumerate(at.sources):
        at.wait_sent(
            outputs.at[index], out_ref.at[at.seq, into, :], back_send.at[index],
            back_recv.at[slot], device,
        )


def attention_forward(qkv, n, collective):
    seqs, groups, rows, span = qkv.shape
    group_rows = rows // 3
    half = n // 2
    vmem = pl.BlockSpec(memory_space=pltpu.VMEM)
    dma = pltpu.SemaphoreType.DMA
    return pl.pallas_call(
        functools.partial(attention_forward_kernel, n, seqs, groups, span, group_rows),
        out_shape=(
            jax.ShapeDtypeStruct((seqs, groups * group_rows, span), jnp.bfloat16),
            jax.ShapeDtypeStruct((n, rows, span), jnp.bfloat16),
            jax.ShapeDtypeStruct((half, group_rows // HEAD, span), jnp.float32),
        ),
        in_specs=[vmem],
        out_specs=(vmem, vmem, vmem),
        scratch_shapes=[
            pltpu.VMEM((half, group_rows, span), jnp.bfloat16),
            pltpu.VMEM((n * span, HEAD), jnp.bfloat16),
            pltpu.VMEM((HEAD, n * span), jnp.bfloat16),
            dma((seqs * groups,)),
            dma((half,)),
            dma((half,)),
            dma((half,)),
            dma((half,)),
            dma((seqs * groups,)),
        ],
        compiler_params=pltpu.CompilerParams(
            collective_id=collective, has_side_effects=True, vmem_limit_bytes=VMEM_BYTES
        ),
    )(qkv)


def attention_backward_kernel(
    n, seqs, groups, span, group_rows,
    d_ref, held, lse_ref, out_ref,
    landing, results, partial_send, partial_recv, key_grads, value_grads,
    key_rows, key_columns, value_rows,
    send, recv, pass_send, pass_recv, back_send, back_recv,
):
    at = HeadPlaces(n, seqs, groups)
    half = n // 2
    at.greet()
    own_rows = [
        d_ref.at[seq, group * group_rows : (group + 1) * group_rows, :]
        for _, seq, group in at.targets
    ]
    for count, (device, seq, group) in enumerate(at.targets):
        at.send(
            own_rows[count], landing.at[at.me // 2], send.at[count], recv.at[at.me // 2], device
        )
    for index in range(half):
        remote(
            landing.at[index], landing.at[index], send.at[0], recv.at[index], at.sibling
        ).wait_recv()
    for count, (device, seq, group) in enumerate(at.targets):
        at.wait_sent(
            own_rows[count], landing.at[at.me // 2], send.at[count], recv.at[at.me // 2], device
        )

    def one_head(head, carry):
        fill_heads(held, head, group_rows, n, span, key_rows, key_columns)
        fill_heads(held, head, 2 * group_rows, n, span, value_rows, None)
        head_rows = pl.ds(pl.multiple_of(head * HEAD, HEAD), HEAD)
        key_grads[head_rows, :] = jnp.zeros((HEAD, n * span), jnp.float32)
        value_grads[head_rows, :] = jnp.zeros((HEAD, n * span), jnp.float32)
        for index, block in enumerate(at.blocks):
            query = held[block, head_rows, :] * jnp.bfloat16(HEAD**-0.5)
            grad = landing[index, head_rows, :]
            log_total = lse_ref[index, pl.ds(head, 1), :]
            clear, reach = 2 * index * span, 2 * (index + 1) * span
            pieces = []
            row_term = jnp.zeros((1, span), jnp.float32)
            for first, last in ((0, clear), (clear, reach)):
                if first == last:
                    continue
                scores = dot(key_rows[first:last, :], query)
                if last == reach:
                    scores = jnp.where(
                        causal(clear, reach - clear, block * span, span), scores, masked_score
                    )
                weights = jnp.exp(scores - log_total)
                d_weights = dot(value_rows[first:last, :], grad)
                row_term = row_term + jnp.sum(weights * d_weights, 0, keepdims=True)
                pieces.append((first, last, weights, d_weights))
            d_query = jnp.zeros((HEAD, span), jnp.float32)
            for first, last, weights, d_weights in pieces:
                d_scores = (weights * (d_weights - row_term)).astype(jnp.bfloat16)
                d_query = d_query + dot(key_columns[:, first:last], d_scores)
                key_grads[head_rows, first:last] += dot(query, d_scores, NT)
                value_grads[head_rows, first:last] += dot(grad, weights.astype(jnp.bfloat16), NT)
            results[index, head_rows, :] = (d_query * HEAD**-0.5).astype(jnp.bfloat16)
        return carry

    lax.fori_loop(0, group_rows // HEAD, one_head, 0)
    passed = []
    for index in range(half):
        other = block_of(index, 1 - at.core)
        place = pl.ds(pl.multiple_of(other * span, span), span)
        partial_send[index, :group_rows, :] = key_grads[:, place].astype(jnp.bfloat16)
        partial_send[index, group_rows:, :] = value_grads[:, place].astype(jnp.bfloat16)
        copy = remote(
            partial_send.at[index], partial_recv.at[index], pass_send.at[index],
            pass_recv.at[index], at.sibling,
        )
        copy.start()
        passed.append(copy)
    slot = at.seq * groups + at.group
    for index, device in enumerate(at.sources):
        passed[index].wait_recv()
        place = pl.ds(pl.multiple_of(at.blocks[index] * span, span), span)
        results[index, group_rows : 2 * group_rows, :] = (
            key_grads[:, place] + partial_recv[index, :group_rows, :].astype(jnp.float32)
        ).astype(jnp.bfloat16)
        results[index, 2 * group_rows :, :] = (
            value_grads[:, place] + partial_recv[index, group_rows:, :].astype(jnp.float32)
        ).astype(jnp.bfloat16)
        at.send(
            results.at[index], out_ref.at[at.seq, at.group], back_send.at[index],
            back_recv.at[slot], device,
        )
    for count, (device, seq, group) in enumerate(at.targets):
        landed = out_ref.at[seq, group]
        remote(landed, landed, back_send.at[0], back_recv.at[count], at.sibling).wait_recv()
    for index, device in enumerate(at.sources):
        passed[index].wait_send()
        at.wait_sent(
            results.at[index], out_ref.at[at.seq, at.group], back_send.at[index],
            back_recv.at[slot], device,
        )


def attention_backward(d, held, lse, seqs, groups, collective):
    n, rows, span = held.shape
    group_rows = rows // 3
    half = n // 2
    vmem = pl.BlockSpec(memory_space=pltpu.VMEM)
    dma = pltpu.SemaphoreType.DMA
    return pl.pallas_call(
        functools.partial(attention_backward_kernel, n, seqs, groups, span, group_rows),
        out_shape=jax.ShapeDtypeStruct((seqs, groups, rows, span), jnp.bfloat16),
        in_specs=[vmem] * 3,
        out_specs=vmem,
        scratch_shapes=[
            pltpu.VMEM((half, group_rows, span), jnp.bfloat16),
            pltpu.VMEM((half, rows, span), jnp.bfloat16),
            pltpu.VMEM((half, 2 * group_rows, span), jnp.bfloat16),
            pltpu.VMEM((half, 2 * group_rows, span), jnp.bfloat16),
            pltpu.VMEM((group_rows, n * span), jnp.float32),
            pltpu.VMEM((group_rows, n * span), jnp.float32),
            pltpu.VMEM((n * span, HEAD), jnp.bfloat16),
            pltpu.VMEM((HEAD, n * span), jnp.bfloat16),
            pltpu.VMEM((n * span, HEAD), jnp.bfloat16),
            dma((seqs * groups,)),
            dma((half,)),
            dma((half,)),
            dma((half,)),
            dma((half,)),
            dma((seqs * groups,)),
        ],
        compiler_params=pltpu.CompilerParams(
            collective_id=collective, has_side_effects=True, vmem_limit_bytes=VMEM_BYTES
        ),
    )(d, held, lse)


TILE = 384


class GradientPart:
    def __init__(self, weight, first_column, columns, axis):
        self.weight, self.first_column, self.columns, self.axis = (
            weight, first_column, columns, axis,
        )


def gradient_parts(half_columns):
    qkv_half, out_half, up_half, down_half = half_columns
    return [
        GradientPart(2, 0, up_half, 0),
        GradientPart(3, 0, down_half, 1),
        GradientPart(1, 0, out_half, 0),
        GradientPart(0, TILE, qkv_half - TILE, 1),
        GradientPart(0, 0, TILE, 0),
    ]


def weight_gradient_kernel(depth, slices, half_columns, tokens, *refs):
    count = len(half_columns)
    parts = gradient_parts(half_columns)
    pieces = len(parts)
    refs = list(refs)

    def take(number):
        taken = refs[:number]
        del refs[:number]
        return taken

    left, right, outs = take(count), take(count), take(count)
    left_other, right_other = take(count), take(count)
    away, arrived, home = take(pieces), take(pieces), take(pieces)
    away_two, arrived_two = take(pieces), take(pieces)
    away_three, arrived_three = take(pieces), take(pieces)
    pair_send, pair_recv, one_send, one_recv, two_send, two_recv, three_send, three_recv = take(8)
    last_send, last_recv = take(2)

    me, core = lax.axis_index("seq"), lax.axis_index("batch")
    level, spot = me // 4, (me // 2 % 2, me % 2)
    across = [level * 4 + spot[0] * 2 + (1 - spot[1]), level * 4 + (1 - spot[0]) * 2 + spot[1]]
    sibling = (me, 1 - core)
    levels = [lax.rem(level + step, depth) for step in range(1, depth)]
    columns_up = [(other * 4 + spot[0] * 2 + spot[1], core) for other in levels]
    greet([sibling, (across[0], core), (across[1], core)] + columns_up)

    exchanged = []
    for weight in range(count):
        half = half_columns[weight]
        theirs = pl.ds(pl.multiple_of((1 - core) * half, 128), half)
        for number, (source, target) in enumerate(
            ((left[weight], left_other[weight]), (right[weight].at[:, theirs], right_other[weight]))
        ):
            slot = 2 * weight + number
            copy = remote(source, target, pair_send.at[slot], pair_recv.at[slot], sibling)
            copy.start()
            exchanged.append(copy)

    def rows_of(ref, part, outer, inner, first):
        mixed = inner * 2 + first if part.axis == 0 else first * 2 + inner
        return ref[outer * 4 + mixed]

    def product(part, first, outers, column):
        half = half_columns[part.weight]
        places = [(outer, inner) for outer in outers for inner in range(2)]
        mine = jnp.concatenate(
            [rows_of(left[part.weight], part, *place, first) for place in places], 0
        )
        other = jnp.concatenate(
            [rows_of(left_other[part.weight], part, *place, first) for place in places], 0
        )
        own = pl.ds(pl.multiple_of(core * half + part.first_column + column, 128), TILE)
        there = pl.ds(pl.multiple_of(part.first_column + column, 128), TILE)
        return dot(mine, right[part.weight][:, own]) + dot(other, right_other[part.weight][:, there])

    def fill(part, first, buffer, kind):
        rows = slices[part.weight]
        outers = [[outer] for outer in range(depth)] if rows * 2 >= TILE else [list(range(depth))]

        def one_column(tile, carry):
            column = tile * TILE
            for group in outers:
                value = product(part, first, group, column)
                buffer[group[0] : group[-1] + 1, :, :, pl.ds(pl.multiple_of(column, 128), TILE)] = (
                    value.reshape(len(group), 2, rows, TILE).astype(kind)
                )
            return carry

        lax.fori_loop(0, part.columns // TILE, one_column, 0)

    waited = set()
    stage_one = []
    for number, part in enumerate(parts):
        for slot in (2 * part.weight, 2 * part.weight + 1):
            if slot not in waited:
                exchanged[slot].wait_recv()
                waited.add(slot)
        mine = spot[1 - part.axis]
        fill(part, 1 - mine, away[number], jnp.bfloat16)
        copy = remote(
            away[number], arrived[number], one_send.at[number], one_recv.at[number],
            (across[part.axis], core),
        )
        copy.start()
        stage_one.append(copy)
        fill(part, mine, home[number], jnp.float32)

    stage_two = []
    for number, part in enumerate(parts):
        stage_one[number].wait_recv()
        mine = spot[part.axis]
        for outer in range(depth):
            away_two[number][outer] = (
                home[number][outer, 1 - mine] + arrived[number][outer, 1 - mine].astype(jnp.float32)
            ).astype(jnp.bfloat16)
        copy = remote(
            away_two[number], arrived_two[number], two_send.at[number], two_recv.at[number],
            (across[1 - part.axis], core),
        )
        copy.start()
        stage_two.append(copy)
        for outer in range(depth):
            home[number][outer, mine] += arrived[number][outer, mine].astype(jnp.float32)

    stage_three = []
    for number, part in enumerate(parts):
        stage_two[number].wait_recv()
        mine = spot[part.axis]
        copies = []
        for step, other in enumerate(levels):
            away_three[number][step] = (
                home[number][other, mine] + arrived_two[number][other].astype(jnp.float32)
            ).astype(jnp.bfloat16)
            slot = number * (depth - 1) + step
            copy = remote(
                away_three[number].at[step], arrived_three[number].at[step], three_send.at[slot],
                three_recv.at[slot], columns_up[step],
            )
            copy.start()
            copies.append(copy)
        stage_three.append(copies)

    last = []
    for number, part in enumerate(parts):
        mine = spot[part.axis]
        total = home[number][level, mine] + arrived_two[number][level].astype(jnp.float32)
        for step in range(depth - 1):
            stage_three[number][step].wait_recv()
            total = total + arrived_three[number][step].astype(jnp.float32)
        place = pl.ds(
            pl.multiple_of(core * half_columns[part.weight] + part.first_column, 128), part.columns
        )
        outs[part.weight][:, place] = total
        filled = outs[part.weight].at[:, place]
        copy = remote(filled, filled, last_send.at[number], last_recv.at[number], sibling)
        copy.start()
        last.append(copy)
    for copy in last:
        copy.wait()
    for copy in exchanged + stage_one + stage_two:
        copy.wait_send()
    for copies in stage_three:
        for copy in copies:
            copy.wait_send()


def weight_gradients(left, right, depth, collective):
    tokens = right[0].shape[0]
    half_columns = tuple(array.shape[1] // 2 for array in right)
    slices = tuple(array.shape[1] for array in left)
    parts = gradient_parts(half_columns)
    vmem = pl.BlockSpec(memory_space=pltpu.VMEM)
    low, wide = jnp.bfloat16, jnp.float32
    dma = pltpu.SemaphoreType.DMA

    def shapes(extent, kind):
        return [
            pltpu.VMEM((*extent, slices[part.weight], part.columns), kind) for part in parts
        ]

    count = len(parts)
    return pl.pallas_call(
        functools.partial(weight_gradient_kernel, depth, slices, half_columns, tokens),
        out_shape=tuple(
            jax.ShapeDtypeStruct((rows, 2 * half), wide)
            for rows, half in zip(slices, half_columns)
        ),
        in_specs=[vmem] * (len(left) + len(right)),
        out_specs=(vmem,) * len(left),
        scratch_shapes=[pltpu.VMEM(array.shape, low) for array in left]
        + [pltpu.VMEM((tokens, half), low) for half in half_columns]
        + shapes((depth, 2), low)
        + shapes((depth, 2), low)
        + shapes((depth, 2), wide)
        + shapes((depth,), low)
        + shapes((depth,), low)
        + shapes((depth - 1,), low)
        + shapes((depth - 1,), low)
        + [dma((2 * len(left),)), dma((2 * len(left),))]
        + [dma((count,))] * 4
        + [dma((count * (depth - 1),))] * 2
        + [dma((count,))] * 2,
        compiler_params=pltpu.CompilerParams(
            collective_id=collective, has_side_effects=True, vmem_limit_bytes=VMEM_BYTES
        ),
    )(*left, *right)


def per_device_by_heads(
    tokens,
    cotangent,
    lengths,
    norm_gain,
    norm_bias,
    w_qkv,
    w_out,
    w_up,
    w_down,
    taps,
    skip,
    ssm_rate,
    ssm_out,
):
    seq_count, span_rows, width = tokens.shape[1:]
    devices = lax.axis_size("seq")
    place = lax.axis_index("seq")
    channels = width // devices
    depth = devices // 4
    groups = depth
    rim = TAPS - 1
    row_count = seq_count * span_rows
    positions = place * span_rows + jnp.arange(span_rows, dtype=jnp.int32)
    validity = (positions[None, :] < lengths[0][:, None]).astype(jnp.float32)[:, :, None]
    rates = lax.dynamic_slice_in_dim(ssm_rate, place * channels, channels, 0)
    weights = lax.dynamic_slice_in_dim(ssm_out, place * channels, channels, 0)
    rates = jnp.concatenate([rates, rates], 1)
    weights = jnp.concatenate([weights, weights], 1)

    def to_channels(value):
        return value.transpose(0, 2, 1)

    def feed_forward(inputs, norm_row, layer):
        normed = layer_norm(inputs, norm_gain[norm_row], norm_bias[norm_row]).astype(jnp.bfloat16)
        raised = dense_product(normed, w_up[layer])
        active = jax.nn.gelu(raised).astype(jnp.bfloat16)
        return normed, raised, active, inputs + dense_product(active, w_down[layer])

    def norm_backward(inputs, norm_row, d_normed):
        pull = jax.vjp(layer_norm, inputs, norm_gain[norm_row], norm_bias[norm_row])[1]
        return pull(d_normed)

    def feed_backward(grad_rows, inputs, raised, norm_row, layer):
        branch = grad_rows.astype(jnp.bfloat16)
        d_active = product_right(branch, w_down[layer])
        d_raised = jax.vjp(jax.nn.gelu, raised)[1](d_active)[0].astype(jnp.bfloat16)
        d_inputs, gain_part, bias_part = norm_backward(
            inputs, norm_row, product_right(d_raised, w_up[layer])
        )
        return grad_rows + d_inputs, branch, d_raised, gain_part, bias_part

    flat_in = (tokens[0].astype(jnp.float32) * validity).reshape(row_count, width)
    normed_one = layer_norm(flat_in, norm_gain[0], norm_bias[0]).astype(jnp.bfloat16)
    qkv_one = dense_product(normed_one, w_qkv[0]).reshape(seq_count, span_rows, 3 * width)
    queries_one = qkv_one[:, :, :width]
    keys_one = qkv_one[:, :, width : 2 * width].astype(jnp.bfloat16)
    values_one = qkv_one[:, :, 2 * width :]
    earlier = passed_along(keys_one[:, span_rows - rim :], "seq", 1)
    extended = jnp.concatenate([earlier, keys_one], 1)

    def tap_rows(offset):
        return extended[:, rim - offset : rim - offset + span_rows].astype(jnp.float32)

    shifted = sum((taps[offset] * tap_rows(offset) for offset in range(TAPS)))
    carried_low = (shifted * values_one * validity).astype(jnp.bfloat16)
    convolved, held = mixer_forward(to_channels(carried_low), rates, weights, devices, 1)
    carried = carried_low.astype(jnp.float32)
    mixer = to_channels(convolved).astype(jnp.float32) + skip * carried
    gated = (queries_one * mixer).reshape(row_count, width).astype(jnp.bfloat16)
    hidden_one = flat_in + dense_product(gated, w_out[0])
    normed_two, raised_one, active_one, hidden_two = feed_forward(hidden_one, 1, 0)
    normed_three = layer_norm(hidden_two, norm_gain[2], norm_bias[2]).astype(jnp.bfloat16)
    qkv_two = dense_product(normed_three, w_qkv[1]).astype(jnp.bfloat16)
    group_rows = width // groups
    qkv_columns = (
        qkv_two.reshape(seq_count, span_rows, 3, groups, group_rows)
        .transpose(0, 3, 2, 4, 1)
        .reshape(seq_count, groups, 3 * group_rows, span_rows)
    )
    attended, kept, log_totals = attention_forward(qkv_columns, devices, 2)
    attended = to_channels(attended).reshape(row_count, width)
    hidden_three = hidden_two + dense_product(attended, w_out[1])
    normed_four, raised_two, active_two, hidden_four = feed_forward(hidden_three, 3, 1)
    output = hidden_four.reshape(seq_count, span_rows, width) * validity

    grad_rows = (cotangent[0].astype(jnp.float32) * validity).reshape(row_count, width)
    grad_rows, branch_four, d_raised_two, gain_four, bias_four = feed_backward(
        grad_rows, hidden_three, raised_two, 3, 1
    )
    branch_three = grad_rows.astype(jnp.bfloat16)
    d_attended = (
        product_right(branch_three, w_out[1])
        .astype(jnp.bfloat16)
        .reshape(seq_count, span_rows, width)
    )
    d_columns = attention_backward(
        to_channels(d_attended), kept, log_totals, seq_count, groups, 3
    )
    d_qkv_two = (
        d_columns.reshape(seq_count, groups, 3, group_rows, span_rows)
        .transpose(0, 4, 2, 1, 3)
        .reshape(row_count, 3 * width)
    )
    d_inputs, gain_three, bias_three = norm_backward(
        hidden_two, 2, product_right(d_qkv_two, w_qkv[1])
    )
    grad_rows = grad_rows + d_inputs

    def sliced(value):
        return value.T.reshape(devices, value.shape[1] // devices, row_count)

    qkv_two_grad, out_two_grad, up_two_grad, down_two_grad = weight_gradients(
        [sliced(normed_three), sliced(attended), sliced(normed_four), sliced(active_two)],
        [d_qkv_two, branch_three, d_raised_two, branch_four],
        depth,
        4,
    )
    grad_rows, branch_two, d_raised_one, gain_two, bias_two = feed_backward(
        grad_rows, hidden_one, raised_one, 1, 0
    )
    branch_one = grad_rows.astype(jnp.bfloat16)
    d_gated = product_right(branch_one, w_out[0]).reshape(seq_count, span_rows, width)
    d_queries = d_gated * mixer
    d_mixer = d_gated * queries_one
    skip_grad = jnp.sum(d_mixer * carried, (0, 1))
    from_conv, rate_grad, weight_grad = mixer_backward(
        to_channels(d_mixer.astype(jnp.bfloat16)), held, rates, weights, devices, 5
    )
    d_carried = d_mixer * skip + to_channels(from_conv).astype(jnp.float32)
    d_shifted = d_carried * values_one * validity
    d_values = d_carried * shifted * validity
    grads_extended = sum(
        (
            jnp.pad(taps[offset] * d_shifted, ((0, 0), (rim - offset, offset), (0, 0)))
            for offset in range(TAPS)
        )
    )
    taps_grad = jnp.stack(
        [jnp.sum(d_shifted * tap_rows(offset), (0, 1)) for offset in range(TAPS)]
    )
    later = passed_along(grads_extended[:, :rim], "seq", -1)
    d_keys = grads_extended[:, rim:] + jnp.pad(later, ((0, 0), (span_rows - rim, 0), (0, 0)))
    d_qkv_one = (
        jnp.concatenate([d_queries, d_keys, d_values], -1)
        .reshape(row_count, 3 * width)
        .astype(jnp.bfloat16)
    )
    d_inputs, gain_one, bias_one = norm_backward(flat_in, 0, product_right(d_qkv_one, w_qkv[0]))
    d_tokens = ((grad_rows + d_inputs).reshape(seq_count, span_rows, width) * validity)[None]
    qkv_one_grad, out_one_grad, up_one_grad, down_one_grad = weight_gradients(
        [sliced(normed_one), sliced(gated), sliced(normed_two), sliced(active_one)],
        [d_qkv_one, branch_one, d_raised_one, branch_two],
        depth,
        6,
    )
    small = jnp.concatenate(
        [
            jnp.stack([gain_one, gain_two, gain_three, gain_four]),
            jnp.stack([bias_one, bias_two, bias_three, bias_four]),
            taps_grad,
            skip_grad[None],
        ],
        0,
    )
    small = lax.psum(small, ("seq", "batch"))
    small = lax.dynamic_slice_in_dim(small, place * channels, channels, 1)
    states = lax.psum(jnp.stack([rate_grad[:, :STATES], weight_grad[:, :STATES]]), "batch")
    return (
        output[None].astype(jnp.bfloat16),
        d_tokens,
        small[:4],
        small[4:7],
        small[7],
        jnp.stack([qkv_one_grad, qkv_two_grad]),
        jnp.stack([out_one_grad, out_two_grad]),
        jnp.stack([up_one_grad, up_two_grad]),
        jnp.stack([down_one_grad, down_two_grad]),
        small[8 : 8 + TAPS],
        small[8 + TAPS],
        states[0],
        states[1],
    )


def fits_by_heads(mesh):
    devices = mesh.shape["seq"]
    return devices == 16 and mesh.shape["batch"] == 2


def solution(mesh):
    placed = (
        P("batch", None, "seq", None),
        P("batch", None, "seq", None),
        P("batch", None),
        P(),
        P(),
        P(),
        P(),
        P(),
        P(),
        P(),
        P(),
        P(),
        P(),
    )
    return jax.shard_map(
        per_device_by_heads if fits_by_heads(mesh) else per_device,
        mesh=mesh,
        in_specs=placed,
        out_specs=(
            P("batch", None, "seq", None),
            P("batch", None, "seq", None),
            P(None, "seq"),
            P(None, "seq"),
            P("seq"),
            P(None, "seq", None),
            P(None, "seq", None),
            P(None, "seq", None),
            P(None, "seq", None),
            P(None, "seq"),
            P("seq"),
            P("seq", None),
            P("seq", None),
        ),
        check_vma=False,
    )
```

```python
import functools
import math
import types

import jax
import jax.numpy as jnp
from jax import lax
from jax.experimental import pallas as pl
from jax.experimental.pallas import tpu as pltpu
from jax.sharding import PartitionSpec as P

HEADS = 12
HEAD = 64
TAPS = 4
STATES = 64
MESH = pl.DeviceIdType.MESH
SEQ = "seq"
BATCH = "batch"
QKV_MORE = "qkv_more"
QKV_LESS = "qkv_less"
DOWN = "down"
OUT = "out"
UP = "up"
QKV = "qkv"
SMALL = "small"
VMEM_BYTES = 60 * 2**20


norm_eps = 1e-05
highest = lax.Precision.HIGHEST
masked_score = -1e30


def for_sending(array):
    return jax.tree.map(lambda a: a.astype(jnp.bfloat16) if a.dtype == jnp.float32 else a, array)


def passed_along(value, axis, steps):
    count = lax.axis_size(axis)
    initial, last = (max(0, -steps), min(count, count - steps))
    return lax.ppermute(value, axis, [(source, source + steps) for source in range(initial, last)])


def layer_norm(inputs, scale_row, shift_row):
    center = inputs - jnp.mean(inputs, -1, keepdims=True)
    spread = jnp.mean(center * center, -1, keepdims=True)
    return center * lax.rsqrt(spread + norm_eps) * scale_row + shift_row


def dense_product(operand_a, operand_b):
    return jnp.dot(operand_a, operand_b, preferred_element_type=jnp.float32)


def product_left(operand_a, operand_b):
    return lax.dot_general(
        operand_a, operand_b, (((0,), (0,)), ((), ())), preferred_element_type=jnp.float32
    )


def product_right(operand_a, operand_b):
    return lax.dot_general(
        operand_a, operand_b, (((1,), (1,)), ((), ())), preferred_element_type=jnp.float32
    )


def angle_table(count_rows, count_cols, period):
    product_index = (
        jnp.arange(count_rows, dtype=jnp.int32)[:, None]
        * jnp.arange(count_cols, dtype=jnp.int32)[None, :]
        % period
    )
    angles = product_index.astype(jnp.float32) * (2.0 * math.pi / period)
    return (jnp.cos(angles), jnp.sin(angles))


def table_einsum(form, table, data):
    return jnp.einsum(form, table, data, precision=highest)


def forward_spectrum(time_parts):
    count_parts = time_parts.shape[0]
    span_rows = time_parts.shape[2]
    count_freq = 2 * count_parts
    cos_parts, sin_parts = angle_table(count_freq, count_parts, count_freq)
    first_real = table_einsum("fp,pjsc->fjsc", cos_parts, time_parts)
    first_imag = -table_einsum("fp,pjsc->fjsc", sin_parts, time_parts)
    cos_twist, sin_twist = angle_table(count_freq, span_rows, count_freq * span_rows)
    cos_twist = cos_twist[:, None, :, None]
    sin_twist = sin_twist[:, None, :, None]
    twist_real = first_real * cos_twist + first_imag * sin_twist
    twist_imag = first_imag * cos_twist - first_real * sin_twist
    cos_span, sin_span = angle_table(span_rows, span_rows, span_rows)
    out_real = table_einsum("ts,fjsc->fjtc", cos_span, twist_real) + table_einsum(
        "ts,fjsc->fjtc", sin_span, twist_imag
    )
    out_imag = table_einsum("ts,fjsc->fjtc", cos_span, twist_imag) - table_einsum(
        "ts,fjsc->fjtc", sin_span, twist_real
    )
    return (out_real, out_imag)


def inverse_spectrum(freq_real, freq_imag):
    count_freq = freq_real.shape[0]
    span_rows = freq_real.shape[2]
    count_parts = count_freq // 2
    fft_length = count_freq * span_rows
    cos_span, sin_span = angle_table(span_rows, span_rows, span_rows)
    first_real = table_einsum("st,fjtc->fjsc", cos_span, freq_real) - table_einsum(
        "st,fjtc->fjsc", sin_span, freq_imag
    )
    first_imag = table_einsum("st,fjtc->fjsc", cos_span, freq_imag) + table_einsum(
        "st,fjtc->fjsc", sin_span, freq_real
    )
    cos_twist, sin_twist = angle_table(count_freq, span_rows, fft_length)
    cos_twist = cos_twist[:, None, :, None]
    sin_twist = sin_twist[:, None, :, None]
    twist_real = first_real * cos_twist - first_imag * sin_twist
    twist_imag = first_imag * cos_twist + first_real * sin_twist
    cos_parts, sin_parts = angle_table(count_parts, count_freq, count_freq)
    summed = table_einsum("pf,fjsc->pjsc", cos_parts, twist_real) - table_einsum(
        "pf,fjsc->pjsc", sin_parts, twist_imag
    )
    return summed / fft_length


def to_frequency(data_low):
    parts = lax.all_to_all(data_low[None], SEQ, split_axis=3, concat_axis=0, tiled=True)
    return forward_spectrum(parts.astype(jnp.float32))


def from_frequency(freq_real, freq_imag):
    time_parts = inverse_spectrum(freq_real, freq_imag)
    joined = lax.all_to_all(
        for_sending(time_parts), SEQ, split_axis=0, concat_axis=3, tiled=True
    ).astype(time_parts.dtype)
    return joined[0]


def kernel_parts(rate_slice, weight_slice, count_freq, span_rows):
    fft_length = count_freq * span_rows
    length_full = fft_length // 2
    frequency = (
        jnp.arange(count_freq, dtype=jnp.int32)[:, None]
        + count_freq * jnp.arange(span_rows, dtype=jnp.int32)[None, :]
    )
    angles = (frequency.astype(jnp.float32) * (2.0 * math.pi / fft_length))[:, None, :, None, None]
    odd_mask = (frequency % 2 == 1)[:, None, :, None, None]
    channels = rate_slice.shape[0]
    blocks = rate_slice.shape[1] // 8
    rate_blocks = rate_slice.reshape(channels, blocks, 8).transpose(1, 0, 2)
    weight_blocks = weight_slice.reshape(channels, blocks, 8).transpose(1, 0, 2)

    def add_block(running, piece_pair):
        rate_part, weight_part = piece_pair
        decays = jnp.exp(-rate_part)
        half_sine = jnp.sin(angles / 2.0)
        real_den = -jnp.expm1(-rate_part) + decays * 2.0 * half_sine * half_sine
        imag_den = decays * jnp.sin(angles)
        numerator = jnp.where(
            odd_mask, 1.0 + jnp.exp(-rate_part * length_full), -jnp.expm1(-rate_part * length_full)
        )
        factor = weight_part * numerator / (real_den * real_den + imag_den * imag_den)
        return (
            (
                running[0] + jnp.sum(factor * real_den, -1),
                running[1] - jnp.sum(factor * imag_den, -1),
            ),
            None,
        )

    zeros_init = jnp.zeros((count_freq, 1, span_rows, channels), jnp.float32)
    return lax.scan(
        jax.checkpoint(add_block), (zeros_init, zeros_init), (rate_blocks, weight_blocks)
    )[0]


def attention_mask(query_positions, key_count, length_value):
    key_positions = jnp.arange(key_count, dtype=jnp.int32)
    return (key_positions[None, :] <= query_positions[:, None]) & (
        key_positions[None, :] < length_value
    )


def head_slice(matrix, head_index):
    return lax.dynamic_slice_in_dim(matrix, head_index * HEAD, HEAD, 1)


def attend_forward(query_low, keys_low, values_low, length_value, query_positions):
    whole_keys, whole_values = (
        lax.all_gather(keys_low, SEQ, axis=0, tiled=True),
        lax.all_gather(values_low, SEQ, axis=0, tiled=True),
    )
    allowed = attention_mask(query_positions, whole_keys.shape[0], length_value)
    score_scale = HEAD ** (-0.5)

    def head_forward(head_index):
        scores = jnp.where(
            allowed,
            score_scale
            * product_right(head_slice(query_low, head_index), head_slice(whole_keys, head_index)),
            masked_score,
        )
        top_score = jnp.max(scores, -1, keepdims=True)
        expos = jnp.exp(scores - top_score)
        totals = jnp.sum(expos, -1, keepdims=True)
        probs_low = (expos / totals).astype(jnp.bfloat16)
        return (
            dense_product(probs_low, head_slice(whole_values, head_index)),
            (top_score + jnp.log(totals))[:, 0],
        )

    head_outputs, log_totals = lax.map(head_forward, jnp.arange(HEADS, dtype=jnp.int32))
    attended = head_outputs.transpose(1, 0, 2).reshape(query_low.shape[0], HEADS * HEAD)
    return (attended, log_totals, whole_keys, whole_values)


def join_heads(head_rows):
    return head_rows.transpose(1, 0, 2).reshape(head_rows.shape[1], HEADS * HEAD)


def attend_backward(
    query_low, whole_keys, whole_values, log_totals, grad_low, length_value, query_positions
):
    allowed = attention_mask(query_positions, whole_keys.shape[0], length_value)
    score_scale = HEAD ** (-0.5)
    span_rows = query_low.shape[0]

    def query_side(head_index):
        head_query = head_slice(query_low, head_index)
        head_keys = head_slice(whole_keys, head_index)
        head_grad = head_slice(grad_low, head_index)
        scores = jnp.where(
            allowed, score_scale * product_right(head_query, head_keys), masked_score
        )
        weights = jnp.exp(scores - log_totals[head_index][:, None])
        d_weights = product_right(head_grad, head_slice(whole_values, head_index))
        row_term = jnp.sum(weights * d_weights, -1, keepdims=True)
        d_scores = (weights * (d_weights - row_term)).astype(jnp.bfloat16)
        d_query = score_scale * dense_product(d_scores, head_keys)
        return (d_query, row_term[:, 0], d_scores, weights)

    def head_backward(head_index):
        d_query, row_term, d_scores, weights = query_side(head_index)
        head_query = head_slice(query_low, head_index)
        head_grad = head_slice(grad_low, head_index)
        d_keys = score_scale * product_left(d_scores, head_query)
        d_values = product_left(weights.astype(jnp.bfloat16), head_grad)
        return (d_query, d_keys, d_values)

    query_grads, key_grads, value_grads = lax.map(head_backward, jnp.arange(HEADS, dtype=jnp.int32))
    count_rows = span_rows * lax.axis_size(SEQ)
    key_part = (
        lax.slice_in_dim(key_grads, 0, count_rows, axis=1)
        .transpose(1, 0, 2)
        .reshape(count_rows, HEADS * HEAD)
    )
    value_part = (
        lax.slice_in_dim(value_grads, 0, count_rows, axis=1)
        .transpose(1, 0, 2)
        .reshape(count_rows, HEADS * HEAD)
    )
    key_value = lax.psum_scatter(
        jnp.stack([key_part, value_part], 1), SEQ, scatter_dimension=0, tiled=True
    )
    return (join_heads(query_grads), key_value[:, 0], key_value[:, 1])


def per_device(
    tokens,
    cotangent,
    lengths,
    norm_gain,
    norm_bias,
    w_qkv,
    w_out,
    w_up,
    w_down,
    taps,
    skip,
    ssm_rate,
    ssm_out,
):
    seq_count = tokens.shape[1]
    span_rows = tokens.shape[2]
    width = tokens.shape[3]
    devices = lax.axis_size(SEQ)
    place = lax.axis_index(SEQ)
    channels = width // devices
    count_freq = 2 * devices
    fft_length = count_freq * span_rows
    rim = TAPS - 1
    row_count = seq_count * span_rows
    query_positions = place * span_rows + jnp.arange(span_rows, dtype=jnp.int32)
    validity = (query_positions[None, :] < lengths[0][:, None]).astype(jnp.float32)[:, :, None]
    rate_slice = lax.dynamic_slice_in_dim(ssm_rate, place * channels, channels, 0)
    weight_slice = lax.dynamic_slice_in_dim(ssm_out, place * channels, channels, 0)

    def spectrum_of(rate_in, weight_in):
        return kernel_parts(rate_in, weight_in, count_freq, span_rows)

    def feed_forward(inputs, norm_row, layer):
        normed_low = layer_norm(inputs, norm_gain[norm_row], norm_bias[norm_row]).astype(
            jnp.bfloat16
        )
        raised = dense_product(normed_low, w_up[layer])
        active_low = jax.nn.gelu(raised).astype(jnp.bfloat16)
        return (normed_low, raised, active_low, inputs + dense_product(active_low, w_down[layer]))

    def norm_backward(inputs, norm_row, d_normed):
        norm_pull = jax.vjp(layer_norm, inputs, norm_gain[norm_row], norm_bias[norm_row])[1]
        return norm_pull(d_normed)

    def feed_backward(grad_rows, inputs, normed_low, raised, active_low, norm_row, layer):
        branch_low = grad_rows.astype(jnp.bfloat16)
        down_grad = product_left(active_low, branch_low)
        d_active = product_right(branch_low, w_down[layer])
        gelu_pull = jax.vjp(jax.nn.gelu, raised)[1]
        d_raised = gelu_pull(d_active)[0].astype(jnp.bfloat16)
        up_grad = product_left(normed_low, d_raised)
        d_inputs, gain_part, bias_part = norm_backward(
            inputs, norm_row, product_right(d_raised, w_up[layer])
        )
        return (grad_rows + d_inputs, down_grad, up_grad, gain_part, bias_part)

    def forward_pass(token_block):
        masked_in = token_block[0].astype(jnp.float32) * validity
        flat_in = masked_in.reshape(row_count, width)
        normed_one = layer_norm(flat_in, norm_gain[0], norm_bias[0]).astype(jnp.bfloat16)
        qkv_one = dense_product(normed_one, w_qkv[0]).reshape(seq_count, span_rows, 3 * width)
        queries_one = qkv_one[:, :, :width]
        keys_one = qkv_one[:, :, width : 2 * width].astype(jnp.bfloat16)
        values_one = qkv_one[:, :, 2 * width :]
        earlier = passed_along(keys_one[:, span_rows - rim :], SEQ, 1)
        extended = jnp.concatenate([earlier, keys_one], 1)
        shifted = sum(
            (
                taps[offset]
                * extended[:, rim - offset : rim - offset + span_rows].astype(jnp.float32)
                for offset in range(TAPS)
            )
        )
        carried_low = (shifted * values_one * validity).astype(jnp.bfloat16)
        carried_real, carried_imag = to_frequency(carried_low)
        kernel_both, kernel_pull = jax.vjp(spectrum_of, rate_slice, weight_slice)
        kernel_real, kernel_imag = kernel_both
        convolved = from_frequency(
            carried_real * kernel_real - carried_imag * kernel_imag,
            carried_real * kernel_imag + carried_imag * kernel_real,
        )
        carried = carried_low.astype(jnp.float32)
        mixer = convolved + skip * carried
        gated_low = (queries_one * mixer).reshape(row_count, width).astype(jnp.bfloat16)
        hidden_one = flat_in + dense_product(gated_low, w_out[0])
        normed_two, raised_one, active_one, hidden_two = feed_forward(hidden_one, 1, 0)
        normed_three = layer_norm(hidden_two, norm_gain[2], norm_bias[2]).astype(jnp.bfloat16)
        qkv_two = (
            dense_product(normed_three, w_qkv[1])
            .astype(jnp.bfloat16)
            .reshape(seq_count, span_rows, 3 * width)
        )
        attended_list = []
        totals_list = []
        keys_list = []
        values_list = []
        for seq_index in range(seq_count):
            attended, log_totals, whole_keys, whole_values = attend_forward(
                qkv_two[seq_index, :, :width],
                qkv_two[seq_index, :, width : 2 * width],
                qkv_two[seq_index, :, 2 * width :],
                lengths[0, seq_index],
                query_positions,
            )
            attended_list.append(attended)
            totals_list.append(log_totals)
            keys_list.append(whole_keys)
            values_list.append(whole_values)
        attended_low = jnp.concatenate(attended_list, 0).astype(jnp.bfloat16)
        hidden_three = hidden_two + dense_product(attended_low, w_out[1])
        normed_four, raised_two, active_two, hidden_four = feed_forward(hidden_three, 3, 1)
        output = hidden_four.reshape(seq_count, span_rows, width) * validity
        saved = types.SimpleNamespace(
            flat_in=flat_in,
            normed_one=normed_one,
            queries_one=queries_one,
            values_one=values_one,
            extended=extended,
            shifted=shifted,
            carried=carried,
            carried_real=carried_real,
            carried_imag=carried_imag,
            kernel_real=kernel_real,
            kernel_imag=kernel_imag,
            kernel_pull=kernel_pull,
            mixer=mixer,
            gated_low=gated_low,
            hidden_one=hidden_one,
            normed_two=normed_two,
            raised_one=raised_one,
            active_one=active_one,
            hidden_two=hidden_two,
            normed_three=normed_three,
            qkv_two=qkv_two,
            totals_list=totals_list,
            keys_list=keys_list,
            values_list=values_list,
            attended_low=attended_low,
            hidden_three=hidden_three,
            normed_four=normed_four,
            raised_two=raised_two,
            active_two=active_two,
        )
        return (output, saved)

    output = forward_pass(tokens)[0]
    saved = forward_pass(lax.optimization_barrier(tokens))[1]
    grad_rows = (cotangent[0].astype(jnp.float32) * validity).reshape(row_count, width)
    grad_rows, down_two, up_two, gain_four, bias_four = feed_backward(
        grad_rows,
        saved.hidden_three,
        saved.normed_four,
        saved.raised_two,
        saved.active_two,
        3,
        1,
    )
    branch_low = grad_rows.astype(jnp.bfloat16)
    out_two = product_left(saved.attended_low, branch_low)
    d_attended = (
        product_right(branch_low, w_out[1])
        .astype(jnp.bfloat16)
        .reshape(seq_count, span_rows, width)
    )
    qkv_two = saved.qkv_two
    grad_parts = []
    for seq_index in range(seq_count):
        d_query_rows, d_key_rows, d_value_rows = attend_backward(
            qkv_two[seq_index, :, :width],
            saved.keys_list[seq_index],
            saved.values_list[seq_index],
            saved.totals_list[seq_index],
            d_attended[seq_index],
            lengths[0, seq_index],
            query_positions,
        )
        grad_parts.append(jnp.concatenate([d_query_rows, d_key_rows, d_value_rows], -1))
    d_qkv_two = jnp.concatenate(grad_parts, 0).astype(jnp.bfloat16)
    qkv_grad_two = product_left(saved.normed_three, d_qkv_two)
    d_inputs, gain_three, bias_three = norm_backward(
        saved.hidden_two, 2, product_right(d_qkv_two, w_qkv[1])
    )
    grad_rows = grad_rows + d_inputs
    grad_rows, down_one, up_one, gain_two, bias_two = feed_backward(
        grad_rows,
        saved.hidden_one,
        saved.normed_two,
        saved.raised_one,
        saved.active_one,
        1,
        0,
    )
    branch_low = grad_rows.astype(jnp.bfloat16)
    out_one = product_left(saved.gated_low, branch_low)
    d_gated = product_right(branch_low, w_out[0]).reshape(seq_count, span_rows, width)
    d_queries = d_gated * saved.mixer
    d_mixer = d_gated * saved.queries_one
    skip_grad = jnp.sum(d_mixer * saved.carried, (0, 1))
    conv_real, conv_imag = to_frequency(d_mixer.astype(jnp.bfloat16))
    kernel_real = saved.kernel_real
    kernel_imag = saved.kernel_imag
    from_conv = from_frequency(
        kernel_real * conv_real + kernel_imag * conv_imag,
        kernel_real * conv_imag - kernel_imag * conv_real,
    )
    d_carried = d_mixer * skip + from_conv
    carried_real = saved.carried_real
    carried_imag = saved.carried_imag
    cot_real = (
        jnp.sum(carried_real * conv_real + carried_imag * conv_imag, 1, keepdims=True) / fft_length
    )
    cot_imag = (
        jnp.sum(carried_real * conv_imag - carried_imag * conv_real, 1, keepdims=True) / fft_length
    )
    rate_grad, weight_grad = saved.kernel_pull((cot_real, cot_imag))
    d_shifted = d_carried * saved.values_one * validity
    d_values = d_carried * saved.shifted * validity
    extended = saved.extended
    grads_extended = sum(
        (
            jnp.pad(taps[offset] * d_shifted, ((0, 0), (rim - offset, offset), (0, 0)))
            for offset in range(TAPS)
        )
    )
    taps_grad = jnp.stack(
        [
            jnp.sum(
                d_shifted
                * extended[:, rim - offset : rim - offset + span_rows].astype(jnp.float32),
                (0, 1),
            )
            for offset in range(TAPS)
        ]
    )
    later = passed_along(grads_extended[:, :rim], SEQ, -1)
    d_keys = grads_extended[:, rim:] + jnp.pad(later, ((0, 0), (span_rows - rim, 0), (0, 0)))
    d_qkv_one = (
        jnp.concatenate([d_queries, d_keys, d_values], -1)
        .reshape(row_count, 3 * width)
        .astype(jnp.bfloat16)
    )
    qkv_grad_one = product_left(saved.normed_one, d_qkv_one)
    d_inputs, gain_one, bias_one = norm_backward(
        saved.flat_in, 0, product_right(d_qkv_one, w_qkv[0])
    )
    d_tokens = ((grad_rows + d_inputs).reshape(seq_count, span_rows, width) * validity)[None]
    gain_sum, bias_sum, qkv_sum, out_sum, up_sum, down_sum, taps_sum, skip_sum = (
        lax.psum_scatter(
            jnp.stack([gain_one, gain_two, gain_three, gain_four]),
            SEQ,
            scatter_dimension=1,
            tiled=True,
        ),
        lax.psum_scatter(
            jnp.stack([bias_one, bias_two, bias_three, bias_four]),
            SEQ,
            scatter_dimension=1,
            tiled=True,
        ),
        lax.psum_scatter(
            jnp.stack([qkv_grad_one, qkv_grad_two]), SEQ, scatter_dimension=1, tiled=True
        ),
        lax.psum_scatter(jnp.stack([out_one, out_two]), SEQ, scatter_dimension=1, tiled=True),
        lax.psum_scatter(jnp.stack([up_one, up_two]), SEQ, scatter_dimension=1, tiled=True),
        lax.psum_scatter(jnp.stack([down_one, down_two]), SEQ, scatter_dimension=1, tiled=True),
        lax.psum_scatter(taps_grad, SEQ, scatter_dimension=1, tiled=True),
        lax.psum_scatter(skip_grad[None], SEQ, scatter_dimension=1, tiled=True),
    )
    totals = (
        lax.psum(gain_sum.astype(jnp.bfloat16), BATCH).astype(jnp.float32),
        lax.psum(bias_sum.astype(jnp.bfloat16), BATCH).astype(jnp.float32),
        lax.psum(qkv_sum.astype(jnp.bfloat16), BATCH).astype(jnp.float32),
        lax.psum(out_sum.astype(jnp.bfloat16), BATCH).astype(jnp.float32),
        lax.psum(up_sum.astype(jnp.bfloat16), BATCH).astype(jnp.float32),
        lax.psum(down_sum.astype(jnp.bfloat16), BATCH).astype(jnp.float32),
        lax.psum(taps_sum.astype(jnp.bfloat16), BATCH).astype(jnp.float32),
        lax.psum(skip_sum.astype(jnp.bfloat16), BATCH).astype(jnp.float32),
        lax.psum(rate_grad.astype(jnp.bfloat16), BATCH).astype(jnp.float32),
        lax.psum(weight_grad.astype(jnp.bfloat16), BATCH).astype(jnp.float32),
    )
    return (
        output[None].astype(jnp.bfloat16),
        d_tokens,
        totals[0],
        totals[1][:3],
        totals[1][3],
        totals[2],
        totals[3],
        totals[4],
        totals[5],
        totals[6],
        totals[7][0],
        totals[8],
        totals[9],
    )


def other_device(place, core, to_place, to_core):
    return jnp.logical_or(place != to_place, core != to_core)


def greet(devices):
    barrier = pltpu.get_barrier_semaphore()
    for device in devices:
        pl.semaphore_signal(barrier, inc=1, device_id=device, device_id_type=MESH)
    pl.semaphore_wait(barrier, len(devices))


def remote(source, target, send_sem, recv_sem, device):
    return pltpu.make_async_remote_copy(
        src_ref=source,
        dst_ref=target,
        send_sem=send_sem,
        recv_sem=recv_sem,
        device_id=device,
        device_id_type=MESH,
    )


def split_low(value):
    upper = value.astype(jnp.bfloat16)
    return upper, (value - upper.astype(jnp.float32)).astype(jnp.bfloat16)


NN = (((1,), (0,)), ((), ()))
NT = (((1,), (1,)), ((), ()))
TN = (((0,), (0,)), ((), ()))


def dot(left, right, form=NN):
    return lax.dot_general(left, right, form, preferred_element_type=jnp.float32)


def dot_fine(left, right, form=NN):
    left_up, left_low = left
    right_up, right_low = right
    total = dot(left_up, right_up, form) + dot(left_up, right_low, form)
    if left_low is not None:
        total = total + dot(left_low, right_up, form)
    return total


def state_tables(rate_row, weight_row, span):
    row = lax.broadcasted_iota(jnp.int32, (span, 2 * STATES), 0)
    lane = lax.broadcasted_iota(jnp.int32, (span, 2 * STATES), 1)
    steps = jnp.where(lane < STATES, span - 1 - row, row + 1).astype(jnp.float32)
    table = jnp.exp(-rate_row * steps)
    lane_row = lax.broadcasted_iota(jnp.int32, (8, 2 * STATES), 1)
    lead = jnp.where(lane_row < STATES, 0.0, weight_row * jnp.exp(rate_row))
    response = lax.dot_general(
        lead, table, NT, precision=highest, preferred_element_type=jnp.float32
    )[:1]
    spread = pltpu.roll(
        jnp.broadcast_to(response, (span, span)), 0, 1, stride=1, stride_axis=0
    )
    later = lax.broadcasted_iota(jnp.int32, (span, span), 1)
    earlier = lax.broadcasted_iota(jnp.int32, (span, span), 0)
    toeplitz = jnp.where(later >= earlier, spread, 0.0)
    return table, steps, toeplitz


def shift_rows(value, count):
    if count > 0:
        return jnp.concatenate([jnp.zeros_like(value[:count]), value[:-count]], 0)
    return jnp.concatenate([value[-count:], jnp.zeros_like(value[:-count])], 0)


def scan_states(value, decay, seqs, blocks, direction):
    step = 1
    while step < blocks:
        value = value + shift_rows(value, direction * step * seqs) * jnp.exp(decay * step)
        step *= 2
    return shift_rows(value, direction * seqs)


def mixer_forward_kernel(
    n, seqs, span, channels, unroll,
    x_ref, rate_ref, weight_ref, y_ref, held_ref,
    flat, flat_out, answer, send, recv, back_send, back_recv, own_sem,
):
    me, core = lax.axis_index(SEQ), lax.axis_index(BATCH)
    peers = [lax.rem(me + step, n) for step in range(1, n)]
    greet([(peer, core) for peer in peers])
    outgoing = []
    for step, peer in enumerate(peers):
        rows = pl.ds(pl.multiple_of(peer * channels, 16), channels)
        copy = remote(
            x_ref.at[:, rows, :], held_ref.at[me], send.at[step], recv.at[step], (peer, core)
        )
        copy.start()
        outgoing.append(copy)
    own_rows = pl.ds(pl.multiple_of(me * channels, 16), channels)
    own = pltpu.make_async_copy(x_ref.at[:, own_rows, :], held_ref.at[me], own_sem.at[0])
    own.start()
    own.wait()
    for copy in outgoing:
        copy.wait()
    total_rows = n * seqs * channels
    flat[...] = held_ref[...].astype(jnp.float32).reshape(total_rows, span)

    def one_channel(channel, carry):
        rate_row = rate_ref[pl.ds(channel, 1), :]
        weight_row = weight_ref[pl.ds(channel, 1), :]
        table, _, toeplitz = state_tables(rate_row, weight_row, span)
        rows = pl.ds(channel, n * seqs, stride=channels)
        data = (flat[rows, :].astype(jnp.bfloat16), None)
        table_parts = split_low(table)
        inner = dot_fine(data, split_low(toeplitz))
        states = dot_fine(data, table_parts)
        states = scan_states(states, -span * rate_row, seqs, n, 1)
        lane = lax.broadcasted_iota(jnp.int32, states.shape, 1)
        weighted = jnp.where(lane < STATES, 0.0, pltpu.roll(states, STATES, 1) * weight_row)
        flat_out[rows, :] = inner + dot_fine(split_low(weighted), table_parts, NT)
        return carry

    lax.fori_loop(0, channels, one_channel, 0, unroll=unroll)
    answer[...] = flat_out[...].reshape(n, seqs, channels, span).astype(jnp.bfloat16)
    outgoing = []
    for step, peer in enumerate(peers):
        copy = remote(
            answer.at[peer], y_ref.at[:, own_rows, :], back_send.at[step], back_recv.at[step],
            (peer, core),
        )
        copy.start()
        outgoing.append(copy)
    own = pltpu.make_async_copy(answer.at[me], y_ref.at[:, own_rows, :], own_sem.at[1])
    own.start()
    own.wait()
    for copy in outgoing:
        copy.wait()


def mixer_forward(x, rates, weights, n, collective):
    seqs, width, span = x.shape
    channels = width // n
    total_rows = n * seqs * channels
    vmem = pl.BlockSpec(memory_space=pltpu.VMEM)
    return pl.pallas_call(
        functools.partial(mixer_forward_kernel, n, seqs, span, channels, 4),
        out_shape=(
            jax.ShapeDtypeStruct(x.shape, jnp.bfloat16),
            jax.ShapeDtypeStruct((n, seqs, channels, span), jnp.bfloat16),
        ),
        in_specs=[vmem] * 3,
        out_specs=(vmem, vmem),
        scratch_shapes=[
            pltpu.VMEM((total_rows, span), jnp.float32),
            pltpu.VMEM((total_rows, span), jnp.float32),
            pltpu.VMEM((n, seqs, channels, span), jnp.bfloat16),
            pltpu.SemaphoreType.DMA((n - 1,)),
            pltpu.SemaphoreType.DMA((n - 1,)),
            pltpu.SemaphoreType.DMA((n - 1,)),
            pltpu.SemaphoreType.DMA((n - 1,)),
            pltpu.SemaphoreType.DMA((2,)),
        ],
        compiler_params=pltpu.CompilerParams(
            collective_id=collective, has_side_effects=True, vmem_limit_bytes=VMEM_BYTES
        ),
    )(x, rates, weights)


def mixer_backward_channel(n, seqs, span, channels, refs, channel):
    rate_row = refs.rates[pl.ds(channel, 1), :]
    weight_row = refs.rate_weights[pl.ds(channel, 1), :]
    table, steps, toeplitz = state_tables(rate_row, weight_row, span)
    rows = pl.ds(channel, n * seqs, stride=channels)
    data = refs.flat_x[rows, :].astype(jnp.bfloat16)
    grad = refs.flat_d[rows, :].astype(jnp.bfloat16)
    table_parts = split_low(table)
    both_parts = split_low(jnp.concatenate([table, table * steps], 1))
    count = n * seqs
    sides = dot_fine((jnp.concatenate([data, grad], 0), None), both_parts)
    lane = lax.broadcasted_iota(jnp.int32, (count, 2 * STATES), 1)
    low_lanes = lane < STATES

    def aligned(value):
        return jnp.where(low_lanes, pltpu.roll(value, STATES, 1), 0.0)

    entering = jnp.where(low_lanes, sides[:count, : 2 * STATES], 0.0)
    entering_steps = jnp.where(low_lanes, sides[:count, 2 * STATES :], 0.0)
    leaving = aligned(sides[count:, : 2 * STATES])
    leaving_steps = aligned(sides[count:, 2 * STATES :])
    decay = -span * rate_row
    states = scan_states(entering, decay, seqs, n, 1)
    states_steps = scan_states(states * jnp.exp(decay), decay, seqs, n, 1)
    returned = scan_states(leaving, decay, seqs, n, -1)
    far_weight = jnp.sum(leaving * states, 0, keepdims=True)
    far_rate = jnp.sum(
        leaving_steps * states + returned * entering_steps + span * (leaving * states_steps),
        0, keepdims=True,
    )
    cross = dot(data, grad, TN)
    later = lax.broadcasted_iota(jnp.int32, (span, span), 1)
    earlier = lax.broadcasted_iota(jnp.int32, (span, span), 0)
    cross = jnp.where(later >= earlier, cross, 0.0)
    met = dot_fine(split_low(cross), both_parts, TN)
    met_plain = pltpu.roll(met[:, : 2 * STATES], STATES, 1)
    met_steps = pltpu.roll(met[:, 2 * STATES :], STATES, 1)
    rise = jnp.exp(span * rate_row)
    near_weight = rise * jnp.sum(table * met_plain, 0, keepdims=True)
    near_rate = rise * jnp.sum(
        table * ((steps - span) * met_plain + met_steps), 0, keepdims=True
    )
    lane_row = lane[:1]
    near_weight = jnp.where(lane_row < STATES, pltpu.roll(near_weight, STATES, 1), 0.0)
    near_rate = jnp.where(lane_row < STATES, pltpu.roll(near_rate, STATES, 1), 0.0)
    refs.weight_grad[pl.ds(channel, 1), :] = near_weight + far_weight
    refs.rate_grad[pl.ds(channel, 1), :] = -weight_row * (near_rate + far_rate)
    inner = dot_fine((grad, None), split_low(toeplitz), NT)
    weighted = returned * weight_row
    refs.flat_out[rows, :] = inner + dot_fine(split_low(weighted), table_parts, NT)


def block_of(index, core):
    return 2 * index + lax.rem(index + core, 2)


def keeper_of(block):
    return lax.rem((block + 1) // 2, 2)


class HeadPlaces:
    def __init__(self, n, seqs, groups):
        self.n, self.seqs, self.groups = n, seqs, groups
        self.me, self.core = lax.axis_index(SEQ), lax.axis_index(BATCH)
        self.group = self.me // (2 * seqs)
        self.seq = lax.rem(self.me // 2, seqs)
        self.batch = lax.rem(self.me, 2)
        self.keeper = keeper_of(self.me)
        self.sibling = (self.me, 1 - self.core)
        self.targets = [
            ((group * 2 * seqs + seq * 2 + self.core, self.keeper), seq, group)
            for seq in range(seqs)
            for group in range(groups)
        ]
        self.blocks = [block_of(index, self.core) for index in range(n // 2)]
        self.sources = [(block, self.batch) for block in self.blocks]

    def is_other(self, device):
        return jnp.logical_or(device[0] != self.me, device[1] != self.core)

    def greet(self):
        barrier = pltpu.get_barrier_semaphore()
        self.signal_all(barrier, [])
        self.wait_all(barrier, 0)

    def signal_all(self, barrier, more):
        for device in [target for target, _, _ in self.targets] + self.sources:

            @pl.when(self.is_other(device))
            def _():
                pl.semaphore_signal(barrier, inc=1, device_id=device, device_id_type=MESH)

        for device in [self.sibling, *more]:
            pl.semaphore_signal(barrier, inc=1, device_id=device, device_id_type=MESH)

    def wait_all(self, barrier, more):
        kept = jnp.logical_and(self.batch == self.core, self.is_kept_here())
        count = len(self.targets) + len(self.sources) + 1 + more
        pl.semaphore_wait(barrier, count - 2 * kept.astype(jnp.int32))

    def is_kept_here(self):
        return self.keeper == self.core

    def send(self, source, target, send_sem, recv_sem, device):
        @pl.when(self.is_other(device))
        def _():
            remote(source, target, send_sem, recv_sem, device).start()

        @pl.when(jnp.logical_not(self.is_other(device)))
        def _():
            pltpu.make_async_copy(source, target, recv_sem).start()

    def wait_sent(self, source, target, send_sem, recv_sem, device):
        @pl.when(self.is_other(device))
        def _():
            remote(source, target, send_sem, recv_sem, device).wait_send()


def fill_heads(held, head, first, n, span, rows_out, columns_out):
    start = pl.multiple_of(first + head * HEAD, HEAD)
    for block in range(n):
        part = held[block, pl.ds(start, HEAD), :]
        if rows_out is not None:
            rows_out[block * span : (block + 1) * span, :] = part.T
        if columns_out is not None:
            columns_out[:, block * span : (block + 1) * span] = part


def causal(first_key, rows, first_query, span):
    key = first_key + lax.broadcasted_iota(jnp.int32, (rows, span), 0)
    query = first_query + lax.broadcasted_iota(jnp.int32, (rows, span), 1)
    return key <= query


def attention_forward_kernel(
    n, seqs, groups, span, group_rows,
    qkv_ref, out_ref, held, lse_ref,
    outputs, key_rows, value_columns,
    send, recv, pass_send, pass_recv, back_send, back_recv,
):
    at = HeadPlaces(n, seqs, groups)
    half = n // 2
    at.greet()
    for count, (device, seq, group) in enumerate(at.targets):
        at.send(qkv_ref.at[seq, group], held.at[at.me], send.at[count], recv.at[at.me // 2], device)
    passed = []
    for index, block in enumerate(at.blocks):
        remote(held.at[block], held.at[block], send.at[0], recv.at[index], at.sibling).wait_recv()
        part = held.at[block, group_rows : 3 * group_rows, :]
        copy = remote(part, part, pass_send.at[index], pass_recv.at[index], at.sibling)
        copy.start()
        passed.append(copy)
    for copy in passed:
        copy.wait()
    for count, (device, seq, group) in enumerate(at.targets):
        at.wait_sent(
            qkv_ref.at[seq, group], held.at[at.me], send.at[count], recv.at[at.me // 2], device
        )

    def one_head(head, carry):
        fill_heads(held, head, group_rows, n, span, key_rows, None)
        fill_heads(held, head, 2 * group_rows, n, span, None, value_columns)
        query_rows = pl.ds(pl.multiple_of(head * HEAD, HEAD), HEAD)
        for index, block in enumerate(at.blocks):
            query = held[block, query_rows, :] * jnp.bfloat16(HEAD**-0.5)
            clear, reach = 2 * index * span, 2 * (index + 1) * span
            edge = dot(key_rows[clear:reach, :], query)
            edge = jnp.where(causal(clear, reach - clear, block * span, span), edge, masked_score)
            top = jnp.max(edge, 0, keepdims=True)
            if index > 0:
                body = dot(key_rows[:clear, :], query)
                top = jnp.maximum(top, jnp.max(body, 0, keepdims=True))
            edge = jnp.exp(edge - top)
            total = jnp.sum(edge, 0, keepdims=True)
            result = dot(value_columns[:, clear:reach], edge.astype(jnp.bfloat16))
            if index > 0:
                body = jnp.exp(body - top)
                total = total + jnp.sum(body, 0, keepdims=True)
                result = result + dot(value_columns[:, :clear], body.astype(jnp.bfloat16))
            outputs[index, query_rows, :] = (result / total).astype(jnp.bfloat16)
            lse_ref[index, pl.ds(head, 1), :] = top + jnp.log(total)
        return carry

    lax.fori_loop(0, group_rows // HEAD, one_head, 0)
    into = pl.ds(pl.multiple_of(at.group * group_rows, 16), group_rows)
    lanes = pl.ds(pl.multiple_of(at.seq * span, span), span)
    slot = at.seq * groups + at.group
    for index, device in enumerate(at.sources):
        at.send(
            outputs.at[index], out_ref.at[into, lanes], back_send.at[index],
            back_recv.at[slot], device,
        )
    for count, (device, seq, group) in enumerate(at.targets):
        landed = out_ref.at[
            group * group_rows : (group + 1) * group_rows, seq * span : (seq + 1) * span
        ]
        remote(landed, landed, back_send.at[0], back_recv.at[count], at.sibling).wait_recv()
    for index, device in enumerate(at.sources):
        at.wait_sent(
            outputs.at[index], out_ref.at[into, lanes], back_send.at[index],
            back_recv.at[slot], device,
        )


def attention_forward(qkv, n, collective):
    seqs, groups, rows, span = qkv.shape
    group_rows = rows // 3
    half = n // 2
    vmem = pl.BlockSpec(memory_space=pltpu.VMEM)
    dma = pltpu.SemaphoreType.DMA
    return pl.pallas_call(
        functools.partial(attention_forward_kernel, n, seqs, groups, span, group_rows),
        out_shape=(
            jax.ShapeDtypeStruct((groups * group_rows, seqs * span), jnp.bfloat16),
            jax.ShapeDtypeStruct((n, rows, span), jnp.bfloat16),
            jax.ShapeDtypeStruct((half, group_rows // HEAD, span), jnp.float32),
        ),
        in_specs=[vmem],
        out_specs=(vmem, vmem, vmem),
        scratch_shapes=[
            pltpu.VMEM((half, group_rows, span), jnp.bfloat16),
            pltpu.VMEM((n * span, HEAD), jnp.bfloat16),
            pltpu.VMEM((HEAD, n * span), jnp.bfloat16),
            dma((seqs * groups,)),
            dma((half,)),
            dma((half,)),
            dma((half,)),
            dma((half,)),
            dma((seqs * groups,)),
        ],
        compiler_params=pltpu.CompilerParams(
            collective_id=collective, has_side_effects=True, vmem_limit_bytes=VMEM_BYTES
        ),
    )(qkv)


TILE = 384
VMEM, HBM = pltpu.VMEM, pl.ANY


def launch(body, inputs, outputs, scratch, copies, collective):
    names = [*inputs, *outputs, *scratch, "send", "recv", "local"]

    def kernel(*refs):
        body(types.SimpleNamespace(**dict(zip(names, refs))))

    dma = pltpu.SemaphoreType.DMA
    results = pl.pallas_call(
        kernel,
        out_shape=tuple(jax.ShapeDtypeStruct(shape, kind) for shape, kind, _ in outputs.values()),
        in_specs=[pl.BlockSpec(memory_space=space) for _, space in inputs.values()],
        out_specs=tuple(pl.BlockSpec(memory_space=space) for _, _, space in outputs.values()),
        scratch_shapes=[pltpu.VMEM(shape, kind) for shape, kind in scratch.values()]
        + [dma((copies,)), dma((copies,)), dma((LOCAL_COPIES,))],
        compiler_params=pltpu.CompilerParams(
            collective_id=collective, has_side_effects=True, vmem_limit_bytes=VMEM_BYTES
        ),
    )(*(array for array, _ in inputs.values()))
    return types.SimpleNamespace(**dict(zip(outputs, results)))


LOCAL_COPIES = 24


class Loads:
    def __init__(self, refs):
        self.semaphores, self.used, self.pending = refs.local, 0, {}

    def start(self, key, source, target):
        copy = pltpu.make_async_copy(source, target, self.semaphores.at[self.used])
        self.used += 1
        copy.start()
        self.pending[key] = copy

    def wait(self, *keys):
        for key in keys:
            self.pending.pop(key).wait()


class Links:
    def __init__(self, refs):
        self.send, self.recv, self.used, self.unsent = refs.send, refs.recv, 0, []

    def slots(self, count):
        self.used += count
        return self.used - count

    def copy(self, source, target, device, slot=None):
        slot = self.slots(1) if slot is None else slot
        made = remote(source, target, self.send.at[slot], self.recv.at[slot], device)
        made.start()
        self.unsent.append(made)
        return made

    def finish(self):
        for made in self.unsent:
            made.wait_send()


class Reducer:
    def __init__(self, refs, links, depth, weights, parts):
        self.refs, self.links, self.depth = refs, links, depth
        self.weights, self.parts = weights, parts
        self.me, self.core = lax.axis_index(SEQ), lax.axis_index(BATCH)
        self.level = self.me // 4
        self.spot = (lax.rem(self.me // 2, 2), lax.rem(self.me, 2))
        base = self.level * 4
        self.across = [
            (base + self.spot[0] * 2 + (1 - self.spot[1]), self.core),
            (base + (1 - self.spot[0]) * 2 + self.spot[1], self.core),
        ]
        self.sibling = (self.me, 1 - self.core)
        self.levels = [lax.rem(self.level + step, depth) for step in range(1, depth)]
        self.column = [
            (other * 4 + self.spot[0] * 2 + self.spot[1], self.core) for other in self.levels
        ]
        self.flights = {}

    def neighbours(self):
        return [self.sibling, *self.across, *self.column]

    def ref(self, name, suffix):
        return getattr(self.refs, name + suffix)

    def exchange(self, weight):
        half = self.weights[weight][1]
        theirs = pl.ds(pl.multiple_of((1 - self.core) * half, 16), half)
        self.flights[weight] = [
            self.links.copy(
                self.ref(weight, "_left"), self.ref(weight, "_left_other"), self.sibling
            ),
            self.links.copy(
                self.ref(weight, "_right").at[theirs, :], self.ref(weight, "_right_other"),
                self.sibling,
            ),
        ]

    def product(self, part, first, outers, column):
        weight, first_column, _, axis = self.parts[part]
        half = self.weights[weight][1]
        places = [
            outer * 4 + (inner * 2 + first if axis == 0 else first * 2 + inner)
            for outer in outers
            for inner in range(2)
        ]
        left, left_other = self.ref(weight, "_left"), self.ref(weight, "_left_other")
        mine = jnp.concatenate([left[place] for place in places], 0)
        other = jnp.concatenate([left_other[place] for place in places], 0)
        start = first_column + column
        own = pl.ds(pl.multiple_of(self.core * half + start, 16), TILE)
        there = pl.ds(pl.multiple_of(start, 16), TILE)
        return dot(mine, self.ref(weight, "_right")[own, :], NT) + dot(
            other, self.ref(weight, "_right_other")[there, :], NT
        )

    def fill(self, part, first, buffer):
        weight, _, columns, _ = self.parts[part]
        rows = self.weights[weight][0]
        outers = [[outer] for outer in range(self.depth)]
        if rows * 2 < TILE:
            outers = [list(range(self.depth))]

        def one_column(tile, carry):
            column = tile * TILE
            place = pl.ds(pl.multiple_of(column, 128), TILE)
            for group in outers:
                value = self.product(part, first, group, column)
                buffer[group[0] : group[-1] + 1, :, :, place] = value.reshape(
                    len(group), 2, rows, TILE
                ).astype(buffer.dtype)
            return carry

        if columns == TILE:
            one_column(0, 0)
        else:
            lax.fori_loop(0, columns // TILE, one_column, 0)

    def first(self, part):
        weight, _, _, axis = self.parts[part]
        for flight in self.flights.pop(weight, ()):
            flight.wait_recv()
        mine = self.spot[1 - axis]
        self.fill(part, 1 - mine, self.ref(part, "_away"))
        self.flights[part] = self.links.copy(
            self.ref(part, "_away"), self.ref(part, "_one"), self.across[axis]
        )
        self.fill(part, mine, self.ref(part, "_home"))

    def first_given(self, part, values):
        axis = self.parts[part][3]
        mine = self.spot[1 - axis]
        for outer in range(self.depth):
            for inner in range(2):
                there, here = (
                    outer * 4 + (inner * 2 + first if axis == 0 else first * 2 + inner)
                    for first in (1 - mine, mine)
                )
                self.ref(part, "_away")[outer, inner] = values[there]
                self.ref(part, "_home")[outer, inner] = values[here]
        self.flights[part] = self.links.copy(
            self.ref(part, "_away"), self.ref(part, "_one"), self.across[axis]
        )

    def second(self, part):
        axis = self.parts[part][3]
        self.flights.pop(part).wait_recv()
        mine = self.spot[axis]
        home, one = self.ref(part, "_home"), self.ref(part, "_one")
        for outer in range(self.depth):
            one[outer, 1 - mine] = (
                home[outer, 1 - mine] + one[outer, 1 - mine].astype(jnp.float32)
            ).astype(one.dtype)
        self.flights[part] = self.links.copy(
            one.at[:, 1 - mine], self.ref(part, "_two"), self.across[1 - axis]
        )
        for outer in range(self.depth):
            home[outer, mine] += one[outer, mine].astype(jnp.float32)

    def third(self, part):
        axis = self.parts[part][3]
        self.flights.pop(part).wait_recv()
        mine = self.spot[axis]
        home, two = self.ref(part, "_home"), self.ref(part, "_two")
        copies = []
        for step, other in enumerate(self.levels):
            two[other] = (home[other, mine] + two[other].astype(jnp.float32)).astype(two.dtype)
            copies.append(
                self.links.copy(two.at[other], self.ref(part, "_three").at[step], self.column[step])
            )
        self.flights[part] = copies

    def total(self, part):
        mine = self.spot[self.parts[part][3]]
        total = self.ref(part, "_home")[self.level, mine]
        total = total + self.ref(part, "_two")[self.level].astype(jnp.float32)
        for step, copy in enumerate(self.flights.pop(part)):
            copy.wait_recv()
            total = total + self.ref(part, "_three")[step].astype(jnp.float32)
        return total

    def fourth(self, part):
        weight, first_column, columns, _ = self.parts[part]
        total = self.total(part)
        start = self.core * self.weights[weight][1] + first_column
        place = pl.ds(pl.multiple_of(start, 128), columns)
        out = self.ref(weight, "_grad")
        out[:, place] = total
        filled = out.at[:, place]
        self.flights[part] = self.links.copy(filled, filled, self.sibling)

    def last(self, part):
        self.flights.pop(part).wait_recv()


def reducer_scratch(weights, parts, depth, tokens):
    low, wide = jnp.bfloat16, jnp.float32
    shapes = {}
    for weight, (rows, half) in weights.items():
        shapes[weight + "_left_other"] = ((4 * depth, rows, tokens), low)
        shapes[weight + "_right_other"] = ((half, tokens), low)
    for part, (weight, _, columns, _) in parts.items():
        rows = weights[weight][0] if weight in weights else weight
        low = wide if weight not in weights else jnp.bfloat16
        shapes[part + "_away"] = ((depth, 2, rows, columns), low)
        shapes[part + "_home"] = ((depth, 2, rows, columns), wide)
        shapes[part + "_one"] = ((depth, 2, rows, columns), low)
        shapes[part + "_two"] = ((depth, rows, columns), low)
        shapes[part + "_three"] = ((depth - 1, rows, columns), low)
    return shapes


def gelu_slope(value):
    scale = math.sqrt(2.0 / math.pi)
    square = value * value
    bent = jnp.tanh(scale * value * (1.0 + 0.044715 * square))
    return 0.5 * (1.0 + bent) + 0.5 * value * (1.0 - bent * bent) * scale * (
        1.0 + 3.0 * 0.044715 * square
    )


def norm_gradient(inputs, gain, grad):
    center = inputs - jnp.mean(inputs, 0, keepdims=True)
    factor = lax.rsqrt(jnp.mean(center * center, 0, keepdims=True) + norm_eps)
    unit = center * factor
    scaled = grad * gain
    result = factor * (
        scaled
        - jnp.mean(scaled, 0, keepdims=True)
        - unit * jnp.mean(scaled * unit, 0, keepdims=True)
    )
    return result, jnp.sum(grad * unit, 1, keepdims=True), jnp.sum(grad, 1, keepdims=True)


def rows_product(matrix, other, out_rows, chunk, store):
    def one_chunk(index, carry):
        rows = pl.ds(pl.multiple_of(index * chunk, 128), chunk)
        store(rows, dot(matrix[rows, :], other))
        return carry

    lax.fori_loop(0, out_rows // chunk, one_chunk, 0)


def back_one_body(n, seqs, groups, span, group_rows, width, hidden_width, refs):
    at = HeadPlaces(n, seqs, groups)
    half = n // 2
    heads = group_rows // HEAD
    tokens = seqs * span
    links, loads = Links(refs), Loads(refs)
    reducer = Reducer(refs, links, groups, back_one_weights(width, hidden_width, n), back_one_parts(width, hidden_width))
    barrier = pltpu.get_barrier_semaphore()
    at.signal_all(barrier, reducer.neighbours()[1:])

    loads.start("w_down", refs.w_down.at[1], refs.down)
    loads.start("cotangent", refs.cotangent, refs.cot)
    loads.start("raised", refs.raised, refs.raised_in)
    loads.start("w_up", refs.w_up.at[1], refs.up)
    loads.start("hidden", refs.hidden, refs.hidden_in)
    loads.start("active", refs.active, refs.down_left)
    loads.start("w_out", refs.w_out.at[1], refs.out)
    loads.start("normed", refs.normed, refs.up_left)
    loads.start("attended", refs.attended, refs.out_left)
    loads.start("held", refs.held, refs.held_in)

    loads.wait("cotangent")
    for seq in range(seqs):
        lanes = slice(seq * span, (seq + 1) * span)
        for first in range(0, width, span):
            piece = refs.cot[seq, :, first : first + span].astype(jnp.float32).T
            refs.grad[first : first + span, lanes] = piece * refs.valid[:, lanes]
    refs.down_right[...] = refs.grad[...].astype(jnp.bfloat16)
    loads.wait("w_down", "raised")

    def store_raised(rows, value):
        slope = gelu_slope(refs.raised_in[rows, :].astype(jnp.float32))
        refs.up_right[rows, :] = (slope * value).astype(jnp.bfloat16)

    rows_product(refs.down, refs.down_right[...], hidden_width, 512, store_raised)
    at.wait_all(barrier, len(reducer.neighbours()) - 1)
    loads.wait("active")
    reducer.exchange(DOWN)
    loads.wait("w_up", "hidden", "normed")
    reducer.exchange(UP)
    d_normed = dot(refs.up[...], refs.up_right[...])
    d_inputs, gain_part, bias_part = norm_gradient(refs.hidden_in[...], refs.gain[...], d_normed)
    refs.small[:, 0:1] = gain_part
    refs.small[:, 1:2] = bias_part
    grad = refs.grad[...] + d_inputs
    refs.grad_out[...] = grad
    refs.out_right[...] = grad.astype(jnp.bfloat16)
    loads.wait("w_out", "attended")
    reducer.exchange(OUT)
    refs.d_attended[...] = dot(refs.out[...], refs.out_right[...]).astype(jnp.bfloat16)

    arrive = links.slots(half)
    leave = links.slots(len(at.targets))
    spread = []
    for count, (device, seq, group) in enumerate(at.targets):
        source = refs.d_attended.at[
            group * group_rows : (group + 1) * group_rows, seq * span : (seq + 1) * span
        ]
        sent = (
            source, refs.landing.at[at.me // 2], refs.send.at[leave + count],
            refs.recv.at[arrive + at.me // 2], device,
        )
        at.send(*sent)
        spread.append(sent)
    loads.wait("held")
    reducer.first(DOWN)
    reducer.first(UP)
    reducer.first(OUT)
    for index in range(half):
        landed = refs.landing.at[index]
        remote(
            landed, landed, refs.send.at[leave], refs.recv.at[arrive + index], at.sibling
        ).wait_recv()

    returned = links.slots(len(at.targets) * heads)
    returning = links.slots(half * heads)
    slot = at.seq * groups + at.group
    going = []
    passed = []

    def send_back(head):
        passed[head].wait_recv()
        for index, device in enumerate(at.sources):
            results = refs.results.at[head, index]
            kept = refs.kept.at[head, index]
            part = refs.partial_recv[head, index].astype(jnp.float32)
            results[1] = (kept[:HEAD] + part[:HEAD]).astype(jnp.bfloat16)
            results[2] = (kept[HEAD:] + part[HEAD:]).astype(jnp.bfloat16)
            into = refs.d_qkv.at[
                :,
                pl.ds(pl.multiple_of(at.group * group_rows + head * HEAD, HEAD), HEAD),
                pl.ds(pl.multiple_of(at.seq * span, span), span),
            ]
            sent = (
                results, into, refs.send.at[returning + head * half + index],
                refs.recv.at[returned + head * len(at.targets) + slot], device,
            )
            at.send(*sent)
            going.append(sent)

    def attend(head):
        fill_heads(refs.held_in, head, group_rows, n, span, refs.key_rows, refs.key_columns)
        fill_heads(refs.held_in, head, 2 * group_rows, n, span, refs.value_rows, None)
        head_rows = slice(head * HEAD, (head + 1) * HEAD)
        refs.key_grads[...] = jnp.zeros_like(refs.key_grads)
        refs.value_grads[...] = jnp.zeros_like(refs.value_grads)
        for index, block in enumerate(at.blocks):
            query = refs.held_in[block, head_rows, :] * jnp.bfloat16(HEAD**-0.5)
            grad = refs.landing[index, head_rows, :]
            log_total = refs.lse[index, head : head + 1, :]
            clear, reach = 2 * index * span, 2 * (index + 1) * span
            pieces = []
            row_term = jnp.zeros((1, span), jnp.float32)
            for first, last in ((0, clear), (clear, reach)):
                if first == last:
                    continue
                scores = dot(refs.key_rows[first:last, :], query)
                if last == reach:
                    scores = jnp.where(
                        causal(clear, reach - clear, block * span, span), scores, masked_score
                    )
                weights = jnp.exp(scores - log_total)
                d_weights = dot(refs.value_rows[first:last, :], grad)
                row_term = row_term + jnp.sum(weights * d_weights, 0, keepdims=True)
                pieces.append((first, last, weights, d_weights))
            d_query = jnp.zeros((HEAD, span), jnp.float32)
            for first, last, weights, d_weights in pieces:
                d_scores = (weights * (d_weights - row_term)).astype(jnp.bfloat16)
                d_query = d_query + dot(refs.key_columns[:, first:last], d_scores)
                refs.key_grads[:, first:last] += dot(query, d_scores, NT)
                refs.value_grads[:, first:last] += dot(grad, weights.astype(jnp.bfloat16), NT)
            refs.results[head, index, 0] = (d_query * HEAD**-0.5).astype(jnp.bfloat16)
        for index in range(half):
            other = pl.ds(pl.multiple_of(block_of(index, 1 - at.core) * span, span), span)
            own = pl.ds(pl.multiple_of(at.blocks[index] * span, span), span)
            refs.partial_send[head, index, :HEAD, :] = refs.key_grads[:, other].astype(jnp.bfloat16)
            refs.partial_send[head, index, HEAD:, :] = refs.value_grads[:, other].astype(jnp.bfloat16)
            refs.kept[head, index, :HEAD, :] = refs.key_grads[:, own]
            refs.kept[head, index, HEAD:, :] = refs.value_grads[:, own]
        passed.append(
            links.copy(refs.partial_send.at[head], refs.partial_recv.at[head], at.sibling)
        )

    for head in range(heads):
        attend(head)
        if head > 0:
            send_back(head - 1)
    reducer.second(DOWN)
    send_back(heads - 1)
    reducer.second(UP)
    reducer.second(OUT)
    for part in (DOWN, UP, OUT):
        reducer.third(part)
    for part in (DOWN, UP, OUT):
        reducer.fourth(part)
    for part in (DOWN, UP, OUT):
        reducer.last(part)
    for head in range(heads):
        for count, (device, seq, group) in enumerate(at.targets):
            landed = refs.d_qkv.at[
                :,
                group * group_rows + head * HEAD : group * group_rows + (head + 1) * HEAD,
                seq * span : (seq + 1) * span,
            ]
            remote(
                landed, landed, refs.send.at[leave],
                refs.recv.at[returned + head * len(at.targets) + count], at.sibling,
            ).wait_recv()
    for sent in spread + going:
        at.wait_sent(*sent)
    links.finish()


def back_one_weights(width, hidden_width, n):
    return {
        DOWN: (hidden_width // n, width // 2),
        UP: (width // n, hidden_width // 2),
        OUT: (width // n, width // 2),
    }


def back_one_parts(width, hidden_width):
    return {
        DOWN: (DOWN, 0, width // 2, 1),
        UP: (UP, 0, hidden_width // 2, 0),
        OUT: (OUT, 0, width // 2, 0),
    }


def back_one(
    cotangent, valid, hidden, raised, normed, active, attended, held, lse, gain,
    w_out, w_up, w_down, collective,
):
    seqs, span, width = cotangent.shape
    n, rows, _ = held.shape
    group_rows = rows // 3
    groups = width // group_rows
    hidden_width = w_up.shape[2]
    tokens = seqs * span
    half, heads = n // 2, group_rows // HEAD
    low, wide = jnp.bfloat16, jnp.float32
    weights, parts = back_one_weights(width, hidden_width, n), back_one_parts(width, hidden_width)
    inputs = dict(
        cotangent=(cotangent, HBM), valid=(valid, VMEM), hidden=(hidden, HBM), raised=(raised, HBM),
        normed=(normed, HBM), active=(active, HBM), attended=(attended, HBM), held=(held, HBM),
        lse=(lse, VMEM), gain=(gain, VMEM), w_out=(w_out, HBM), w_up=(w_up, HBM),
        w_down=(w_down, HBM),
    )
    outputs = dict(
        d_qkv=((3, width, tokens), low, VMEM),
        grad_out=((width, tokens), wide, VMEM),
        small=((width, 2), wide, VMEM),
        down_grad=((weights[DOWN][0], width), wide, VMEM),
        up_grad=((weights[UP][0], hidden_width), wide, VMEM),
        out_grad=((weights[OUT][0], width), wide, VMEM),
    )
    scratch = dict(
        down=(w_down.shape[1:], low), up=(w_up.shape[1:], low), out=(w_out.shape[1:], low),
        cot=(cotangent.shape, low), grad=((width, tokens), wide), hidden_in=((width, tokens), wide),
        raised_in=(raised.shape, raised.dtype), d_attended=((width, tokens), low),
        down_left=(active.shape, low), down_right=((width, tokens), low),
        up_left=(normed.shape, low), up_right=((hidden_width, tokens), low),
        out_left=(attended.shape, low), out_right=((width, tokens), low),
        held_in=(held.shape, low), landing=((half, group_rows, span), low),
        results=((heads, half, 3, HEAD, span), low), kept=((heads, half, 2 * HEAD, span), wide),
        partial_send=((heads, half, 2 * HEAD, span), low),
        partial_recv=((heads, half, 2 * HEAD, span), low),
        key_grads=((HEAD, n * span), wide), value_grads=((HEAD, n * span), wide),
        key_rows=((n * span, HEAD), low), key_columns=((HEAD, n * span), low),
        value_rows=((n * span, HEAD), low),
        **reducer_scratch(weights, parts, groups, tokens),
    )
    body = functools.partial(
        back_one_body, n, seqs, groups, span, group_rows, width, hidden_width
    )
    return launch(body, inputs, outputs, scratch, 120, collective)


def back_two_weights(width, hidden_width, n):
    return {
        QKV: (width // n, 3 * width // 2),
        DOWN: (hidden_width // n, width // 2),
        UP: (width // n, hidden_width // 2),
        OUT: (width // n, width // 2),
    }


def back_two_parts(width, hidden_width):
    return {
        QKV_MORE: (QKV, TILE, 3 * width // 2 - TILE, 1),
        QKV_LESS: (QKV, 0, TILE, 0),
        DOWN: (DOWN, 0, width // 2, 1),
        UP: (UP, 0, hidden_width // 2, 0),
        OUT: (OUT, 0, width // 2, 0),
    }


def back_two_body(n, seqs, span, width, hidden_width, refs):
    channels = width // n
    me, core = lax.axis_index(SEQ), lax.axis_index(BATCH)
    peers = [lax.rem(me + step, n) for step in range(1, n)]
    links, loads = Links(refs), Loads(refs)
    weights, parts = back_two_weights(width, hidden_width, n), back_two_parts(width, hidden_width)
    reducer = Reducer(refs, links, n // 4, weights, parts)
    barrier = pltpu.get_barrier_semaphore()
    for device in [(peer, core) for peer in peers] + [reducer.sibling]:
        pl.semaphore_signal(barrier, inc=1, device_id=device, device_id_type=MESH)
    loads.start("w_qkv", refs.w_qkv.at[1], refs.qkv)
    loads.start("d_qkv", refs.d_qkv, refs.qkv_right)
    loads.start("hidden_two", refs.hidden_two, refs.hidden_two_in)
    loads.start("grad", refs.grad, refs.grad_now)
    loads.start("normed_three", refs.normed_three, refs.qkv_left)
    loads.start("w_down", refs.w_down.at[0], refs.down)
    loads.start("raised", refs.raised, refs.raised_in)
    loads.start("w_up", refs.w_up.at[0], refs.up)
    loads.start("active", refs.active, refs.down_left)
    loads.start("hidden_one", refs.hidden_one, refs.hidden_one_in)
    loads.start("normed_two", refs.normed_two, refs.up_left)
    loads.start("w_out", refs.w_out.at[0], refs.out)
    loads.start("gated", refs.gated, refs.out_left)
    loads.start("queries", refs.queries, refs.queries_in)
    loads.start("mixer", refs.mixer, refs.mixer_in)
    loads.start("carried", refs.carried, refs.carried_in)
    loads.start("held", refs.held, refs.held_in)

    loads.wait("w_qkv", "d_qkv")
    d_normed = dot(refs.qkv[...], refs.qkv_right[...])
    pl.semaphore_wait(barrier, n)
    loads.wait("normed_three")
    reducer.exchange(QKV)
    loads.wait("hidden_two", "grad")
    d_inputs, gain_part, bias_part = norm_gradient(
        refs.hidden_two_in[...], refs.gains[:, 2:3], d_normed
    )
    refs.small[:, 0:1] = gain_part
    refs.small[:, 1:2] = bias_part
    grad = refs.grad_now[...] + d_inputs
    refs.grad_now[...] = grad
    refs.down_right[...] = grad.astype(jnp.bfloat16)
    loads.wait("w_down", "raised", "active")
    reducer.exchange(DOWN)

    def store_raised(rows, value):
        slope = gelu_slope(refs.raised_in[rows, :].astype(jnp.float32))
        refs.up_right[rows, :] = (slope * value).astype(jnp.bfloat16)

    rows_product(refs.down, refs.down_right[...], hidden_width, 512, store_raised)
    loads.wait("w_up", "hidden_one", "normed_two")
    reducer.exchange(UP)
    d_normed = dot(refs.up[...], refs.up_right[...])
    d_inputs, gain_part, bias_part = norm_gradient(
        refs.hidden_one_in[...], refs.gains[:, 1:2], d_normed
    )
    refs.small[:, 2:3] = gain_part
    refs.small[:, 3:4] = bias_part
    grad = refs.grad_now[...] + d_inputs
    refs.grad_out[...] = grad
    refs.out_right[...] = grad.astype(jnp.bfloat16)
    loads.wait("w_out", "gated", "queries", "mixer", "carried")
    reducer.exchange(OUT)
    d_gated = dot(refs.out[...], refs.out_right[...])
    d_mixer = d_gated * refs.queries_in[...]
    for seq in range(seqs):
        refs.d_conv[seq] = d_mixer[:, seq * span : (seq + 1) * span].astype(jnp.bfloat16)
    going = []
    arrive, answered = links.slots(n - 1), links.slots(n - 1)
    for step, peer in enumerate(peers):
        rows = pl.ds(pl.multiple_of(peer * channels, 16), channels)
        going.append(
            links.copy(refs.d_conv.at[:, rows, :], refs.landing.at[me], (peer, core), arrive + step)
        )
    own_rows = pl.ds(pl.multiple_of(me * channels, 16), channels)
    loads.start("own", refs.d_conv.at[:, own_rows, :], refs.landing.at[me])
    refs.d_mixer[...] = d_mixer
    refs.d_queries[...] = (d_gated * refs.mixer_in[...]).astype(jnp.bfloat16)
    refs.small[:, 4:5] = jnp.sum(d_mixer * refs.carried_in[...].astype(jnp.float32), 1, keepdims=True)

    reducer.first(QKV_MORE)
    reducer.first(QKV_LESS)
    reducer.first(DOWN)
    reducer.first(UP)
    reducer.first(OUT)
    total_rows = n * seqs * channels
    loads.wait("held")
    refs.flat_x[...] = refs.held_in[...].astype(jnp.float32).reshape(total_rows, span)
    loads.wait("own")
    for copy in going:
        copy.wait_recv()
    refs.flat_d[...] = refs.landing[...].astype(jnp.float32).reshape(total_rows, span)

    def one_channel(channel, carry):
        mixer_backward_channel(n, seqs, span, channels, refs, channel)
        return carry

    reducer.second(QKV_MORE)
    reducer.second(QKV_LESS)
    lax.fori_loop(0, channels // 2, one_channel, 0, unroll=2)
    reducer.second(DOWN)
    reducer.third(QKV_MORE)
    reducer.third(QKV_LESS)
    lax.fori_loop(channels // 2, channels, one_channel, 0, unroll=2)
    refs.answer[...] = refs.flat_out[...].reshape(n, seqs, channels, span).astype(jnp.bfloat16)
    back = []
    for step, peer in enumerate(peers):
        back.append(
            links.copy(
                refs.answer.at[peer], refs.from_conv.at[:, own_rows, :], (peer, core),
                answered + step,
            )
        )
    loads.start("answer", refs.answer.at[me], refs.from_conv.at[:, own_rows, :])
    states = [
        links.copy(refs.rate_grad, refs.rate_other, reducer.sibling),
        links.copy(refs.weight_grad, refs.weight_other, reducer.sibling),
    ]
    reducer.second(UP)
    reducer.second(OUT)
    for part in (DOWN, UP, OUT):
        reducer.third(part)
    for copy in states:
        copy.wait_recv()
    refs.rate_sum[...] = refs.rate_grad[...] + refs.rate_other[...]
    refs.weight_sum[...] = refs.weight_grad[...] + refs.weight_other[...]
    for part in parts:
        reducer.fourth(part)
    for part in parts:
        reducer.last(part)
    loads.wait("answer")
    for copy in back:
        copy.wait_recv()
    links.finish()


def back_two(
    d_qkv, grad, hidden_two, normed_three, raised, normed_two, active, hidden_one, gated,
    queries, mixer, carried, held, gains, rates, rate_weights, w_qkv, w_out, w_up, w_down, collective,
):
    n, seqs, channels, span = held.shape
    width, hidden_width = w_up.shape[1:]
    tokens = seqs * span
    low, wide = jnp.bfloat16, jnp.float32
    weights, parts = back_two_weights(width, hidden_width, n), back_two_parts(width, hidden_width)
    inputs = dict(
        d_qkv=(d_qkv, HBM), grad=(grad, HBM), hidden_two=(hidden_two, HBM),
        normed_three=(normed_three, HBM), raised=(raised, HBM), normed_two=(normed_two, HBM),
        active=(active, HBM), hidden_one=(hidden_one, HBM), gated=(gated, HBM),
        queries=(queries, HBM), mixer=(mixer, HBM), carried=(carried, HBM), held=(held, HBM),
        gains=(gains, VMEM), rates=(rates, VMEM), rate_weights=(rate_weights, VMEM),
        w_qkv=(w_qkv, HBM), w_out=(w_out, HBM), w_up=(w_up, HBM), w_down=(w_down, HBM),
    )
    square, state = (width, tokens), (channels, 2 * STATES)
    outputs = dict(
        from_conv=((seqs, width, span), low, VMEM),
        d_mixer=(square, wide, VMEM),
        d_queries=(square, low, VMEM),
        grad_out=(square, wide, VMEM),
        small=((width, 5), wide, VMEM),
        rate_sum=(state, wide, VMEM),
        weight_sum=(state, wide, VMEM),
        qkv_grad=((weights[QKV][0], 3 * width), wide, VMEM),
        down_grad=((weights[DOWN][0], width), wide, VMEM),
        up_grad=((weights[UP][0], hidden_width), wide, VMEM),
        out_grad=((weights[OUT][0], width), wide, VMEM),
    )
    flat = (n * seqs * channels, span)
    scratch = dict(
        qkv=(w_qkv.shape[1:], low), down=(w_down.shape[1:], low), up=(w_up.shape[1:], low),
        out=(w_out.shape[1:], low),
        qkv_left=(normed_three.shape, low), qkv_right=((3 * width, tokens), low),
        down_left=(active.shape, low), down_right=(square, low),
        up_left=(normed_two.shape, low), up_right=((hidden_width, tokens), low),
        out_left=(gated.shape, low), out_right=(square, low),
        hidden_two_in=(square, wide), hidden_one_in=(square, wide), grad_now=(square, wide),
        raised_in=(raised.shape, raised.dtype), queries_in=(square, queries.dtype),
        mixer_in=(square, mixer.dtype), carried_in=(square, low), held_in=(held.shape, low),
        d_conv=((seqs, width, span), low), landing=(held.shape, low), answer=(held.shape, low),
        flat_x=(flat, wide), flat_d=(flat, wide), flat_out=(flat, wide),
        rate_grad=(state, wide), weight_grad=(state, wide),
        rate_other=(state, wide), weight_other=(state, wide),
        **reducer_scratch(weights, parts, n // 4, tokens),
    )
    body = functools.partial(back_two_body, n, seqs, span, width, hidden_width)
    return launch(body, inputs, outputs, scratch, 100, collective)


def back_three_weights(width, n):
    return {QKV: (width // n, 3 * width // 2)}


def back_three_parts(width, n):
    return {
        SMALL: (width // n, 0, 128, 0),
        QKV_MORE: (QKV, TILE, 3 * width // 2 - TILE, 1),
        QKV_LESS: (QKV, 0, TILE, 0),
    }


def back_three_body(n, seqs, span, width, refs):
    me, core = lax.axis_index(SEQ), lax.axis_index(BATCH)
    links, loads = Links(refs), Loads(refs)
    weights, parts = back_three_weights(width, n), back_three_parts(width, n)
    reducer = Reducer(refs, links, n // 4, weights, parts)
    barrier = pltpu.get_barrier_semaphore()
    before, after = (lax.rem(me + n - 1, n), core), (lax.rem(me + 1, n), core)
    greeted = [*reducer.neighbours(), before, after]
    for device in greeted:
        pl.semaphore_signal(barrier, inc=1, device_id=device, device_id_type=MESH)
    tokens = seqs * span
    loads.start("from_conv", refs.from_conv, refs.conv_in)
    loads.start("d_mixer", refs.d_mixer, refs.mixer_in)
    loads.start("values", refs.values, refs.values_in)
    loads.start("shifted", refs.shifted, refs.shifted_in)
    loads.start("keys", refs.keys, refs.keys_in)
    loads.start("d_queries", refs.d_queries, refs.qkv_right.at[:width, :])
    loads.start("w_qkv", refs.w_qkv.at[0], refs.qkv)
    loads.start("normed", refs.normed, refs.qkv_left)
    loads.start("hidden", refs.hidden, refs.hidden_in)
    loads.start("grad", refs.grad, refs.grad_in)
    loads.wait("from_conv", "d_mixer", "values", "shifted")
    valid = refs.valid[...]
    conv = jnp.concatenate([refs.conv_in[seq] for seq in range(seqs)], 1).astype(jnp.float32)
    d_carried = (refs.mixer_in[...] * refs.skip[...] + conv) * valid
    d_shifted = d_carried * refs.values_in[...]
    refs.d_shifted[...] = d_shifted
    for seq in range(seqs):
        for first in range(0, width, span):
            turned = d_shifted[first : first + span, seq * span : (seq + 1) * span].T
            refs.rim_out[seq, :, first : first + span] = turned[: refs.rim_out.shape[1]]
    refs.qkv_right[2 * width :, :] = (d_carried * refs.shifted_in[...]).astype(jnp.bfloat16)
    pl.semaphore_wait(barrier, len(greeted))
    halo = links.copy(refs.rim_out, refs.rim_in, before)
    loads.wait("keys")
    halo.wait_recv()
    lane = lax.broadcasted_iota(jnp.int32, (width, span), 1)
    there = jnp.where(me == n - 1, 0.0, 1.0)
    rim = refs.rim_in.shape[1]
    tap_sums = [jnp.zeros((width, 1), jnp.float32) for _ in range(TAPS)]
    for seq in range(seqs):
        lanes = slice(seq * span, (seq + 1) * span)
        own = refs.d_shifted[:, lanes]
        keys = refs.keys_in[:, lanes].astype(jnp.float32)
        pieces = []
        for first in range(0, width, span):
            piece = refs.rim_in[seq, :, first : first + span] * there
            piece = jnp.concatenate([piece, jnp.zeros((span - rim, span), jnp.float32)], 0)
            pieces.append(piece.T)
        following = jnp.concatenate(pieces, 0)
        d_keys = jnp.zeros((width, span), jnp.float32)
        for offset in range(TAPS):
            moved = own
            if offset > 0:
                moved = jnp.where(
                    lane < span - offset,
                    pltpu.roll(own, span - offset, 1),
                    pltpu.roll(following, span - offset, 1),
                )
            d_keys = d_keys + refs.taps[:, offset : offset + 1] * moved
            tap_sums[offset] = tap_sums[offset] + jnp.sum(moved * keys, 1, keepdims=True)
        refs.qkv_right[width : 2 * width, lanes] = d_keys.astype(jnp.bfloat16)
    loads.wait("d_queries", "normed")
    reducer.exchange(QKV)
    loads.wait("w_qkv", "hidden", "grad")
    d_normed = dot(refs.qkv[...], refs.qkv_right[...])
    d_inputs, gain_part, bias_part = norm_gradient(refs.hidden_in[...], refs.gain[...], d_normed)
    refs.total[...] = (refs.grad_in[...] + d_inputs) * valid
    refs.sums[...] = refs.small_in[...]
    for offset in range(TAPS):
        refs.sums[:, 8 + offset : 9 + offset] = tap_sums[offset]
    refs.sums[:, 0:1] = gain_part
    refs.sums[:, 4:5] = bias_part
    shared = links.copy(refs.sums, refs.sums_other, reducer.sibling)
    reducer.first(QKV_MORE)
    reducer.first(QKV_LESS)
    shared.wait_recv()
    rows = width // n
    refs.slices[...] = (refs.sums[...] + refs.sums_other[...]).reshape(n, rows, 128)
    reducer.first_given(SMALL, refs.slices)
    for seq in range(seqs):
        for first in range(0, width, span):
            refs.d_tokens[seq, :, first : first + span] = refs.total[
                first : first + span, seq * span : (seq + 1) * span
            ].T
    order = (QKV_MORE, QKV_LESS, SMALL)
    for part in order:
        reducer.second(part)
    for part in order:
        reducer.third(part)
    reducer.fourth(QKV_MORE)
    reducer.fourth(QKV_LESS)
    total = reducer.total(SMALL)
    padded = jnp.concatenate([total, jnp.zeros((128 - rows, 128), jnp.float32)], 0).T
    refs.small_sum[...] = padded[: refs.small_sum.shape[0], :rows]
    reducer.last(QKV_MORE)
    reducer.last(QKV_LESS)
    links.finish()


def back_three(
    from_conv, d_mixer, d_queries, values, shifted, keys, grad, hidden, normed, valid, gain, skip,
    taps, small, w_qkv, collective,
):
    seqs, width, span = from_conv.shape
    n = normed.shape[0]
    tokens = seqs * span
    low, wide = jnp.bfloat16, jnp.float32
    weights, parts = back_three_weights(width, n), back_three_parts(width, n)
    inputs = dict(
        from_conv=(from_conv, HBM), d_mixer=(d_mixer, HBM), d_queries=(d_queries, HBM),
        values=(values, HBM), shifted=(shifted, HBM), keys=(keys, HBM), grad=(grad, HBM),
        hidden=(hidden, HBM), normed=(normed, HBM), valid=(valid, VMEM), gain=(gain, VMEM),
        skip=(skip, VMEM), taps=(taps, VMEM), small_in=(small, VMEM), w_qkv=(w_qkv, HBM),
    )
    square = (width, tokens)
    outputs = dict(
        d_tokens=((seqs, span, width), wide, VMEM),
        qkv_grad=((width // n, 3 * width), wide, VMEM),
        small_sum=((16, width // n), wide, VMEM),
    )
    scratch = dict(
        qkv=(w_qkv.shape[1:], low), qkv_left=(normed.shape, low), qkv_right=((3 * width, tokens), low),
        conv_in=(from_conv.shape, low), mixer_in=(square, wide), values_in=(square, values.dtype),
        shifted_in=(square, shifted.dtype), keys_in=(square, low), hidden_in=(square, wide),
        grad_in=(square, wide), d_shifted=(square, wide), total=(square, wide),
        rim_out=((seqs, 8, width), wide), rim_in=((seqs, 8, width), wide),
        sums=((width, 128), wide), sums_other=((width, 128), wide),
        slices=((n, width // n, 128), wide),
        **reducer_scratch(weights, parts, n // 4, tokens),
    )
    body = functools.partial(back_three_body, n, seqs, span, width)
    return launch(body, inputs, outputs, scratch, 40, collective)


def per_device_by_heads(
    tokens,
    cotangent,
    lengths,
    norm_gain,
    norm_bias,
    w_qkv,
    w_out,
    w_up,
    w_down,
    taps,
    skip,
    ssm_rate,
    ssm_out,
):
    seq_count, span_rows, width = tokens.shape[1:]
    devices = lax.axis_size(SEQ)
    place = lax.axis_index(SEQ)
    channels = width // devices
    depth = devices // 4
    groups = depth
    rim = TAPS - 1
    row_count = seq_count * span_rows
    positions = place * span_rows + jnp.arange(span_rows, dtype=jnp.int32)
    validity = (positions[None, :] < lengths[0][:, None]).astype(jnp.float32)[:, :, None]
    rates = lax.dynamic_slice_in_dim(ssm_rate, place * channels, channels, 0)
    weights = lax.dynamic_slice_in_dim(ssm_out, place * channels, channels, 0)
    rates = jnp.concatenate([rates, rates], 1)
    weights = jnp.concatenate([weights, weights], 1)

    def to_channels(value):
        return value.transpose(0, 2, 1)

    def feed_forward(inputs, norm_row, layer):
        normed = layer_norm(inputs, norm_gain[norm_row], norm_bias[norm_row]).astype(jnp.bfloat16)
        raised = dense_product(normed, w_up[layer])
        active = jax.nn.gelu(raised).astype(jnp.bfloat16)
        return normed, raised, active, inputs + dense_product(active, w_down[layer])

    flat_in = (tokens[0].astype(jnp.float32) * validity).reshape(row_count, width)
    normed_one = layer_norm(flat_in, norm_gain[0], norm_bias[0]).astype(jnp.bfloat16)
    qkv_one = dense_product(normed_one, w_qkv[0]).reshape(seq_count, span_rows, 3 * width)
    queries_one = qkv_one[:, :, :width]
    keys_one = qkv_one[:, :, width : 2 * width].astype(jnp.bfloat16)
    values_one = qkv_one[:, :, 2 * width :]
    earlier = passed_along(keys_one[:, span_rows - rim :], SEQ, 1)
    extended = jnp.concatenate([earlier, keys_one], 1)

    def tap_rows(offset):
        return extended[:, rim - offset : rim - offset + span_rows].astype(jnp.float32)

    shifted = sum((taps[offset] * tap_rows(offset) for offset in range(TAPS)))
    carried_low = (shifted * values_one * validity).astype(jnp.bfloat16)
    convolved, held = mixer_forward(to_channels(carried_low), rates, weights, devices, 1)
    carried = carried_low.astype(jnp.float32)
    mixer = to_channels(convolved).astype(jnp.float32) + skip * carried
    gated = (queries_one * mixer).reshape(row_count, width).astype(jnp.bfloat16)
    hidden_one = flat_in + dense_product(gated, w_out[0])
    normed_two, raised_one, active_one, hidden_two = feed_forward(hidden_one, 1, 0)
    normed_three = layer_norm(hidden_two, norm_gain[2], norm_bias[2]).astype(jnp.bfloat16)
    qkv_two = dense_product(normed_three, w_qkv[1]).astype(jnp.bfloat16)
    group_rows = width // groups
    qkv_columns = (
        qkv_two.reshape(seq_count, span_rows, 3, groups, group_rows)
        .transpose(0, 3, 2, 4, 1)
        .reshape(seq_count, groups, 3 * group_rows, span_rows)
    )
    attended, kept, log_totals = attention_forward(qkv_columns, devices, 2)
    attended_columns = attended
    attended = attended.T
    hidden_three = hidden_two + dense_product(attended, w_out[1])
    normed_four, raised_two, active_two, hidden_four = feed_forward(hidden_three, 3, 1)
    output = hidden_four.reshape(seq_count, span_rows, width) * validity

    def sliced(value):
        return value.T.reshape(devices, value.shape[1] // devices, row_count)

    valid = validity.reshape(1, row_count)
    back = back_one(
        cotangent[0], valid, hidden_three.T, raised_two.T, sliced(normed_four), sliced(active_two),
        attended_columns.reshape(devices, channels, row_count), kept, log_totals,
        norm_gain[3][:, None], w_out, w_up, w_down, 3,
    )
    out_two_grad, up_two_grad, down_two_grad = back.out_grad, back.up_grad, back.down_grad
    flat = row_count, width

    def turned(value):
        return value.reshape(flat).T

    gains = norm_gain.T
    more = back_two(
        back.d_qkv.reshape(3 * width, row_count), back.grad_out, hidden_two.T, sliced(normed_three),
        raised_one.T, sliced(normed_two), sliced(active_one), hidden_one.T, sliced(gated),
        turned(queries_one), turned(mixer), turned(carried_low), held, gains, rates, weights,
        w_qkv, w_out, w_up, w_down, 4,
    )
    none = jnp.zeros((width, 1), jnp.float32)
    small = jnp.concatenate(
        [
            none, more.small[:, 2:3], more.small[:, 0:1], back.small[:, 0:1],
            none, more.small[:, 3:4], more.small[:, 1:2], back.small[:, 1:2],
            none, none, none, none, more.small[:, 4:5],
            jnp.zeros((width, 128 - 13), jnp.float32),
        ],
        1,
    )
    end = back_three(
        more.from_conv, more.d_mixer, more.d_queries, turned(values_one), turned(shifted),
        turned(keys_one), more.grad_out, flat_in.T, sliced(normed_one), valid,
        gains[:, 0:1], skip[:, None], taps.T, small, w_qkv, 5,
    )
    small = end.small_sum
    return (
        output[None].astype(jnp.bfloat16),
        end.d_tokens[None],
        small[:4],
        small[4:7],
        small[7],
        jnp.stack([end.qkv_grad, more.qkv_grad]),
        jnp.stack([more.out_grad, out_two_grad]),
        jnp.stack([more.up_grad, up_two_grad]),
        jnp.stack([more.down_grad, down_two_grad]),
        small[8 : 8 + TAPS],
        small[8 + TAPS],
        more.rate_sum[:, :STATES],
        more.weight_sum[:, :STATES],
    )


def fits_by_heads(mesh):
    devices = mesh.shape[SEQ]
    return devices == 16 and mesh.shape[BATCH] == 2


def solution(mesh):
    placed = (
        P(BATCH, None, SEQ, None),
        P(BATCH, None, SEQ, None),
        P(BATCH, None),
        P(),
        P(),
        P(),
        P(),
        P(),
        P(),
        P(),
        P(),
        P(),
        P(),
    )
    return jax.shard_map(
        per_device_by_heads if fits_by_heads(mesh) else per_device,
        mesh=mesh,
        in_specs=placed,
        out_specs=(
            P(BATCH, None, SEQ, None),
            P(BATCH, None, SEQ, None),
            P(None, SEQ),
            P(None, SEQ),
            P(SEQ),
            P(None, SEQ, None),
            P(None, SEQ, None),
            P(None, SEQ, None),
            P(None, SEQ, None),
            P(None, SEQ),
            P(SEQ),
            P(SEQ, None),
            P(SEQ, None),
        ),
        check_vma=False,
    )
```

```python
import functools
import math
import types

import jax
import jax.numpy as jnp
from jax import lax
from jax.experimental import pallas as pl
from jax.experimental.pallas import tpu as pltpu
from jax.sharding import PartitionSpec as P

HEADS = 12
HEAD = 64
TAPS = 4
STATES = 64
MESH = pl.DeviceIdType.MESH
SEQ = "seq"
BATCH = "batch"
QKV_MORE = "qkv_more"
QKV_LESS = "qkv_less"
DOWN = "down"
OUT = "out"
UP = "up"
QKV = "qkv"
SMALL = "small"
VMEM_BYTES = 63 * 2**20


norm_eps = 1e-05
highest = lax.Precision.HIGHEST
masked_score = -1e30


def for_sending(array):
    return jax.tree.map(lambda a: a.astype(jnp.bfloat16) if a.dtype == jnp.float32 else a, array)


def passed_along(value, axis, steps):
    count = lax.axis_size(axis)
    initial, last = (max(0, -steps), min(count, count - steps))
    return lax.ppermute(value, axis, [(source, source + steps) for source in range(initial, last)])


def layer_norm(inputs, scale_row, shift_row):
    center = inputs - jnp.mean(inputs, -1, keepdims=True)
    spread = jnp.mean(center * center, -1, keepdims=True)
    return center * lax.rsqrt(spread + norm_eps) * scale_row + shift_row


def dense_product(operand_a, operand_b):
    return jnp.dot(operand_a, operand_b, preferred_element_type=jnp.float32)


def product_left(operand_a, operand_b):
    return lax.dot_general(
        operand_a, operand_b, (((0,), (0,)), ((), ())), preferred_element_type=jnp.float32
    )


def product_right(operand_a, operand_b):
    return lax.dot_general(
        operand_a, operand_b, (((1,), (1,)), ((), ())), preferred_element_type=jnp.float32
    )


def angle_table(count_rows, count_cols, period):
    product_index = (
        jnp.arange(count_rows, dtype=jnp.int32)[:, None]
        * jnp.arange(count_cols, dtype=jnp.int32)[None, :]
        % period
    )
    angles = product_index.astype(jnp.float32) * (2.0 * math.pi / period)
    return (jnp.cos(angles), jnp.sin(angles))


def table_einsum(form, table, data):
    return jnp.einsum(form, table, data, precision=highest)


def forward_spectrum(time_parts):
    count_parts = time_parts.shape[0]
    span_rows = time_parts.shape[2]
    count_freq = 2 * count_parts
    cos_parts, sin_parts = angle_table(count_freq, count_parts, count_freq)
    first_real = table_einsum("fp,pjsc->fjsc", cos_parts, time_parts)
    first_imag = -table_einsum("fp,pjsc->fjsc", sin_parts, time_parts)
    cos_twist, sin_twist = angle_table(count_freq, span_rows, count_freq * span_rows)
    cos_twist = cos_twist[:, None, :, None]
    sin_twist = sin_twist[:, None, :, None]
    twist_real = first_real * cos_twist + first_imag * sin_twist
    twist_imag = first_imag * cos_twist - first_real * sin_twist
    cos_span, sin_span = angle_table(span_rows, span_rows, span_rows)
    out_real = table_einsum("ts,fjsc->fjtc", cos_span, twist_real) + table_einsum(
        "ts,fjsc->fjtc", sin_span, twist_imag
    )
    out_imag = table_einsum("ts,fjsc->fjtc", cos_span, twist_imag) - table_einsum(
        "ts,fjsc->fjtc", sin_span, twist_real
    )
    return (out_real, out_imag)


def inverse_spectrum(freq_real, freq_imag):
    count_freq = freq_real.shape[0]
    span_rows = freq_real.shape[2]
    count_parts = count_freq // 2
    fft_length = count_freq * span_rows
    cos_span, sin_span = angle_table(span_rows, span_rows, span_rows)
    first_real = table_einsum("st,fjtc->fjsc", cos_span, freq_real) - table_einsum(
        "st,fjtc->fjsc", sin_span, freq_imag
    )
    first_imag = table_einsum("st,fjtc->fjsc", cos_span, freq_imag) + table_einsum(
        "st,fjtc->fjsc", sin_span, freq_real
    )
    cos_twist, sin_twist = angle_table(count_freq, span_rows, fft_length)
    cos_twist = cos_twist[:, None, :, None]
    sin_twist = sin_twist[:, None, :, None]
    twist_real = first_real * cos_twist - first_imag * sin_twist
    twist_imag = first_imag * cos_twist + first_real * sin_twist
    cos_parts, sin_parts = angle_table(count_parts, count_freq, count_freq)
    summed = table_einsum("pf,fjsc->pjsc", cos_parts, twist_real) - table_einsum(
        "pf,fjsc->pjsc", sin_parts, twist_imag
    )
    return summed / fft_length


def to_frequency(data_low):
    parts = lax.all_to_all(data_low[None], SEQ, split_axis=3, concat_axis=0, tiled=True)
    return forward_spectrum(parts.astype(jnp.float32))


def from_frequency(freq_real, freq_imag):
    time_parts = inverse_spectrum(freq_real, freq_imag)
    joined = lax.all_to_all(
        for_sending(time_parts), SEQ, split_axis=0, concat_axis=3, tiled=True
    ).astype(time_parts.dtype)
    return joined[0]


def kernel_parts(rate_slice, weight_slice, count_freq, span_rows):
    fft_length = count_freq * span_rows
    length_full = fft_length // 2
    frequency = (
        jnp.arange(count_freq, dtype=jnp.int32)[:, None]
        + count_freq * jnp.arange(span_rows, dtype=jnp.int32)[None, :]
    )
    angles = (frequency.astype(jnp.float32) * (2.0 * math.pi / fft_length))[:, None, :, None, None]
    odd_mask = (frequency % 2 == 1)[:, None, :, None, None]
    channels = rate_slice.shape[0]
    blocks = rate_slice.shape[1] // 8
    rate_blocks = rate_slice.reshape(channels, blocks, 8).transpose(1, 0, 2)
    weight_blocks = weight_slice.reshape(channels, blocks, 8).transpose(1, 0, 2)

    def add_block(running, piece_pair):
        rate_part, weight_part = piece_pair
        decays = jnp.exp(-rate_part)
        half_sine = jnp.sin(angles / 2.0)
        real_den = -jnp.expm1(-rate_part) + decays * 2.0 * half_sine * half_sine
        imag_den = decays * jnp.sin(angles)
        numerator = jnp.where(
            odd_mask, 1.0 + jnp.exp(-rate_part * length_full), -jnp.expm1(-rate_part * length_full)
        )
        factor = weight_part * numerator / (real_den * real_den + imag_den * imag_den)
        return (
            (
                running[0] + jnp.sum(factor * real_den, -1),
                running[1] - jnp.sum(factor * imag_den, -1),
            ),
            None,
        )

    zeros_init = jnp.zeros((count_freq, 1, span_rows, channels), jnp.float32)
    return lax.scan(
        jax.checkpoint(add_block), (zeros_init, zeros_init), (rate_blocks, weight_blocks)
    )[0]


def attention_mask(query_positions, key_count, length_value):
    key_positions = jnp.arange(key_count, dtype=jnp.int32)
    return (key_positions[None, :] <= query_positions[:, None]) & (
        key_positions[None, :] < length_value
    )


def head_slice(matrix, head_index):
    return lax.dynamic_slice_in_dim(matrix, head_index * HEAD, HEAD, 1)


def attend_forward(query_low, keys_low, values_low, length_value, query_positions):
    whole_keys, whole_values = (
        lax.all_gather(keys_low, SEQ, axis=0, tiled=True),
        lax.all_gather(values_low, SEQ, axis=0, tiled=True),
    )
    allowed = attention_mask(query_positions, whole_keys.shape[0], length_value)
    score_scale = HEAD ** (-0.5)

    def head_forward(head_index):
        scores = jnp.where(
            allowed,
            score_scale
            * product_right(head_slice(query_low, head_index), head_slice(whole_keys, head_index)),
            masked_score,
        )
        top_score = jnp.max(scores, -1, keepdims=True)
        expos = jnp.exp(scores - top_score)
        totals = jnp.sum(expos, -1, keepdims=True)
        probs_low = (expos / totals).astype(jnp.bfloat16)
        return (
            dense_product(probs_low, head_slice(whole_values, head_index)),
            (top_score + jnp.log(totals))[:, 0],
        )

    head_outputs, log_totals = lax.map(head_forward, jnp.arange(HEADS, dtype=jnp.int32))
    attended = head_outputs.transpose(1, 0, 2).reshape(query_low.shape[0], HEADS * HEAD)
    return (attended, log_totals, whole_keys, whole_values)


def join_heads(head_rows):
    return head_rows.transpose(1, 0, 2).reshape(head_rows.shape[1], HEADS * HEAD)


def attend_backward(
    query_low, whole_keys, whole_values, log_totals, grad_low, length_value, query_positions
):
    allowed = attention_mask(query_positions, whole_keys.shape[0], length_value)
    score_scale = HEAD ** (-0.5)
    span_rows = query_low.shape[0]

    def query_side(head_index):
        head_query = head_slice(query_low, head_index)
        head_keys = head_slice(whole_keys, head_index)
        head_grad = head_slice(grad_low, head_index)
        scores = jnp.where(
            allowed, score_scale * product_right(head_query, head_keys), masked_score
        )
        weights = jnp.exp(scores - log_totals[head_index][:, None])
        d_weights = product_right(head_grad, head_slice(whole_values, head_index))
        row_term = jnp.sum(weights * d_weights, -1, keepdims=True)
        d_scores = (weights * (d_weights - row_term)).astype(jnp.bfloat16)
        d_query = score_scale * dense_product(d_scores, head_keys)
        return (d_query, row_term[:, 0], d_scores, weights)

    def head_backward(head_index):
        d_query, row_term, d_scores, weights = query_side(head_index)
        head_query = head_slice(query_low, head_index)
        head_grad = head_slice(grad_low, head_index)
        d_keys = score_scale * product_left(d_scores, head_query)
        d_values = product_left(weights.astype(jnp.bfloat16), head_grad)
        return (d_query, d_keys, d_values)

    query_grads, key_grads, value_grads = lax.map(head_backward, jnp.arange(HEADS, dtype=jnp.int32))
    count_rows = span_rows * lax.axis_size(SEQ)
    key_part = (
        lax.slice_in_dim(key_grads, 0, count_rows, axis=1)
        .transpose(1, 0, 2)
        .reshape(count_rows, HEADS * HEAD)
    )
    value_part = (
        lax.slice_in_dim(value_grads, 0, count_rows, axis=1)
        .transpose(1, 0, 2)
        .reshape(count_rows, HEADS * HEAD)
    )
    key_value = lax.psum_scatter(
        jnp.stack([key_part, value_part], 1), SEQ, scatter_dimension=0, tiled=True
    )
    return (join_heads(query_grads), key_value[:, 0], key_value[:, 1])


def per_device(
    tokens,
    cotangent,
    lengths,
    norm_gain,
    norm_bias,
    w_qkv,
    w_out,
    w_up,
    w_down,
    taps,
    skip,
    ssm_rate,
    ssm_out,
):
    seq_count = tokens.shape[1]
    span_rows = tokens.shape[2]
    width = tokens.shape[3]
    devices = lax.axis_size(SEQ)
    place = lax.axis_index(SEQ)
    channels = width // devices
    count_freq = 2 * devices
    fft_length = count_freq * span_rows
    rim = TAPS - 1
    row_count = seq_count * span_rows
    query_positions = place * span_rows + jnp.arange(span_rows, dtype=jnp.int32)
    validity = (query_positions[None, :] < lengths[0][:, None]).astype(jnp.float32)[:, :, None]
    rate_slice = lax.dynamic_slice_in_dim(ssm_rate, place * channels, channels, 0)
    weight_slice = lax.dynamic_slice_in_dim(ssm_out, place * channels, channels, 0)

    def spectrum_of(rate_in, weight_in):
        return kernel_parts(rate_in, weight_in, count_freq, span_rows)

    def feed_forward(inputs, norm_row, layer):
        normed_low = layer_norm(inputs, norm_gain[norm_row], norm_bias[norm_row]).astype(
            jnp.bfloat16
        )
        raised = dense_product(normed_low, w_up[layer])
        active_low = jax.nn.gelu(raised).astype(jnp.bfloat16)
        return (normed_low, raised, active_low, inputs + dense_product(active_low, w_down[layer]))

    def norm_backward(inputs, norm_row, d_normed):
        norm_pull = jax.vjp(layer_norm, inputs, norm_gain[norm_row], norm_bias[norm_row])[1]
        return norm_pull(d_normed)

    def feed_backward(grad_rows, inputs, normed_low, raised, active_low, norm_row, layer):
        branch_low = grad_rows.astype(jnp.bfloat16)
        down_grad = product_left(active_low, branch_low)
        d_active = product_right(branch_low, w_down[layer])
        gelu_pull = jax.vjp(jax.nn.gelu, raised)[1]
        d_raised = gelu_pull(d_active)[0].astype(jnp.bfloat16)
        up_grad = product_left(normed_low, d_raised)
        d_inputs, gain_part, bias_part = norm_backward(
            inputs, norm_row, product_right(d_raised, w_up[layer])
        )
        return (grad_rows + d_inputs, down_grad, up_grad, gain_part, bias_part)

    def forward_pass(token_block):
        masked_in = token_block[0].astype(jnp.float32) * validity
        flat_in = masked_in.reshape(row_count, width)
        normed_one = layer_norm(flat_in, norm_gain[0], norm_bias[0]).astype(jnp.bfloat16)
        qkv_one = dense_product(normed_one, w_qkv[0]).reshape(seq_count, span_rows, 3 * width)
        queries_one = qkv_one[:, :, :width]
        keys_one = qkv_one[:, :, width : 2 * width].astype(jnp.bfloat16)
        values_one = qkv_one[:, :, 2 * width :]
        earlier = passed_along(keys_one[:, span_rows - rim :], SEQ, 1)
        extended = jnp.concatenate([earlier, keys_one], 1)
        shifted = sum(
            (
                taps[offset]
                * extended[:, rim - offset : rim - offset + span_rows].astype(jnp.float32)
                for offset in range(TAPS)
            )
        )
        carried_low = (shifted * values_one * validity).astype(jnp.bfloat16)
        carried_real, carried_imag = to_frequency(carried_low)
        kernel_both, kernel_pull = jax.vjp(spectrum_of, rate_slice, weight_slice)
        kernel_real, kernel_imag = kernel_both
        convolved = from_frequency(
            carried_real * kernel_real - carried_imag * kernel_imag,
            carried_real * kernel_imag + carried_imag * kernel_real,
        )
        carried = carried_low.astype(jnp.float32)
        mixer = convolved + skip * carried
        gated_low = (queries_one * mixer).reshape(row_count, width).astype(jnp.bfloat16)
        hidden_one = flat_in + dense_product(gated_low, w_out[0])
        normed_two, raised_one, active_one, hidden_two = feed_forward(hidden_one, 1, 0)
        normed_three = layer_norm(hidden_two, norm_gain[2], norm_bias[2]).astype(jnp.bfloat16)
        qkv_two = (
            dense_product(normed_three, w_qkv[1])
            .astype(jnp.bfloat16)
            .reshape(seq_count, span_rows, 3 * width)
        )
        attended_list = []
        totals_list = []
        keys_list = []
        values_list = []
        for seq_index in range(seq_count):
            attended, log_totals, whole_keys, whole_values = attend_forward(
                qkv_two[seq_index, :, :width],
                qkv_two[seq_index, :, width : 2 * width],
                qkv_two[seq_index, :, 2 * width :],
                lengths[0, seq_index],
                query_positions,
            )
            attended_list.append(attended)
            totals_list.append(log_totals)
            keys_list.append(whole_keys)
            values_list.append(whole_values)
        attended_low = jnp.concatenate(attended_list, 0).astype(jnp.bfloat16)
        hidden_three = hidden_two + dense_product(attended_low, w_out[1])
        normed_four, raised_two, active_two, hidden_four = feed_forward(hidden_three, 3, 1)
        output = hidden_four.reshape(seq_count, span_rows, width) * validity
        saved = types.SimpleNamespace(
            flat_in=flat_in,
            normed_one=normed_one,
            queries_one=queries_one,
            values_one=values_one,
            extended=extended,
            shifted=shifted,
            carried=carried,
            carried_real=carried_real,
            carried_imag=carried_imag,
            kernel_real=kernel_real,
            kernel_imag=kernel_imag,
            kernel_pull=kernel_pull,
            mixer=mixer,
            gated_low=gated_low,
            hidden_one=hidden_one,
            normed_two=normed_two,
            raised_one=raised_one,
            active_one=active_one,
            hidden_two=hidden_two,
            normed_three=normed_three,
            qkv_two=qkv_two,
            totals_list=totals_list,
            keys_list=keys_list,
            values_list=values_list,
            attended_low=attended_low,
            hidden_three=hidden_three,
            normed_four=normed_four,
            raised_two=raised_two,
            active_two=active_two,
        )
        return (output, saved)

    output = forward_pass(tokens)[0]
    saved = forward_pass(lax.optimization_barrier(tokens))[1]
    grad_rows = (cotangent[0].astype(jnp.float32) * validity).reshape(row_count, width)
    grad_rows, down_two, up_two, gain_four, bias_four = feed_backward(
        grad_rows,
        saved.hidden_three,
        saved.normed_four,
        saved.raised_two,
        saved.active_two,
        3,
        1,
    )
    branch_low = grad_rows.astype(jnp.bfloat16)
    out_two = product_left(saved.attended_low, branch_low)
    d_attended = (
        product_right(branch_low, w_out[1])
        .astype(jnp.bfloat16)
        .reshape(seq_count, span_rows, width)
    )
    qkv_two = saved.qkv_two
    grad_parts = []
    for seq_index in range(seq_count):
        d_query_rows, d_key_rows, d_value_rows = attend_backward(
            qkv_two[seq_index, :, :width],
            saved.keys_list[seq_index],
            saved.values_list[seq_index],
            saved.totals_list[seq_index],
            d_attended[seq_index],
            lengths[0, seq_index],
            query_positions,
        )
        grad_parts.append(jnp.concatenate([d_query_rows, d_key_rows, d_value_rows], -1))
    d_qkv_two = jnp.concatenate(grad_parts, 0).astype(jnp.bfloat16)
    qkv_grad_two = product_left(saved.normed_three, d_qkv_two)
    d_inputs, gain_three, bias_three = norm_backward(
        saved.hidden_two, 2, product_right(d_qkv_two, w_qkv[1])
    )
    grad_rows = grad_rows + d_inputs
    grad_rows, down_one, up_one, gain_two, bias_two = feed_backward(
        grad_rows,
        saved.hidden_one,
        saved.normed_two,
        saved.raised_one,
        saved.active_one,
        1,
        0,
    )
    branch_low = grad_rows.astype(jnp.bfloat16)
    out_one = product_left(saved.gated_low, branch_low)
    d_gated = product_right(branch_low, w_out[0]).reshape(seq_count, span_rows, width)
    d_queries = d_gated * saved.mixer
    d_mixer = d_gated * saved.queries_one
    skip_grad = jnp.sum(d_mixer * saved.carried, (0, 1))
    conv_real, conv_imag = to_frequency(d_mixer.astype(jnp.bfloat16))
    kernel_real = saved.kernel_real
    kernel_imag = saved.kernel_imag
    from_conv = from_frequency(
        kernel_real * conv_real + kernel_imag * conv_imag,
        kernel_real * conv_imag - kernel_imag * conv_real,
    )
    d_carried = d_mixer * skip + from_conv
    carried_real = saved.carried_real
    carried_imag = saved.carried_imag
    cot_real = (
        jnp.sum(carried_real * conv_real + carried_imag * conv_imag, 1, keepdims=True) / fft_length
    )
    cot_imag = (
        jnp.sum(carried_real * conv_imag - carried_imag * conv_real, 1, keepdims=True) / fft_length
    )
    rate_grad, weight_grad = saved.kernel_pull((cot_real, cot_imag))
    d_shifted = d_carried * saved.values_one * validity
    d_values = d_carried * saved.shifted * validity
    extended = saved.extended
    grads_extended = sum(
        (
            jnp.pad(taps[offset] * d_shifted, ((0, 0), (rim - offset, offset), (0, 0)))
            for offset in range(TAPS)
        )
    )
    taps_grad = jnp.stack(
        [
            jnp.sum(
                d_shifted
                * extended[:, rim - offset : rim - offset + span_rows].astype(jnp.float32),
                (0, 1),
            )
            for offset in range(TAPS)
        ]
    )
    later = passed_along(grads_extended[:, :rim], SEQ, -1)
    d_keys = grads_extended[:, rim:] + jnp.pad(later, ((0, 0), (span_rows - rim, 0), (0, 0)))
    d_qkv_one = (
        jnp.concatenate([d_queries, d_keys, d_values], -1)
        .reshape(row_count, 3 * width)
        .astype(jnp.bfloat16)
    )
    qkv_grad_one = product_left(saved.normed_one, d_qkv_one)
    d_inputs, gain_one, bias_one = norm_backward(
        saved.flat_in, 0, product_right(d_qkv_one, w_qkv[0])
    )
    d_tokens = ((grad_rows + d_inputs).reshape(seq_count, span_rows, width) * validity)[None]
    gain_sum, bias_sum, qkv_sum, out_sum, up_sum, down_sum, taps_sum, skip_sum = (
        lax.psum_scatter(
            jnp.stack([gain_one, gain_two, gain_three, gain_four]),
            SEQ,
            scatter_dimension=1,
            tiled=True,
        ),
        lax.psum_scatter(
            jnp.stack([bias_one, bias_two, bias_three, bias_four]),
            SEQ,
            scatter_dimension=1,
            tiled=True,
        ),
        lax.psum_scatter(
            jnp.stack([qkv_grad_one, qkv_grad_two]), SEQ, scatter_dimension=1, tiled=True
        ),
        lax.psum_scatter(jnp.stack([out_one, out_two]), SEQ, scatter_dimension=1, tiled=True),
        lax.psum_scatter(jnp.stack([up_one, up_two]), SEQ, scatter_dimension=1, tiled=True),
        lax.psum_scatter(jnp.stack([down_one, down_two]), SEQ, scatter_dimension=1, tiled=True),
        lax.psum_scatter(taps_grad, SEQ, scatter_dimension=1, tiled=True),
        lax.psum_scatter(skip_grad[None], SEQ, scatter_dimension=1, tiled=True),
    )
    totals = (
        lax.psum(gain_sum.astype(jnp.bfloat16), BATCH).astype(jnp.float32),
        lax.psum(bias_sum.astype(jnp.bfloat16), BATCH).astype(jnp.float32),
        lax.psum(qkv_sum.astype(jnp.bfloat16), BATCH).astype(jnp.float32),
        lax.psum(out_sum.astype(jnp.bfloat16), BATCH).astype(jnp.float32),
        lax.psum(up_sum.astype(jnp.bfloat16), BATCH).astype(jnp.float32),
        lax.psum(down_sum.astype(jnp.bfloat16), BATCH).astype(jnp.float32),
        lax.psum(taps_sum.astype(jnp.bfloat16), BATCH).astype(jnp.float32),
        lax.psum(skip_sum.astype(jnp.bfloat16), BATCH).astype(jnp.float32),
        lax.psum(rate_grad.astype(jnp.bfloat16), BATCH).astype(jnp.float32),
        lax.psum(weight_grad.astype(jnp.bfloat16), BATCH).astype(jnp.float32),
    )
    return (
        output[None].astype(jnp.bfloat16),
        d_tokens,
        totals[0],
        totals[1][:3],
        totals[1][3],
        totals[2],
        totals[3],
        totals[4],
        totals[5],
        totals[6],
        totals[7][0],
        totals[8],
        totals[9],
    )


def other_device(place, core, to_place, to_core):
    return jnp.logical_or(place != to_place, core != to_core)


def greet(devices):
    barrier = pltpu.get_barrier_semaphore()
    for device in devices:
        pl.semaphore_signal(barrier, inc=1, device_id=device, device_id_type=MESH)
    pl.semaphore_wait(barrier, len(devices))


def remote(source, target, send_sem, recv_sem, device):
    return pltpu.make_async_remote_copy(
        src_ref=source,
        dst_ref=target,
        send_sem=send_sem,
        recv_sem=recv_sem,
        device_id=device,
        device_id_type=MESH,
    )


def split_low(value):
    upper = value.astype(jnp.bfloat16)
    return upper, (value - upper.astype(jnp.float32)).astype(jnp.bfloat16)


NN = (((1,), (0,)), ((), ()))
NT = (((1,), (1,)), ((), ()))
TN = (((0,), (0,)), ((), ()))


def dot(left, right, form=NN):
    return lax.dot_general(left, right, form, preferred_element_type=jnp.float32)


def dot_fine(left, right, form=NN):
    left_up, left_low = left
    right_up, right_low = right
    total = dot(left_up, right_up, form) + dot(left_up, right_low, form)
    if left_low is not None:
        total = total + dot(left_low, right_up, form)
    return total


def state_steps(span):
    row = lax.broadcasted_iota(jnp.int32, (span, 2 * STATES), 0)
    lane = lax.broadcasted_iota(jnp.int32, (span, 2 * STATES), 1)
    return jnp.where(lane < STATES, span - 1 - row, row + 1).astype(jnp.float32)


def state_tables(rate_row, weight_row, span):
    steps = state_steps(span)
    table = jnp.exp(-rate_row * steps)
    lane_row = lax.broadcasted_iota(jnp.int32, (8, 2 * STATES), 1)
    lead = jnp.where(lane_row < STATES, 0.0, weight_row * jnp.exp(rate_row))
    response = lax.dot_general(
        lead, table, NT, precision=highest, preferred_element_type=jnp.float32
    )[:1]
    spread = pltpu.roll(
        jnp.broadcast_to(response, (span, span)), 0, 1, stride=1, stride_axis=0
    )
    later = lax.broadcasted_iota(jnp.int32, (span, span), 1)
    earlier = lax.broadcasted_iota(jnp.int32, (span, span), 0)
    toeplitz = jnp.where(later >= earlier, spread, 0.0)
    return table, toeplitz


def shift_rows(value, count):
    if count > 0:
        return jnp.concatenate([jnp.zeros_like(value[:count]), value[:-count]], 0)
    return jnp.concatenate([value[-count:], jnp.zeros_like(value[:-count])], 0)


def scan_states(value, decay, seqs, blocks, direction):
    step = 1
    while step < blocks:
        value = value + shift_rows(value, direction * step * seqs) * jnp.exp(decay * step)
        step *= 2
    return shift_rows(value, direction * seqs)


def fill_tables(channels, span, refs):
    def one_channel(channel, carry):
        table, toeplitz = state_tables(
            refs.rates[pl.ds(channel, 1), :], refs.rate_weights[pl.ds(channel, 1), :], span
        )
        refs.near_up[channel], refs.near_low[channel] = split_low(toeplitz)
        refs.table_up[channel], refs.table_low[channel] = split_low(table)
        return carry

    lax.fori_loop(0, channels, one_channel, 0, unroll=4)


def table_scratch(channels, span):
    shape = ((channels, span, span), jnp.bfloat16)
    return dict(near_up=shape, near_low=shape, table_up=shape, table_low=shape)


def mixer_forward_channel(n, seqs, span, channels, refs, channel):
    rate_row = refs.rates[pl.ds(channel, 1), :]
    weight_row = refs.rate_weights[pl.ds(channel, 1), :]
    rows = pl.ds(channel, n * seqs, stride=channels)
    data = (refs.flat_x[rows, :].astype(jnp.bfloat16), None)
    table_parts = (refs.table_up[channel], refs.table_low[channel])
    inner = dot_fine(data, (refs.near_up[channel], refs.near_low[channel]))
    states = scan_states(dot_fine(data, table_parts), -span * rate_row, seqs, n, 1)
    lane = lax.broadcasted_iota(jnp.int32, states.shape, 1)
    weighted = jnp.where(lane < STATES, 0.0, pltpu.roll(states, STATES, 1) * weight_row)
    refs.flat_out[rows, :] = inner + dot_fine(split_low(weighted), table_parts, NT)


def mixer_backward_channel(n, seqs, span, channels, refs, channel):
    rate_row = refs.rates[pl.ds(channel, 1), :]
    weight_row = refs.rate_weights[pl.ds(channel, 1), :]
    table_parts = (refs.table_up[channel], refs.table_low[channel])
    table = table_parts[0].astype(jnp.float32) + table_parts[1].astype(jnp.float32)
    steps = state_steps(span)
    rows = pl.ds(channel, n * seqs, stride=channels)
    data = refs.flat_x[rows, :].astype(jnp.bfloat16)
    grad = refs.flat_d[rows, :].astype(jnp.bfloat16)
    stepped_parts = split_low(table * steps)
    both_parts = [jnp.concatenate(pair, 1) for pair in zip(table_parts, stepped_parts)]
    count = n * seqs
    sides = dot_fine((jnp.concatenate([data, grad], 0), None), both_parts)
    lane = lax.broadcasted_iota(jnp.int32, (count, 2 * STATES), 1)
    low_lanes = lane < STATES

    def aligned(value):
        return jnp.where(low_lanes, pltpu.roll(value, STATES, 1), 0.0)

    entering = jnp.where(low_lanes, sides[:count, : 2 * STATES], 0.0)
    entering_steps = jnp.where(low_lanes, sides[:count, 2 * STATES :], 0.0)
    leaving = aligned(sides[count:, : 2 * STATES])
    leaving_steps = aligned(sides[count:, 2 * STATES :])
    decay = -span * rate_row
    states = scan_states(entering, decay, seqs, n, 1)
    states_steps = scan_states(states * jnp.exp(decay), decay, seqs, n, 1)
    returned = scan_states(leaving, decay, seqs, n, -1)
    far_weight = jnp.sum(leaving * states, 0, keepdims=True)
    far_rate = jnp.sum(
        leaving_steps * states + returned * entering_steps + span * (leaving * states_steps),
        0, keepdims=True,
    )
    cross = dot(grad, data, TN)
    later = lax.broadcasted_iota(jnp.int32, (span, span), 0)
    earlier = lax.broadcasted_iota(jnp.int32, (span, span), 1)
    cross = jnp.where(later >= earlier, cross, 0.0)
    met = dot_fine(split_low(cross), both_parts)
    met_plain = pltpu.roll(met[:, : 2 * STATES], STATES, 1)
    met_steps = pltpu.roll(met[:, 2 * STATES :], STATES, 1)
    rise = jnp.exp(span * rate_row)
    near_weight = rise * jnp.sum(table * met_plain, 0, keepdims=True)
    near_rate = rise * jnp.sum(
        table * ((steps - span) * met_plain + met_steps), 0, keepdims=True
    )
    lane_row = lane[:1]
    near_weight = jnp.where(lane_row < STATES, pltpu.roll(near_weight, STATES, 1), 0.0)
    near_rate = jnp.where(lane_row < STATES, pltpu.roll(near_rate, STATES, 1), 0.0)
    refs.weight_grad[pl.ds(channel, 1), :] = near_weight + far_weight
    refs.rate_grad[pl.ds(channel, 1), :] = -weight_row * (near_rate + far_rate)
    inner = dot_fine((grad, None), (refs.near_up[channel], refs.near_low[channel]), NT)
    weighted = returned * weight_row
    refs.flat_out[rows, :] = inner + dot_fine(split_low(weighted), table_parts, NT)


def block_of(index, core):
    return 2 * index + lax.rem(index + core, 2)


def keeper_of(block):
    return lax.rem((block + 1) // 2, 2)


class HeadPlaces:
    def __init__(self, n, seqs, groups):
        self.n, self.seqs, self.groups = n, seqs, groups
        self.me, self.core = lax.axis_index(SEQ), lax.axis_index(BATCH)
        self.group = self.me // (2 * seqs)
        self.seq = lax.rem(self.me // 2, seqs)
        self.batch = lax.rem(self.me, 2)
        self.keeper = keeper_of(self.me)
        self.sibling = (self.me, 1 - self.core)
        self.targets = [
            ((group * 2 * seqs + seq * 2 + self.core, self.keeper), seq, group)
            for seq in range(seqs)
            for group in range(groups)
        ]
        self.blocks = [block_of(index, self.core) for index in range(n // 2)]
        self.sources = [(block, self.batch) for block in self.blocks]

    def is_other(self, device):
        return jnp.logical_or(device[0] != self.me, device[1] != self.core)

    def greet(self):
        barrier = pltpu.get_barrier_semaphore()
        self.signal_all(barrier, [])
        self.wait_all(barrier, 0)

    def signal_all(self, barrier, more):
        for device in [target for target, _, _ in self.targets] + self.sources:

            @pl.when(self.is_other(device))
            def _():
                pl.semaphore_signal(barrier, inc=1, device_id=device, device_id_type=MESH)

        for device in [self.sibling, *more]:
            pl.semaphore_signal(barrier, inc=1, device_id=device, device_id_type=MESH)

    def wait_all(self, barrier, more):
        kept = jnp.logical_and(self.batch == self.core, self.is_kept_here())
        count = len(self.targets) + len(self.sources) + 1 + more
        pl.semaphore_wait(barrier, count - 2 * kept.astype(jnp.int32))

    def is_kept_here(self):
        return self.keeper == self.core

    def send(self, source, target, send_sem, recv_sem, device):
        @pl.when(self.is_other(device))
        def _():
            remote(source, target, send_sem, recv_sem, device).start()

        @pl.when(jnp.logical_not(self.is_other(device)))
        def _():
            pltpu.make_async_copy(source, target, recv_sem).start()

    def wait_sent(self, source, target, send_sem, recv_sem, device):
        @pl.when(self.is_other(device))
        def _():
            remote(source, target, send_sem, recv_sem, device).wait_send()


def fill_head(held, head, part, n, span, rows_out, columns_out):
    for block in range(n):
        piece = held[head, block, part * HEAD : (part + 1) * HEAD, :]
        if rows_out is not None:
            rows_out[block * span : (block + 1) * span, :] = piece.T
        if columns_out is not None:
            columns_out[:, block * span : (block + 1) * span] = piece


def causal(first_key, rows, first_query, span):
    key = first_key + lax.broadcasted_iota(jnp.int32, (rows, span), 0)
    query = first_query + lax.broadcasted_iota(jnp.int32, (rows, span), 1)
    return key <= query


TILE = 384
VMEM, HBM = pltpu.VMEM, pl.ANY


def launch(body, inputs, outputs, scratch, copies, collective):
    names = [*inputs, *outputs, *scratch, "send", "recv", "local"]

    def kernel(*refs):
        body(types.SimpleNamespace(**dict(zip(names, refs))))

    dma = pltpu.SemaphoreType.DMA
    results = pl.pallas_call(
        kernel,
        out_shape=tuple(jax.ShapeDtypeStruct(shape, kind) for shape, kind, _ in outputs.values()),
        in_specs=[pl.BlockSpec(memory_space=space) for _, space in inputs.values()],
        out_specs=tuple(pl.BlockSpec(memory_space=space) for _, _, space in outputs.values()),
        scratch_shapes=[pltpu.VMEM(shape, kind) for shape, kind in scratch.values()]
        + [dma((copies,)), dma((copies,)), dma((LOCAL_COPIES,))],
        compiler_params=pltpu.CompilerParams(
            collective_id=collective, has_side_effects=True, vmem_limit_bytes=VMEM_BYTES
        ),
    )(*(array for array, _ in inputs.values()))
    return types.SimpleNamespace(**dict(zip(outputs, results)))


LOCAL_COPIES = 64


class Loads:
    def __init__(self, refs):
        self.semaphores, self.used = refs.local, 0

    def start(self, source, target):
        copy = pltpu.make_async_copy(source, target, self.semaphores.at[self.used])
        self.used += 1
        copy.start()
        return copy


class Links:
    def __init__(self, refs):
        self.send, self.recv, self.used, self.unsent = refs.send, refs.recv, 0, []

    def slots(self, count):
        self.used += count
        return self.used - count

    def copy(self, source, target, device, slot=None):
        slot = self.slots(1) if slot is None else slot
        made = remote(source, target, self.send.at[slot], self.recv.at[slot], device)
        made.start()
        self.unsent.append(made)
        return made

    def finish(self):
        for made in self.unsent:
            made.wait_send()


class Reducer:
    def __init__(self, refs, links, depth, weights, parts):
        self.refs, self.links, self.depth = refs, links, depth
        self.weights, self.parts = weights, parts
        self.me, self.core = lax.axis_index(SEQ), lax.axis_index(BATCH)
        self.level = self.me // 4
        self.spot = (lax.rem(self.me // 2, 2), lax.rem(self.me, 2))
        base = self.level * 4
        self.across = [
            (base + self.spot[0] * 2 + (1 - self.spot[1]), self.core),
            (base + (1 - self.spot[0]) * 2 + self.spot[1], self.core),
        ]
        self.sibling = (self.me, 1 - self.core)
        self.levels = [lax.rem(self.level + step, depth) for step in range(1, depth)]
        self.column = [
            (other * 4 + self.spot[0] * 2 + self.spot[1], self.core) for other in self.levels
        ]
        self.flights = {}

    def neighbours(self):
        return [self.sibling, *self.across, *self.column]

    def ref(self, name, suffix):
        return getattr(self.refs, name + suffix)

    def exchange(self, weight):
        half = self.weights[weight][1]
        theirs = pl.ds(pl.multiple_of((1 - self.core) * half, 16), half)
        self.flights[weight] = [
            self.links.copy(
                self.ref(weight, "_left"), self.ref(weight, "_left_other"), self.sibling
            ),
            self.links.copy(
                self.ref(weight, "_right").at[theirs, :], self.ref(weight, "_right_other"),
                self.sibling,
            ),
        ]

    def product(self, part, first, outers, column):
        weight, first_column, _, axis = self.parts[part]
        half = self.weights[weight][1]
        places = [
            outer * 4 + (inner * 2 + first if axis == 0 else first * 2 + inner)
            for outer in outers
            for inner in range(2)
        ]
        left, left_other = self.ref(weight, "_left"), self.ref(weight, "_left_other")
        mine = jnp.concatenate([left[place] for place in places], 0)
        other = jnp.concatenate([left_other[place] for place in places], 0)
        start = first_column + column
        own = pl.ds(pl.multiple_of(self.core * half + start, 16), TILE)
        there = pl.ds(pl.multiple_of(start, 16), TILE)
        return dot(mine, self.ref(weight, "_right")[own, :], NT) + dot(
            other, self.ref(weight, "_right_other")[there, :], NT
        )

    def fill(self, part, first, buffer):
        weight, _, columns, _ = self.parts[part]
        rows = self.weights[weight][0]
        outers = [[outer] for outer in range(self.depth)]
        if rows * 2 < TILE:
            outers = [list(range(self.depth))]

        def one_column(tile, carry):
            column = tile * TILE
            place = pl.ds(pl.multiple_of(column, 128), TILE)
            for group in outers:
                value = self.product(part, first, group, column)
                buffer[group[0] : group[-1] + 1, :, :, place] = value.reshape(
                    len(group), 2, rows, TILE
                ).astype(buffer.dtype)
            return carry

        if columns == TILE:
            one_column(0, 0)
        else:
            lax.fori_loop(0, columns // TILE, one_column, 0)

    def first(self, part):
        weight, _, _, axis = self.parts[part]
        for flight in self.flights.pop(weight, ()):
            flight.wait_recv()
        mine = self.spot[1 - axis]
        self.fill(part, 1 - mine, self.ref(part, "_away"))
        self.flights[part] = self.links.copy(
            self.ref(part, "_away"), self.ref(part, "_one"), self.across[axis]
        )
        self.fill(part, mine, self.ref(part, "_home"))

    def first_given(self, part, values):
        axis = self.parts[part][3]
        mine = self.spot[1 - axis]
        for outer in range(self.depth):
            for inner in range(2):
                there, here = (
                    outer * 4 + (inner * 2 + first if axis == 0 else first * 2 + inner)
                    for first in (1 - mine, mine)
                )
                self.ref(part, "_away")[outer, inner] = values[there]
                self.ref(part, "_home")[outer, inner] = values[here]
        self.flights[part] = self.links.copy(
            self.ref(part, "_away"), self.ref(part, "_one"), self.across[axis]
        )

    def second(self, part):
        axis = self.parts[part][3]
        self.flights.pop(part).wait_recv()
        mine = self.spot[axis]
        home, one = self.ref(part, "_home"), self.ref(part, "_one")
        for outer in range(self.depth):
            one[outer, 1 - mine] = (
                home[outer, 1 - mine].astype(jnp.float32)
                + one[outer, 1 - mine].astype(jnp.float32)
            ).astype(one.dtype)
        self.flights[part] = self.links.copy(
            one.at[:, 1 - mine], self.ref(part, "_two"), self.across[1 - axis]
        )
        for outer in range(self.depth):
            home[outer, mine] = (
                home[outer, mine].astype(jnp.float32) + one[outer, mine].astype(jnp.float32)
            ).astype(home.dtype)

    def third(self, part):
        axis = self.parts[part][3]
        self.flights.pop(part).wait_recv()
        mine = self.spot[axis]
        home, two = self.ref(part, "_home"), self.ref(part, "_two")
        copies = []
        for step, other in enumerate(self.levels):
            two[other] = (
                home[other, mine].astype(jnp.float32) + two[other].astype(jnp.float32)
            ).astype(two.dtype)
            copies.append(
                self.links.copy(two.at[other], self.ref(part, "_three").at[step], self.column[step])
            )
        self.flights[part] = copies

    def total(self, part):
        mine = self.spot[self.parts[part][3]]
        total = self.ref(part, "_home")[self.level, mine].astype(jnp.float32)
        total = total + self.ref(part, "_two")[self.level].astype(jnp.float32)
        for step, copy in enumerate(self.flights.pop(part)):
            copy.wait_recv()
            total = total + self.ref(part, "_three")[step].astype(jnp.float32)
        return total

    def fourth(self, part):
        weight, first_column, columns, _ = self.parts[part]
        total = self.total(part)
        start = self.core * self.weights[weight][1] + first_column
        place = pl.ds(pl.multiple_of(start, 128), columns)
        out = self.ref(weight, "_grad")
        out[:, place] = total
        filled = out.at[:, place]
        self.flights[part] = self.links.copy(filled, filled, self.sibling)

    def last(self, part):
        self.flights.pop(part).wait_recv()


def reducer_scratch(weights, parts, depth, tokens):
    low, wide = jnp.bfloat16, jnp.float32
    shapes = {}
    for weight, (rows, half) in weights.items():
        shapes[weight + "_left_other"] = ((4 * depth, rows, tokens), low)
        shapes[weight + "_right_other"] = ((half, tokens), low)
    for part, (weight, _, columns, _) in parts.items():
        rows = weights[weight][0] if weight in weights else weight
        low = wide if weight not in weights else jnp.bfloat16
        shapes[part + "_away"] = ((depth, 2, rows, columns), low)
        shapes[part + "_home"] = ((depth, 2, rows, columns), low)
        shapes[part + "_one"] = ((depth, 2, rows, columns), low)
        shapes[part + "_two"] = ((depth, rows, columns), low)
        shapes[part + "_three"] = ((depth - 1, rows, columns), low)
    return shapes


def gelu_slope(value):
    scale = math.sqrt(2.0 / math.pi)
    square = value * value
    bent = jnp.tanh(scale * value * (1.0 + 0.044715 * square))
    return 0.5 * (1.0 + bent) + 0.5 * value * (1.0 - bent * bent) * scale * (
        1.0 + 3.0 * 0.044715 * square
    )


def gelu_and_slope(value):
    scale = math.sqrt(2.0 / math.pi)
    square = value * value
    bent = jnp.tanh(scale * value * (1.0 + 0.044715 * square))
    half = 0.5 * (1.0 + bent)
    slope = half + 0.5 * value * (1.0 - bent * bent) * scale * (1.0 + 3.0 * 0.044715 * square)
    return value * half, slope


def norm_gradient(inputs, gain, grad):
    center = inputs - jnp.mean(inputs, 0, keepdims=True)
    factor = lax.rsqrt(jnp.mean(center * center, 0, keepdims=True) + norm_eps)
    unit = center * factor
    scaled = grad * gain
    result = factor * (
        scaled
        - jnp.mean(scaled, 0, keepdims=True)
        - unit * jnp.mean(scaled * unit, 0, keepdims=True)
    )
    return result, jnp.sum(grad * unit, 1, keepdims=True), jnp.sum(grad, 1, keepdims=True)


def rows_product(matrix, other, out_rows, chunk, store):
    def one_chunk(index, carry):
        rows = pl.ds(pl.multiple_of(index * chunk, 128), chunk)
        store(rows, dot(matrix[rows, :], other))
        return carry

    lax.fori_loop(0, out_rows // chunk, one_chunk, 0)


def back_one_body(n, seqs, groups, span, group_rows, width, hidden_width, refs):
    at = HeadPlaces(n, seqs, groups)
    half = n // 2
    heads = group_rows // HEAD
    tokens = seqs * span
    links, loads = Links(refs), Loads(refs)
    reducer = Reducer(refs, links, groups, back_one_weights(width, hidden_width, n), back_one_parts(width, hidden_width))
    barrier = pltpu.get_barrier_semaphore()
    at.signal_all(barrier, reducer.neighbours()[1:])

    load_w_down = loads.start(refs.w_down.at[1], refs.down)
    load_cotangent = loads.start(refs.cotangent, refs.cot)
    load_slope = loads.start(refs.slope, refs.slope_in)
    load_w_up = loads.start(refs.w_up.at[1], refs.up)
    load_hidden = loads.start(refs.hidden, refs.hidden_in)
    load_active = loads.start(refs.active, refs.down_left)
    load_w_out = loads.start(refs.w_out.at[1], refs.out)
    load_normed = loads.start(refs.normed, refs.up_left)
    load_attended = loads.start(refs.attended, refs.out_left)
    load_held = loads.start(refs.held, refs.held_in)

    load_cotangent.wait()
    for seq in range(seqs):
        lanes = slice(seq * span, (seq + 1) * span)
        for first in range(0, width, span):
            piece = refs.cot[seq, :, first : first + span].astype(jnp.float32).T
            refs.grad[first : first + span, lanes] = piece * refs.valid[:, lanes]
    refs.down_right[...] = refs.grad[...].astype(jnp.bfloat16)
    load_w_down.wait()
    load_slope.wait()

    def store_raised(rows, value):
        slope = refs.slope_in[rows, :].astype(jnp.float32)
        refs.up_right[rows, :] = (slope * value).astype(jnp.bfloat16)

    rows_product(refs.down, refs.down_right[...], hidden_width, 512, store_raised)
    at.wait_all(barrier, len(reducer.neighbours()) - 1)
    load_active.wait()
    reducer.exchange(DOWN)
    load_w_up.wait()
    load_hidden.wait()
    load_normed.wait()
    reducer.exchange(UP)
    d_normed = dot(refs.up[...], refs.up_right[...])
    d_inputs, gain_part, bias_part = norm_gradient(refs.hidden_in[...], refs.gain[...], d_normed)
    refs.small[:, 0:1] = gain_part
    refs.small[:, 1:2] = bias_part
    grad = refs.grad[...] + d_inputs
    refs.grad_out[...] = grad
    refs.out_right[...] = grad.astype(jnp.bfloat16)
    load_w_out.wait()
    load_attended.wait()
    reducer.exchange(OUT)
    refs.d_attended[...] = dot(refs.out[...], refs.out_right[...]).astype(jnp.bfloat16)

    arrive = links.slots(half)
    leave = links.slots(len(at.targets))
    spread = []
    for count, (device, seq, group) in enumerate(at.targets):
        source = refs.d_attended.at[
            group * group_rows : (group + 1) * group_rows, seq * span : (seq + 1) * span
        ]
        sent = (
            source, refs.landing.at[at.me // 2], refs.send.at[leave + count],
            refs.recv.at[arrive + at.me // 2], device,
        )
        at.send(*sent)
        spread.append(sent)
    load_held.wait()
    reducer.first(DOWN)
    reducer.first(UP)
    reducer.first(OUT)
    for index in range(half):
        landed = refs.landing.at[index]
        remote(
            landed, landed, refs.send.at[leave], refs.recv.at[arrive + index], at.sibling
        ).wait_recv()

    returned = links.slots(len(at.targets) * heads)
    returning = links.slots(half * heads)
    slot = at.seq * groups + at.group
    going = []
    passed = []

    def send_back(head):
        passed[head].wait_recv()
        for index, device in enumerate(at.sources):
            results = refs.results.at[head, index]
            kept = refs.kept.at[head, index]
            part = refs.partial_recv[head, index].astype(jnp.float32)
            results[1] = (kept[:HEAD] + part[:HEAD]).astype(jnp.bfloat16)
            results[2] = (kept[HEAD:] + part[HEAD:]).astype(jnp.bfloat16)
            into = refs.d_qkv.at[
                :,
                pl.ds(pl.multiple_of(at.group * group_rows + head * HEAD, HEAD), HEAD),
                pl.ds(pl.multiple_of(at.seq * span, span), span),
            ]
            sent = (
                results, into, refs.send.at[returning + head * half + index],
                refs.recv.at[returned + head * len(at.targets) + slot], device,
            )
            at.send(*sent)
            going.append(sent)

    def attend(head):
        fill_head(refs.held_in, head, 1, n, span, refs.key_rows, refs.key_columns)
        fill_head(refs.held_in, head, 2, n, span, refs.value_rows, None)
        head_rows = slice(head * HEAD, (head + 1) * HEAD)
        refs.key_grads[...] = jnp.zeros_like(refs.key_grads)
        refs.value_grads[...] = jnp.zeros_like(refs.value_grads)
        for index, block in enumerate(at.blocks):
            query = refs.held_in[head, block, :HEAD, :] * jnp.bfloat16(HEAD**-0.5)
            grad = refs.landing[index, head_rows, :]
            log_total = refs.lse[index, head : head + 1, :]
            clear, reach = 2 * index * span, 2 * (index + 1) * span
            pieces = []
            row_term = jnp.zeros((1, span), jnp.float32)
            for first, last in ((0, clear), (clear, reach)):
                if first == last:
                    continue
                scores = dot(refs.key_rows[first:last, :], query)
                if last == reach:
                    scores = jnp.where(
                        causal(clear, reach - clear, block * span, span), scores, masked_score
                    )
                weights = jnp.exp(scores - log_total)
                d_weights = dot(refs.value_rows[first:last, :], grad)
                row_term = row_term + jnp.sum(weights * d_weights, 0, keepdims=True)
                pieces.append((first, last, weights, d_weights))
            d_query = jnp.zeros((HEAD, span), jnp.float32)
            for first, last, weights, d_weights in pieces:
                d_scores = (weights * (d_weights - row_term)).astype(jnp.bfloat16)
                d_query = d_query + dot(refs.key_columns[:, first:last], d_scores)
                refs.key_grads[:, first:last] += dot(query, d_scores, NT)
                refs.value_grads[:, first:last] += dot(grad, weights.astype(jnp.bfloat16), NT)
            refs.results[head, index, 0] = (d_query * HEAD**-0.5).astype(jnp.bfloat16)
        for index in range(half):
            other = pl.ds(pl.multiple_of(block_of(index, 1 - at.core) * span, span), span)
            own = pl.ds(pl.multiple_of(at.blocks[index] * span, span), span)
            refs.partial_send[head, index, :HEAD, :] = refs.key_grads[:, other].astype(jnp.bfloat16)
            refs.partial_send[head, index, HEAD:, :] = refs.value_grads[:, other].astype(jnp.bfloat16)
            refs.kept[head, index, :HEAD, :] = refs.key_grads[:, own]
            refs.kept[head, index, HEAD:, :] = refs.value_grads[:, own]
        passed.append(
            links.copy(refs.partial_send.at[head], refs.partial_recv.at[head], at.sibling)
        )

    for head in range(heads):
        attend(head)
        if head > 0:
            send_back(head - 1)
    reducer.second(DOWN)
    send_back(heads - 1)
    reducer.second(UP)
    reducer.second(OUT)
    for part in (DOWN, UP, OUT):
        reducer.third(part)
    for part in (DOWN, UP, OUT):
        reducer.fourth(part)
    for part in (DOWN, UP, OUT):
        reducer.last(part)
    for head in range(heads):
        for count, (device, seq, group) in enumerate(at.targets):
            landed = refs.d_qkv.at[
                :,
                group * group_rows + head * HEAD : group * group_rows + (head + 1) * HEAD,
                seq * span : (seq + 1) * span,
            ]
            remote(
                landed, landed, refs.send.at[leave],
                refs.recv.at[returned + head * len(at.targets) + count], at.sibling,
            ).wait_recv()
    for sent in spread + going:
        at.wait_sent(*sent)
    links.finish()


def back_one_weights(width, hidden_width, n):
    return {
        DOWN: (hidden_width // n, width // 2),
        UP: (width // n, hidden_width // 2),
        OUT: (width // n, width // 2),
    }


def back_one_parts(width, hidden_width):
    return {
        DOWN: (DOWN, 0, width // 2, 1),
        UP: (UP, 0, hidden_width // 2, 0),
        OUT: (OUT, 0, width // 2, 0),
    }


def back_one(
    cotangent, valid, hidden, slope, normed, active, attended, held, lse, gain,
    w_out, w_up, w_down, collective,
):
    seqs, span, width = cotangent.shape
    heads, n = held.shape[:2]
    group_rows = heads * HEAD
    groups = width // group_rows
    hidden_width = w_up.shape[2]
    tokens = seqs * span
    half = n // 2
    low, wide = jnp.bfloat16, jnp.float32
    weights, parts = back_one_weights(width, hidden_width, n), back_one_parts(width, hidden_width)
    inputs = dict(
        cotangent=(cotangent, HBM), valid=(valid, VMEM), hidden=(hidden, HBM), slope=(slope, HBM),
        normed=(normed, HBM), active=(active, HBM), attended=(attended, HBM), held=(held, HBM),
        lse=(lse, VMEM), gain=(gain, VMEM), w_out=(w_out, HBM), w_up=(w_up, HBM),
        w_down=(w_down, HBM),
    )
    outputs = dict(
        d_qkv=((3, width, tokens), low, VMEM),
        grad_out=((width, tokens), wide, VMEM),
        small=((width, 2), wide, VMEM),
        down_grad=((weights[DOWN][0], width), wide, VMEM),
        up_grad=((weights[UP][0], hidden_width), wide, VMEM),
        out_grad=((weights[OUT][0], width), wide, VMEM),
    )
    scratch = dict(
        down=(w_down.shape[1:], low), up=(w_up.shape[1:], low), out=(w_out.shape[1:], low),
        cot=(cotangent.shape, low), grad=((width, tokens), wide), hidden_in=((width, tokens), wide),
        slope_in=(slope.shape, low), d_attended=((width, tokens), low),
        down_left=(active.shape, low), down_right=((width, tokens), low),
        up_left=(normed.shape, low), up_right=((hidden_width, tokens), low),
        out_left=(attended.shape, low), out_right=((width, tokens), low),
        held_in=(held.shape, low), landing=((half, group_rows, span), low),
        results=((heads, half, 3, HEAD, span), low), kept=((heads, half, 2 * HEAD, span), wide),
        partial_send=((heads, half, 2 * HEAD, span), low),
        partial_recv=((heads, half, 2 * HEAD, span), low),
        key_grads=((HEAD, n * span), wide), value_grads=((HEAD, n * span), wide),
        key_rows=((n * span, HEAD), low), key_columns=((HEAD, n * span), low),
        value_rows=((n * span, HEAD), low),
        **reducer_scratch(weights, parts, groups, tokens),
    )
    body = functools.partial(
        back_one_body, n, seqs, groups, span, group_rows, width, hidden_width
    )
    return launch(body, inputs, outputs, scratch, 120, collective)


def back_two_weights(width, hidden_width, n):
    return {
        QKV: (width // n, 3 * width // 2),
        DOWN: (hidden_width // n, width // 2),
        UP: (width // n, hidden_width // 2),
        OUT: (width // n, width // 2),
    }


def back_two_parts(width, hidden_width):
    return {
        QKV_MORE: (QKV, TILE, 3 * width // 2 - TILE, 1),
        QKV_LESS: (QKV, 0, TILE, 0),
        DOWN: (DOWN, 0, width // 2, 1),
        UP: (UP, 0, hidden_width // 2, 0),
        OUT: (OUT, 0, width // 2, 0),
    }


def back_two_body(n, seqs, span, width, hidden_width, refs):
    channels = width // n
    me, core = lax.axis_index(SEQ), lax.axis_index(BATCH)
    peers = [lax.rem(me + step, n) for step in range(1, n)]
    links, loads = Links(refs), Loads(refs)
    weights, parts = back_two_weights(width, hidden_width, n), back_two_parts(width, hidden_width)
    reducer = Reducer(refs, links, n // 4, weights, parts)
    barrier = pltpu.get_barrier_semaphore()
    for device in [(peer, core) for peer in peers] + [reducer.sibling]:
        pl.semaphore_signal(barrier, inc=1, device_id=device, device_id_type=MESH)
    load_w_qkv = loads.start(refs.w_qkv.at[1], refs.qkv)
    load_d_qkv = loads.start(refs.d_qkv, refs.qkv_right)
    load_hidden_two = loads.start(refs.hidden_two, refs.hidden_two_in)
    load_grad = loads.start(refs.grad, refs.grad_now)
    load_normed_three = loads.start(refs.normed_three, refs.qkv_left)
    load_w_down = loads.start(refs.w_down.at[0], refs.down)
    load_slope = loads.start(refs.slope, refs.slope_in)
    load_w_up = loads.start(refs.w_up.at[0], refs.up)
    load_active = loads.start(refs.active, refs.down_left)
    load_hidden_one = loads.start(refs.hidden_one, refs.hidden_one_in)
    load_normed_two = loads.start(refs.normed_two, refs.up_left)
    load_w_out = loads.start(refs.w_out.at[0], refs.out)
    load_gated = loads.start(refs.gated, refs.out_left)
    load_queries = loads.start(refs.queries, refs.queries_in)
    load_mixer = loads.start(refs.mixer, refs.mixer_in)
    load_carried = loads.start(refs.carried, refs.carried_in)
    load_held = loads.start(refs.held, refs.held_in)

    load_w_qkv.wait()
    load_d_qkv.wait()
    d_normed = dot(refs.qkv[...], refs.qkv_right[...])
    pl.semaphore_wait(barrier, n)
    load_normed_three.wait()
    reducer.exchange(QKV)
    load_hidden_two.wait()
    load_grad.wait()
    d_inputs, gain_part, bias_part = norm_gradient(
        refs.hidden_two_in[...], refs.gains[:, 2:3], d_normed
    )
    refs.small[:, 0:1] = gain_part
    refs.small[:, 1:2] = bias_part
    grad = refs.grad_now[...] + d_inputs
    refs.grad_now[...] = grad
    refs.down_right[...] = grad.astype(jnp.bfloat16)
    load_w_down.wait()
    load_slope.wait()
    load_active.wait()
    reducer.exchange(DOWN)

    def store_raised(rows, value):
        slope = refs.slope_in[rows, :].astype(jnp.float32)
        refs.up_right[rows, :] = (slope * value).astype(jnp.bfloat16)

    rows_product(refs.down, refs.down_right[...], hidden_width, 512, store_raised)
    load_w_up.wait()
    load_hidden_one.wait()
    load_normed_two.wait()
    reducer.exchange(UP)
    d_normed = dot(refs.up[...], refs.up_right[...])
    d_inputs, gain_part, bias_part = norm_gradient(
        refs.hidden_one_in[...], refs.gains[:, 1:2], d_normed
    )
    refs.small[:, 2:3] = gain_part
    refs.small[:, 3:4] = bias_part
    grad = refs.grad_now[...] + d_inputs
    refs.grad_out[...] = grad
    refs.out_right[...] = grad.astype(jnp.bfloat16)
    load_w_out.wait()
    load_gated.wait()
    load_queries.wait()
    load_mixer.wait()
    load_carried.wait()
    reducer.exchange(OUT)
    d_gated = dot(refs.out[...], refs.out_right[...])
    d_mixer = d_gated * refs.queries_in[...]
    for seq in range(seqs):
        refs.d_conv[seq] = d_mixer[:, seq * span : (seq + 1) * span].astype(jnp.bfloat16)
    going = []
    arrive, answered = links.slots(n - 1), links.slots(n - 1)
    for step, peer in enumerate(peers):
        rows = pl.ds(pl.multiple_of(peer * channels, 16), channels)
        going.append(
            links.copy(refs.d_conv.at[:, rows, :], refs.landing.at[me], (peer, core), arrive + step)
        )
    own_rows = pl.ds(pl.multiple_of(me * channels, 16), channels)
    load_own = loads.start(refs.d_conv.at[:, own_rows, :], refs.landing.at[me])
    refs.d_mixer[...] = d_mixer
    refs.d_queries[...] = (d_gated * refs.mixer_in[...]).astype(jnp.bfloat16)
    refs.small[:, 4:5] = sum(
        jnp.sum(
            d_mixer[:, seq * span : (seq + 1) * span] * refs.carried_in[seq].astype(jnp.float32), 1,
            keepdims=True,
        )
        for seq in range(seqs)
    )

    reducer.first(QKV_MORE)
    reducer.first(QKV_LESS)
    reducer.first(DOWN)
    reducer.first(UP)
    reducer.first(OUT)
    total_rows = n * seqs * channels
    fill_tables(channels, span, refs)
    load_held.wait()
    refs.flat_x[...] = refs.held_in[...].astype(jnp.float32).reshape(total_rows, span)
    load_own.wait()
    for copy in going:
        copy.wait_recv()
    refs.flat_d[...] = refs.landing[...].astype(jnp.float32).reshape(total_rows, span)

    def one_channel(channel, carry):
        mixer_backward_channel(n, seqs, span, channels, refs, channel)
        return carry

    reducer.second(QKV_MORE)
    reducer.second(QKV_LESS)
    lax.fori_loop(0, channels // 2, one_channel, 0, unroll=4)
    reducer.second(DOWN)
    reducer.third(QKV_MORE)
    reducer.third(QKV_LESS)
    lax.fori_loop(channels // 2, channels, one_channel, 0, unroll=4)
    refs.answer[...] = refs.flat_out[...].reshape(n, seqs, channels, span).astype(jnp.bfloat16)
    back = []
    for step, peer in enumerate(peers):
        back.append(
            links.copy(
                refs.answer.at[peer], refs.from_conv.at[:, own_rows, :], (peer, core),
                answered + step,
            )
        )
    load_answer = loads.start(refs.answer.at[me], refs.from_conv.at[:, own_rows, :])
    states = [
        links.copy(refs.rate_grad, refs.rate_other, reducer.sibling),
        links.copy(refs.weight_grad, refs.weight_other, reducer.sibling),
    ]
    reducer.second(UP)
    reducer.second(OUT)
    for part in (DOWN, UP, OUT):
        reducer.third(part)
    for copy in states:
        copy.wait_recv()
    refs.rate_sum[...] = refs.rate_grad[...] + refs.rate_other[...]
    refs.weight_sum[...] = refs.weight_grad[...] + refs.weight_other[...]
    for part in parts:
        reducer.fourth(part)
    for part in parts:
        reducer.last(part)
    load_answer.wait()
    for copy in back:
        copy.wait_recv()
    links.finish()


def back_two(
    d_qkv, grad, hidden_two, normed_three, slope, normed_two, active, hidden_one, gated,
    queries, mixer, carried, held, gains, rates, rate_weights, w_qkv, w_out, w_up, w_down, collective,
):
    n, seqs, channels, span = held.shape
    width, hidden_width = w_up.shape[1:]
    tokens = seqs * span
    low, wide = jnp.bfloat16, jnp.float32
    weights, parts = back_two_weights(width, hidden_width, n), back_two_parts(width, hidden_width)
    inputs = dict(
        d_qkv=(d_qkv, HBM), grad=(grad, HBM), hidden_two=(hidden_two, HBM),
        normed_three=(normed_three, HBM), slope=(slope, HBM), normed_two=(normed_two, HBM),
        active=(active, HBM), hidden_one=(hidden_one, HBM), gated=(gated, HBM),
        queries=(queries, HBM), mixer=(mixer, HBM), carried=(carried, HBM), held=(held, HBM),
        gains=(gains, VMEM), rates=(rates, VMEM), rate_weights=(rate_weights, VMEM),
        w_qkv=(w_qkv, HBM), w_out=(w_out, HBM), w_up=(w_up, HBM), w_down=(w_down, HBM),
    )
    square, state = (width, tokens), (channels, 2 * STATES)
    outputs = dict(
        from_conv=((seqs, width, span), low, VMEM),
        d_mixer=(square, wide, VMEM),
        d_queries=(square, low, VMEM),
        grad_out=(square, wide, VMEM),
        small=((width, 5), wide, VMEM),
        rate_sum=(state, wide, VMEM),
        weight_sum=(state, wide, VMEM),
        qkv_grad=((weights[QKV][0], 3 * width), wide, VMEM),
        down_grad=((weights[DOWN][0], width), wide, VMEM),
        up_grad=((weights[UP][0], hidden_width), wide, VMEM),
        out_grad=((weights[OUT][0], width), wide, VMEM),
    )
    flat = (n * seqs * channels, span)
    scratch = dict(
        qkv=(w_qkv.shape[1:], low), down=(w_down.shape[1:], low), up=(w_up.shape[1:], low),
        out=(w_out.shape[1:], low),
        qkv_left=(normed_three.shape, low), qkv_right=((3 * width, tokens), low),
        down_left=(active.shape, low), down_right=(square, low),
        up_left=(normed_two.shape, low), up_right=((hidden_width, tokens), low),
        out_left=(gated.shape, low), out_right=(square, low),
        hidden_two_in=(square, wide), hidden_one_in=(square, wide), grad_now=(square, wide),
        slope_in=(slope.shape, low), queries_in=(square, queries.dtype),
        mixer_in=(square, mixer.dtype), carried_in=(carried.shape, low), held_in=(held.shape, low),
        d_conv=((seqs, width, span), low), landing=(held.shape, low), answer=(held.shape, low),
        flat_x=(flat, wide), flat_d=(flat, wide), flat_out=(flat, wide), **table_scratch(channels, span),
        rate_grad=(state, wide), weight_grad=(state, wide),
        rate_other=(state, wide), weight_other=(state, wide),
        **reducer_scratch(weights, parts, n // 4, tokens),
    )
    body = functools.partial(back_two_body, n, seqs, span, width, hidden_width)
    return launch(body, inputs, outputs, scratch, 100, collective)


def back_three_weights(width, n):
    return {QKV: (width // n, 3 * width // 2)}


def back_three_parts(width, n):
    return {
        SMALL: (width // n, 0, 128, 0),
        QKV_MORE: (QKV, TILE, 3 * width // 2 - TILE, 1),
        QKV_LESS: (QKV, 0, TILE, 0),
    }


def back_three_body(n, seqs, span, width, refs):
    me, core = lax.axis_index(SEQ), lax.axis_index(BATCH)
    links, loads = Links(refs), Loads(refs)
    weights, parts = back_three_weights(width, n), back_three_parts(width, n)
    reducer = Reducer(refs, links, n // 4, weights, parts)
    barrier = pltpu.get_barrier_semaphore()
    before, after = (lax.rem(me + n - 1, n), core), (lax.rem(me + 1, n), core)
    greeted = [*reducer.neighbours(), before, after]
    for device in greeted:
        pl.semaphore_signal(barrier, inc=1, device_id=device, device_id_type=MESH)
    tokens = seqs * span
    load_from_conv = loads.start(refs.from_conv, refs.conv_in)
    load_d_mixer = loads.start(refs.d_mixer, refs.mixer_in)
    load_values = loads.start(refs.values, refs.values_in)
    load_shifted = loads.start(refs.shifted, refs.shifted_in)
    load_keys = loads.start(refs.keys, refs.keys_in)
    load_d_queries = loads.start(refs.d_queries, refs.qkv_right.at[:width, :])
    load_w_qkv = loads.start(refs.w_qkv.at[0], refs.qkv)
    load_normed = loads.start(refs.normed, refs.qkv_left)
    load_tokens = loads.start(refs.tokens, refs.tokens_in)
    load_grad = loads.start(refs.grad, refs.grad_in)
    load_from_conv.wait()
    load_d_mixer.wait()
    load_values.wait()
    load_shifted.wait()
    valid = refs.valid[...]
    conv = jnp.concatenate([refs.conv_in[seq] for seq in range(seqs)], 1).astype(jnp.float32)
    d_carried = (refs.mixer_in[...] * refs.skip[...] + conv) * valid
    d_shifted = d_carried * refs.values_in[...]
    refs.d_shifted[...] = d_shifted
    for seq in range(seqs):
        for first in range(0, width, span):
            turned = d_shifted[first : first + span, seq * span : (seq + 1) * span].T
            refs.rim_out[seq, :, first : first + span] = turned[: refs.rim_out.shape[1]]
    refs.qkv_right[2 * width :, :] = (d_carried * refs.shifted_in[...]).astype(jnp.bfloat16)
    pl.semaphore_wait(barrier, len(greeted))
    halo = links.copy(refs.rim_out, refs.rim_in, before)
    load_keys.wait()
    halo.wait_recv()
    lane = lax.broadcasted_iota(jnp.int32, (width, span), 1)
    there = jnp.where(me == n - 1, 0.0, 1.0)
    rim = refs.rim_in.shape[1]
    tap_sums = [jnp.zeros((width, 1), jnp.float32) for _ in range(TAPS)]
    for seq in range(seqs):
        lanes = slice(seq * span, (seq + 1) * span)
        own = refs.d_shifted[:, lanes]
        keys = refs.keys_in[:, lanes].astype(jnp.float32)
        pieces = []
        for first in range(0, width, span):
            piece = refs.rim_in[seq, :, first : first + span] * there
            piece = jnp.concatenate([piece, jnp.zeros((span - rim, span), jnp.float32)], 0)
            pieces.append(piece.T)
        following = jnp.concatenate(pieces, 0)
        d_keys = jnp.zeros((width, span), jnp.float32)
        for offset in range(TAPS):
            moved = own
            if offset > 0:
                moved = jnp.where(
                    lane < span - offset,
                    pltpu.roll(own, span - offset, 1),
                    pltpu.roll(following, span - offset, 1),
                )
            d_keys = d_keys + refs.taps[:, offset : offset + 1] * moved
            tap_sums[offset] = tap_sums[offset] + jnp.sum(moved * keys, 1, keepdims=True)
        refs.qkv_right[width : 2 * width, lanes] = d_keys.astype(jnp.bfloat16)
    load_d_queries.wait()
    load_normed.wait()
    reducer.exchange(QKV)
    load_w_qkv.wait()
    load_tokens.wait()
    load_grad.wait()
    d_normed = dot(refs.qkv[...], refs.qkv_right[...])
    flat_in = jnp.concatenate(
        [refs.tokens_in[seq].astype(jnp.float32).T for seq in range(seqs)], 1
    )
    d_inputs, gain_part, bias_part = norm_gradient(flat_in * valid, refs.gain[...], d_normed)
    refs.total[...] = (refs.grad_in[...] + d_inputs) * valid
    refs.sums[...] = refs.small_in[...]
    for offset in range(TAPS):
        refs.sums[:, 8 + offset : 9 + offset] = tap_sums[offset]
    refs.sums[:, 0:1] = gain_part
    refs.sums[:, 4:5] = bias_part
    shared = links.copy(refs.sums, refs.sums_other, reducer.sibling)
    reducer.first(QKV_MORE)
    reducer.first(QKV_LESS)
    shared.wait_recv()
    rows = width // n
    refs.slices[...] = (refs.sums[...] + refs.sums_other[...]).reshape(n, rows, 128)
    reducer.first_given(SMALL, refs.slices)
    for seq in range(seqs):
        for first in range(0, width, span):
            refs.d_tokens[seq, :, first : first + span] = refs.total[
                first : first + span, seq * span : (seq + 1) * span
            ].T
    order = (QKV_MORE, QKV_LESS, SMALL)
    for part in order:
        reducer.second(part)
    for part in order:
        reducer.third(part)
    reducer.fourth(QKV_MORE)
    reducer.fourth(QKV_LESS)
    total = reducer.total(SMALL)
    padded = jnp.concatenate([total, jnp.zeros((128 - rows, 128), jnp.float32)], 0).T
    refs.small_sum[...] = padded[: refs.small_sum.shape[0], :rows]
    reducer.last(QKV_MORE)
    reducer.last(QKV_LESS)
    links.finish()


def back_three(
    from_conv, d_mixer, d_queries, values, shifted, keys, grad, tokens, normed, valid, gain, skip,
    taps, small, w_qkv, collective,
):
    seqs, width, span = from_conv.shape
    n = normed.shape[0]
    columns = seqs * span
    low, wide = jnp.bfloat16, jnp.float32
    weights, parts = back_three_weights(width, n), back_three_parts(width, n)
    inputs = dict(
        from_conv=(from_conv, HBM), d_mixer=(d_mixer, HBM), d_queries=(d_queries, HBM),
        values=(values, HBM), shifted=(shifted, HBM), keys=(keys, HBM), grad=(grad, HBM),
        tokens=(tokens, HBM), normed=(normed, HBM), valid=(valid, VMEM), gain=(gain, VMEM),
        skip=(skip, VMEM), taps=(taps, VMEM), small_in=(small, VMEM), w_qkv=(w_qkv, HBM),
    )
    square = (width, columns)
    outputs = dict(
        d_tokens=((seqs, span, width), wide, VMEM),
        qkv_grad=((width // n, 3 * width), wide, VMEM),
        small_sum=((16, width // n), wide, VMEM),
    )
    scratch = dict(
        qkv=(w_qkv.shape[1:], low), qkv_left=(normed.shape, low), qkv_right=((3 * width, columns), low),
        conv_in=(from_conv.shape, low), mixer_in=(square, wide), values_in=(square, values.dtype),
        shifted_in=(square, shifted.dtype), keys_in=(square, low), tokens_in=(tokens.shape, low),
        grad_in=(square, wide), d_shifted=(square, wide), total=(square, wide),
        rim_out=((seqs, 8, width), wide), rim_in=((seqs, 8, width), wide),
        sums=((width, 128), wide), sums_other=((width, 128), wide),
        slices=((n, width // n, 128), wide),
        **reducer_scratch(weights, parts, n // 4, columns),
    )
    body = functools.partial(back_three_body, n, seqs, span, width)
    return launch(body, inputs, outputs, scratch, 40, collective)


def earlier_rows(own, before, steps):
    if steps == 0:
        return own
    moved = pltpu.roll(own, steps, 0)
    rim = before.shape[0]
    row = lax.broadcasted_iota(jnp.int32, (rim, own.shape[1]), 0)
    front = jnp.where(row < steps, pltpu.roll(before, steps, 0), moved[:rim])
    return jnp.concatenate([front, moved[rim:]], 0)


def forward_body(n, seqs, groups, span, group_rows, width, hidden_width, refs):
    at = HeadPlaces(n, seqs, groups)
    me, core = at.me, at.core
    channels = width // n
    half, heads = n // 2, group_rows // HEAD
    tokens = seqs * span
    links, loads = Links(refs), Loads(refs)
    peers = [lax.rem(me + step, n) for step in range(1, n)]
    after = (lax.rem(me + 1, n), core)
    barrier = pltpu.get_barrier_semaphore()
    at.signal_all(barrier, [(peer, core) for peer in peers])
    outgoing = []

    def save(source, target):
        outgoing.append(loads.start(source, target))

    load_tokens = loads.start(refs.tokens, refs.tokens_in)
    load_qkv = loads.start(refs.w_qkv.at[0], refs.qkv)
    load_out = loads.start(refs.w_out.at[0], refs.out)
    load_up = loads.start(refs.w_up.at[0], refs.up)
    load_down = loads.start(refs.w_down.at[0], refs.down)

    def normed(value, row, target):
        result = layer_norm(value, refs.gains[row : row + 1], refs.biases[row : row + 1])
        result = result.astype(jnp.bfloat16)
        target[...] = result.T
        return result

    valid = refs.valid[...]
    load_tokens.wait()
    flat_in = jnp.concatenate([refs.tokens_in[seq] for seq in range(seqs)], 0)
    flat_in = flat_in.astype(jnp.float32) * valid
    refs.flat_in[...] = flat_in
    normed_one = normed(flat_in, 0, refs.normed_one_t)
    load_qkv.wait()
    keys = dot(normed_one, refs.qkv[:, width : 2 * width]).astype(jnp.bfloat16)
    refs.keys[...] = keys
    rim = refs.rim_in.shape[1]
    at.wait_all(barrier, n - 1)
    for seq in range(seqs):
        refs.rim_out[seq] = refs.keys[(seq + 1) * span - rim : (seq + 1) * span, :]
    halo = links.copy(refs.rim_out, refs.rim_in, after)
    refs.values[...] = dot(normed_one, refs.qkv[:, 2 * width :])
    refs.queries[...] = dot(normed_one, refs.qkv[:, :width])
    load_qkv = loads.start(refs.w_qkv.at[1], refs.qkv)
    halo.wait_recv()
    there = jnp.where(me == 0, 0.0, 1.0)
    for seq in range(seqs):
        rows = slice(seq * span, (seq + 1) * span)
        before = refs.rim_in[seq].astype(jnp.float32) * there
        own = refs.keys[rows, :].astype(jnp.float32)
        shifted = jnp.zeros_like(own)
        for offset in range(TAPS):
            shifted = shifted + refs.taps[offset : offset + 1] * earlier_rows(own, before, offset)
        refs.shifted[rows, :] = shifted
        carried = (shifted * refs.values[rows, :] * valid[rows]).astype(jnp.bfloat16)
        refs.carried[rows, :] = carried
        refs.carried_t[seq] = carried.T

    going = []
    arrive, answered = links.slots(n - 1), links.slots(n - 1)
    for step, peer in enumerate(peers):
        rows = pl.ds(pl.multiple_of(peer * channels, 16), channels)
        going.append(
            links.copy(
                refs.carried_t.at[:, rows, :], refs.mixed_in.at[me], (peer, core), arrive + step
            )
        )
    own_rows = pl.ds(pl.multiple_of(me * channels, 16), channels)
    own_copy = loads.start(refs.carried_t.at[:, own_rows, :], refs.mixed_in.at[me])
    fill_tables(channels, span, refs)
    refs.square_t[...] = refs.values[...].T
    save(refs.square_t, refs.values_t)
    refs.square_two_t[...] = refs.shifted[...].T
    save(refs.square_two_t, refs.shifted_t)
    refs.keys_out[...] = refs.keys[...].T
    save(refs.keys_out, refs.keys_t)
    refs.queries_out[...] = refs.queries[...].T
    save(refs.queries_out, refs.queries_t)
    save(refs.normed_one_t, refs.normed_one)
    save(refs.carried_t, refs.carried_out)
    total_rows = n * seqs * channels
    own_copy.wait()
    for copy in going:
        copy.wait_recv()
    save(refs.mixed_in, refs.mixed_held)
    refs.flat_x[...] = refs.mixed_in[...].astype(jnp.float32).reshape(total_rows, span)

    def one_channel(channel, carry):
        mixer_forward_channel(n, seqs, span, channels, refs, channel)
        return carry

    lax.fori_loop(0, channels, one_channel, 0, unroll=4)
    refs.answer[...] = refs.flat_out[...].reshape(n, seqs, channels, span).astype(jnp.bfloat16)
    back = []
    for step, peer in enumerate(peers):
        back.append(
            links.copy(
                refs.answer.at[peer], refs.convolved.at[:, own_rows, :], (peer, core),
                answered + step,
            )
        )
    own_copy = loads.start(refs.answer.at[me], refs.convolved.at[:, own_rows, :])
    own_copy.wait()
    for copy in back:
        copy.wait_recv()
    for seq in range(seqs):
        rows = slice(seq * span, (seq + 1) * span)
        convolved = refs.convolved[seq].astype(jnp.float32).T
        mixer = convolved + refs.skip[...] * refs.carried[rows, :].astype(jnp.float32)
        refs.gated[rows, :] = (refs.queries[rows, :] * mixer).astype(jnp.bfloat16)
        refs.mixer_out[:, rows] = mixer.T
    save(refs.mixer_out, refs.mixer_t)
    refs.gated_out[...] = refs.gated[...].T
    save(refs.gated_out, refs.gated_t)
    load_out.wait()
    hidden = refs.flat_in[...] + dot(refs.gated[...], refs.out[...])
    load_out = loads.start(refs.w_out.at[1], refs.out)

    def feed_forward(hidden, row, hidden_out, normed_out, active_out, slope_out, up, down):
        hidden_out[...] = hidden.T
        refs.hidden[...] = hidden
        refs.normed[...] = normed(hidden, row, normed_out)
        up.wait()

        def one_chunk(index, carry):
            columns = pl.ds(pl.multiple_of(index * width, 128), width)
            active, slope = gelu_and_slope(dot(refs.normed[...], refs.up[:, columns]))
            active = active.astype(jnp.bfloat16)
            refs.active[:, columns] = active
            active_out[columns, :] = active.T
            slope_out[columns, :] = slope.astype(jnp.bfloat16).T
            return carry

        lax.fori_loop(0, hidden_width // width, one_chunk, 0)
        down.wait()
        return refs.hidden[...] + dot(refs.active[...], refs.down[...])

    hidden = feed_forward(
        hidden, 1, refs.hidden_one_t, refs.normed_two_t, refs.active_one_t, refs.slope_one_t,
        load_up, load_down,
    )
    load_up = loads.start(refs.w_up.at[1], refs.up)
    load_down = loads.start(refs.w_down.at[1], refs.down)
    refs.hidden[...] = hidden
    refs.normed[...] = normed(hidden, 2, refs.normed_three_t)
    load_qkv.wait()
    for part in range(3):
        columns = dot(refs.normed[...], refs.qkv[:, part * width : (part + 1) * width])
        columns = columns.astype(jnp.bfloat16)
        for seq in range(seqs):
            turned = columns[seq * span : (seq + 1) * span].T
            for head in range(groups * heads):
                refs.spread[head % heads, seq, head // heads, part * HEAD : (part + 1) * HEAD] = (
                    turned[head * HEAD : (head + 1) * HEAD]
                )

    count = len(at.targets)
    arrive, leave = links.slots(heads * half), links.slots(heads * count)
    passing = links.slots(heads * half)
    spread = []
    for head in range(heads):
        for number, (device, seq, group) in enumerate(at.targets):
            sent = (
                refs.spread.at[head, seq, group], refs.held.at[head, me],
                refs.send.at[leave + head * count + number],
                refs.recv.at[arrive + head * half + me // 2], device,
            )
            at.send(*sent)
            spread.append(sent)
    refs.hidden_two_t[...] = hidden.T
    for source, target in (
        (refs.hidden_one_t, refs.hidden_one_out), (refs.normed_two_t, refs.normed_two),
        (refs.active_one_t, refs.active_one), (refs.slope_one_t, refs.slope_one),
        (refs.hidden_two_t, refs.hidden_two_out), (refs.normed_three_t, refs.normed_three),
    ):
        save(source, target)

    returned, returning = links.slots(heads * count), links.slots(heads * half)
    slot = at.seq * groups + at.group
    going = []

    def gather(head):
        for index, block in enumerate(at.blocks):
            landed = refs.held.at[head, block]
            remote(
                landed, landed, refs.send.at[leave], refs.recv.at[arrive + head * half + index],
                at.sibling,
            ).wait_recv()
            part = refs.held.at[head, block, HEAD : 3 * HEAD]
            links.copy(part, part, at.sibling, passing + head * half + index)
        for index in range(half):
            part = refs.held.at[head, block_of(index, 1 - core), HEAD : 3 * HEAD]
            remote(
                part, part, refs.send.at[leave], refs.recv.at[passing + head * half + index],
                at.sibling,
            ).wait_recv()

    def attend(head):
        fill_head(refs.held, head, 1, n, span, refs.key_rows, None)
        fill_head(refs.held, head, 2, n, span, None, refs.value_columns)
        for index, block in enumerate(at.blocks):
            query = refs.held[head, block, :HEAD, :] * jnp.bfloat16(HEAD**-0.5)
            clear, reach = 2 * index * span, 2 * (index + 1) * span
            edge = dot(refs.key_rows[clear:reach, :], query)
            edge = jnp.where(causal(clear, reach - clear, block * span, span), edge, masked_score)
            top = jnp.max(edge, 0, keepdims=True)
            if index > 0:
                body = dot(refs.key_rows[:clear, :], query)
                top = jnp.maximum(top, jnp.max(body, 0, keepdims=True))
            edge = jnp.exp(edge - top)
            total = jnp.sum(edge, 0, keepdims=True)
            result = dot(refs.value_columns[:, clear:reach], edge.astype(jnp.bfloat16))
            if index > 0:
                body = jnp.exp(body - top)
                total = total + jnp.sum(body, 0, keepdims=True)
                result = result + dot(refs.value_columns[:, :clear], body.astype(jnp.bfloat16))
            refs.outputs[head, index] = (result / total).astype(jnp.bfloat16)
            refs.lse[index, head : head + 1, :] = top + jnp.log(total)
        into = refs.attended_t.at[
            pl.ds(pl.multiple_of(at.group * group_rows + head * HEAD, HEAD), HEAD),
            pl.ds(pl.multiple_of(at.seq * span, span), span),
        ]
        for index, device in enumerate(at.sources):
            sent = (
                refs.outputs.at[head, index], into, refs.send.at[returning + head * half + index],
                refs.recv.at[returned + head * count + slot], device,
            )
            at.send(*sent)
            going.append(sent)

    for head in range(heads):
        gather(head)
        attend(head)
    save(refs.held, refs.held_out)
    for head in range(heads):
        for number, (device, seq, group) in enumerate(at.targets):
            first = group * group_rows + head * HEAD
            landed = refs.attended_t.at[first : first + HEAD, seq * span : (seq + 1) * span]
            remote(
                landed, landed, refs.send.at[leave],
                refs.recv.at[returned + head * count + number], at.sibling,
            ).wait_recv()
    save(refs.attended_t, refs.attended)
    load_out.wait()
    hidden = refs.hidden[...] + dot(refs.attended_t[...].T, refs.out[...])
    hidden = feed_forward(
        hidden, 3, refs.hidden_three_t, refs.normed_four_t, refs.active_two_t, refs.slope_two_t,
        load_up, load_down,
    )
    for source, target in (
        (refs.hidden_three_t, refs.hidden_three_out), (refs.normed_four_t, refs.normed_four),
        (refs.active_two_t, refs.active_two), (refs.slope_two_t, refs.slope_two),
    ):
        save(source, target)
    hidden = (hidden * valid).astype(jnp.bfloat16)
    for seq in range(seqs):
        refs.mixed[seq] = hidden[seq * span : (seq + 1) * span]
    for copy in outgoing:
        copy.wait()
    for sent in spread + going:
        at.wait_sent(*sent)
    links.finish()


def forward(
    tokens, valid, gains, biases, taps, skip, rates, rate_weights, w_qkv, w_out, w_up, w_down, n,
    groups, collective,
):
    seqs, span, width = tokens.shape
    hidden_width = w_up.shape[2]
    group_rows, channels = width // groups, width // n
    rows = seqs * span
    half, heads = n // 2, group_rows // HEAD
    low, wide = jnp.bfloat16, jnp.float32
    inputs = dict(
        tokens=(tokens, HBM), valid=(valid, VMEM), gains=(gains, VMEM), biases=(biases, VMEM),
        taps=(taps, VMEM), skip=(skip, VMEM), rates=(rates, VMEM), rate_weights=(rate_weights, VMEM),
        w_qkv=(w_qkv, HBM), w_out=(w_out, HBM), w_up=(w_up, HBM), w_down=(w_down, HBM),
    )
    square, tall, by_head = (width, rows), (hidden_width, rows), (heads, n, 3 * HEAD, span)
    mixed = (n, seqs, channels, span)
    outputs = dict(
        mixed=((seqs, span, width), low, VMEM),
        lse=((half, heads, span), wide, VMEM),
        held_out=(by_head, low, HBM), mixed_held=(mixed, low, HBM),
        carried_out=((seqs, width, span), low, HBM),
        values_t=(square, wide, HBM), shifted_t=(square, wide, HBM), keys_t=(square, low, HBM),
        queries_t=(square, wide, HBM), mixer_t=(square, wide, HBM), gated_t=(square, low, HBM),
        attended=(square, low, HBM),
        normed_one=(square, low, HBM), normed_two=(square, low, HBM),
        normed_three=(square, low, HBM), normed_four=(square, low, HBM),
        hidden_one_out=(square, wide, HBM), hidden_two_out=(square, wide, HBM),
        hidden_three_out=(square, wide, HBM),
        active_one=(tall, low, HBM), active_two=(tall, low, HBM),
        slope_one=(tall, low, HBM), slope_two=(tall, low, HBM),
    )
    flat = (n * seqs * channels, span)
    lying = (rows, width)
    scratch = dict(
        qkv=(w_qkv.shape[1:], low), out=(w_out.shape[1:], low), up=(w_up.shape[1:], low),
        down=(w_down.shape[1:], low), tokens_in=(tokens.shape, low), flat_in=(lying, wide),
        keys=(lying, low), values=(lying, wide), queries=(lying, wide), shifted=(lying, wide),
        carried=(lying, low), gated=(lying, low), hidden=(lying, wide), normed=(lying, low),
        active=((rows, hidden_width), low), rim_in=((seqs, 16, width), low),
        rim_out=((seqs, 16, width), low), carried_t=((seqs, width, span), low),
        convolved=((seqs, width, span), low), mixed_in=(mixed, low), answer=(mixed, low),
        flat_x=(flat, wide), flat_out=(flat, wide), **table_scratch(channels, span),
        square_t=(square, wide), square_two_t=(square, wide), keys_out=(square, low),
        queries_out=(square, wide), mixer_out=(square, wide), gated_out=(square, low),
        attended_t=(square, low), normed_one_t=(square, low), normed_two_t=(square, low),
        normed_three_t=(square, low), normed_four_t=(square, low), hidden_one_t=(square, wide),
        hidden_two_t=(square, wide), hidden_three_t=(square, wide), active_one_t=(tall, low),
        active_two_t=(tall, low), slope_one_t=(tall, low), slope_two_t=(tall, low),
        spread=((heads, seqs, groups, 3 * HEAD, span), low), held=(by_head, low),
        outputs=((heads, half, HEAD, span), low), key_rows=((n * span, HEAD), low),
        value_columns=((HEAD, n * span), low),
    )
    body = functools.partial(
        forward_body, n, seqs, groups, span, group_rows, width, hidden_width
    )
    return launch(body, inputs, outputs, scratch, 200, collective)


def per_device_by_heads(
    tokens,
    cotangent,
    lengths,
    norm_gain,
    norm_bias,
    w_qkv,
    w_out,
    w_up,
    w_down,
    taps,
    skip,
    ssm_rate,
    ssm_out,
):
    seq_count, span_rows, width = tokens.shape[1:]
    devices = lax.axis_size(SEQ)
    place = lax.axis_index(SEQ)
    channels = width // devices
    groups = devices // 4
    row_count = seq_count * span_rows
    positions = place * span_rows + jnp.arange(span_rows, dtype=jnp.int32)
    validity = (positions[None, :] < lengths[0][:, None]).astype(jnp.float32)
    valid = validity.reshape(1, row_count)
    rates = lax.dynamic_slice_in_dim(ssm_rate, place * channels, channels, 0)
    weights = lax.dynamic_slice_in_dim(ssm_out, place * channels, channels, 0)
    rates = jnp.concatenate([rates, rates], 1)
    weights = jnp.concatenate([weights, weights], 1)
    gains = norm_gain.T
    kept = forward(
        tokens[0], validity.reshape(row_count, 1), norm_gain, norm_bias, taps, skip[None], rates,
        weights, w_qkv, w_out, w_up, w_down, devices, groups, 1,
    )

    def sliced(value):
        return value.reshape(devices, value.shape[0] // devices, row_count)

    back = back_one(
        cotangent[0], valid, kept.hidden_three_out, kept.slope_two, sliced(kept.normed_four),
        sliced(kept.active_two), sliced(kept.attended), kept.held_out, kept.lse, gains[:, 3:4],
        w_out, w_up, w_down, 3,
    )
    more = back_two(
        back.d_qkv.reshape(3 * width, row_count), back.grad_out, kept.hidden_two_out,
        sliced(kept.normed_three), kept.slope_one, sliced(kept.normed_two),
        sliced(kept.active_one), kept.hidden_one_out, sliced(kept.gated_t), kept.queries_t,
        kept.mixer_t, kept.carried_out, kept.mixed_held, gains, rates, weights, w_qkv, w_out, w_up,
        w_down, 4,
    )
    none = jnp.zeros((width, 1), jnp.float32)
    small = jnp.concatenate(
        [
            none, more.small[:, 2:3], more.small[:, 0:1], back.small[:, 0:1],
            none, more.small[:, 3:4], more.small[:, 1:2], back.small[:, 1:2],
            none, none, none, none, more.small[:, 4:5],
            jnp.zeros((width, 128 - 13), jnp.float32),
        ],
        1,
    )
    end = back_three(
        more.from_conv, more.d_mixer, more.d_queries, kept.values_t, kept.shifted_t, kept.keys_t,
        more.grad_out, tokens[0], sliced(kept.normed_one), valid, gains[:, 0:1], skip[:, None],
        taps.T, small, w_qkv, 5,
    )
    small = end.small_sum
    return (
        kept.mixed[None],
        end.d_tokens[None],
        small[:4],
        small[4:7],
        small[7],
        jnp.stack([end.qkv_grad, more.qkv_grad]),
        jnp.stack([more.out_grad, back.out_grad]),
        jnp.stack([more.up_grad, back.up_grad]),
        jnp.stack([more.down_grad, back.down_grad]),
        small[8 : 8 + TAPS],
        small[8 + TAPS],
        more.rate_sum[:, :STATES],
        more.weight_sum[:, :STATES],
    )


def fits_by_heads(mesh):
    devices = mesh.shape[SEQ]
    return devices == 16 and mesh.shape[BATCH] == 2


def solution(mesh):
    placed = (
        P(BATCH, None, SEQ, None),
        P(BATCH, None, SEQ, None),
        P(BATCH, None),
        P(),
        P(),
        P(),
        P(),
        P(),
        P(),
        P(),
        P(),
        P(),
        P(),
    )
    return jax.shard_map(
        per_device_by_heads if fits_by_heads(mesh) else per_device,
        mesh=mesh,
        in_specs=placed,
        out_specs=(
            P(BATCH, None, SEQ, None),
            P(BATCH, None, SEQ, None),
            P(None, SEQ),
            P(None, SEQ),
            P(SEQ),
            P(None, SEQ, None),
            P(None, SEQ, None),
            P(None, SEQ, None),
            P(None, SEQ, None),
            P(None, SEQ),
            P(SEQ),
            P(SEQ, None),
            P(SEQ, None),
        ),
        check_vma=False,
    )
```

```python
import functools
import math
import types

import jax
import jax.numpy as jnp
from jax import lax
from jax.experimental import pallas as pl
from jax.experimental.pallas import tpu as pltpu
from jax.sharding import PartitionSpec as P

HEADS = 12
HEAD = 64
TAPS = 4
STATES = 64
MESH = pl.DeviceIdType.MESH
SEQ = "seq"
BATCH = "batch"
QKV_MORE = "qkv_more"
QKV_LESS = "qkv_less"
DOWN = "down"
OUT = "out"
UP = "up"
QKV = "qkv"
SMALL = "small"
VMEM_BYTES = 63 * 2**20


norm_eps = 1e-05
highest = lax.Precision.HIGHEST
masked_score = -1e30


def for_sending(array):
    return jax.tree.map(lambda a: a.astype(jnp.bfloat16) if a.dtype == jnp.float32 else a, array)


def passed_along(value, axis, steps):
    count = lax.axis_size(axis)
    initial, last = (max(0, -steps), min(count, count - steps))
    return lax.ppermute(value, axis, [(source, source + steps) for source in range(initial, last)])


def layer_norm(inputs, scale_row, shift_row):
    center = inputs - jnp.mean(inputs, -1, keepdims=True)
    spread = jnp.mean(center * center, -1, keepdims=True)
    return center * lax.rsqrt(spread + norm_eps) * scale_row + shift_row


def dense_product(operand_a, operand_b):
    return jnp.dot(operand_a, operand_b, preferred_element_type=jnp.float32)


def product_left(operand_a, operand_b):
    return lax.dot_general(
        operand_a, operand_b, (((0,), (0,)), ((), ())), preferred_element_type=jnp.float32
    )


def product_right(operand_a, operand_b):
    return lax.dot_general(
        operand_a, operand_b, (((1,), (1,)), ((), ())), preferred_element_type=jnp.float32
    )


def angle_table(count_rows, count_cols, period):
    product_index = (
        jnp.arange(count_rows, dtype=jnp.int32)[:, None]
        * jnp.arange(count_cols, dtype=jnp.int32)[None, :]
        % period
    )
    angles = product_index.astype(jnp.float32) * (2.0 * math.pi / period)
    return (jnp.cos(angles), jnp.sin(angles))


def table_einsum(form, table, data):
    return jnp.einsum(form, table, data, precision=highest)


def forward_spectrum(time_parts):
    count_parts = time_parts.shape[0]
    span_rows = time_parts.shape[2]
    count_freq = 2 * count_parts
    cos_parts, sin_parts = angle_table(count_freq, count_parts, count_freq)
    first_real = table_einsum("fp,pjsc->fjsc", cos_parts, time_parts)
    first_imag = -table_einsum("fp,pjsc->fjsc", sin_parts, time_parts)
    cos_twist, sin_twist = angle_table(count_freq, span_rows, count_freq * span_rows)
    cos_twist = cos_twist[:, None, :, None]
    sin_twist = sin_twist[:, None, :, None]
    twist_real = first_real * cos_twist + first_imag * sin_twist
    twist_imag = first_imag * cos_twist - first_real * sin_twist
    cos_span, sin_span = angle_table(span_rows, span_rows, span_rows)
    out_real = table_einsum("ts,fjsc->fjtc", cos_span, twist_real) + table_einsum(
        "ts,fjsc->fjtc", sin_span, twist_imag
    )
    out_imag = table_einsum("ts,fjsc->fjtc", cos_span, twist_imag) - table_einsum(
        "ts,fjsc->fjtc", sin_span, twist_real
    )
    return (out_real, out_imag)


def inverse_spectrum(freq_real, freq_imag):
    count_freq = freq_real.shape[0]
    span_rows = freq_real.shape[2]
    count_parts = count_freq // 2
    fft_length = count_freq * span_rows
    cos_span, sin_span = angle_table(span_rows, span_rows, span_rows)
    first_real = table_einsum("st,fjtc->fjsc", cos_span, freq_real) - table_einsum(
        "st,fjtc->fjsc", sin_span, freq_imag
    )
    first_imag = table_einsum("st,fjtc->fjsc", cos_span, freq_imag) + table_einsum(
        "st,fjtc->fjsc", sin_span, freq_real
    )
    cos_twist, sin_twist = angle_table(count_freq, span_rows, fft_length)
    cos_twist = cos_twist[:, None, :, None]
    sin_twist = sin_twist[:, None, :, None]
    twist_real = first_real * cos_twist - first_imag * sin_twist
    twist_imag = first_imag * cos_twist + first_real * sin_twist
    cos_parts, sin_parts = angle_table(count_parts, count_freq, count_freq)
    summed = table_einsum("pf,fjsc->pjsc", cos_parts, twist_real) - table_einsum(
        "pf,fjsc->pjsc", sin_parts, twist_imag
    )
    return summed / fft_length


def to_frequency(data_low):
    parts = lax.all_to_all(data_low[None], SEQ, split_axis=3, concat_axis=0, tiled=True)
    return forward_spectrum(parts.astype(jnp.float32))


def from_frequency(freq_real, freq_imag):
    time_parts = inverse_spectrum(freq_real, freq_imag)
    joined = lax.all_to_all(
        for_sending(time_parts), SEQ, split_axis=0, concat_axis=3, tiled=True
    ).astype(time_parts.dtype)
    return joined[0]


def kernel_parts(rate_slice, weight_slice, count_freq, span_rows):
    fft_length = count_freq * span_rows
    length_full = fft_length // 2
    frequency = (
        jnp.arange(count_freq, dtype=jnp.int32)[:, None]
        + count_freq * jnp.arange(span_rows, dtype=jnp.int32)[None, :]
    )
    angles = (frequency.astype(jnp.float32) * (2.0 * math.pi / fft_length))[:, None, :, None, None]
    odd_mask = (frequency % 2 == 1)[:, None, :, None, None]
    channels = rate_slice.shape[0]
    blocks = rate_slice.shape[1] // 8
    rate_blocks = rate_slice.reshape(channels, blocks, 8).transpose(1, 0, 2)
    weight_blocks = weight_slice.reshape(channels, blocks, 8).transpose(1, 0, 2)

    def add_block(running, piece_pair):
        rate_part, weight_part = piece_pair
        decays = jnp.exp(-rate_part)
        half_sine = jnp.sin(angles / 2.0)
        real_den = -jnp.expm1(-rate_part) + decays * 2.0 * half_sine * half_sine
        imag_den = decays * jnp.sin(angles)
        numerator = jnp.where(
            odd_mask, 1.0 + jnp.exp(-rate_part * length_full), -jnp.expm1(-rate_part * length_full)
        )
        factor = weight_part * numerator / (real_den * real_den + imag_den * imag_den)
        return (
            (
                running[0] + jnp.sum(factor * real_den, -1),
                running[1] - jnp.sum(factor * imag_den, -1),
            ),
            None,
        )

    zeros_init = jnp.zeros((count_freq, 1, span_rows, channels), jnp.float32)
    return lax.scan(
        jax.checkpoint(add_block), (zeros_init, zeros_init), (rate_blocks, weight_blocks)
    )[0]


def attention_mask(query_positions, key_count, length_value):
    key_positions = jnp.arange(key_count, dtype=jnp.int32)
    return (key_positions[None, :] <= query_positions[:, None]) & (
        key_positions[None, :] < length_value
    )


def head_slice(matrix, head_index):
    return lax.dynamic_slice_in_dim(matrix, head_index * HEAD, HEAD, 1)


def attend_forward(query_low, keys_low, values_low, length_value, query_positions):
    whole_keys, whole_values = (
        lax.all_gather(keys_low, SEQ, axis=0, tiled=True),
        lax.all_gather(values_low, SEQ, axis=0, tiled=True),
    )
    allowed = attention_mask(query_positions, whole_keys.shape[0], length_value)
    score_scale = HEAD ** (-0.5)

    def head_forward(head_index):
        scores = jnp.where(
            allowed,
            score_scale
            * product_right(head_slice(query_low, head_index), head_slice(whole_keys, head_index)),
            masked_score,
        )
        top_score = jnp.max(scores, -1, keepdims=True)
        expos = jnp.exp(scores - top_score)
        totals = jnp.sum(expos, -1, keepdims=True)
        probs_low = (expos / totals).astype(jnp.bfloat16)
        return (
            dense_product(probs_low, head_slice(whole_values, head_index)),
            (top_score + jnp.log(totals))[:, 0],
        )

    head_outputs, log_totals = lax.map(head_forward, jnp.arange(HEADS, dtype=jnp.int32))
    attended = head_outputs.transpose(1, 0, 2).reshape(query_low.shape[0], HEADS * HEAD)
    return (attended, log_totals, whole_keys, whole_values)


def join_heads(head_rows):
    return head_rows.transpose(1, 0, 2).reshape(head_rows.shape[1], HEADS * HEAD)


def attend_backward(
    query_low, whole_keys, whole_values, log_totals, grad_low, length_value, query_positions
):
    allowed = attention_mask(query_positions, whole_keys.shape[0], length_value)
    score_scale = HEAD ** (-0.5)
    span_rows = query_low.shape[0]

    def query_side(head_index):
        head_query = head_slice(query_low, head_index)
        head_keys = head_slice(whole_keys, head_index)
        head_grad = head_slice(grad_low, head_index)
        scores = jnp.where(
            allowed, score_scale * product_right(head_query, head_keys), masked_score
        )
        weights = jnp.exp(scores - log_totals[head_index][:, None])
        d_weights = product_right(head_grad, head_slice(whole_values, head_index))
        row_term = jnp.sum(weights * d_weights, -1, keepdims=True)
        d_scores = (weights * (d_weights - row_term)).astype(jnp.bfloat16)
        d_query = score_scale * dense_product(d_scores, head_keys)
        return (d_query, row_term[:, 0], d_scores, weights)

    def head_backward(head_index):
        d_query, row_term, d_scores, weights = query_side(head_index)
        head_query = head_slice(query_low, head_index)
        head_grad = head_slice(grad_low, head_index)
        d_keys = score_scale * product_left(d_scores, head_query)
        d_values = product_left(weights.astype(jnp.bfloat16), head_grad)
        return (d_query, d_keys, d_values)

    query_grads, key_grads, value_grads = lax.map(head_backward, jnp.arange(HEADS, dtype=jnp.int32))
    count_rows = span_rows * lax.axis_size(SEQ)
    key_part = (
        lax.slice_in_dim(key_grads, 0, count_rows, axis=1)
        .transpose(1, 0, 2)
        .reshape(count_rows, HEADS * HEAD)
    )
    value_part = (
        lax.slice_in_dim(value_grads, 0, count_rows, axis=1)
        .transpose(1, 0, 2)
        .reshape(count_rows, HEADS * HEAD)
    )
    key_value = lax.psum_scatter(
        jnp.stack([key_part, value_part], 1), SEQ, scatter_dimension=0, tiled=True
    )
    return (join_heads(query_grads), key_value[:, 0], key_value[:, 1])


def per_device(
    tokens,
    cotangent,
    lengths,
    norm_gain,
    norm_bias,
    w_qkv,
    w_out,
    w_up,
    w_down,
    taps,
    skip,
    ssm_rate,
    ssm_out,
):
    seq_count = tokens.shape[1]
    span_rows = tokens.shape[2]
    width = tokens.shape[3]
    devices = lax.axis_size(SEQ)
    place = lax.axis_index(SEQ)
    channels = width // devices
    count_freq = 2 * devices
    fft_length = count_freq * span_rows
    rim = TAPS - 1
    row_count = seq_count * span_rows
    query_positions = place * span_rows + jnp.arange(span_rows, dtype=jnp.int32)
    validity = (query_positions[None, :] < lengths[0][:, None]).astype(jnp.float32)[:, :, None]
    rate_slice = lax.dynamic_slice_in_dim(ssm_rate, place * channels, channels, 0)
    weight_slice = lax.dynamic_slice_in_dim(ssm_out, place * channels, channels, 0)

    def spectrum_of(rate_in, weight_in):
        return kernel_parts(rate_in, weight_in, count_freq, span_rows)

    def feed_forward(inputs, norm_row, layer):
        normed_low = layer_norm(inputs, norm_gain[norm_row], norm_bias[norm_row]).astype(
            jnp.bfloat16
        )
        raised = dense_product(normed_low, w_up[layer])
        active_low = jax.nn.gelu(raised).astype(jnp.bfloat16)
        return (normed_low, raised, active_low, inputs + dense_product(active_low, w_down[layer]))

    def norm_backward(inputs, norm_row, d_normed):
        norm_pull = jax.vjp(layer_norm, inputs, norm_gain[norm_row], norm_bias[norm_row])[1]
        return norm_pull(d_normed)

    def feed_backward(grad_rows, inputs, normed_low, raised, active_low, norm_row, layer):
        branch_low = grad_rows.astype(jnp.bfloat16)
        down_grad = product_left(active_low, branch_low)
        d_active = product_right(branch_low, w_down[layer])
        gelu_pull = jax.vjp(jax.nn.gelu, raised)[1]
        d_raised = gelu_pull(d_active)[0].astype(jnp.bfloat16)
        up_grad = product_left(normed_low, d_raised)
        d_inputs, gain_part, bias_part = norm_backward(
            inputs, norm_row, product_right(d_raised, w_up[layer])
        )
        return (grad_rows + d_inputs, down_grad, up_grad, gain_part, bias_part)

    def forward_pass(token_block):
        masked_in = token_block[0].astype(jnp.float32) * validity
        flat_in = masked_in.reshape(row_count, width)
        normed_one = layer_norm(flat_in, norm_gain[0], norm_bias[0]).astype(jnp.bfloat16)
        qkv_one = dense_product(normed_one, w_qkv[0]).reshape(seq_count, span_rows, 3 * width)
        queries_one = qkv_one[:, :, :width]
        keys_one = qkv_one[:, :, width : 2 * width].astype(jnp.bfloat16)
        values_one = qkv_one[:, :, 2 * width :]
        earlier = passed_along(keys_one[:, span_rows - rim :], SEQ, 1)
        extended = jnp.concatenate([earlier, keys_one], 1)
        shifted = sum(
            (
                taps[offset]
                * extended[:, rim - offset : rim - offset + span_rows].astype(jnp.float32)
                for offset in range(TAPS)
            )
        )
        carried_low = (shifted * values_one * validity).astype(jnp.bfloat16)
        carried_real, carried_imag = to_frequency(carried_low)
        kernel_both, kernel_pull = jax.vjp(spectrum_of, rate_slice, weight_slice)
        kernel_real, kernel_imag = kernel_both
        convolved = from_frequency(
            carried_real * kernel_real - carried_imag * kernel_imag,
            carried_real * kernel_imag + carried_imag * kernel_real,
        )
        carried = carried_low.astype(jnp.float32)
        mixer = convolved + skip * carried
        gated_low = (queries_one * mixer).reshape(row_count, width).astype(jnp.bfloat16)
        hidden_one = flat_in + dense_product(gated_low, w_out[0])
        normed_two, raised_one, active_one, hidden_two = feed_forward(hidden_one, 1, 0)
        normed_three = layer_norm(hidden_two, norm_gain[2], norm_bias[2]).astype(jnp.bfloat16)
        qkv_two = (
            dense_product(normed_three, w_qkv[1])
            .astype(jnp.bfloat16)
            .reshape(seq_count, span_rows, 3 * width)
        )
        attended_list = []
        totals_list = []
        keys_list = []
        values_list = []
        for seq_index in range(seq_count):
            attended, log_totals, whole_keys, whole_values = attend_forward(
                qkv_two[seq_index, :, :width],
                qkv_two[seq_index, :, width : 2 * width],
                qkv_two[seq_index, :, 2 * width :],
                lengths[0, seq_index],
                query_positions,
            )
            attended_list.append(attended)
            totals_list.append(log_totals)
            keys_list.append(whole_keys)
            values_list.append(whole_values)
        attended_low = jnp.concatenate(attended_list, 0).astype(jnp.bfloat16)
        hidden_three = hidden_two + dense_product(attended_low, w_out[1])
        normed_four, raised_two, active_two, hidden_four = feed_forward(hidden_three, 3, 1)
        output = hidden_four.reshape(seq_count, span_rows, width) * validity
        saved = types.SimpleNamespace(
            flat_in=flat_in,
            normed_one=normed_one,
            queries_one=queries_one,
            values_one=values_one,
            extended=extended,
            shifted=shifted,
            carried=carried,
            carried_real=carried_real,
            carried_imag=carried_imag,
            kernel_real=kernel_real,
            kernel_imag=kernel_imag,
            kernel_pull=kernel_pull,
            mixer=mixer,
            gated_low=gated_low,
            hidden_one=hidden_one,
            normed_two=normed_two,
            raised_one=raised_one,
            active_one=active_one,
            hidden_two=hidden_two,
            normed_three=normed_three,
            qkv_two=qkv_two,
            totals_list=totals_list,
            keys_list=keys_list,
            values_list=values_list,
            attended_low=attended_low,
            hidden_three=hidden_three,
            normed_four=normed_four,
            raised_two=raised_two,
            active_two=active_two,
        )
        return (output, saved)

    output = forward_pass(tokens)[0]
    saved = forward_pass(lax.optimization_barrier(tokens))[1]
    grad_rows = (cotangent[0].astype(jnp.float32) * validity).reshape(row_count, width)
    grad_rows, down_two, up_two, gain_four, bias_four = feed_backward(
        grad_rows,
        saved.hidden_three,
        saved.normed_four,
        saved.raised_two,
        saved.active_two,
        3,
        1,
    )
    branch_low = grad_rows.astype(jnp.bfloat16)
    out_two = product_left(saved.attended_low, branch_low)
    d_attended = (
        product_right(branch_low, w_out[1])
        .astype(jnp.bfloat16)
        .reshape(seq_count, span_rows, width)
    )
    qkv_two = saved.qkv_two
    grad_parts = []
    for seq_index in range(seq_count):
        d_query_rows, d_key_rows, d_value_rows = attend_backward(
            qkv_two[seq_index, :, :width],
            saved.keys_list[seq_index],
            saved.values_list[seq_index],
            saved.totals_list[seq_index],
            d_attended[seq_index],
            lengths[0, seq_index],
            query_positions,
        )
        grad_parts.append(jnp.concatenate([d_query_rows, d_key_rows, d_value_rows], -1))
    d_qkv_two = jnp.concatenate(grad_parts, 0).astype(jnp.bfloat16)
    qkv_grad_two = product_left(saved.normed_three, d_qkv_two)
    d_inputs, gain_three, bias_three = norm_backward(
        saved.hidden_two, 2, product_right(d_qkv_two, w_qkv[1])
    )
    grad_rows = grad_rows + d_inputs
    grad_rows, down_one, up_one, gain_two, bias_two = feed_backward(
        grad_rows,
        saved.hidden_one,
        saved.normed_two,
        saved.raised_one,
        saved.active_one,
        1,
        0,
    )
    branch_low = grad_rows.astype(jnp.bfloat16)
    out_one = product_left(saved.gated_low, branch_low)
    d_gated = product_right(branch_low, w_out[0]).reshape(seq_count, span_rows, width)
    d_queries = d_gated * saved.mixer
    d_mixer = d_gated * saved.queries_one
    skip_grad = jnp.sum(d_mixer * saved.carried, (0, 1))
    conv_real, conv_imag = to_frequency(d_mixer.astype(jnp.bfloat16))
    kernel_real = saved.kernel_real
    kernel_imag = saved.kernel_imag
    from_conv = from_frequency(
        kernel_real * conv_real + kernel_imag * conv_imag,
        kernel_real * conv_imag - kernel_imag * conv_real,
    )
    d_carried = d_mixer * skip + from_conv
    carried_real = saved.carried_real
    carried_imag = saved.carried_imag
    cot_real = (
        jnp.sum(carried_real * conv_real + carried_imag * conv_imag, 1, keepdims=True) / fft_length
    )
    cot_imag = (
        jnp.sum(carried_real * conv_imag - carried_imag * conv_real, 1, keepdims=True) / fft_length
    )
    rate_grad, weight_grad = saved.kernel_pull((cot_real, cot_imag))
    d_shifted = d_carried * saved.values_one * validity
    d_values = d_carried * saved.shifted * validity
    extended = saved.extended
    grads_extended = sum(
        (
            jnp.pad(taps[offset] * d_shifted, ((0, 0), (rim - offset, offset), (0, 0)))
            for offset in range(TAPS)
        )
    )
    taps_grad = jnp.stack(
        [
            jnp.sum(
                d_shifted
                * extended[:, rim - offset : rim - offset + span_rows].astype(jnp.float32),
                (0, 1),
            )
            for offset in range(TAPS)
        ]
    )
    later = passed_along(grads_extended[:, :rim], SEQ, -1)
    d_keys = grads_extended[:, rim:] + jnp.pad(later, ((0, 0), (span_rows - rim, 0), (0, 0)))
    d_qkv_one = (
        jnp.concatenate([d_queries, d_keys, d_values], -1)
        .reshape(row_count, 3 * width)
        .astype(jnp.bfloat16)
    )
    qkv_grad_one = product_left(saved.normed_one, d_qkv_one)
    d_inputs, gain_one, bias_one = norm_backward(
        saved.flat_in, 0, product_right(d_qkv_one, w_qkv[0])
    )
    d_tokens = ((grad_rows + d_inputs).reshape(seq_count, span_rows, width) * validity)[None]
    gain_sum, bias_sum, qkv_sum, out_sum, up_sum, down_sum, taps_sum, skip_sum = (
        lax.psum_scatter(
            jnp.stack([gain_one, gain_two, gain_three, gain_four]),
            SEQ,
            scatter_dimension=1,
            tiled=True,
        ),
        lax.psum_scatter(
            jnp.stack([bias_one, bias_two, bias_three, bias_four]),
            SEQ,
            scatter_dimension=1,
            tiled=True,
        ),
        lax.psum_scatter(
            jnp.stack([qkv_grad_one, qkv_grad_two]), SEQ, scatter_dimension=1, tiled=True
        ),
        lax.psum_scatter(jnp.stack([out_one, out_two]), SEQ, scatter_dimension=1, tiled=True),
        lax.psum_scatter(jnp.stack([up_one, up_two]), SEQ, scatter_dimension=1, tiled=True),
        lax.psum_scatter(jnp.stack([down_one, down_two]), SEQ, scatter_dimension=1, tiled=True),
        lax.psum_scatter(taps_grad, SEQ, scatter_dimension=1, tiled=True),
        lax.psum_scatter(skip_grad[None], SEQ, scatter_dimension=1, tiled=True),
    )
    totals = (
        lax.psum(gain_sum.astype(jnp.bfloat16), BATCH).astype(jnp.float32),
        lax.psum(bias_sum.astype(jnp.bfloat16), BATCH).astype(jnp.float32),
        lax.psum(qkv_sum.astype(jnp.bfloat16), BATCH).astype(jnp.float32),
        lax.psum(out_sum.astype(jnp.bfloat16), BATCH).astype(jnp.float32),
        lax.psum(up_sum.astype(jnp.bfloat16), BATCH).astype(jnp.float32),
        lax.psum(down_sum.astype(jnp.bfloat16), BATCH).astype(jnp.float32),
        lax.psum(taps_sum.astype(jnp.bfloat16), BATCH).astype(jnp.float32),
        lax.psum(skip_sum.astype(jnp.bfloat16), BATCH).astype(jnp.float32),
        lax.psum(rate_grad.astype(jnp.bfloat16), BATCH).astype(jnp.float32),
        lax.psum(weight_grad.astype(jnp.bfloat16), BATCH).astype(jnp.float32),
    )
    return (
        output[None].astype(jnp.bfloat16),
        d_tokens,
        totals[0],
        totals[1][:3],
        totals[1][3],
        totals[2],
        totals[3],
        totals[4],
        totals[5],
        totals[6],
        totals[7][0],
        totals[8],
        totals[9],
    )


def other_device(place, core, to_place, to_core):
    return jnp.logical_or(place != to_place, core != to_core)


def greet(devices):
    barrier = pltpu.get_barrier_semaphore()
    for device in devices:
        pl.semaphore_signal(barrier, inc=1, device_id=device, device_id_type=MESH)
    pl.semaphore_wait(barrier, len(devices))


def remote(source, target, send_sem, recv_sem, device):
    return pltpu.make_async_remote_copy(
        src_ref=source,
        dst_ref=target,
        send_sem=send_sem,
        recv_sem=recv_sem,
        device_id=device,
        device_id_type=MESH,
    )


def split_low(value):
    upper = value.astype(jnp.bfloat16)
    return upper, (value - upper.astype(jnp.float32)).astype(jnp.bfloat16)


NN = (((1,), (0,)), ((), ()))
NT = (((1,), (1,)), ((), ()))
TN = (((0,), (0,)), ((), ()))


def dot(left, right, form=NN):
    return lax.dot_general(left, right, form, preferred_element_type=jnp.float32)


def dot_fine(left, right, form=NN):
    left_up, left_low = left
    right_up, right_low = right
    total = dot(left_up, right_up, form) + dot(left_up, right_low, form)
    if left_low is not None:
        total = total + dot(left_low, right_up, form)
    return total


def state_steps(span):
    row = lax.broadcasted_iota(jnp.int32, (span, 2 * STATES), 0)
    lane = lax.broadcasted_iota(jnp.int32, (span, 2 * STATES), 1)
    return jnp.where(lane < STATES, span - 1 - row, row + 1).astype(jnp.float32)


def state_tables(rate_row, weight_row, span):
    steps = state_steps(span)
    table = jnp.exp(-rate_row * steps)
    lane_row = lax.broadcasted_iota(jnp.int32, (8, 2 * STATES), 1)
    lead = jnp.where(lane_row < STATES, 0.0, weight_row * jnp.exp(rate_row))
    response = lax.dot_general(
        lead, table, NT, precision=highest, preferred_element_type=jnp.float32
    )[:1]
    spread = pltpu.roll(
        jnp.broadcast_to(response, (span, span)), 0, 1, stride=1, stride_axis=0
    )
    later = lax.broadcasted_iota(jnp.int32, (span, span), 1)
    earlier = lax.broadcasted_iota(jnp.int32, (span, span), 0)
    toeplitz = jnp.where(later >= earlier, spread, 0.0)
    return table, toeplitz


def shift_rows(value, count):
    if count > 0:
        return jnp.concatenate([jnp.zeros_like(value[:count]), value[:-count]], 0)
    return jnp.concatenate([value[-count:], jnp.zeros_like(value[:-count])], 0)


def scan_states(value, decay, seqs, blocks, direction):
    step = 1
    while step < blocks:
        value = value + shift_rows(value, direction * step * seqs) * jnp.exp(decay * step)
        step *= 2
    return shift_rows(value, direction * seqs)


def fill_tables(channels, span, refs):
    def one_channel(channel, carry):
        table, toeplitz = state_tables(
            refs.rates[pl.ds(channel, 1), :], refs.rate_weights[pl.ds(channel, 1), :], span
        )
        refs.near_up[channel], refs.near_low[channel] = split_low(toeplitz)
        refs.table_up[channel], refs.table_low[channel] = split_low(table)
        return carry

    lax.fori_loop(0, channels, one_channel, 0, unroll=4)


def table_scratch(channels, span):
    shape = ((channels, span, span), jnp.bfloat16)
    return dict(near_up=shape, near_low=shape, table_up=shape, table_low=shape)


def mixer_forward_channel(n, seqs, span, channels, refs, channel):
    rate_row = refs.rates[pl.ds(channel, 1), :]
    weight_row = refs.rate_weights[pl.ds(channel, 1), :]
    rows = pl.ds(channel, n * seqs, stride=channels)
    data = (refs.flat_x[rows, :].astype(jnp.bfloat16), None)
    table_parts = (refs.table_up[channel], refs.table_low[channel])
    inner = dot_fine(data, (refs.near_up[channel], refs.near_low[channel]))
    states = scan_states(dot_fine(data, table_parts), -span * rate_row, seqs, n, 1)
    lane = lax.broadcasted_iota(jnp.int32, states.shape, 1)
    weighted = jnp.where(lane < STATES, 0.0, pltpu.roll(states, STATES, 1) * weight_row)
    refs.flat_out[rows, :] = inner + dot_fine(split_low(weighted), table_parts, NT)


def mixer_backward_channel(n, seqs, span, channels, refs, channel):
    rate_row = refs.rates[pl.ds(channel, 1), :]
    weight_row = refs.rate_weights[pl.ds(channel, 1), :]
    table_parts = (refs.table_up[channel], refs.table_low[channel])
    table = table_parts[0].astype(jnp.float32) + table_parts[1].astype(jnp.float32)
    steps = state_steps(span)
    rows = pl.ds(channel, n * seqs, stride=channels)
    data = refs.flat_x[rows, :].astype(jnp.bfloat16)
    grad = refs.flat_d[rows, :].astype(jnp.bfloat16)
    stepped_parts = split_low(table * steps)
    both_parts = [jnp.concatenate(pair, 1) for pair in zip(table_parts, stepped_parts)]
    count = n * seqs
    sides = dot_fine((jnp.concatenate([data, grad], 0), None), both_parts)
    lane = lax.broadcasted_iota(jnp.int32, (count, 2 * STATES), 1)
    low_lanes = lane < STATES

    def aligned(value):
        return jnp.where(low_lanes, pltpu.roll(value, STATES, 1), 0.0)

    entering = jnp.where(low_lanes, sides[:count, : 2 * STATES], 0.0)
    entering_steps = jnp.where(low_lanes, sides[:count, 2 * STATES :], 0.0)
    leaving = aligned(sides[count:, : 2 * STATES])
    leaving_steps = aligned(sides[count:, 2 * STATES :])
    decay = -span * rate_row
    states = scan_states(entering, decay, seqs, n, 1)
    states_steps = scan_states(states * jnp.exp(decay), decay, seqs, n, 1)
    returned = scan_states(leaving, decay, seqs, n, -1)
    far_weight = jnp.sum(leaving * states, 0, keepdims=True)
    far_rate = jnp.sum(
        leaving_steps * states + returned * entering_steps + span * (leaving * states_steps),
        0, keepdims=True,
    )
    cross = dot(grad, data, TN)
    later = lax.broadcasted_iota(jnp.int32, (span, span), 0)
    earlier = lax.broadcasted_iota(jnp.int32, (span, span), 1)
    cross = jnp.where(later >= earlier, cross, 0.0)
    met = dot_fine(split_low(cross), both_parts)
    met_plain = pltpu.roll(met[:, : 2 * STATES], STATES, 1)
    met_steps = pltpu.roll(met[:, 2 * STATES :], STATES, 1)
    rise = jnp.exp(span * rate_row)
    near_weight = rise * jnp.sum(table * met_plain, 0, keepdims=True)
    near_rate = rise * jnp.sum(
        table * ((steps - span) * met_plain + met_steps), 0, keepdims=True
    )
    lane_row = lane[:1]
    near_weight = jnp.where(lane_row < STATES, pltpu.roll(near_weight, STATES, 1), 0.0)
    near_rate = jnp.where(lane_row < STATES, pltpu.roll(near_rate, STATES, 1), 0.0)
    refs.weight_grad[pl.ds(channel, 1), :] = near_weight + far_weight
    refs.rate_grad[pl.ds(channel, 1), :] = -weight_row * (near_rate + far_rate)
    inner = dot_fine((grad, None), (refs.near_up[channel], refs.near_low[channel]), NT)
    weighted = returned * weight_row
    refs.flat_d[rows, :] = inner + dot_fine(split_low(weighted), table_parts, NT)


def block_of(index, core):
    return 2 * index + lax.rem(index + core, 2)


def keeper_of(block):
    return lax.rem((block + 1) // 2, 2)


class HeadPlaces:
    def __init__(self, n, seqs, groups):
        self.n, self.seqs, self.groups = n, seqs, groups
        self.me, self.core = lax.axis_index(SEQ), lax.axis_index(BATCH)
        self.group = self.me // (2 * seqs)
        self.seq = lax.rem(self.me // 2, seqs)
        self.batch = lax.rem(self.me, 2)
        self.keeper = keeper_of(self.me)
        self.sibling = (self.me, 1 - self.core)
        self.targets = [
            ((group * 2 * seqs + seq * 2 + self.core, self.keeper), seq, group)
            for seq in range(seqs)
            for group in range(groups)
        ]
        self.blocks = [block_of(index, self.core) for index in range(n // 2)]
        self.sources = [(block, self.batch) for block in self.blocks]

    def is_other(self, device):
        return jnp.logical_or(device[0] != self.me, device[1] != self.core)

    def greet(self):
        barrier = pltpu.get_barrier_semaphore()
        self.signal_all(barrier, [])
        self.wait_all(barrier, 0)

    def signal_all(self, barrier, more):
        for device in [target for target, _, _ in self.targets] + self.sources:

            @pl.when(self.is_other(device))
            def _():
                pl.semaphore_signal(barrier, inc=1, device_id=device, device_id_type=MESH)

        for device in [self.sibling, *more]:
            pl.semaphore_signal(barrier, inc=1, device_id=device, device_id_type=MESH)

    def wait_all(self, barrier, more):
        kept = jnp.logical_and(self.batch == self.core, self.is_kept_here())
        count = len(self.targets) + len(self.sources) + 1 + more
        pl.semaphore_wait(barrier, count - 2 * kept.astype(jnp.int32))

    def is_kept_here(self):
        return self.keeper == self.core

    def send(self, source, target, send_sem, recv_sem, device):
        @pl.when(self.is_other(device))
        def _():
            remote(source, target, send_sem, recv_sem, device).start()

        @pl.when(jnp.logical_not(self.is_other(device)))
        def _():
            pltpu.make_async_copy(source, target, recv_sem).start()

    def wait_sent(self, source, target, send_sem, recv_sem, device):
        @pl.when(self.is_other(device))
        def _():
            remote(source, target, send_sem, recv_sem, device).wait_send()


def fill_head(held, head, part, n, span, rows_out, columns_out):
    for block in range(n):
        piece = held[head, block, part * HEAD : (part + 1) * HEAD, :]
        if rows_out is not None:
            rows_out[block * span : (block + 1) * span, :] = piece.T
        if columns_out is not None:
            columns_out[:, block * span : (block + 1) * span] = piece


def causal(first_key, rows, first_query, span):
    key = first_key + lax.broadcasted_iota(jnp.int32, (rows, span), 0)
    query = first_query + lax.broadcasted_iota(jnp.int32, (rows, span), 1)
    return key <= query


TILE = 384
VMEM, HBM = pltpu.VMEM, pl.ANY


def launch(body, inputs, outputs, scratch, copies, collective):
    names = [*inputs, *outputs, *scratch, "send", "recv", "local"]

    def kernel(*refs):
        body(types.SimpleNamespace(**dict(zip(names, refs))))

    dma = pltpu.SemaphoreType.DMA
    results = pl.pallas_call(
        kernel,
        out_shape=tuple(jax.ShapeDtypeStruct(shape, kind) for shape, kind, _ in outputs.values()),
        in_specs=[pl.BlockSpec(memory_space=space) for _, space in inputs.values()],
        out_specs=tuple(pl.BlockSpec(memory_space=space) for _, _, space in outputs.values()),
        scratch_shapes=[pltpu.VMEM(shape, kind) for shape, kind in scratch.values()]
        + [dma((copies,)), dma((copies,)), dma((LOCAL_COPIES,))],
        compiler_params=pltpu.CompilerParams(
            collective_id=collective, has_side_effects=True, vmem_limit_bytes=VMEM_BYTES
        ),
    )(*(array for array, _ in inputs.values()))
    return types.SimpleNamespace(**dict(zip(outputs, results)))


LOCAL_COPIES = 64


class Loads:
    def __init__(self, refs):
        self.semaphores, self.used = refs.local, 0

    def start(self, source, target):
        copy = pltpu.make_async_copy(source, target, self.semaphores.at[self.used])
        self.used += 1
        copy.start()
        return copy


class Links:
    def __init__(self, refs):
        self.send, self.recv, self.used, self.unsent = refs.send, refs.recv, 0, []

    def slots(self, count):
        self.used += count
        return self.used - count

    def copy(self, source, target, device, slot=None):
        slot = self.slots(1) if slot is None else slot
        made = remote(source, target, self.send.at[slot], self.recv.at[slot], device)
        made.start()
        self.unsent.append(made)
        return made

    def finish(self):
        for made in self.unsent:
            made.wait_send()


class Piece:
    def __init__(self, weight, first_row, first_column, axis):
        self.weight, self.first_row, self.first_column, self.axis = (
            weight, first_row, first_column, axis,
        )


ROWS = 48


def pieces_of(weights, order):
    pieces = []
    for weight, axes in order:
        rows, half = weights[weight]
        places = [
            (first_row, first_column)
            for first_column in range(0, half, TILE)
            for first_row in range(0, rows, ROWS)
        ]
        for count, place in enumerate(places):
            pieces.append(Piece(weight, *place, axes[count % len(axes)]))
    return pieces


class Reducer:
    def __init__(self, refs, links, depth, weights, pieces, given):
        self.refs, self.links, self.depth, self.weights = refs, links, depth, weights
        self.me, self.core = lax.axis_index(SEQ), lax.axis_index(BATCH)
        self.level = self.me // 4
        self.spot = (lax.rem(self.me // 2, 2), lax.rem(self.me, 2))
        base = self.level * 4
        self.across = [
            (base + self.spot[0] * 2 + (1 - self.spot[1]), self.core),
            (base + (1 - self.spot[0]) * 2 + self.spot[1], self.core),
        ]
        self.sibling = (self.me, 1 - self.core)
        self.levels = [lax.rem(self.level + step, depth) for step in range(1, depth)]
        self.column = [
            (other * 4 + self.spot[0] * 2 + self.spot[1], self.core) for other in self.levels
        ]
        self.slots = {piece: slot for slot, piece in enumerate(pieces)}
        self.middles = {piece: slot for slot, piece in enumerate(given)}
        self.exchanges, self.flights = {}, {}

    def neighbours(self):
        return [self.sibling, *self.across, *self.column]

    def exchange(self, weight, left, right):
        half = self.weights[weight][1]
        theirs = pl.ds(pl.multiple_of((1 - self.core) * half, 16), half)
        self.exchanges[weight] = (
            left, right,
            [
                self.links.copy(left[0], left[1], self.sibling),
                self.links.copy(right[0].at[theirs, :], right[1], self.sibling),
            ],
        )

    def product(self, piece, first):
        left, right, copies = self.exchanges[piece.weight]
        while copies:
            copies.pop().wait_recv()
        places = [
            outer * 4 + (inner * 2 + first if piece.axis == 0 else first * 2 + inner)
            for outer in range(self.depth)
            for inner in range(2)
        ]
        rows = slice(piece.first_row, piece.first_row + ROWS)
        mine, other = (
            jnp.concatenate([side[place, rows, :] for place in places], 0) for side in left
        )
        start = self.core * self.weights[piece.weight][1] + piece.first_column
        own = pl.ds(pl.multiple_of(start, 16), TILE)
        there = slice(piece.first_column, piece.first_column + TILE)
        total = dot(mine, right[0][own, :], NT) + dot(other, right[1][there, :], NT)
        return total.reshape(self.depth, 2, ROWS, TILE)

    def first(self, piece):
        slot = self.slots[piece]
        away = self.refs.away.at[slot]
        away[...] = self.product(piece, 1 - self.spot[1 - piece.axis]).astype(jnp.bfloat16)
        self.flights[piece] = self.links.copy(
            away, self.refs.one.at[slot], self.across[piece.axis]
        )

    def second(self, piece):
        slot = self.slots[piece]
        self.flights.pop(piece).wait_recv()
        one = self.refs.one.at[slot]
        total = self.product(piece, self.spot[1 - piece.axis]) + one[...].astype(jnp.float32)
        one[...] = total.astype(jnp.bfloat16)
        self.flights[piece] = self.links.copy(
            one.at[:, 1 - self.spot[piece.axis]], self.refs.two.at[slot],
            self.across[1 - piece.axis],
        )

    def middle(self, piece, into, place):
        slot = self.slots[piece]
        self.flights.pop(piece).wait_recv()
        kept = self.refs.one[slot, :, self.spot[piece.axis]].astype(jnp.float32)
        into[place] = (kept + self.refs.two[slot].astype(jnp.float32)).astype(into.dtype)

    def third(self, piece):
        if piece not in self.middles:
            self.middles[piece] = len(self.middles)
            self.middle(piece, self.refs.mid, self.middles[piece])
        place = self.middles[piece]
        self.flights[piece] = [
            self.links.copy(
                self.refs.mid.at[place, other], self.refs.three.at[place, step], self.column[step]
            )
            for step, other in enumerate(self.levels)
        ]

    def fourth(self, piece, out):
        place = self.middles[piece]
        total = self.refs.mid[place, self.level].astype(jnp.float32)
        for step, copy in enumerate(self.flights.pop(piece)):
            copy.wait_recv()
            total = total + self.refs.three[place, step].astype(jnp.float32)
        start = self.core * self.weights[piece.weight][1] + piece.first_column
        filled = out.at[
            piece.first_row : piece.first_row + ROWS, pl.ds(pl.multiple_of(start, 128), TILE)
        ]
        filled[...] = total
        self.flights[piece] = self.links.copy(filled, filled, self.sibling)

    def last(self, piece):
        self.flights.pop(piece).wait_recv()


def reducer_scratch(weights, pieces, middles, depth, tokens):
    low = jnp.bfloat16
    shapes = dict(
        away=((len(pieces), depth, 2, ROWS, TILE), low),
        one=((len(pieces), depth, 2, ROWS, TILE), low),
        two=((len(pieces), depth, ROWS, TILE), low),
    )
    if middles > 0:
        shapes.update(
            mid=((middles, depth, ROWS, TILE), low), three=((middles, depth - 1, ROWS, TILE), low)
        )
    return shapes


def gelu_slope(value):
    scale = math.sqrt(2.0 / math.pi)
    square = value * value
    bent = jnp.tanh(scale * value * (1.0 + 0.044715 * square))
    return 0.5 * (1.0 + bent) + 0.5 * value * (1.0 - bent * bent) * scale * (
        1.0 + 3.0 * 0.044715 * square
    )


def gelu_and_slope(value):
    scale = math.sqrt(2.0 / math.pi)
    square = value * value
    bent = jnp.tanh(scale * value * (1.0 + 0.044715 * square))
    half = 0.5 * (1.0 + bent)
    slope = half + 0.5 * value * (1.0 - bent * bent) * scale * (1.0 + 3.0 * 0.044715 * square)
    return value * half, slope


def norm_gradient(inputs, gain, grad):
    center = inputs - jnp.mean(inputs, 0, keepdims=True)
    factor = lax.rsqrt(jnp.mean(center * center, 0, keepdims=True) + norm_eps)
    unit = center * factor
    scaled = grad * gain
    result = factor * (
        scaled
        - jnp.mean(scaled, 0, keepdims=True)
        - unit * jnp.mean(scaled * unit, 0, keepdims=True)
    )
    return result, jnp.sum(grad * unit, 1, keepdims=True), jnp.sum(grad, 1, keepdims=True)


def rows_product(matrix, other, out_rows, chunk, store):
    def one_chunk(index, carry):
        rows = pl.ds(pl.multiple_of(index * chunk, 128), chunk)
        store(rows, dot(matrix[rows, :], other))
        return carry

    lax.fori_loop(0, out_rows // chunk, one_chunk, 0)


def back_one_body(n, seqs, groups, span, group_rows, width, hidden_width, refs):
    at = HeadPlaces(n, seqs, groups)
    half = n // 2
    heads = group_rows // HEAD
    tokens = seqs * span
    links, loads = Links(refs), Loads(refs)
    weights = gradient_weights(width, hidden_width, n)
    pieces = pieces_of(weights, BACK_ONE_ORDER)
    reducer = Reducer(refs, links, groups, weights, pieces, [])
    down, up, out = [[piece for piece in pieces if piece.weight == weight] for weight in (DOWN, UP, OUT)]
    barrier = pltpu.get_barrier_semaphore()
    at.signal_all(barrier, reducer.neighbours()[1:])

    load_w_down = loads.start(refs.w_down.at[1], refs.down)
    load_cotangent = loads.start(refs.cotangent, refs.cot)
    load_slope = loads.start(refs.slope, refs.slope_in)
    load_w_up = loads.start(refs.w_up.at[1], refs.up)
    load_hidden = loads.start(refs.hidden, refs.hidden_in)
    load_active = loads.start(refs.active, refs.down_left)
    load_w_out = loads.start(refs.w_out.at[1], refs.out)
    load_normed = loads.start(refs.normed, refs.up_left)
    load_attended = loads.start(refs.attended, refs.out_left)
    load_held = loads.start(refs.held, refs.held_in)

    load_cotangent.wait()
    for seq in range(seqs):
        lanes = slice(seq * span, (seq + 1) * span)
        for first in range(0, width, span):
            piece = refs.cot[seq, :, first : first + span].astype(jnp.float32).T
            refs.grad[first : first + span, lanes] = piece * refs.valid[:, lanes]
    refs.down_right[...] = refs.grad[...].astype(jnp.bfloat16)
    load_w_down.wait()
    load_slope.wait()

    def store_raised(rows, value):
        slope = refs.slope_in[rows, :].astype(jnp.float32)
        refs.up_right[rows, :] = (slope * value).astype(jnp.bfloat16)

    rows_product(refs.down, refs.down_right[...], hidden_width, 512, store_raised)
    at.wait_all(barrier, len(reducer.neighbours()) - 1)
    load_active.wait()
    reducer.exchange(DOWN, (refs.down_left, refs.down_left_other), (refs.down_right, refs.down_right_other))
    load_w_up.wait()
    load_hidden.wait()
    load_normed.wait()
    reducer.exchange(UP, (refs.up_left, refs.up_left_other), (refs.up_right, refs.up_right_other))
    d_normed = dot(refs.up[...], refs.up_right[...])
    d_inputs, gain_part, bias_part = norm_gradient(refs.hidden_in[...], refs.gain[...], d_normed)
    refs.small[:, 0:1] = gain_part
    refs.small[:, 1:2] = bias_part
    grad = refs.grad[...] + d_inputs
    refs.grad_out[...] = grad
    refs.out_right[...] = grad.astype(jnp.bfloat16)
    load_w_out.wait()
    load_attended.wait()
    reducer.exchange(OUT, (refs.out_left, refs.out_left_other), (refs.out_right, refs.out_right_other))
    refs.d_attended[...] = dot(refs.out[...], refs.out_right[...]).astype(jnp.bfloat16)

    arrive = links.slots(half)
    leave = links.slots(len(at.targets))
    spread = []
    for count, (device, seq, group) in enumerate(at.targets):
        source = refs.d_attended.at[
            group * group_rows : (group + 1) * group_rows, seq * span : (seq + 1) * span
        ]
        sent = (
            source, refs.landing.at[at.me // 2], refs.send.at[leave + count],
            refs.recv.at[arrive + at.me // 2], device,
        )
        at.send(*sent)
        spread.append(sent)
    load_held.wait()
    started = [piece for pair in zip(down, up) for piece in pair] + out
    for piece in started:
        reducer.first(piece)
    for index in range(half):
        landed = refs.landing.at[index]
        remote(
            landed, landed, refs.send.at[leave], refs.recv.at[arrive + index], at.sibling
        ).wait_recv()

    returned = links.slots(len(at.targets) * heads)
    returning = links.slots(half * heads)
    slot = at.seq * groups + at.group
    going = []
    passed = []

    def send_back(head):
        passed[head].wait_recv()
        for index, device in enumerate(at.sources):
            results = refs.results.at[head, index]
            kept = refs.kept.at[head, index]
            part = refs.partial_recv[head, index].astype(jnp.float32)
            results[1] = (kept[:HEAD] + part[:HEAD]).astype(jnp.bfloat16)
            results[2] = (kept[HEAD:] + part[HEAD:]).astype(jnp.bfloat16)
            into = refs.d_qkv.at[
                :,
                pl.ds(pl.multiple_of(at.group * group_rows + head * HEAD, HEAD), HEAD),
                pl.ds(pl.multiple_of(at.seq * span, span), span),
            ]
            sent = (
                results, into, refs.send.at[returning + head * half + index],
                refs.recv.at[returned + head * len(at.targets) + slot], device,
            )
            at.send(*sent)
            going.append(sent)

    def attend(head):
        fill_head(refs.held_in, head, 1, n, span, refs.key_rows, refs.key_columns)
        fill_head(refs.held_in, head, 2, n, span, refs.value_rows, None)
        head_rows = slice(head * HEAD, (head + 1) * HEAD)
        refs.key_grads[...] = jnp.zeros_like(refs.key_grads)
        refs.value_grads[...] = jnp.zeros_like(refs.value_grads)
        for index, block in enumerate(at.blocks):
            query = refs.held_in[head, block, :HEAD, :] * jnp.bfloat16(HEAD**-0.5)
            grad = refs.landing[index, head_rows, :]
            log_total = refs.lse[index, head : head + 1, :]
            clear, reach = 2 * index * span, 2 * (index + 1) * span
            pieces = []
            row_term = jnp.zeros((1, span), jnp.float32)
            for first, last in ((0, clear), (clear, reach)):
                if first == last:
                    continue
                scores = dot(refs.key_rows[first:last, :], query)
                if last == reach:
                    scores = jnp.where(
                        causal(clear, reach - clear, block * span, span), scores, masked_score
                    )
                weights = jnp.exp(scores - log_total)
                d_weights = dot(refs.value_rows[first:last, :], grad)
                row_term = row_term + jnp.sum(weights * d_weights, 0, keepdims=True)
                pieces.append((first, last, weights, d_weights))
            d_query = jnp.zeros((HEAD, span), jnp.float32)
            for first, last, weights, d_weights in pieces:
                d_scores = (weights * (d_weights - row_term)).astype(jnp.bfloat16)
                d_query = d_query + dot(refs.key_columns[:, first:last], d_scores)
                refs.key_grads[:, first:last] += dot(query, d_scores, NT)
                refs.value_grads[:, first:last] += dot(grad, weights.astype(jnp.bfloat16), NT)
            refs.results[head, index, 0] = (d_query * HEAD**-0.5).astype(jnp.bfloat16)
        for index in range(half):
            other = pl.ds(pl.multiple_of(block_of(index, 1 - at.core) * span, span), span)
            own = pl.ds(pl.multiple_of(at.blocks[index] * span, span), span)
            refs.partial_send[head, index, :HEAD, :] = refs.key_grads[:, other].astype(jnp.bfloat16)
            refs.partial_send[head, index, HEAD:, :] = refs.value_grads[:, other].astype(jnp.bfloat16)
            refs.kept[head, index, :HEAD, :] = refs.key_grads[:, own]
            refs.kept[head, index, HEAD:, :] = refs.value_grads[:, own]
        passed.append(
            links.copy(refs.partial_send.at[head], refs.partial_recv.at[head], at.sibling)
        )

    waiting = list(started)
    for head in range(heads):
        attend(head)
        if head > 0:
            send_back(head - 1)
        for _ in range(2 + head):
            reducer.second(waiting.pop(0))
    send_back(heads - 1)
    while waiting:
        reducer.second(waiting.pop(0))
    for place, piece in enumerate(pieces):
        reducer.middle(piece, refs.mid_out, place)
    for head in range(heads):
        for count, (device, seq, group) in enumerate(at.targets):
            landed = refs.d_qkv.at[
                :,
                group * group_rows + head * HEAD : group * group_rows + (head + 1) * HEAD,
                seq * span : (seq + 1) * span,
            ]
            remote(
                landed, landed, refs.send.at[leave],
                refs.recv.at[returned + head * len(at.targets) + count], at.sibling,
            ).wait_recv()
    for sent in spread + going:
        at.wait_sent(*sent)
    links.finish()


def gradient_weights(width, hidden_width, n):
    return {
        QKV: (width // n, 3 * width // 2),
        DOWN: (hidden_width // n, width // 2),
        UP: (width // n, hidden_width // 2),
        OUT: (width // n, width // 2),
    }


BACK_ONE_ORDER = ((DOWN, (1,)), (UP, (0,)), (OUT, (0,)))
BACK_TWO_ORDER = ((QKV, (1, 0, 1)), (DOWN, (1,)), (UP, (0,)), (OUT, (0,)))
BACK_THREE_ORDER = ((QKV, (1, 0, 0)),)


def back_one(
    cotangent, valid, hidden, slope, normed, active, attended, held, lse, gain,
    w_out, w_up, w_down, collective,
):
    seqs, span, width = cotangent.shape
    heads, n = held.shape[:2]
    group_rows = heads * HEAD
    groups = width // group_rows
    hidden_width = w_up.shape[2]
    tokens = seqs * span
    half = n // 2
    low, wide = jnp.bfloat16, jnp.float32
    weights = gradient_weights(width, hidden_width, n)
    pieces = pieces_of(weights, BACK_ONE_ORDER)
    inputs = dict(
        cotangent=(cotangent, HBM), valid=(valid, VMEM), hidden=(hidden, HBM), slope=(slope, HBM),
        normed=(normed, HBM), active=(active, HBM), attended=(attended, HBM), held=(held, HBM),
        lse=(lse, VMEM), gain=(gain, VMEM), w_out=(w_out, HBM), w_up=(w_up, HBM),
        w_down=(w_down, HBM),
    )
    outputs = dict(
        d_qkv=((3, width, tokens), low, VMEM),
        grad_out=((width, tokens), wide, VMEM),
        small=((width, 2), wide, VMEM),
        mid_out=((len(pieces), groups, ROWS, TILE), low, VMEM),
    )
    scratch = dict(
        down=(w_down.shape[1:], low), up=(w_up.shape[1:], low), out=(w_out.shape[1:], low),
        cot=(cotangent.shape, low), grad=((width, tokens), wide), hidden_in=((width, tokens), wide),
        slope_in=(slope.shape, low), d_attended=((width, tokens), low),
        down_left=(active.shape, low), down_right=((width, tokens), low),
        up_left=(normed.shape, low), up_right=((hidden_width, tokens), low),
        out_left=(attended.shape, low), out_right=((width, tokens), low),
        held_in=(held.shape, low), landing=((half, group_rows, span), low),
        results=((heads, half, 3, HEAD, span), low), kept=((heads, half, 2 * HEAD, span), wide),
        partial_send=((heads, half, 2 * HEAD, span), low),
        partial_recv=((heads, half, 2 * HEAD, span), low),
        key_grads=((HEAD, n * span), wide), value_grads=((HEAD, n * span), wide),
        key_rows=((n * span, HEAD), low), key_columns=((HEAD, n * span), low),
        value_rows=((n * span, HEAD), low),
        down_left_other=(active.shape, low), down_right_other=((width // 2, tokens), low),
        up_left_other=(normed.shape, low), up_right_other=((hidden_width // 2, tokens), low),
        out_left_other=(attended.shape, low), out_right_other=((width // 2, tokens), low),
        **reducer_scratch(weights, pieces, 0, groups, tokens),
    )
    body = functools.partial(
        back_one_body, n, seqs, groups, span, group_rows, width, hidden_width
    )
    return launch(body, inputs, outputs, scratch, 120, collective)


def back_two_body(n, seqs, span, width, hidden_width, refs):
    channels = width // n
    me, core = lax.axis_index(SEQ), lax.axis_index(BATCH)
    peers = [lax.rem(me + step, n) for step in range(1, n)]
    links, loads = Links(refs), Loads(refs)
    weights = gradient_weights(width, hidden_width, n)
    pieces, given = pieces_of(weights, BACK_TWO_ORDER), pieces_of(weights, BACK_ONE_ORDER)
    reducer = Reducer(refs, links, n // 4, weights, pieces, given)
    outs = {QKV: refs.qkv_grad, DOWN: refs.down_grad, UP: refs.up_grad, OUT: refs.out_grad}
    qkv, down, up, out = [
        [piece for piece in pieces if piece.weight == weight] for weight in (QKV, DOWN, UP, OUT)
    ]
    barrier = pltpu.get_barrier_semaphore()
    for device in [(peer, core) for peer in peers] + [reducer.sibling]:
        pl.semaphore_signal(barrier, inc=1, device_id=device, device_id_type=MESH)
    load_mid = loads.start(refs.mid_in, refs.mid.at[: len(given)])
    load_w_qkv = loads.start(refs.w_qkv.at[1], refs.qkv)
    load_d_qkv = loads.start(refs.d_qkv, refs.qkv_right)
    load_hidden_two = loads.start(refs.hidden_two, refs.hidden_two_in)
    load_grad = loads.start(refs.grad, refs.grad_now)
    load_normed_three = loads.start(refs.normed_three, refs.qkv_left)
    load_w_down = loads.start(refs.w_down.at[0], refs.down)
    load_slope = loads.start(refs.slope, refs.slope_in)
    load_w_up = loads.start(refs.w_up.at[0], refs.up)
    load_active = loads.start(refs.active, refs.down_left)
    load_hidden_one = loads.start(refs.hidden_one, refs.hidden_one_in)
    load_normed_two = loads.start(refs.normed_two, refs.up_left)
    load_w_out = loads.start(refs.w_out.at[0], refs.out)
    load_gated = loads.start(refs.gated, refs.out_left)
    load_queries = loads.start(refs.queries, refs.queries_in)
    load_mixer = loads.start(refs.mixer, refs.mixer_in)
    load_carried = loads.start(refs.carried, refs.carried_in)
    load_held = loads.start(refs.held, refs.held_in)

    load_w_qkv.wait()
    load_d_qkv.wait()
    d_normed = dot(refs.qkv[...], refs.qkv_right[...])
    pl.semaphore_wait(barrier, n)
    load_mid.wait()
    thirds = list(given)
    for _ in range(4):
        reducer.third(thirds.pop(0))
    load_normed_three.wait()
    reducer.exchange(QKV, (refs.qkv_left, refs.qkv_left_other), (refs.qkv_right, refs.qkv_right_other))
    load_hidden_two.wait()
    load_grad.wait()
    d_inputs, gain_part, bias_part = norm_gradient(
        refs.hidden_two_in[...], refs.gains[:, 2:3], d_normed
    )
    refs.small[:, 0:1] = gain_part
    refs.small[:, 1:2] = bias_part
    grad = refs.grad_now[...] + d_inputs
    refs.grad_now[...] = grad
    refs.down_right[...] = grad.astype(jnp.bfloat16)
    load_w_down.wait()
    load_slope.wait()
    load_active.wait()
    reducer.exchange(DOWN, (refs.down_left, refs.down_left_other), (refs.down_right, refs.down_right_other))

    def store_raised(rows, value):
        slope = refs.slope_in[rows, :].astype(jnp.float32)
        refs.up_right[rows, :] = (slope * value).astype(jnp.bfloat16)

    rows_product(refs.down, refs.down_right[...], hidden_width, 512, store_raised)
    for piece in qkv:
        reducer.first(piece)
    load_w_up.wait()
    load_hidden_one.wait()
    load_normed_two.wait()
    reducer.exchange(UP, (refs.up_left, refs.up_left_other), (refs.up_right, refs.up_right_other))
    d_normed = dot(refs.up[...], refs.up_right[...])
    d_inputs, gain_part, bias_part = norm_gradient(
        refs.hidden_one_in[...], refs.gains[:, 1:2], d_normed
    )
    refs.small[:, 2:3] = gain_part
    refs.small[:, 3:4] = bias_part
    grad = refs.grad_now[...] + d_inputs
    refs.grad_out[...] = grad
    refs.out_right[...] = grad.astype(jnp.bfloat16)
    load_w_out.wait()
    load_gated.wait()
    load_queries.wait()
    load_mixer.wait()
    load_carried.wait()
    reducer.exchange(OUT, (refs.out_left, refs.out_left_other), (refs.out_right, refs.out_right_other))
    d_gated = dot(refs.out[...], refs.out_right[...])
    d_mixer = d_gated * refs.queries_in[...]
    for seq in range(seqs):
        refs.d_conv[seq] = d_mixer[:, seq * span : (seq + 1) * span].astype(jnp.bfloat16)
    going = []
    arrive, answered = links.slots(n - 1), links.slots(n - 1)
    for step, peer in enumerate(peers):
        rows = pl.ds(pl.multiple_of(peer * channels, 16), channels)
        going.append(
            links.copy(refs.d_conv.at[:, rows, :], refs.landing.at[me], (peer, core), arrive + step)
        )
    own_rows = pl.ds(pl.multiple_of(me * channels, 16), channels)
    load_own = loads.start(refs.d_conv.at[:, own_rows, :], refs.landing.at[me])
    refs.d_mixer[...] = d_mixer
    refs.d_queries[...] = (d_gated * refs.mixer_in[...]).astype(jnp.bfloat16)
    refs.small[:, 4:5] = sum(
        jnp.sum(
            d_mixer[:, seq * span : (seq + 1) * span] * refs.carried_in[seq].astype(jnp.float32), 1,
            keepdims=True,
        )
        for seq in range(seqs)
    )

    while thirds:
        reducer.third(thirds.pop(0))
    started = qkv + [piece for pair in zip(down, up) for piece in pair] + out
    for piece in started[3:]:
        reducer.first(piece)
    for piece in qkv:
        reducer.second(piece)
    waiting = started[3:]
    total_rows = n * seqs * channels
    fill_tables(channels, span, refs)
    load_held.wait()
    refs.flat_x[...] = refs.held_in[...].astype(jnp.float32).reshape(total_rows, span)
    load_own.wait()
    for copy in going:
        copy.wait_recv()
    refs.flat_d[...] = refs.landing[...].astype(jnp.float32).reshape(total_rows, span)

    def one_channel(channel, carry):
        mixer_backward_channel(n, seqs, span, channels, refs, channel)
        return carry

    lax.fori_loop(0, channels // 2, one_channel, 0, unroll=4)
    for piece in qkv:
        reducer.third(piece)
    for _ in range(3):
        reducer.second(waiting.pop(0))
    lax.fori_loop(channels // 2, channels, one_channel, 0, unroll=4)
    refs.landing[...] = refs.flat_d[...].reshape(n, seqs, channels, span).astype(jnp.bfloat16)
    back = []
    for step, peer in enumerate(peers):
        back.append(
            links.copy(
                refs.landing.at[peer], refs.from_conv.at[:, own_rows, :], (peer, core),
                answered + step,
            )
        )
    load_answer = loads.start(refs.landing.at[me], refs.from_conv.at[:, own_rows, :])
    states = [
        links.copy(refs.rate_grad, refs.rate_other, reducer.sibling),
        links.copy(refs.weight_grad, refs.weight_other, reducer.sibling),
    ]
    while waiting:
        reducer.second(waiting.pop(0))
    finished = given + qkv
    for piece in finished:
        reducer.fourth(piece, outs[piece.weight])
    for copy in states:
        copy.wait_recv()
    refs.rate_sum[...] = refs.rate_grad[...] + refs.rate_other[...]
    refs.weight_sum[...] = refs.weight_grad[...] + refs.weight_other[...]
    for place, piece in enumerate(down + up + out):
        reducer.middle(piece, refs.mid_out, place)
    for piece in finished:
        reducer.last(piece)
    load_answer.wait()
    for copy in back:
        copy.wait_recv()
    links.finish()


def back_two(
    mid, d_qkv, grad, hidden_two, normed_three, slope, normed_two, active, hidden_one, gated,
    queries, mixer, carried, held, gains, rates, rate_weights, w_qkv, w_out, w_up, w_down, collective,
):
    n, seqs, channels, span = held.shape
    width, hidden_width = w_up.shape[1:]
    tokens = seqs * span
    low, wide = jnp.bfloat16, jnp.float32
    weights = gradient_weights(width, hidden_width, n)
    pieces = pieces_of(weights, BACK_TWO_ORDER)
    inputs = dict(
        mid_in=(mid, HBM), d_qkv=(d_qkv, HBM), grad=(grad, HBM), hidden_two=(hidden_two, HBM),
        normed_three=(normed_three, HBM), slope=(slope, HBM), normed_two=(normed_two, HBM),
        active=(active, HBM), hidden_one=(hidden_one, HBM), gated=(gated, HBM),
        queries=(queries, HBM), mixer=(mixer, HBM), carried=(carried, HBM), held=(held, HBM),
        gains=(gains, VMEM), rates=(rates, VMEM), rate_weights=(rate_weights, VMEM),
        w_qkv=(w_qkv, HBM), w_out=(w_out, HBM), w_up=(w_up, HBM), w_down=(w_down, HBM),
    )
    square, state = (width, tokens), (channels, 2 * STATES)
    outputs = dict(
        from_conv=((seqs, width, span), low, VMEM),
        d_mixer=(square, wide, VMEM),
        d_queries=(square, low, VMEM),
        grad_out=(square, wide, VMEM),
        small=((width, 5), wide, VMEM),
        rate_sum=(state, wide, VMEM),
        weight_sum=(state, wide, VMEM),
        qkv_grad=((width // n, 3 * width), wide, VMEM),
        down_grad=((hidden_width // n, width), wide, VMEM),
        up_grad=((width // n, hidden_width), wide, VMEM),
        out_grad=((width // n, width), wide, VMEM),
        mid_out=((len(pieces) - 3, n // 4, ROWS, TILE), low, VMEM),
    )
    flat = (n * seqs * channels, span)
    scratch = dict(
        qkv=(w_qkv.shape[1:], low), down=(w_down.shape[1:], low), up=(w_up.shape[1:], low),
        out=(w_out.shape[1:], low),
        qkv_left=(normed_three.shape, low), qkv_right=((3 * width, tokens), low),
        down_left=(active.shape, low), down_right=(square, low),
        up_left=(normed_two.shape, low), up_right=((hidden_width, tokens), low),
        out_left=(gated.shape, low), out_right=(square, low),
        hidden_two_in=(square, wide), hidden_one_in=(square, wide), grad_now=(square, wide),
        slope_in=(slope.shape, low), queries_in=(square, queries.dtype),
        mixer_in=(square, mixer.dtype), carried_in=(carried.shape, low), held_in=(held.shape, low),
        d_conv=((seqs, width, span), low), landing=(held.shape, low),
        flat_x=(flat, wide), flat_d=(flat, wide), **table_scratch(channels, span),
        rate_grad=(state, wide), weight_grad=(state, wide),
        rate_other=(state, wide), weight_other=(state, wide),
        qkv_left_other=(normed_three.shape, low), qkv_right_other=((3 * width // 2, tokens), low),
        down_left_other=(active.shape, low), down_right_other=((width // 2, tokens), low),
        up_left_other=(normed_two.shape, low), up_right_other=((hidden_width // 2, tokens), low),
        out_left_other=(gated.shape, low), out_right_other=((width // 2, tokens), low),
        **reducer_scratch(weights, pieces, mid.shape[0] + 3, n // 4, tokens),
    )
    body = functools.partial(back_two_body, n, seqs, span, width, hidden_width)
    return launch(body, inputs, outputs, scratch, 160, collective)


def back_three_body(n, seqs, span, width, hidden_width, refs):
    me, core = lax.axis_index(SEQ), lax.axis_index(BATCH)
    links, loads = Links(refs), Loads(refs)
    weights = gradient_weights(width, hidden_width, n)
    pieces, given = pieces_of(weights, BACK_THREE_ORDER), pieces_of(weights, BACK_ONE_ORDER)
    reducer = Reducer(refs, links, n // 4, weights, pieces, given)
    outs = {QKV: refs.qkv_grad, DOWN: refs.down_grad, UP: refs.up_grad, OUT: refs.out_grad}
    stacked = (
        (refs.qkv_all, refs.qkv_grad, refs.qkv_two), (refs.down_all, refs.down_grad, refs.down_two),
        (refs.up_all, refs.up_grad, refs.up_two), (refs.out_all, refs.out_grad, refs.out_two),
    )
    barrier = pltpu.get_barrier_semaphore()
    before, after = (lax.rem(me + n - 1, n), core), (lax.rem(me + 1, n), core)
    greeted = [*reducer.neighbours(), before, after]
    for device in greeted:
        pl.semaphore_signal(barrier, inc=1, device_id=device, device_id_type=MESH)
    tokens = seqs * span
    load_mid = loads.start(refs.mid_in, refs.mid.at[: len(given)])
    load_from_conv = loads.start(refs.from_conv, refs.conv_in)
    load_d_mixer = loads.start(refs.d_mixer, refs.mixer_in)
    load_values = loads.start(refs.values, refs.values_in)
    load_shifted = loads.start(refs.shifted, refs.shifted_in)
    load_keys = loads.start(refs.keys, refs.keys_in)
    load_d_queries = loads.start(refs.d_queries, refs.qkv_right.at[:width, :])
    load_w_qkv = loads.start(refs.w_qkv.at[0], refs.qkv)
    load_normed = loads.start(refs.normed, refs.qkv_left)
    load_tokens = loads.start(refs.tokens, refs.tokens_in)
    load_grad = loads.start(refs.grad, refs.grad_in)
    load_from_conv.wait()
    load_d_mixer.wait()
    load_values.wait()
    load_shifted.wait()
    valid = refs.valid[...]
    conv = jnp.concatenate([refs.conv_in[seq] for seq in range(seqs)], 1).astype(jnp.float32)
    d_carried = (refs.mixer_in[...] * refs.skip[...] + conv) * valid
    d_shifted = d_carried * refs.values_in[...]
    refs.d_shifted[...] = d_shifted
    for seq in range(seqs):
        for first in range(0, width, span):
            turned = d_shifted[first : first + span, seq * span : (seq + 1) * span].T
            refs.rim_out[seq, :, first : first + span] = turned[: refs.rim_out.shape[1]]
    refs.qkv_right[2 * width :, :] = (d_carried * refs.shifted_in[...]).astype(jnp.bfloat16)
    pl.semaphore_wait(barrier, len(greeted))
    halo = links.copy(refs.rim_out, refs.rim_in, before)
    load_mid.wait()
    for piece in given:
        reducer.third(piece)
    saves = [loads.start(second, whole.at[1]) for whole, _, second in stacked]
    load_keys.wait()
    halo.wait_recv()
    lane = lax.broadcasted_iota(jnp.int32, (width, span), 1)
    there = jnp.where(me == n - 1, 0.0, 1.0)
    rim = refs.rim_in.shape[1]
    tap_sums = [jnp.zeros((width, 1), jnp.float32) for _ in range(TAPS)]
    for seq in range(seqs):
        lanes = slice(seq * span, (seq + 1) * span)
        own = refs.d_shifted[:, lanes]
        keys = refs.keys_in[:, lanes].astype(jnp.float32)
        turned = []
        for first in range(0, width, span):
            piece = refs.rim_in[seq, :, first : first + span] * there
            piece = jnp.concatenate([piece, jnp.zeros((span - rim, span), jnp.float32)], 0)
            turned.append(piece.T)
        following = jnp.concatenate(turned, 0)
        d_keys = jnp.zeros((width, span), jnp.float32)
        for offset in range(TAPS):
            moved = own
            if offset > 0:
                moved = jnp.where(
                    lane < span - offset,
                    pltpu.roll(own, span - offset, 1),
                    pltpu.roll(following, span - offset, 1),
                )
            d_keys = d_keys + refs.taps[:, offset : offset + 1] * moved
            tap_sums[offset] = tap_sums[offset] + jnp.sum(moved * keys, 1, keepdims=True)
        refs.qkv_right[width : 2 * width, lanes] = d_keys.astype(jnp.bfloat16)
    load_d_queries.wait()
    load_normed.wait()
    reducer.exchange(QKV, (refs.qkv_left, refs.qkv_left_other), (refs.qkv_right, refs.qkv_right_other))
    load_w_qkv.wait()
    load_tokens.wait()
    load_grad.wait()
    d_normed = dot(refs.qkv[...], refs.qkv_right[...])
    flat_in = jnp.concatenate(
        [refs.tokens_in[seq].astype(jnp.float32).T for seq in range(seqs)], 1
    )
    d_inputs, gain_part, bias_part = norm_gradient(flat_in * valid, refs.gain[...], d_normed)
    refs.total[...] = (refs.grad_in[...] + d_inputs) * valid
    refs.sums[...] = refs.small_in[...]
    for offset in range(TAPS):
        refs.sums[:, 8 + offset : 9 + offset] = tap_sums[offset]
    refs.sums[:, 0:1] = gain_part
    refs.sums[:, 4:5] = bias_part
    shared = links.copy(refs.sums, refs.sums_other, reducer.sibling)
    for piece in pieces:
        reducer.first(piece)
    shared.wait_recv()
    rows = width // n
    refs.slices[...] = (refs.sums[...] + refs.sums_other[...]).reshape(n, rows, 128)
    depth = n // 4
    y, x = reducer.spot
    for outer in range(depth):
        for inner in range(2):
            refs.small_away[outer, inner] = refs.slices[outer * 4 + inner * 2 + 1 - x]
    small = links.copy(refs.small_away, refs.small_one, reducer.across[0])
    for seq in range(seqs):
        for first in range(0, width, span):
            refs.d_tokens[seq, :, first : first + span] = refs.total[
                first : first + span, seq * span : (seq + 1) * span
            ].T
    for piece in pieces:
        reducer.second(piece)
    small.wait_recv()
    for outer in range(depth):
        for inner in range(2):
            refs.small_one[outer, inner] += refs.slices[outer * 4 + inner * 2 + x]
    small = links.copy(refs.small_one.at[:, 1 - y], refs.small_two, reducer.across[1])
    for piece in given:
        reducer.fourth(piece, outs[piece.weight])
    for piece in pieces:
        reducer.third(piece)
    small.wait_recv()
    for outer in range(depth):
        refs.small_two[outer] += refs.small_one[outer, y]
    smalls = [
        links.copy(refs.small_two.at[other], refs.small_three.at[step], reducer.column[step])
        for step, other in enumerate(reducer.levels)
    ]
    for piece in pieces:
        reducer.fourth(piece, outs[piece.weight])
    total = refs.small_two[reducer.level]
    for step, copy in enumerate(smalls):
        copy.wait_recv()
        total = total + refs.small_three[step]
    padded = jnp.concatenate([total, jnp.zeros((128 - rows, 128), jnp.float32)], 0).T
    refs.small_sum[...] = padded[: refs.small_sum.shape[0], :rows]
    for piece in given + pieces:
        reducer.last(piece)
    saves += [loads.start(mine, whole.at[0]) for whole, mine, _ in stacked]
    for copy in saves:
        copy.wait()
    links.finish()


def back_three(
    from_conv, d_mixer, d_queries, values, shifted, keys, grad, tokens, normed, valid, gain, skip,
    taps, small, w_qkv, mid, qkv_two, down_two, up_two, out_two, collective,
):
    seqs, width, span = from_conv.shape
    n = normed.shape[0]
    columns = seqs * span
    low, wide = jnp.bfloat16, jnp.float32
    hidden_width = up_two.shape[1]
    weights = gradient_weights(width, hidden_width, n)
    pieces = pieces_of(weights, BACK_THREE_ORDER)
    inputs = dict(
        from_conv=(from_conv, HBM), d_mixer=(d_mixer, HBM), d_queries=(d_queries, HBM),
        values=(values, HBM), shifted=(shifted, HBM), keys=(keys, HBM), grad=(grad, HBM),
        tokens=(tokens, HBM), normed=(normed, HBM), valid=(valid, VMEM), gain=(gain, VMEM),
        skip=(skip, VMEM), taps=(taps, VMEM), small_in=(small, VMEM), w_qkv=(w_qkv, HBM),
        mid_in=(mid, HBM), qkv_two=(qkv_two, HBM), down_two=(down_two, HBM), up_two=(up_two, HBM),
        out_two=(out_two, HBM),
    )
    square = (width, columns)
    outputs = dict(
        d_tokens=((seqs, span, width), wide, VMEM),
        qkv_all=((2, *qkv_two.shape), wide, HBM), down_all=((2, *down_two.shape), wide, HBM),
        up_all=((2, *up_two.shape), wide, HBM), out_all=((2, *out_two.shape), wide, HBM),
        small_sum=((16, width // n), wide, VMEM),
    )
    scratch = dict(
        qkv=(w_qkv.shape[1:], low), qkv_left=(normed.shape, low), qkv_right=((3 * width, columns), low),
        conv_in=(from_conv.shape, low), mixer_in=(square, wide), values_in=(square, values.dtype),
        shifted_in=(square, shifted.dtype), keys_in=(square, low), tokens_in=(tokens.shape, low),
        grad_in=(square, wide), d_shifted=(square, wide), total=(square, wide),
        rim_out=((seqs, 8, width), wide), rim_in=((seqs, 8, width), wide),
        sums=((width, 128), wide), sums_other=((width, 128), wide),
        slices=((n, width // n, 128), wide),
        qkv_left_other=(normed.shape, low), qkv_right_other=((3 * width // 2, columns), low),
        qkv_grad=(qkv_two.shape, wide), down_grad=(down_two.shape, wide),
        up_grad=(up_two.shape, wide), out_grad=(out_two.shape, wide),
        small_away=((n // 4, 2, width // n, 128), wide), small_one=((n // 4, 2, width // n, 128), wide),
        small_two=((n // 4, width // n, 128), wide), small_three=((n // 4 - 1, width // n, 128), wide),
        **reducer_scratch(weights, pieces, mid.shape[0] + len(pieces), n // 4, columns),
    )
    body = functools.partial(back_three_body, n, seqs, span, width, hidden_width)
    return launch(body, inputs, outputs, scratch, 100, collective)


def earlier_rows(own, before, steps):
    if steps == 0:
        return own
    moved = pltpu.roll(own, steps, 0)
    rim = before.shape[0]
    row = lax.broadcasted_iota(jnp.int32, (rim, own.shape[1]), 0)
    front = jnp.where(row < steps, pltpu.roll(before, steps, 0), moved[:rim])
    return jnp.concatenate([front, moved[rim:]], 0)


def forward_body(n, seqs, groups, span, group_rows, width, hidden_width, refs):
    at = HeadPlaces(n, seqs, groups)
    me, core = at.me, at.core
    channels = width // n
    half, heads = n // 2, group_rows // HEAD
    tokens = seqs * span
    links, loads = Links(refs), Loads(refs)
    peers = [lax.rem(me + step, n) for step in range(1, n)]
    after = (lax.rem(me + 1, n), core)
    barrier = pltpu.get_barrier_semaphore()
    at.signal_all(barrier, [(peer, core) for peer in peers])
    outgoing = []

    def save(source, target):
        outgoing.append(loads.start(source, target))

    load_tokens = loads.start(refs.tokens, refs.tokens_in)
    load_qkv = loads.start(refs.w_qkv.at[0], refs.qkv)
    load_out = loads.start(refs.w_out.at[0], refs.out)
    load_up = loads.start(refs.w_up.at[0], refs.up)
    load_down = loads.start(refs.w_down.at[0], refs.down)

    def normed(value, row, target):
        result = layer_norm(value, refs.gains[row : row + 1], refs.biases[row : row + 1])
        result = result.astype(jnp.bfloat16)
        target[...] = result.T
        return result

    valid = refs.valid[...]
    load_tokens.wait()
    flat_in = jnp.concatenate([refs.tokens_in[seq] for seq in range(seqs)], 0)
    flat_in = flat_in.astype(jnp.float32) * valid
    refs.flat_in[...] = flat_in
    normed_one = normed(flat_in, 0, refs.normed_one_t)
    load_qkv.wait()
    keys = dot(normed_one, refs.qkv[:, width : 2 * width]).astype(jnp.bfloat16)
    refs.keys[...] = keys
    rim = refs.rim_in.shape[1]
    at.wait_all(barrier, n - 1)
    for seq in range(seqs):
        refs.rim_out[seq] = refs.keys[(seq + 1) * span - rim : (seq + 1) * span, :]
    halo = links.copy(refs.rim_out, refs.rim_in, after)
    refs.values[...] = dot(normed_one, refs.qkv[:, 2 * width :])
    refs.queries[...] = dot(normed_one, refs.qkv[:, :width])
    load_qkv = loads.start(refs.w_qkv.at[1], refs.qkv)
    halo.wait_recv()
    there = jnp.where(me == 0, 0.0, 1.0)
    for seq in range(seqs):
        rows = slice(seq * span, (seq + 1) * span)
        before = refs.rim_in[seq].astype(jnp.float32) * there
        own = refs.keys[rows, :].astype(jnp.float32)
        shifted = jnp.zeros_like(own)
        for offset in range(TAPS):
            shifted = shifted + refs.taps[offset : offset + 1] * earlier_rows(own, before, offset)
        refs.shifted[rows, :] = shifted
        carried = (shifted * refs.values[rows, :] * valid[rows]).astype(jnp.bfloat16)
        refs.carried[rows, :] = carried
        refs.carried_t[seq] = carried.T

    going = []
    arrive, answered = links.slots(n - 1), links.slots(n - 1)
    for step, peer in enumerate(peers):
        rows = pl.ds(pl.multiple_of(peer * channels, 16), channels)
        going.append(
            links.copy(
                refs.carried_t.at[:, rows, :], refs.mixed_in.at[me], (peer, core), arrive + step
            )
        )
    own_rows = pl.ds(pl.multiple_of(me * channels, 16), channels)
    own_copy = loads.start(refs.carried_t.at[:, own_rows, :], refs.mixed_in.at[me])
    fill_tables(channels, span, refs)
    refs.square_t[...] = refs.values[...].T
    save(refs.square_t, refs.values_t)
    refs.square_two_t[...] = refs.shifted[...].T
    save(refs.square_two_t, refs.shifted_t)
    refs.keys_out[...] = refs.keys[...].T
    save(refs.keys_out, refs.keys_t)
    refs.queries_out[...] = refs.queries[...].T
    save(refs.queries_out, refs.queries_t)
    save(refs.normed_one_t, refs.normed_one)
    save(refs.carried_t, refs.carried_out)
    total_rows = n * seqs * channels
    own_copy.wait()
    for copy in going:
        copy.wait_recv()
    save(refs.mixed_in, refs.mixed_held)
    refs.flat_x[...] = refs.mixed_in[...].astype(jnp.float32).reshape(total_rows, span)

    def one_channel(channel, carry):
        mixer_forward_channel(n, seqs, span, channels, refs, channel)
        return carry

    lax.fori_loop(0, channels, one_channel, 0, unroll=4)
    refs.answer[...] = refs.flat_out[...].reshape(n, seqs, channels, span).astype(jnp.bfloat16)
    back = []
    for step, peer in enumerate(peers):
        back.append(
            links.copy(
                refs.answer.at[peer], refs.convolved.at[:, own_rows, :], (peer, core),
                answered + step,
            )
        )
    own_copy = loads.start(refs.answer.at[me], refs.convolved.at[:, own_rows, :])
    own_copy.wait()
    for copy in back:
        copy.wait_recv()
    for seq in range(seqs):
        rows = slice(seq * span, (seq + 1) * span)
        convolved = refs.convolved[seq].astype(jnp.float32).T
        mixer = convolved + refs.skip[...] * refs.carried[rows, :].astype(jnp.float32)
        refs.gated[rows, :] = (refs.queries[rows, :] * mixer).astype(jnp.bfloat16)
        refs.mixer_out[:, rows] = mixer.T
    save(refs.mixer_out, refs.mixer_t)
    refs.gated_out[...] = refs.gated[...].T
    save(refs.gated_out, refs.gated_t)
    load_out.wait()
    hidden = refs.flat_in[...] + dot(refs.gated[...], refs.out[...])
    load_out = loads.start(refs.w_out.at[1], refs.out)

    def feed_forward(hidden, row, hidden_out, normed_out, active_out, slope_out, up, down):
        hidden_out[...] = hidden.T
        refs.hidden[...] = hidden
        refs.normed[...] = normed(hidden, row, normed_out)
        up.wait()

        def one_chunk(index, carry):
            columns = pl.ds(pl.multiple_of(index * width, 128), width)
            active, slope = gelu_and_slope(dot(refs.normed[...], refs.up[:, columns]))
            active = active.astype(jnp.bfloat16)
            refs.active[:, columns] = active
            active_out[columns, :] = active.T
            slope_out[columns, :] = slope.astype(jnp.bfloat16).T
            return carry

        lax.fori_loop(0, hidden_width // width, one_chunk, 0)
        down.wait()
        return refs.hidden[...] + dot(refs.active[...], refs.down[...])

    hidden = feed_forward(
        hidden, 1, refs.hidden_one_t, refs.normed_two_t, refs.active_one_t, refs.slope_one_t,
        load_up, load_down,
    )
    load_up = loads.start(refs.w_up.at[1], refs.up)
    load_down = loads.start(refs.w_down.at[1], refs.down)
    refs.hidden[...] = hidden
    refs.normed[...] = normed(hidden, 2, refs.normed_three_t)
    load_qkv.wait()
    for part in range(3):
        columns = dot(refs.normed[...], refs.qkv[:, part * width : (part + 1) * width])
        columns = columns.astype(jnp.bfloat16)
        for seq in range(seqs):
            turned = columns[seq * span : (seq + 1) * span].T
            for head in range(groups * heads):
                refs.spread[head % heads, seq, head // heads, part * HEAD : (part + 1) * HEAD] = (
                    turned[head * HEAD : (head + 1) * HEAD]
                )

    count = len(at.targets)
    arrive, leave = links.slots(heads * half), links.slots(heads * count)
    passing = links.slots(heads * half)
    spread = []
    for head in range(heads):
        for number, (device, seq, group) in enumerate(at.targets):
            sent = (
                refs.spread.at[head, seq, group], refs.held.at[head, me],
                refs.send.at[leave + head * count + number],
                refs.recv.at[arrive + head * half + me // 2], device,
            )
            at.send(*sent)
            spread.append(sent)
    refs.hidden_two_t[...] = hidden.T
    for source, target in (
        (refs.hidden_one_t, refs.hidden_one_out), (refs.normed_two_t, refs.normed_two),
        (refs.active_one_t, refs.active_one), (refs.slope_one_t, refs.slope_one),
        (refs.hidden_two_t, refs.hidden_two_out), (refs.normed_three_t, refs.normed_three),
    ):
        save(source, target)

    returned, returning = links.slots(heads * count), links.slots(heads * half)
    slot = at.seq * groups + at.group
    going = []

    def gather(head):
        for index, block in enumerate(at.blocks):
            landed = refs.held.at[head, block]
            remote(
                landed, landed, refs.send.at[leave], refs.recv.at[arrive + head * half + index],
                at.sibling,
            ).wait_recv()
            part = refs.held.at[head, block, HEAD : 3 * HEAD]
            links.copy(part, part, at.sibling, passing + head * half + index)
        for index in range(half):
            part = refs.held.at[head, block_of(index, 1 - core), HEAD : 3 * HEAD]
            remote(
                part, part, refs.send.at[leave], refs.recv.at[passing + head * half + index],
                at.sibling,
            ).wait_recv()

    def attend(head):
        fill_head(refs.held, head, 1, n, span, refs.key_rows, None)
        fill_head(refs.held, head, 2, n, span, None, refs.value_columns)
        for index, block in enumerate(at.blocks):
            query = refs.held[head, block, :HEAD, :] * jnp.bfloat16(HEAD**-0.5)
            clear, reach = 2 * index * span, 2 * (index + 1) * span
            edge = dot(refs.key_rows[clear:reach, :], query)
            edge = jnp.where(causal(clear, reach - clear, block * span, span), edge, masked_score)
            top = jnp.max(edge, 0, keepdims=True)
            if index > 0:
                body = dot(refs.key_rows[:clear, :], query)
                top = jnp.maximum(top, jnp.max(body, 0, keepdims=True))
            edge = jnp.exp(edge - top)
            total = jnp.sum(edge, 0, keepdims=True)
            result = dot(refs.value_columns[:, clear:reach], edge.astype(jnp.bfloat16))
            if index > 0:
                body = jnp.exp(body - top)
                total = total + jnp.sum(body, 0, keepdims=True)
                result = result + dot(refs.value_columns[:, :clear], body.astype(jnp.bfloat16))
            refs.outputs[head, index] = (result / total).astype(jnp.bfloat16)
            refs.lse[index, head : head + 1, :] = top + jnp.log(total)
        into = refs.attended_t.at[
            pl.ds(pl.multiple_of(at.group * group_rows + head * HEAD, HEAD), HEAD),
            pl.ds(pl.multiple_of(at.seq * span, span), span),
        ]
        for index, device in enumerate(at.sources):
            sent = (
                refs.outputs.at[head, index], into, refs.send.at[returning + head * half + index],
                refs.recv.at[returned + head * count + slot], device,
            )
            at.send(*sent)
            going.append(sent)

    for head in range(heads):
        gather(head)
        attend(head)
    save(refs.held, refs.held_out)
    for head in range(heads):
        for number, (device, seq, group) in enumerate(at.targets):
            first = group * group_rows + head * HEAD
            landed = refs.attended_t.at[first : first + HEAD, seq * span : (seq + 1) * span]
            remote(
                landed, landed, refs.send.at[leave],
                refs.recv.at[returned + head * count + number], at.sibling,
            ).wait_recv()
    save(refs.attended_t, refs.attended)
    load_out.wait()
    hidden = refs.hidden[...] + dot(refs.attended_t[...].T, refs.out[...])
    hidden = feed_forward(
        hidden, 3, refs.hidden_three_t, refs.normed_four_t, refs.active_two_t, refs.slope_two_t,
        load_up, load_down,
    )
    for source, target in (
        (refs.hidden_three_t, refs.hidden_three_out), (refs.normed_four_t, refs.normed_four),
        (refs.active_two_t, refs.active_two), (refs.slope_two_t, refs.slope_two),
    ):
        save(source, target)
    hidden = (hidden * valid).astype(jnp.bfloat16)
    for seq in range(seqs):
        refs.mixed[seq] = hidden[seq * span : (seq + 1) * span]
    for copy in outgoing:
        copy.wait()
    for sent in spread + going:
        at.wait_sent(*sent)
    links.finish()


def forward(
    tokens, valid, gains, biases, taps, skip, rates, rate_weights, w_qkv, w_out, w_up, w_down, n,
    groups, collective,
):
    seqs, span, width = tokens.shape
    hidden_width = w_up.shape[2]
    group_rows, channels = width // groups, width // n
    rows = seqs * span
    half, heads = n // 2, group_rows // HEAD
    low, wide = jnp.bfloat16, jnp.float32
    inputs = dict(
        tokens=(tokens, HBM), valid=(valid, VMEM), gains=(gains, VMEM), biases=(biases, VMEM),
        taps=(taps, VMEM), skip=(skip, VMEM), rates=(rates, VMEM), rate_weights=(rate_weights, VMEM),
        w_qkv=(w_qkv, HBM), w_out=(w_out, HBM), w_up=(w_up, HBM), w_down=(w_down, HBM),
    )
    square, tall, by_head = (width, rows), (hidden_width, rows), (heads, n, 3 * HEAD, span)
    mixed = (n, seqs, channels, span)
    outputs = dict(
        mixed=((seqs, span, width), low, VMEM),
        lse=((half, heads, span), wide, VMEM),
        held_out=(by_head, low, HBM), mixed_held=(mixed, low, HBM),
        carried_out=((seqs, width, span), low, HBM),
        values_t=(square, wide, HBM), shifted_t=(square, wide, HBM), keys_t=(square, low, HBM),
        queries_t=(square, wide, HBM), mixer_t=(square, wide, HBM), gated_t=(square, low, HBM),
        attended=(square, low, HBM),
        normed_one=(square, low, HBM), normed_two=(square, low, HBM),
        normed_three=(square, low, HBM), normed_four=(square, low, HBM),
        hidden_one_out=(square, wide, HBM), hidden_two_out=(square, wide, HBM),
        hidden_three_out=(square, wide, HBM),
        active_one=(tall, low, HBM), active_two=(tall, low, HBM),
        slope_one=(tall, low, HBM), slope_two=(tall, low, HBM),
    )
    flat = (n * seqs * channels, span)
    lying = (rows, width)
    scratch = dict(
        qkv=(w_qkv.shape[1:], low), out=(w_out.shape[1:], low), up=(w_up.shape[1:], low),
        down=(w_down.shape[1:], low), tokens_in=(tokens.shape, low), flat_in=(lying, wide),
        keys=(lying, low), values=(lying, wide), queries=(lying, wide), shifted=(lying, wide),
        carried=(lying, low), gated=(lying, low), hidden=(lying, wide), normed=(lying, low),
        active=((rows, hidden_width), low), rim_in=((seqs, 16, width), low),
        rim_out=((seqs, 16, width), low), carried_t=((seqs, width, span), low),
        convolved=((seqs, width, span), low), mixed_in=(mixed, low), answer=(mixed, low),
        flat_x=(flat, wide), flat_out=(flat, wide), **table_scratch(channels, span),
        square_t=(square, wide), square_two_t=(square, wide), keys_out=(square, low),
        queries_out=(square, wide), mixer_out=(square, wide), gated_out=(square, low),
        attended_t=(square, low), normed_one_t=(square, low), normed_two_t=(square, low),
        normed_three_t=(square, low), normed_four_t=(square, low), hidden_one_t=(square, wide),
        hidden_two_t=(square, wide), hidden_three_t=(square, wide), active_one_t=(tall, low),
        active_two_t=(tall, low), slope_one_t=(tall, low), slope_two_t=(tall, low),
        spread=((heads, seqs, groups, 3 * HEAD, span), low), held=(by_head, low),
        outputs=((heads, half, HEAD, span), low), key_rows=((n * span, HEAD), low),
        value_columns=((HEAD, n * span), low),
    )
    body = functools.partial(
        forward_body, n, seqs, groups, span, group_rows, width, hidden_width
    )
    return launch(body, inputs, outputs, scratch, 200, collective)


def per_device_by_heads(
    tokens,
    cotangent,
    lengths,
    norm_gain,
    norm_bias,
    w_qkv,
    w_out,
    w_up,
    w_down,
    taps,
    skip,
    ssm_rate,
    ssm_out,
):
    seq_count, span_rows, width = tokens.shape[1:]
    devices = lax.axis_size(SEQ)
    place = lax.axis_index(SEQ)
    channels = width // devices
    groups = devices // 4
    row_count = seq_count * span_rows
    positions = place * span_rows + jnp.arange(span_rows, dtype=jnp.int32)
    validity = (positions[None, :] < lengths[0][:, None]).astype(jnp.float32)
    valid = validity.reshape(1, row_count)
    rates = lax.dynamic_slice_in_dim(ssm_rate, place * channels, channels, 0)
    weights = lax.dynamic_slice_in_dim(ssm_out, place * channels, channels, 0)
    rates = jnp.concatenate([rates, rates], 1)
    weights = jnp.concatenate([weights, weights], 1)
    gains = norm_gain.T
    kept = forward(
        tokens[0], validity.reshape(row_count, 1), norm_gain, norm_bias, taps, skip[None], rates,
        weights, w_qkv, w_out, w_up, w_down, devices, groups, 1,
    )

    def sliced(value):
        return value.reshape(devices, value.shape[0] // devices, row_count)

    back = back_one(
        cotangent[0], valid, kept.hidden_three_out, kept.slope_two, sliced(kept.normed_four),
        sliced(kept.active_two), sliced(kept.attended), kept.held_out, kept.lse, gains[:, 3:4],
        w_out, w_up, w_down, 3,
    )
    more = back_two(
        back.mid_out, back.d_qkv.reshape(3 * width, row_count), back.grad_out, kept.hidden_two_out,
        sliced(kept.normed_three), kept.slope_one, sliced(kept.normed_two),
        sliced(kept.active_one), kept.hidden_one_out, sliced(kept.gated_t), kept.queries_t,
        kept.mixer_t, kept.carried_out, kept.mixed_held, gains, rates, weights, w_qkv, w_out, w_up,
        w_down, 4,
    )
    none = jnp.zeros((width, 1), jnp.float32)
    small = jnp.concatenate(
        [
            none, more.small[:, 2:3], more.small[:, 0:1], back.small[:, 0:1],
            none, more.small[:, 3:4], more.small[:, 1:2], back.small[:, 1:2],
            none, none, none, none, more.small[:, 4:5],
            jnp.zeros((width, 128 - 13), jnp.float32),
        ],
        1,
    )
    end = back_three(
        more.from_conv, more.d_mixer, more.d_queries, kept.values_t, kept.shifted_t, kept.keys_t,
        more.grad_out, tokens[0], sliced(kept.normed_one), valid, gains[:, 0:1], skip[:, None],
        taps.T, small, w_qkv, more.mid_out, more.qkv_grad, more.down_grad, more.up_grad,
        more.out_grad, 5,
    )
    small = end.small_sum
    return (
        kept.mixed[None],
        end.d_tokens[None],
        small[:4],
        small[4:7],
        small[7],
        end.qkv_all,
        end.out_all,
        end.up_all,
        end.down_all,
        small[8 : 8 + TAPS],
        small[8 + TAPS],
        more.rate_sum[:, :STATES],
        more.weight_sum[:, :STATES],
    )


def fits_by_heads(mesh):
    devices = mesh.shape[SEQ]
    return devices == 16 and mesh.shape[BATCH] == 2


def solution(mesh):
    placed = (
        P(BATCH, None, SEQ, None),
        P(BATCH, None, SEQ, None),
        P(BATCH, None),
        P(),
        P(),
        P(),
        P(),
        P(),
        P(),
        P(),
        P(),
        P(),
        P(),
    )
    return jax.shard_map(
        per_device_by_heads if fits_by_heads(mesh) else per_device,
        mesh=mesh,
        in_specs=placed,
        out_specs=(
            P(BATCH, None, SEQ, None),
            P(BATCH, None, SEQ, None),
            P(None, SEQ),
            P(None, SEQ),
            P(SEQ),
            P(None, SEQ, None),
            P(None, SEQ, None),
            P(None, SEQ, None),
            P(None, SEQ, None),
            P(None, SEQ),
            P(SEQ),
            P(SEQ, None),
            P(SEQ, None),
        ),
        check_vma=False,
    )
```

```python
import functools
import math
import types

import jax
import jax.numpy as jnp
from jax import lax
from jax.experimental import pallas as pl
from jax.experimental.pallas import tpu as pltpu
from jax.sharding import PartitionSpec as P

HEADS = 12
HEAD = 64
TAPS = 4
STATES = 64
KEPT = "_kept"
MESH = pl.DeviceIdType.MESH
SEQ = "seq"
BATCH = "batch"
QKV_MORE = "qkv_more"
QKV_LESS = "qkv_less"
DOWN = "down"
OUT = "out"
UP = "up"
QKV = "qkv"
SMALL = "small"
VMEM_BYTES = 63 * 2**20


norm_eps = 1e-05
highest = lax.Precision.HIGHEST
masked_score = -1e30


def for_sending(array):
    return jax.tree.map(lambda a: a.astype(jnp.bfloat16) if a.dtype == jnp.float32 else a, array)


def passed_along(value, axis, steps):
    count = lax.axis_size(axis)
    initial, last = (max(0, -steps), min(count, count - steps))
    return lax.ppermute(value, axis, [(source, source + steps) for source in range(initial, last)])


def layer_norm(inputs, scale_row, shift_row):
    center = inputs - jnp.mean(inputs, -1, keepdims=True)
    spread = jnp.mean(center * center, -1, keepdims=True)
    return center * lax.rsqrt(spread + norm_eps) * scale_row + shift_row


def dense_product(operand_a, operand_b):
    return jnp.dot(operand_a, operand_b, preferred_element_type=jnp.float32)


def product_left(operand_a, operand_b):
    return lax.dot_general(
        operand_a, operand_b, (((0,), (0,)), ((), ())), preferred_element_type=jnp.float32
    )


def product_right(operand_a, operand_b):
    return lax.dot_general(
        operand_a, operand_b, (((1,), (1,)), ((), ())), preferred_element_type=jnp.float32
    )


def angle_table(count_rows, count_cols, period):
    product_index = (
        jnp.arange(count_rows, dtype=jnp.int32)[:, None]
        * jnp.arange(count_cols, dtype=jnp.int32)[None, :]
        % period
    )
    angles = product_index.astype(jnp.float32) * (2.0 * math.pi / period)
    return (jnp.cos(angles), jnp.sin(angles))


def table_einsum(form, table, data):
    return jnp.einsum(form, table, data, precision=highest)


def forward_spectrum(time_parts):
    count_parts = time_parts.shape[0]
    span_rows = time_parts.shape[2]
    count_freq = 2 * count_parts
    cos_parts, sin_parts = angle_table(count_freq, count_parts, count_freq)
    first_real = table_einsum("fp,pjsc->fjsc", cos_parts, time_parts)
    first_imag = -table_einsum("fp,pjsc->fjsc", sin_parts, time_parts)
    cos_twist, sin_twist = angle_table(count_freq, span_rows, count_freq * span_rows)
    cos_twist = cos_twist[:, None, :, None]
    sin_twist = sin_twist[:, None, :, None]
    twist_real = first_real * cos_twist + first_imag * sin_twist
    twist_imag = first_imag * cos_twist - first_real * sin_twist
    cos_span, sin_span = angle_table(span_rows, span_rows, span_rows)
    out_real = table_einsum("ts,fjsc->fjtc", cos_span, twist_real) + table_einsum(
        "ts,fjsc->fjtc", sin_span, twist_imag
    )
    out_imag = table_einsum("ts,fjsc->fjtc", cos_span, twist_imag) - table_einsum(
        "ts,fjsc->fjtc", sin_span, twist_real
    )
    return (out_real, out_imag)


def inverse_spectrum(freq_real, freq_imag):
    count_freq = freq_real.shape[0]
    span_rows = freq_real.shape[2]
    count_parts = count_freq // 2
    fft_length = count_freq * span_rows
    cos_span, sin_span = angle_table(span_rows, span_rows, span_rows)
    first_real = table_einsum("st,fjtc->fjsc", cos_span, freq_real) - table_einsum(
        "st,fjtc->fjsc", sin_span, freq_imag
    )
    first_imag = table_einsum("st,fjtc->fjsc", cos_span, freq_imag) + table_einsum(
        "st,fjtc->fjsc", sin_span, freq_real
    )
    cos_twist, sin_twist = angle_table(count_freq, span_rows, fft_length)
    cos_twist = cos_twist[:, None, :, None]
    sin_twist = sin_twist[:, None, :, None]
    twist_real = first_real * cos_twist - first_imag * sin_twist
    twist_imag = first_imag * cos_twist + first_real * sin_twist
    cos_parts, sin_parts = angle_table(count_parts, count_freq, count_freq)
    summed = table_einsum("pf,fjsc->pjsc", cos_parts, twist_real) - table_einsum(
        "pf,fjsc->pjsc", sin_parts, twist_imag
    )
    return summed / fft_length


def to_frequency(data_low):
    parts = lax.all_to_all(data_low[None], SEQ, split_axis=3, concat_axis=0, tiled=True)
    return forward_spectrum(parts.astype(jnp.float32))


def from_frequency(freq_real, freq_imag):
    time_parts = inverse_spectrum(freq_real, freq_imag)
    joined = lax.all_to_all(
        for_sending(time_parts), SEQ, split_axis=0, concat_axis=3, tiled=True
    ).astype(time_parts.dtype)
    return joined[0]


def kernel_parts(rate_slice, weight_slice, count_freq, span_rows):
    fft_length = count_freq * span_rows
    length_full = fft_length // 2
    frequency = (
        jnp.arange(count_freq, dtype=jnp.int32)[:, None]
        + count_freq * jnp.arange(span_rows, dtype=jnp.int32)[None, :]
    )
    angles = (frequency.astype(jnp.float32) * (2.0 * math.pi / fft_length))[:, None, :, None, None]
    odd_mask = (frequency % 2 == 1)[:, None, :, None, None]
    channels = rate_slice.shape[0]
    blocks = rate_slice.shape[1] // 8
    rate_blocks = rate_slice.reshape(channels, blocks, 8).transpose(1, 0, 2)
    weight_blocks = weight_slice.reshape(channels, blocks, 8).transpose(1, 0, 2)

    def add_block(running, piece_pair):
        rate_part, weight_part = piece_pair
        decays = jnp.exp(-rate_part)
        half_sine = jnp.sin(angles / 2.0)
        real_den = -jnp.expm1(-rate_part) + decays * 2.0 * half_sine * half_sine
        imag_den = decays * jnp.sin(angles)
        numerator = jnp.where(
            odd_mask, 1.0 + jnp.exp(-rate_part * length_full), -jnp.expm1(-rate_part * length_full)
        )
        factor = weight_part * numerator / (real_den * real_den + imag_den * imag_den)
        return (
            (
                running[0] + jnp.sum(factor * real_den, -1),
                running[1] - jnp.sum(factor * imag_den, -1),
            ),
            None,
        )

    zeros_init = jnp.zeros((count_freq, 1, span_rows, channels), jnp.float32)
    return lax.scan(
        jax.checkpoint(add_block), (zeros_init, zeros_init), (rate_blocks, weight_blocks)
    )[0]


def attention_mask(query_positions, key_count, length_value):
    key_positions = jnp.arange(key_count, dtype=jnp.int32)
    return (key_positions[None, :] <= query_positions[:, None]) & (
        key_positions[None, :] < length_value
    )


def head_slice(matrix, head_index):
    return lax.dynamic_slice_in_dim(matrix, head_index * HEAD, HEAD, 1)


def attend_forward(query_low, keys_low, values_low, length_value, query_positions):
    whole_keys, whole_values = (
        lax.all_gather(keys_low, SEQ, axis=0, tiled=True),
        lax.all_gather(values_low, SEQ, axis=0, tiled=True),
    )
    allowed = attention_mask(query_positions, whole_keys.shape[0], length_value)
    score_scale = HEAD ** (-0.5)

    def head_forward(head_index):
        scores = jnp.where(
            allowed,
            score_scale
            * product_right(head_slice(query_low, head_index), head_slice(whole_keys, head_index)),
            masked_score,
        )
        top_score = jnp.max(scores, -1, keepdims=True)
        expos = jnp.exp(scores - top_score)
        totals = jnp.sum(expos, -1, keepdims=True)
        probs_low = (expos / totals).astype(jnp.bfloat16)
        return (
            dense_product(probs_low, head_slice(whole_values, head_index)),
            (top_score + jnp.log(totals))[:, 0],
        )

    head_outputs, log_totals = lax.map(head_forward, jnp.arange(HEADS, dtype=jnp.int32))
    attended = head_outputs.transpose(1, 0, 2).reshape(query_low.shape[0], HEADS * HEAD)
    return (attended, log_totals, whole_keys, whole_values)


def join_heads(head_rows):
    return head_rows.transpose(1, 0, 2).reshape(head_rows.shape[1], HEADS * HEAD)


def attend_backward(
    query_low, whole_keys, whole_values, log_totals, grad_low, length_value, query_positions
):
    allowed = attention_mask(query_positions, whole_keys.shape[0], length_value)
    score_scale = HEAD ** (-0.5)
    span_rows = query_low.shape[0]

    def query_side(head_index):
        head_query = head_slice(query_low, head_index)
        head_keys = head_slice(whole_keys, head_index)
        head_grad = head_slice(grad_low, head_index)
        scores = jnp.where(
            allowed, score_scale * product_right(head_query, head_keys), masked_score
        )
        weights = jnp.exp(scores - log_totals[head_index][:, None])
        d_weights = product_right(head_grad, head_slice(whole_values, head_index))
        row_term = jnp.sum(weights * d_weights, -1, keepdims=True)
        d_scores = (weights * (d_weights - row_term)).astype(jnp.bfloat16)
        d_query = score_scale * dense_product(d_scores, head_keys)
        return (d_query, row_term[:, 0], d_scores, weights)

    def head_backward(head_index):
        d_query, row_term, d_scores, weights = query_side(head_index)
        head_query = head_slice(query_low, head_index)
        head_grad = head_slice(grad_low, head_index)
        d_keys = score_scale * product_left(d_scores, head_query)
        d_values = product_left(weights.astype(jnp.bfloat16), head_grad)
        return (d_query, d_keys, d_values)

    query_grads, key_grads, value_grads = lax.map(head_backward, jnp.arange(HEADS, dtype=jnp.int32))
    count_rows = span_rows * lax.axis_size(SEQ)
    key_part = (
        lax.slice_in_dim(key_grads, 0, count_rows, axis=1)
        .transpose(1, 0, 2)
        .reshape(count_rows, HEADS * HEAD)
    )
    value_part = (
        lax.slice_in_dim(value_grads, 0, count_rows, axis=1)
        .transpose(1, 0, 2)
        .reshape(count_rows, HEADS * HEAD)
    )
    key_value = lax.psum_scatter(
        jnp.stack([key_part, value_part], 1), SEQ, scatter_dimension=0, tiled=True
    )
    return (join_heads(query_grads), key_value[:, 0], key_value[:, 1])


def per_device(
    tokens,
    cotangent,
    lengths,
    norm_gain,
    norm_bias,
    w_qkv,
    w_out,
    w_up,
    w_down,
    taps,
    skip,
    ssm_rate,
    ssm_out,
):
    seq_count = tokens.shape[1]
    span_rows = tokens.shape[2]
    width = tokens.shape[3]
    devices = lax.axis_size(SEQ)
    place = lax.axis_index(SEQ)
    channels = width // devices
    count_freq = 2 * devices
    fft_length = count_freq * span_rows
    rim = TAPS - 1
    row_count = seq_count * span_rows
    query_positions = place * span_rows + jnp.arange(span_rows, dtype=jnp.int32)
    validity = (query_positions[None, :] < lengths[0][:, None]).astype(jnp.float32)[:, :, None]
    rate_slice = lax.dynamic_slice_in_dim(ssm_rate, place * channels, channels, 0)
    weight_slice = lax.dynamic_slice_in_dim(ssm_out, place * channels, channels, 0)

    def spectrum_of(rate_in, weight_in):
        return kernel_parts(rate_in, weight_in, count_freq, span_rows)

    def feed_forward(inputs, norm_row, layer):
        normed_low = layer_norm(inputs, norm_gain[norm_row], norm_bias[norm_row]).astype(
            jnp.bfloat16
        )
        raised = dense_product(normed_low, w_up[layer])
        active_low = jax.nn.gelu(raised).astype(jnp.bfloat16)
        return (normed_low, raised, active_low, inputs + dense_product(active_low, w_down[layer]))

    def norm_backward(inputs, norm_row, d_normed):
        norm_pull = jax.vjp(layer_norm, inputs, norm_gain[norm_row], norm_bias[norm_row])[1]
        return norm_pull(d_normed)

    def feed_backward(grad_rows, inputs, normed_low, raised, active_low, norm_row, layer):
        branch_low = grad_rows.astype(jnp.bfloat16)
        down_grad = product_left(active_low, branch_low)
        d_active = product_right(branch_low, w_down[layer])
        gelu_pull = jax.vjp(jax.nn.gelu, raised)[1]
        d_raised = gelu_pull(d_active)[0].astype(jnp.bfloat16)
        up_grad = product_left(normed_low, d_raised)
        d_inputs, gain_part, bias_part = norm_backward(
            inputs, norm_row, product_right(d_raised, w_up[layer])
        )
        return (grad_rows + d_inputs, down_grad, up_grad, gain_part, bias_part)

    def forward_pass(token_block):
        masked_in = token_block[0].astype(jnp.float32) * validity
        flat_in = masked_in.reshape(row_count, width)
        normed_one = layer_norm(flat_in, norm_gain[0], norm_bias[0]).astype(jnp.bfloat16)
        qkv_one = dense_product(normed_one, w_qkv[0]).reshape(seq_count, span_rows, 3 * width)
        queries_one = qkv_one[:, :, :width]
        keys_one = qkv_one[:, :, width : 2 * width].astype(jnp.bfloat16)
        values_one = qkv_one[:, :, 2 * width :]
        earlier = passed_along(keys_one[:, span_rows - rim :], SEQ, 1)
        extended = jnp.concatenate([earlier, keys_one], 1)
        shifted = sum(
            (
                taps[offset]
                * extended[:, rim - offset : rim - offset + span_rows].astype(jnp.float32)
                for offset in range(TAPS)
            )
        )
        carried_low = (shifted * values_one * validity).astype(jnp.bfloat16)
        carried_real, carried_imag = to_frequency(carried_low)
        kernel_both, kernel_pull = jax.vjp(spectrum_of, rate_slice, weight_slice)
        kernel_real, kernel_imag = kernel_both
        convolved = from_frequency(
            carried_real * kernel_real - carried_imag * kernel_imag,
            carried_real * kernel_imag + carried_imag * kernel_real,
        )
        carried = carried_low.astype(jnp.float32)
        mixer = convolved + skip * carried
        gated_low = (queries_one * mixer).reshape(row_count, width).astype(jnp.bfloat16)
        hidden_one = flat_in + dense_product(gated_low, w_out[0])
        normed_two, raised_one, active_one, hidden_two = feed_forward(hidden_one, 1, 0)
        normed_three = layer_norm(hidden_two, norm_gain[2], norm_bias[2]).astype(jnp.bfloat16)
        qkv_two = (
            dense_product(normed_three, w_qkv[1])
            .astype(jnp.bfloat16)
            .reshape(seq_count, span_rows, 3 * width)
        )
        attended_list = []
        totals_list = []
        keys_list = []
        values_list = []
        for seq_index in range(seq_count):
            attended, log_totals, whole_keys, whole_values = attend_forward(
                qkv_two[seq_index, :, :width],
                qkv_two[seq_index, :, width : 2 * width],
                qkv_two[seq_index, :, 2 * width :],
                lengths[0, seq_index],
                query_positions,
            )
            attended_list.append(attended)
            totals_list.append(log_totals)
            keys_list.append(whole_keys)
            values_list.append(whole_values)
        attended_low = jnp.concatenate(attended_list, 0).astype(jnp.bfloat16)
        hidden_three = hidden_two + dense_product(attended_low, w_out[1])
        normed_four, raised_two, active_two, hidden_four = feed_forward(hidden_three, 3, 1)
        output = hidden_four.reshape(seq_count, span_rows, width) * validity
        saved = types.SimpleNamespace(
            flat_in=flat_in,
            normed_one=normed_one,
            queries_one=queries_one,
            values_one=values_one,
            extended=extended,
            shifted=shifted,
            carried=carried,
            carried_real=carried_real,
            carried_imag=carried_imag,
            kernel_real=kernel_real,
            kernel_imag=kernel_imag,
            kernel_pull=kernel_pull,
            mixer=mixer,
            gated_low=gated_low,
            hidden_one=hidden_one,
            normed_two=normed_two,
            raised_one=raised_one,
            active_one=active_one,
            hidden_two=hidden_two,
            normed_three=normed_three,
            qkv_two=qkv_two,
            totals_list=totals_list,
            keys_list=keys_list,
            values_list=values_list,
            attended_low=attended_low,
            hidden_three=hidden_three,
            normed_four=normed_four,
            raised_two=raised_two,
            active_two=active_two,
        )
        return (output, saved)

    output = forward_pass(tokens)[0]
    saved = forward_pass(lax.optimization_barrier(tokens))[1]
    grad_rows = (cotangent[0].astype(jnp.float32) * validity).reshape(row_count, width)
    grad_rows, down_two, up_two, gain_four, bias_four = feed_backward(
        grad_rows,
        saved.hidden_three,
        saved.normed_four,
        saved.raised_two,
        saved.active_two,
        3,
        1,
    )
    branch_low = grad_rows.astype(jnp.bfloat16)
    out_two = product_left(saved.attended_low, branch_low)
    d_attended = (
        product_right(branch_low, w_out[1])
        .astype(jnp.bfloat16)
        .reshape(seq_count, span_rows, width)
    )
    qkv_two = saved.qkv_two
    grad_parts = []
    for seq_index in range(seq_count):
        d_query_rows, d_key_rows, d_value_rows = attend_backward(
            qkv_two[seq_index, :, :width],
            saved.keys_list[seq_index],
            saved.values_list[seq_index],
            saved.totals_list[seq_index],
            d_attended[seq_index],
            lengths[0, seq_index],
            query_positions,
        )
        grad_parts.append(jnp.concatenate([d_query_rows, d_key_rows, d_value_rows], -1))
    d_qkv_two = jnp.concatenate(grad_parts, 0).astype(jnp.bfloat16)
    qkv_grad_two = product_left(saved.normed_three, d_qkv_two)
    d_inputs, gain_three, bias_three = norm_backward(
        saved.hidden_two, 2, product_right(d_qkv_two, w_qkv[1])
    )
    grad_rows = grad_rows + d_inputs
    grad_rows, down_one, up_one, gain_two, bias_two = feed_backward(
        grad_rows,
        saved.hidden_one,
        saved.normed_two,
        saved.raised_one,
        saved.active_one,
        1,
        0,
    )
    branch_low = grad_rows.astype(jnp.bfloat16)
    out_one = product_left(saved.gated_low, branch_low)
    d_gated = product_right(branch_low, w_out[0]).reshape(seq_count, span_rows, width)
    d_queries = d_gated * saved.mixer
    d_mixer = d_gated * saved.queries_one
    skip_grad = jnp.sum(d_mixer * saved.carried, (0, 1))
    conv_real, conv_imag = to_frequency(d_mixer.astype(jnp.bfloat16))
    kernel_real = saved.kernel_real
    kernel_imag = saved.kernel_imag
    from_conv = from_frequency(
        kernel_real * conv_real + kernel_imag * conv_imag,
        kernel_real * conv_imag - kernel_imag * conv_real,
    )
    d_carried = d_mixer * skip + from_conv
    carried_real = saved.carried_real
    carried_imag = saved.carried_imag
    cot_real = (
        jnp.sum(carried_real * conv_real + carried_imag * conv_imag, 1, keepdims=True) / fft_length
    )
    cot_imag = (
        jnp.sum(carried_real * conv_imag - carried_imag * conv_real, 1, keepdims=True) / fft_length
    )
    rate_grad, weight_grad = saved.kernel_pull((cot_real, cot_imag))
    d_shifted = d_carried * saved.values_one * validity
    d_values = d_carried * saved.shifted * validity
    extended = saved.extended
    grads_extended = sum(
        (
            jnp.pad(taps[offset] * d_shifted, ((0, 0), (rim - offset, offset), (0, 0)))
            for offset in range(TAPS)
        )
    )
    taps_grad = jnp.stack(
        [
            jnp.sum(
                d_shifted
                * extended[:, rim - offset : rim - offset + span_rows].astype(jnp.float32),
                (0, 1),
            )
            for offset in range(TAPS)
        ]
    )
    later = passed_along(grads_extended[:, :rim], SEQ, -1)
    d_keys = grads_extended[:, rim:] + jnp.pad(later, ((0, 0), (span_rows - rim, 0), (0, 0)))
    d_qkv_one = (
        jnp.concatenate([d_queries, d_keys, d_values], -1)
        .reshape(row_count, 3 * width)
        .astype(jnp.bfloat16)
    )
    qkv_grad_one = product_left(saved.normed_one, d_qkv_one)
    d_inputs, gain_one, bias_one = norm_backward(
        saved.flat_in, 0, product_right(d_qkv_one, w_qkv[0])
    )
    d_tokens = ((grad_rows + d_inputs).reshape(seq_count, span_rows, width) * validity)[None]
    gain_sum, bias_sum, qkv_sum, out_sum, up_sum, down_sum, taps_sum, skip_sum = (
        lax.psum_scatter(
            jnp.stack([gain_one, gain_two, gain_three, gain_four]),
            SEQ,
            scatter_dimension=1,
            tiled=True,
        ),
        lax.psum_scatter(
            jnp.stack([bias_one, bias_two, bias_three, bias_four]),
            SEQ,
            scatter_dimension=1,
            tiled=True,
        ),
        lax.psum_scatter(
            jnp.stack([qkv_grad_one, qkv_grad_two]), SEQ, scatter_dimension=1, tiled=True
        ),
        lax.psum_scatter(jnp.stack([out_one, out_two]), SEQ, scatter_dimension=1, tiled=True),
        lax.psum_scatter(jnp.stack([up_one, up_two]), SEQ, scatter_dimension=1, tiled=True),
        lax.psum_scatter(jnp.stack([down_one, down_two]), SEQ, scatter_dimension=1, tiled=True),
        lax.psum_scatter(taps_grad, SEQ, scatter_dimension=1, tiled=True),
        lax.psum_scatter(skip_grad[None], SEQ, scatter_dimension=1, tiled=True),
    )
    totals = (
        lax.psum(gain_sum.astype(jnp.bfloat16), BATCH).astype(jnp.float32),
        lax.psum(bias_sum.astype(jnp.bfloat16), BATCH).astype(jnp.float32),
        lax.psum(qkv_sum.astype(jnp.bfloat16), BATCH).astype(jnp.float32),
        lax.psum(out_sum.astype(jnp.bfloat16), BATCH).astype(jnp.float32),
        lax.psum(up_sum.astype(jnp.bfloat16), BATCH).astype(jnp.float32),
        lax.psum(down_sum.astype(jnp.bfloat16), BATCH).astype(jnp.float32),
        lax.psum(taps_sum.astype(jnp.bfloat16), BATCH).astype(jnp.float32),
        lax.psum(skip_sum.astype(jnp.bfloat16), BATCH).astype(jnp.float32),
        lax.psum(rate_grad.astype(jnp.bfloat16), BATCH).astype(jnp.float32),
        lax.psum(weight_grad.astype(jnp.bfloat16), BATCH).astype(jnp.float32),
    )
    return (
        output[None].astype(jnp.bfloat16),
        d_tokens,
        totals[0],
        totals[1][:3],
        totals[1][3],
        totals[2],
        totals[3],
        totals[4],
        totals[5],
        totals[6],
        totals[7][0],
        totals[8],
        totals[9],
    )


def other_device(place, core, to_place, to_core):
    return jnp.logical_or(place != to_place, core != to_core)


def greet(devices):
    barrier = pltpu.get_barrier_semaphore()
    for device in devices:
        pl.semaphore_signal(barrier, inc=1, device_id=device, device_id_type=MESH)
    pl.semaphore_wait(barrier, len(devices))


def remote(source, target, send_sem, recv_sem, device):
    return pltpu.make_async_remote_copy(
        src_ref=source,
        dst_ref=target,
        send_sem=send_sem,
        recv_sem=recv_sem,
        device_id=device,
        device_id_type=MESH,
    )


def split_low(value):
    upper = value.astype(jnp.bfloat16)
    return upper, (value - upper.astype(jnp.float32)).astype(jnp.bfloat16)


NN = (((1,), (0,)), ((), ()))
NT = (((1,), (1,)), ((), ()))
TN = (((0,), (0,)), ((), ()))


def dot(left, right, form=NN):
    return lax.dot_general(left, right, form, preferred_element_type=jnp.float32)


def dot_fine(left, right, form=NN):
    left_up, left_low = left
    right_up, right_low = right
    total = dot(left_up, right_up, form) + dot(left_up, right_low, form)
    if left_low is not None:
        total = total + dot(left_low, right_up, form)
    return total


def state_steps(span):
    row = lax.broadcasted_iota(jnp.int32, (span, 2 * STATES), 0)
    lane = lax.broadcasted_iota(jnp.int32, (span, 2 * STATES), 1)
    return jnp.where(lane < STATES, span - 1 - row, row + 1).astype(jnp.float32)


def state_tables(rate_row, weight_row, span):
    steps = state_steps(span)
    table = jnp.exp(-rate_row * steps)
    lane_row = lax.broadcasted_iota(jnp.int32, (8, 2 * STATES), 1)
    lead = jnp.where(lane_row < STATES, 0.0, weight_row * jnp.exp(rate_row))
    response = lax.dot_general(
        lead, table, NT, precision=highest, preferred_element_type=jnp.float32
    )[:1]
    spread = pltpu.roll(
        jnp.broadcast_to(response, (span, span)), 0, 1, stride=1, stride_axis=0
    )
    later = lax.broadcasted_iota(jnp.int32, (span, span), 1)
    earlier = lax.broadcasted_iota(jnp.int32, (span, span), 0)
    toeplitz = jnp.where(later >= earlier, spread, 0.0)
    return table, toeplitz


def shift_rows(value, count):
    if count > 0:
        return jnp.concatenate([jnp.zeros_like(value[:count]), value[:-count]], 0)
    return jnp.concatenate([value[-count:], jnp.zeros_like(value[:-count])], 0)


def scan_states(value, decay, seqs, blocks, direction):
    step = 1
    while step < blocks:
        value = value + shift_rows(value, direction * step * seqs) * jnp.exp(decay * step)
        step *= 2
    return shift_rows(value, direction * seqs)


SHARE = 16


def fill_tables(first, last, span, refs):
    def one_channel(channel, carry):
        table, toeplitz = state_tables(
            refs.rates[pl.ds(channel, 1), :], refs.rate_weights[pl.ds(channel, 1), :], span
        )
        refs.near_up[channel], refs.near_low[channel] = split_low(toeplitz)
        refs.table_up[channel], refs.table_low[channel] = split_low(table)
        return carry

    lax.fori_loop(first, last, one_channel, 0, unroll=4)


def fill_rates(refs, loads, channels):
    rows = pl.ds(pl.multiple_of(lax.axis_index(SEQ) * channels, 8), channels)
    copies = [
        loads.start(refs.all_rates.at[rows, :], refs.rates_in),
        loads.start(refs.all_weights.at[rows, :], refs.weights_in),
    ]

    def finish():
        for copy in copies:
            copy.wait()
        refs.rates[...] = jnp.concatenate([refs.rates_in[...]] * 2, 1)
        refs.rate_weights[...] = jnp.concatenate([refs.weights_in[...]] * 2, 1)

    return finish


def rate_scratch(channels):
    half, whole = ((channels, STATES), jnp.float32), ((channels, 2 * STATES), jnp.float32)
    return dict(rates_in=half, weights_in=half, rates=whole, rate_weights=whole)


def valid_positions(lengths, seqs, span, axis):
    shape = (span, 1) if axis == 0 else (1, span)
    position = lax.axis_index(SEQ) * span + lax.broadcasted_iota(jnp.int32, shape, axis)
    parts = [
        jnp.where(position < lengths[0:1, seq : seq + 1], 1.0, 0.0).astype(jnp.float32)
        for seq in range(seqs)
    ]
    return jnp.concatenate(parts, axis)


def table_scratch(channels, span):
    shape = ((channels, span, span), jnp.bfloat16)
    return dict(near_up=shape, near_low=shape, table_up=shape, table_low=shape)


def mixer_forward_channel(n, seqs, refs, part, local):
    span, channel = refs.flat_x.shape[-1], part * SHARE + local
    rate_row = refs.rates[pl.ds(channel, 1), :]
    weight_row = refs.rate_weights[pl.ds(channel, 1), :]
    rows = pl.ds(local, n * seqs, stride=SHARE)
    data = (refs.flat_x[part, rows, :].astype(jnp.bfloat16), None)
    table_parts = (refs.table_up[channel], refs.table_low[channel])
    inner = dot_fine(data, (refs.near_up[channel], refs.near_low[channel]))
    states = scan_states(dot_fine(data, table_parts), -span * rate_row, seqs, n, 1)
    lane = lax.broadcasted_iota(jnp.int32, states.shape, 1)
    weighted = jnp.where(lane < STATES, 0.0, pltpu.roll(states, STATES, 1) * weight_row)
    refs.flat_out[part, rows, :] = inner + dot_fine(split_low(weighted), table_parts, NT)


def mixer_backward_channel(n, seqs, refs, part, local):
    span, channel = refs.flat_x.shape[-1], part * SHARE + local
    rate_row = refs.rates[pl.ds(channel, 1), :]
    weight_row = refs.rate_weights[pl.ds(channel, 1), :]
    table_parts = (refs.table_up[channel], refs.table_low[channel])
    table = table_parts[0].astype(jnp.float32) + table_parts[1].astype(jnp.float32)
    steps = state_steps(span)
    rows = pl.ds(local, n * seqs, stride=SHARE)
    data = refs.flat_x[part, rows, :].astype(jnp.bfloat16)
    grad = refs.flat_d[part, rows, :].astype(jnp.bfloat16)
    stepped_parts = split_low(table * steps)
    both_parts = [jnp.concatenate(pair, 1) for pair in zip(table_parts, stepped_parts)]
    count = n * seqs
    sides = dot_fine((jnp.concatenate([data, grad], 0), None), both_parts)
    lane = lax.broadcasted_iota(jnp.int32, (count, 2 * STATES), 1)
    low_lanes = lane < STATES

    def aligned(value):
        return jnp.where(low_lanes, pltpu.roll(value, STATES, 1), 0.0)

    entering = jnp.where(low_lanes, sides[:count, : 2 * STATES], 0.0)
    entering_steps = jnp.where(low_lanes, sides[:count, 2 * STATES :], 0.0)
    leaving = aligned(sides[count:, : 2 * STATES])
    leaving_steps = aligned(sides[count:, 2 * STATES :])
    decay = -span * rate_row
    states = scan_states(entering, decay, seqs, n, 1)
    states_steps = scan_states(states * jnp.exp(decay), decay, seqs, n, 1)
    returned = scan_states(leaving, decay, seqs, n, -1)
    far_weight = jnp.sum(leaving * states, 0, keepdims=True)
    far_rate = jnp.sum(
        leaving_steps * states + returned * entering_steps + span * (leaving * states_steps),
        0, keepdims=True,
    )
    cross = dot(grad, data, TN)
    later = lax.broadcasted_iota(jnp.int32, (span, span), 0)
    earlier = lax.broadcasted_iota(jnp.int32, (span, span), 1)
    cross = jnp.where(later >= earlier, cross, 0.0)
    met = dot_fine(split_low(cross), both_parts)
    met_plain = pltpu.roll(met[:, : 2 * STATES], STATES, 1)
    met_steps = pltpu.roll(met[:, 2 * STATES :], STATES, 1)
    rise = jnp.exp(span * rate_row)
    near_weight = rise * jnp.sum(table * met_plain, 0, keepdims=True)
    near_rate = rise * jnp.sum(
        table * ((steps - span) * met_plain + met_steps), 0, keepdims=True
    )
    lane_row = lane[:1]
    near_weight = jnp.where(lane_row < STATES, pltpu.roll(near_weight, STATES, 1), 0.0)
    near_rate = jnp.where(lane_row < STATES, pltpu.roll(near_rate, STATES, 1), 0.0)
    refs.weight_grad[pl.ds(channel, 1), :] = near_weight + far_weight
    refs.rate_grad[pl.ds(channel, 1), :] = -weight_row * (near_rate + far_rate)
    inner = dot_fine((grad, None), (refs.near_up[channel], refs.near_low[channel]), NT)
    weighted = returned * weight_row
    refs.flat_d[part, rows, :] = inner + dot_fine(split_low(weighted), table_parts, NT)


def block_of(index, core):
    return 2 * index + lax.rem(index + core, 2)


def keeper_of(block):
    return lax.rem((block + 1) // 2, 2)


class HeadPlaces:
    def __init__(self, n, seqs, groups):
        self.n, self.seqs, self.groups = n, seqs, groups
        self.me, self.core = lax.axis_index(SEQ), lax.axis_index(BATCH)
        self.group = self.me // (2 * seqs)
        self.seq = lax.rem(self.me // 2, seqs)
        self.batch = lax.rem(self.me, 2)
        self.keeper = keeper_of(self.me)
        self.sibling = (self.me, 1 - self.core)
        self.targets = [
            ((group * 2 * seqs + seq * 2 + self.core, self.keeper), seq, group)
            for seq in range(seqs)
            for group in range(groups)
        ]
        self.blocks = [block_of(index, self.core) for index in range(n // 2)]
        self.sources = [(block, self.batch) for block in self.blocks]

    def is_other(self, device):
        return jnp.logical_or(device[0] != self.me, device[1] != self.core)

    def greet(self):
        barrier = pltpu.get_barrier_semaphore()
        self.signal_all(barrier, [])
        self.wait_all(barrier, 0)

    def signal_all(self, barrier, more):
        for device in [target for target, _, _ in self.targets] + self.sources:

            @pl.when(self.is_other(device))
            def _():
                pl.semaphore_signal(barrier, inc=1, device_id=device, device_id_type=MESH)

        for device in [self.sibling, *more]:
            pl.semaphore_signal(barrier, inc=1, device_id=device, device_id_type=MESH)

    def wait_all(self, barrier, more):
        kept = jnp.logical_and(self.batch == self.core, self.is_kept_here())
        count = len(self.targets) + len(self.sources) + 1 + more
        pl.semaphore_wait(barrier, count - 2 * kept.astype(jnp.int32))

    def is_kept_here(self):
        return self.keeper == self.core

    def send(self, source, target, send_sem, recv_sem, device):
        @pl.when(self.is_other(device))
        def _():
            remote(source, target, send_sem, recv_sem, device).start()

        @pl.when(jnp.logical_not(self.is_other(device)))
        def _():
            pltpu.make_async_copy(source, target, recv_sem).start()

    def wait_sent(self, source, target, send_sem, recv_sem, device):
        @pl.when(self.is_other(device))
        def _():
            remote(source, target, send_sem, recv_sem, device).wait_send()


def fill_head(held, head, part, n, span, rows_out, columns_out):
    for block in range(n):
        piece = held[head, block, part * HEAD : (part + 1) * HEAD, :]
        if rows_out is not None:
            rows_out[block * span : (block + 1) * span, :] = piece.T
        if columns_out is not None:
            columns_out[:, block * span : (block + 1) * span] = piece


def causal(first_key, rows, first_query, span):
    key = first_key + lax.broadcasted_iota(jnp.int32, (rows, span), 0)
    query = first_query + lax.broadcasted_iota(jnp.int32, (rows, span), 1)
    return key <= query


TILE = 384
VMEM, HBM = pltpu.VMEM, pl.ANY


def launch(body, inputs, outputs, scratch, copies, collective):
    names = [*inputs, *outputs, *scratch, "send", "recv", "local"]

    def kernel(*refs):
        body(types.SimpleNamespace(**dict(zip(names, refs))))

    dma = pltpu.SemaphoreType.DMA
    results = pl.pallas_call(
        kernel,
        out_shape=tuple(jax.ShapeDtypeStruct(shape, kind) for shape, kind, _ in outputs.values()),
        in_specs=[pl.BlockSpec(memory_space=space) for _, space in inputs.values()],
        out_specs=tuple(pl.BlockSpec(memory_space=space) for _, _, space in outputs.values()),
        scratch_shapes=[pltpu.VMEM(shape, kind) for shape, kind in scratch.values()]
        + [dma((copies,)), dma((copies,)), dma((LOCAL_COPIES,))],
        compiler_params=pltpu.CompilerParams(
            collective_id=collective, has_side_effects=True, vmem_limit_bytes=VMEM_BYTES
        ),
    )(*(array for array, _ in inputs.values()))
    return types.SimpleNamespace(**dict(zip(outputs, results)))


LOCAL_COPIES = 64


class Loads:
    def __init__(self, refs):
        self.semaphores, self.used = refs.local, 0

    def start(self, source, target):
        copy = pltpu.make_async_copy(source, target, self.semaphores.at[self.used])
        self.used += 1
        copy.start()
        return copy


class Links:
    def __init__(self, refs):
        self.send, self.recv, self.used, self.unsent = refs.send, refs.recv, 0, []

    def slots(self, count):
        self.used += count
        return self.used - count

    def copy(self, source, target, device, slot=None):
        slot = self.slots(1) if slot is None else slot
        made = remote(source, target, self.send.at[slot], self.recv.at[slot], device)
        made.start()
        self.unsent.append(made)
        return made

    def finish(self):
        for made in self.unsent:
            made.wait_send()


class Piece:
    def __init__(self, weight, first_row, first_column, axis):
        self.weight, self.first_row, self.first_column, self.axis = (
            weight, first_row, first_column, axis,
        )


ROWS = 48


def pieces_of(weights, order):
    pieces = []
    for weight, first, last, axes in order:
        rows, half = weights[weight]
        places = [
            (first_row, first_column)
            for first_column in range(0, half, TILE)
            for first_row in range(0, rows, ROWS)
        ]
        for count, place in enumerate(places[first:last]):
            pieces.append(Piece(weight, *place, axes[count % len(axes)]))
    return pieces


class Reducer:
    def __init__(self, refs, links, depth, weights, pieces, given):
        self.refs, self.links, self.depth, self.weights = refs, links, depth, weights
        self.me, self.core = lax.axis_index(SEQ), lax.axis_index(BATCH)
        self.level = self.me // 4
        self.spot = (lax.rem(self.me // 2, 2), lax.rem(self.me, 2))
        base = self.level * 4
        self.across = [
            (base + self.spot[0] * 2 + (1 - self.spot[1]), self.core),
            (base + (1 - self.spot[0]) * 2 + self.spot[1], self.core),
        ]
        self.sibling = (self.me, 1 - self.core)
        self.levels = [lax.rem(self.level + step, depth) for step in range(1, depth)]
        self.column = [
            (other * 4 + self.spot[0] * 2 + self.spot[1], self.core) for other in self.levels
        ]
        self.slots = {piece: slot for slot, piece in enumerate(pieces)}
        self.middles = {piece: slot for slot, piece in enumerate(given)}
        self.exchanges, self.flights = {}, {}

    def neighbours(self):
        return [self.sibling, *self.across, *self.column]

    def exchange(self, weight, left, right):
        half = self.weights[weight][1]
        theirs = pl.ds(pl.multiple_of((1 - self.core) * half, 16), half)
        self.exchanges[weight] = (
            left, right,
            [
                self.links.copy(left[0], left[1], self.sibling),
                self.links.copy(right[0].at[theirs, :], right[1], self.sibling),
            ],
        )

    def product(self, piece, first):
        left, right, copies = self.exchanges[piece.weight]
        while copies:
            copies.pop().wait_recv()
        places = [
            outer * 4 + (inner * 2 + first if piece.axis == 0 else first * 2 + inner)
            for outer in range(self.depth)
            for inner in range(2)
        ]
        rows = slice(piece.first_row, piece.first_row + ROWS)
        mine, other = (
            jnp.concatenate([side[place, rows, :] for place in places], 0) for side in left
        )
        start = self.core * self.weights[piece.weight][1] + piece.first_column
        own = pl.ds(pl.multiple_of(start, 16), TILE)
        there = slice(piece.first_column, piece.first_column + TILE)
        total = dot(mine, right[0][own, :], NT) + dot(other, right[1][there, :], NT)
        return total.reshape(self.depth, 2, ROWS, TILE)

    def first(self, piece):
        slot = self.slots[piece]
        away = self.refs.away.at[slot]
        away[...] = self.product(piece, 1 - self.spot[1 - piece.axis]).astype(jnp.bfloat16)
        self.flights[piece] = self.links.copy(
            away, self.refs.one.at[slot], self.across[piece.axis]
        )

    def second(self, piece):
        slot = self.slots[piece]
        self.flights.pop(piece).wait_recv()
        one = self.refs.one.at[slot]
        total = self.product(piece, self.spot[1 - piece.axis]) + one[...].astype(jnp.float32)
        one[...] = total.astype(jnp.bfloat16)
        self.flights[piece] = self.links.copy(
            one.at[:, 1 - self.spot[piece.axis]], self.refs.two.at[slot],
            self.across[1 - piece.axis],
        )

    def middle(self, piece, into, place):
        slot = self.slots[piece]
        self.flights.pop(piece).wait_recv()
        kept = self.refs.one[slot, :, self.spot[piece.axis]].astype(jnp.float32)
        into[place] = (kept + self.refs.two[slot].astype(jnp.float32)).astype(into.dtype)

    def third(self, piece):
        if piece not in self.middles:
            self.middles[piece] = len(self.middles)
            self.middle(piece, self.refs.mid, self.middles[piece])
        place = self.middles[piece]
        self.flights[piece] = [
            self.links.copy(
                self.refs.mid.at[place, other], self.refs.three.at[place, step], self.column[step]
            )
            for step, other in enumerate(self.levels)
        ]

    def fourth(self, piece, out):
        place = self.middles[piece]
        total = self.refs.mid[place, self.level].astype(jnp.float32)
        for step, copy in enumerate(self.flights.pop(piece)):
            copy.wait_recv()
            total = total + self.refs.three[place, step].astype(jnp.float32)
        start = self.core * self.weights[piece.weight][1] + piece.first_column
        filled = out.at[
            piece.first_row : piece.first_row + ROWS, pl.ds(pl.multiple_of(start, 128), TILE)
        ]
        filled[...] = total
        self.flights[piece] = self.links.copy(filled, filled, self.sibling)

    def last(self, piece):
        self.flights.pop(piece).wait_recv()


def reducer_scratch(weights, pieces, middles, depth, tokens):
    low = jnp.bfloat16
    shapes = dict(
        away=((len(pieces), depth, 2, ROWS, TILE), low),
        one=((len(pieces), depth, 2, ROWS, TILE), low),
        two=((len(pieces), depth, ROWS, TILE), low),
    )
    if middles > 0:
        shapes.update(
            mid=((middles, depth, ROWS, TILE), low), three=((middles, depth - 1, ROWS, TILE), low)
        )
    return shapes


def gelu_slope(value):
    scale = math.sqrt(2.0 / math.pi)
    square = value * value
    bent = jnp.tanh(scale * value * (1.0 + 0.044715 * square))
    return 0.5 * (1.0 + bent) + 0.5 * value * (1.0 - bent * bent) * scale * (
        1.0 + 3.0 * 0.044715 * square
    )


def norm_gradient(inputs, gain, grad):
    center = inputs - jnp.mean(inputs, 0, keepdims=True)
    factor = lax.rsqrt(jnp.mean(center * center, 0, keepdims=True) + norm_eps)
    unit = center * factor
    scaled = grad * gain
    result = factor * (
        scaled
        - jnp.mean(scaled, 0, keepdims=True)
        - unit * jnp.mean(scaled * unit, 0, keepdims=True)
    )
    return result, jnp.sum(grad * unit, 1, keepdims=True), jnp.sum(grad, 1, keepdims=True)


def rows_product(matrix, other, out_rows, chunk, store):
    def one_chunk(index, carry):
        rows = pl.ds(pl.multiple_of(index * chunk, 128), chunk)
        store(rows, dot(matrix[rows, :], other))
        return carry

    lax.fori_loop(0, out_rows // chunk, one_chunk, 0)


def back_one_body(n, seqs, groups, span, group_rows, width, hidden_width, refs):
    at = HeadPlaces(n, seqs, groups)
    half = n // 2
    heads = group_rows // HEAD
    tokens = seqs * span
    links, loads = Links(refs), Loads(refs)
    weights = gradient_weights(width, hidden_width, n)
    pieces = pieces_of(weights, BACK_ONE_ORDER)
    reducer = Reducer(refs, links, groups, weights, pieces, [])
    down, up, out = [[piece for piece in pieces if piece.weight == weight] for weight in (DOWN, UP, OUT)]
    barrier = pltpu.get_barrier_semaphore()
    at.signal_all(barrier, reducer.neighbours()[1:])

    load_cotangent = loads.start(refs.cotangent, refs.cot)
    load_active = loads.start(refs.active, refs.down_left)
    load_w_down = loads.start(refs.w_down.at[1], refs.down)
    load_slope = loads.start(refs.slope, refs.slope_in)
    load_w_up = loads.start(refs.w_up.at[1], refs.up)
    load_hidden = loads.start(refs.hidden, refs.hidden_in)
    load_w_out = loads.start(refs.w_out.at[1], refs.out)
    load_normed = loads.start(refs.normed, refs.up_left)
    load_attended = loads.start(refs.attended, refs.out_left)
    load_held = loads.start(refs.held, refs.held_in)

    valid = valid_positions(refs.lengths, seqs, span, 1)
    load_cotangent.wait()
    for seq in range(seqs):
        lanes = slice(seq * span, (seq + 1) * span)
        for first in range(0, width, span):
            piece = refs.cot[seq, :, first : first + span].astype(jnp.float32).T
            refs.grad[first : first + span, lanes] = piece * valid[:, lanes]
    refs.down_right[...] = refs.grad[...].astype(jnp.bfloat16)

    def store_raised(rows, value):
        slope = refs.slope_in[rows, :].astype(jnp.float32)
        refs.up_right[rows, :] = (slope * value).astype(jnp.bfloat16)

    at.wait_all(barrier, len(reducer.neighbours()) - 1)
    load_active.wait()
    reducer.exchange(DOWN, (refs.down_left, refs.down_left_other), (refs.down_right, refs.down_right_other))
    load_w_down.wait()
    load_slope.wait()
    rows_product(refs.down, refs.down_right[...], hidden_width, 512, store_raised)
    for piece in down[:2]:
        reducer.first(piece)
    load_w_up.wait()
    load_hidden.wait()
    load_normed.wait()
    reducer.exchange(UP, (refs.up_left, refs.up_left_other), (refs.up_right, refs.up_right_other))
    d_normed = dot(refs.up[...], refs.up_right[...])
    for piece in down[2:]:
        reducer.first(piece)
    d_inputs, gain_part, bias_part = norm_gradient(refs.hidden_in[...], refs.columns[:, 3:4], d_normed)
    refs.small[...] = jnp.zeros_like(refs.small)
    refs.small[:, 3:4] = gain_part
    refs.small[:, 7:8] = bias_part
    grad = refs.grad[...] + d_inputs
    refs.grad_out[...] = grad
    refs.out_right[...] = grad.astype(jnp.bfloat16)
    load_w_out.wait()
    load_attended.wait()
    reducer.exchange(OUT, (refs.out_left, refs.out_left_other), (refs.out_right, refs.out_right_other))
    refs.d_attended[...] = dot(refs.out[...], refs.out_right[...]).astype(jnp.bfloat16)

    count = len(at.targets)
    arrive, leave = links.slots(heads * half), links.slots(heads * count)
    spread = []
    for head in range(heads):
        for number, (device, seq, group) in enumerate(at.targets):
            first = group * group_rows + head * HEAD
            sent = (
                refs.d_attended.at[first : first + HEAD, seq * span : (seq + 1) * span],
                refs.landing.at[head, at.me // 2], refs.send.at[leave + head * count + number],
                refs.recv.at[arrive + head * half + at.me // 2], device,
            )
            at.send(*sent)
            spread.append(sent)
    load_held.wait()
    started = down + up + out
    for piece in up + out:
        reducer.first(piece)

    returned = links.slots(len(at.targets) * heads)
    returning = links.slots(half * heads)
    slot = at.seq * groups + at.group
    going = []
    passed = []

    def send_back(head):
        passed[head].wait_recv()
        for index, device in enumerate(at.sources):
            results = refs.results.at[head, index]
            kept = refs.kept.at[head, index]
            part = refs.partial_recv[head, index].astype(jnp.float32)
            results[1] = (kept[:HEAD] + part[:HEAD]).astype(jnp.bfloat16)
            results[2] = (kept[HEAD:] + part[HEAD:]).astype(jnp.bfloat16)
            into = refs.d_qkv.at[
                :,
                pl.ds(pl.multiple_of(at.group * group_rows + head * HEAD, HEAD), HEAD),
                pl.ds(pl.multiple_of(at.seq * span, span), span),
            ]
            sent = (
                results, into, refs.send.at[returning + head * half + index],
                refs.recv.at[returned + head * len(at.targets) + slot], device,
            )
            at.send(*sent)
            going.append(sent)

    def attend(head):
        for index in range(half):
            landed = refs.landing.at[head, index]
            remote(
                landed, landed, refs.send.at[leave], refs.recv.at[arrive + head * half + index],
                at.sibling,
            ).wait_recv()
        fill_head(refs.held_in, head, 1, n, span, refs.key_rows, refs.key_columns)
        fill_head(refs.held_in, head, 2, n, span, refs.value_rows, None)
        refs.key_grads[...] = jnp.zeros_like(refs.key_grads)
        refs.value_grads[...] = jnp.zeros_like(refs.value_grads)
        for index, block in enumerate(at.blocks):
            query = refs.held_in[head, block, :HEAD, :] * jnp.bfloat16(HEAD**-0.5)
            grad = refs.landing[head, index]
            log_total = refs.lse[index, head : head + 1, :]
            clear, reach = 2 * index * span, 2 * (index + 1) * span
            pieces = []
            row_term = jnp.zeros((1, span), jnp.float32)
            for first, last in ((0, clear), (clear, reach)):
                if first == last:
                    continue
                scores = dot(refs.key_rows[first:last, :], query)
                if last == reach:
                    scores = jnp.where(
                        causal(clear, reach - clear, block * span, span), scores, masked_score
                    )
                weights = jnp.exp(scores - log_total)
                d_weights = dot(refs.value_rows[first:last, :], grad)
                row_term = row_term + jnp.sum(weights * d_weights, 0, keepdims=True)
                pieces.append((first, last, weights, d_weights))
            d_query = jnp.zeros((HEAD, span), jnp.float32)
            for first, last, weights, d_weights in pieces:
                d_scores = (weights * (d_weights - row_term)).astype(jnp.bfloat16)
                d_query = d_query + dot(refs.key_columns[:, first:last], d_scores)
                refs.key_grads[:, first:last] += dot(query, d_scores, NT)
                refs.value_grads[:, first:last] += dot(grad, weights.astype(jnp.bfloat16), NT)
            refs.results[head, index, 0] = (d_query * HEAD**-0.5).astype(jnp.bfloat16)
        for index in range(half):
            other = pl.ds(pl.multiple_of(block_of(index, 1 - at.core) * span, span), span)
            own = pl.ds(pl.multiple_of(at.blocks[index] * span, span), span)
            refs.partial_send[head, index, :HEAD, :] = refs.key_grads[:, other].astype(jnp.bfloat16)
            refs.partial_send[head, index, HEAD:, :] = refs.value_grads[:, other].astype(jnp.bfloat16)
            refs.kept[head, index, :HEAD, :] = refs.key_grads[:, own]
            refs.kept[head, index, HEAD:, :] = refs.value_grads[:, own]
        passed.append(
            links.copy(refs.partial_send.at[head], refs.partial_recv.at[head], at.sibling)
        )

    waiting = list(started)
    for head in range(heads):
        attend(head)
        if head > 0:
            send_back(head - 1)
        if head < heads - 1:
            for _ in range(2):
                reducer.second(waiting.pop(0))
    reducer.second(waiting.pop(0))
    send_back(heads - 1)
    while waiting:
        reducer.second(waiting.pop(0))
    for place, piece in enumerate(pieces):
        reducer.middle(piece, refs.mid_out, place)
    for head in range(heads):
        for count, (device, seq, group) in enumerate(at.targets):
            landed = refs.d_qkv.at[
                :,
                group * group_rows + head * HEAD : group * group_rows + (head + 1) * HEAD,
                seq * span : (seq + 1) * span,
            ]
            remote(
                landed, landed, refs.send.at[leave],
                refs.recv.at[returned + head * len(at.targets) + count], at.sibling,
            ).wait_recv()
    for sent in spread + going:
        at.wait_sent(*sent)
    links.finish()


def gradient_weights(width, hidden_width, n):
    return {
        QKV: (width // n, 3 * width // 2),
        DOWN: (hidden_width // n, width // 2),
        UP: (width // n, hidden_width // 2),
        OUT: (width // n, width // 2),
    }


BACK_ONE_ORDER = ((DOWN, 0, 4, (1, 0)), (UP, 0, 4, (1, 0)), (OUT, 0, 1, (0,)))
BACK_TWO_FIRST = ((QKV, 0, 3, (1, 0, 1)),)
BACK_TWO_ORDER = ((DOWN, 0, 4, (0, 1)), (UP, 0, 1, (0,)))
BACK_THREE_FIRST = ((UP, 1, 4, (1, 0, 1)), (OUT, 0, 1, (0,)))
BACK_THREE_ORDER = ((QKV, 0, 3, (1, 0, 1)),)


def back_one(
    cotangent, lengths, hidden, slope, normed, active, attended, held, lse, columns,
    w_out, w_up, w_down, collective,
):
    seqs, span, width = cotangent.shape
    heads, n = held.shape[:2]
    group_rows = heads * HEAD
    groups = width // group_rows
    hidden_width = w_up.shape[2]
    tokens = seqs * span
    half = n // 2
    low, wide = jnp.bfloat16, jnp.float32
    weights = gradient_weights(width, hidden_width, n)
    pieces = pieces_of(weights, BACK_ONE_ORDER)
    inputs = dict(
        cotangent=(cotangent, HBM), lengths=(lengths, VMEM), hidden=(hidden, HBM), slope=(slope, HBM),
        normed=(normed, HBM), active=(active, HBM), attended=(attended, HBM), held=(held, HBM),
        lse=(lse, VMEM), columns=(columns, VMEM), w_out=(w_out, HBM), w_up=(w_up, HBM),
        w_down=(w_down, HBM),
    )
    outputs = dict(
        d_qkv=((3, width, tokens), low, VMEM),
        grad_out=((width, tokens), wide, VMEM),
        small=((width, 128), wide, VMEM),
        mid_out=((len(pieces), groups, ROWS, TILE), low, VMEM),
    )
    scratch = dict(
        down=(w_down.shape[1:], low), up=(w_up.shape[1:], low), out=(w_out.shape[1:], low),
        cot=(cotangent.shape, low), grad=((width, tokens), wide), hidden_in=((width, tokens), wide),
        slope_in=(slope.shape, low), d_attended=((width, tokens), low),
        down_left=(active.shape, low), down_right=((width, tokens), low),
        up_left=(normed.shape, low), up_right=((hidden_width, tokens), low),
        out_left=(attended.shape, low), out_right=((width, tokens), low),
        held_in=(held.shape, low), landing=((heads, half, HEAD, span), low),
        results=((heads, half, 3, HEAD, span), low), kept=((heads, half, 2 * HEAD, span), wide),
        partial_send=((heads, half, 2 * HEAD, span), low),
        partial_recv=((heads, half, 2 * HEAD, span), low),
        key_grads=((HEAD, n * span), wide), value_grads=((HEAD, n * span), wide),
        key_rows=((n * span, HEAD), low), key_columns=((HEAD, n * span), low),
        value_rows=((n * span, HEAD), low),
        down_left_other=(active.shape, low), down_right_other=((width // 2, tokens), low),
        up_left_other=(normed.shape, low), up_right_other=((hidden_width // 2, tokens), low),
        out_left_other=(attended.shape, low), out_right_other=((width // 2, tokens), low),
        **reducer_scratch(weights, pieces, 0, groups, tokens),
    )
    body = functools.partial(
        back_one_body, n, seqs, groups, span, group_rows, width, hidden_width
    )
    return launch(body, inputs, outputs, scratch, 160, collective)


def back_two_body(n, seqs, span, width, hidden_width, refs):
    channels = width // n
    me, core = lax.axis_index(SEQ), lax.axis_index(BATCH)
    peers = [lax.rem(me + step, n) for step in range(1, n)]
    links, loads = Links(refs), Loads(refs)
    weights = gradient_weights(width, hidden_width, n)
    qkv, later = pieces_of(weights, BACK_TWO_FIRST), pieces_of(weights, BACK_TWO_ORDER)
    given = pieces_of(weights, BACK_ONE_ORDER)
    reducer = Reducer(refs, links, n // 4, weights, qkv + later, given)
    outs = {QKV: refs.qkv_grad, DOWN: refs.down_grad, UP: refs.up_grad, OUT: refs.out_grad}
    barrier = pltpu.get_barrier_semaphore()
    for device in [(peer, core) for peer in peers] + [reducer.sibling]:
        pl.semaphore_signal(barrier, inc=1, device_id=device, device_id_type=MESH)
    load_d_qkv = loads.start(refs.d_qkv, refs.qkv_right)
    load_normed_three = loads.start(refs.normed_three, refs.qkv_left)
    load_mid = loads.start(refs.mid_in, refs.mid.at[: len(given)])
    load_w_qkv = loads.start(refs.w_qkv.at[1], refs.qkv)
    load_hidden_two = loads.start(refs.hidden_two, refs.hidden_two_in)
    load_grad = loads.start(refs.grad, refs.grad_now)
    load_w_down = loads.start(refs.w_down.at[0], refs.down)
    load_slope = loads.start(refs.slope, refs.slope_in)
    load_w_up = loads.start(refs.w_up.at[0], refs.up)
    load_active = loads.start(refs.active, refs.down_left)
    load_hidden_one = loads.start(refs.hidden_one, refs.hidden_one_in)
    load_normed_two = loads.start(refs.normed_two, refs.up_left)
    load_w_out = loads.start(refs.w_out.at[0], refs.out)
    load_queries = loads.start(refs.queries, refs.queries_in)
    load_mixer = loads.start(refs.mixer, refs.mixer_in)
    load_carried = loads.start(refs.carried, refs.carried_in)
    finish_rates = fill_rates(refs, loads, channels)
    load_tables = [
        loads.start(getattr(refs, name + KEPT), getattr(refs, name))
        for name in table_scratch(channels, span)
    ]
    load_held = loads.start(refs.held, refs.held_in)

    load_d_qkv.wait()
    load_normed_three.wait()
    pl.semaphore_wait(barrier, n)
    reducer.exchange(QKV, (refs.qkv_left, refs.qkv_left_other), (refs.qkv_right, refs.qkv_right_other))
    load_mid.wait()
    thirds = list(given)
    for _ in range(4):
        reducer.third(thirds.pop(0))
    load_w_qkv.wait()
    d_normed = dot(refs.qkv[...], refs.qkv_right[...])
    for piece in qkv:
        reducer.first(piece)
    load_hidden_two.wait()
    load_grad.wait()
    d_inputs, gain_part, bias_part = norm_gradient(
        refs.hidden_two_in[...], refs.columns[:, 2:3], d_normed
    )
    refs.small[...] = refs.small_in[...]
    refs.small[:, 2:3] = gain_part
    refs.small[:, 6:7] = bias_part
    grad = refs.grad_now[...] + d_inputs
    refs.grad_now[...] = grad
    refs.down_right[...] = grad.astype(jnp.bfloat16)
    load_w_down.wait()
    load_slope.wait()
    load_active.wait()
    reducer.exchange(DOWN, (refs.down_left, refs.down_left_other), (refs.down_right, refs.down_right_other))

    def store_raised(rows, value):
        slope = refs.slope_in[rows, :].astype(jnp.float32)
        refs.up_right[rows, :] = (slope * value).astype(jnp.bfloat16)

    rows_product(refs.down, refs.down_right[...], hidden_width, 512, store_raised)
    save_raised = loads.start(refs.up_right, refs.d_raised)
    load_w_up.wait()
    load_hidden_one.wait()
    load_normed_two.wait()
    reducer.exchange(UP, (refs.up_left, refs.up_left_other), (refs.up_right, refs.up_right_other))
    d_normed = dot(refs.up[...], refs.up_right[...])
    d_inputs, gain_part, bias_part = norm_gradient(
        refs.hidden_one_in[...], refs.columns[:, 1:2], d_normed
    )
    refs.small[:, 1:2] = gain_part
    refs.small[:, 5:6] = bias_part
    grad = refs.grad_now[...] + d_inputs
    refs.grad_out[...] = grad
    out_right = grad.astype(jnp.bfloat16)
    load_w_out.wait()
    load_queries.wait()
    load_mixer.wait()
    load_carried.wait()
    d_gated = dot(refs.out[...], out_right)
    d_mixer = d_gated * refs.queries_in[...]
    for seq in range(seqs):
        refs.d_conv[seq] = d_mixer[:, seq * span : (seq + 1) * span].astype(jnp.bfloat16)
    shares = channels // SHARE
    arrive, answered = links.slots(shares * n), links.slots(shares * n)

    def share_rows(device, share):
        return pl.ds(pl.multiple_of(device * channels + share * SHARE, 16), SHARE)

    going, own_copies = [], []
    for share in range(shares):
        within = slice(share * SHARE, (share + 1) * SHARE)
        for step, peer in enumerate(peers):
            going.append(
                links.copy(
                    refs.d_conv.at[:, share_rows(peer, share), :],
                    refs.landing.at[me, :, within, :], (peer, core), arrive + share * n + step,
                )
            )
        own_copies.append(
            loads.start(
                refs.d_conv.at[:, share_rows(me, share), :], refs.landing.at[me, :, within, :]
            )
        )
    refs.d_mixer[...] = d_mixer
    refs.d_queries[...] = (d_gated * refs.mixer_in[...]).astype(jnp.bfloat16)
    refs.small[:, 12:13] = sum(
        jnp.sum(
            d_mixer[:, seq * span : (seq + 1) * span] * refs.carried_in[seq].astype(jnp.float32), 1,
            keepdims=True,
        )
        for seq in range(seqs)
    )

    while thirds:
        reducer.third(thirds.pop(0))
    for piece in later:
        reducer.first(piece)
    for piece in qkv:
        reducer.second(piece)
    waiting = list(later)
    load_held.wait()
    finish_rates()
    for copy in load_tables:
        copy.wait()
    back, back_own = [], []
    for share in range(shares):
        within = slice(share * SHARE, (share + 1) * SHARE)
        own_copies[share].wait()
        for copy in going[share * len(peers) : (share + 1) * len(peers)]:
            copy.wait_recv()
        for flat, source in ((refs.flat_x, refs.held_in), (refs.flat_d, refs.landing)):
            flat[share] = (
                source[:, :, within, :].astype(jnp.float32).reshape(n * seqs * SHARE, span)
            )

        def one_channel(local, carry):
            mixer_backward_channel(n, seqs, refs, share, local)
            return carry

        lax.fori_loop(0, SHARE, one_channel, 0, unroll=4)
        refs.answer[:, :, within, :] = (
            refs.flat_d[share].reshape(n, seqs, SHARE, span).astype(jnp.bfloat16)
        )
        for step, peer in enumerate(peers):
            back.append(
                links.copy(
                    refs.answer.at[peer, :, within, :],
                    refs.from_conv.at[:, share_rows(me, share), :], (peer, core),
                    answered + share * n + step,
                )
            )
        back_own.append(
            loads.start(
                refs.answer.at[me, :, within, :], refs.from_conv.at[:, share_rows(me, share), :]
            )
        )
        reducer.third(qkv[share])
        for _ in range(min(len(waiting), 1 + share)):
            reducer.second(waiting.pop(0))
    states = [
        links.copy(refs.rate_grad, refs.rate_other, reducer.sibling),
        links.copy(refs.weight_grad, refs.weight_other, reducer.sibling),
    ]
    while waiting:
        reducer.second(waiting.pop(0))
    finished = given + qkv
    for piece in finished:
        reducer.fourth(piece, outs[piece.weight])
    for copy in states:
        copy.wait_recv()
    refs.rate_sum[...] = (refs.rate_grad[...] + refs.rate_other[...])[:, :STATES]
    refs.weight_sum[...] = (refs.weight_grad[...] + refs.weight_other[...])[:, :STATES]
    for place, piece in enumerate(later):
        reducer.middle(piece, refs.mid_out, place)
    for piece in finished:
        reducer.last(piece)
    for copy in back_own:
        copy.wait()
    for copy in back:
        copy.wait_recv()
    save_raised.wait()
    links.finish()


def back_two(
    tables, mid, d_qkv, grad, hidden_two, normed_three, slope, normed_two, active, hidden_one,
    queries, mixer, carried, held, columns, small, rates, rate_weights, w_qkv, w_out, w_up, w_down, collective,
):
    n, seqs, channels, span = held.shape
    width, hidden_width = w_up.shape[1:]
    tokens = seqs * span
    low, wide = jnp.bfloat16, jnp.float32
    weights = gradient_weights(width, hidden_width, n)
    pieces = pieces_of(weights, BACK_TWO_FIRST + BACK_TWO_ORDER)
    inputs = dict(
        **{name + KEPT: (table, HBM) for name, table in tables.items()}, mid_in=(mid, HBM), d_qkv=(d_qkv, HBM), grad=(grad, HBM), hidden_two=(hidden_two, HBM),
        normed_three=(normed_three, HBM), slope=(slope, HBM), normed_two=(normed_two, HBM),
        active=(active, HBM), hidden_one=(hidden_one, HBM),
        queries=(queries, HBM), mixer=(mixer, HBM), carried=(carried, HBM), held=(held, HBM),
        columns=(columns, VMEM), small_in=(small, VMEM), all_rates=(rates, HBM), all_weights=(rate_weights, HBM),
        w_qkv=(w_qkv, HBM), w_out=(w_out, HBM), w_up=(w_up, HBM), w_down=(w_down, HBM),
    )
    square, state = (width, tokens), (channels, 2 * STATES)
    outputs = dict(
        from_conv=((seqs, width, span), low, VMEM),
        d_mixer=(square, wide, VMEM),
        d_queries=(square, low, VMEM),
        grad_out=(square, wide, VMEM),
        small=((width, 128), wide, VMEM),
        rate_sum=((channels, STATES), wide, VMEM),
        weight_sum=((channels, STATES), wide, VMEM),
        qkv_grad=((width // n, 3 * width), wide, VMEM),
        down_grad=((hidden_width // n, width), wide, VMEM),
        up_grad=((width // n, hidden_width), wide, VMEM),
        out_grad=((width // n, width), wide, VMEM),
        d_raised=((hidden_width, tokens), low, HBM),
        mid_out=((len(pieces) - 3, n // 4, ROWS, TILE), low, VMEM),
    )
    flat = (channels // SHARE, n * seqs * SHARE, span)
    scratch = dict(
        qkv=(w_qkv.shape[1:], low), down=(w_down.shape[1:], low), up=(w_up.shape[1:], low),
        out=(w_out.shape[1:], low),
        qkv_left=(normed_three.shape, low), qkv_right=((3 * width, tokens), low),
        down_left=(active.shape, low), down_right=(square, low),
        up_left=(normed_two.shape, low), up_right=((hidden_width, tokens), low),
        hidden_two_in=(square, wide), hidden_one_in=(square, wide), grad_now=(square, wide),
        slope_in=(slope.shape, low), queries_in=(square, queries.dtype),
        mixer_in=(square, mixer.dtype), carried_in=(carried.shape, low), held_in=(held.shape, low),
        d_conv=((seqs, width, span), low), landing=(held.shape, low), answer=(held.shape, low),
        flat_x=(flat, wide), flat_d=(flat, wide), **table_scratch(channels, span),
        **rate_scratch(channels),
        rate_grad=(state, wide), weight_grad=(state, wide),
        rate_other=(state, wide), weight_other=(state, wide),
        qkv_left_other=(normed_three.shape, low), qkv_right_other=((3 * width // 2, tokens), low),
        down_left_other=(active.shape, low), down_right_other=((width // 2, tokens), low),
        up_left_other=(normed_two.shape, low), up_right_other=((hidden_width // 2, tokens), low),
        **reducer_scratch(weights, pieces, mid.shape[0] + 3, n // 4, tokens),
    )
    body = functools.partial(back_two_body, n, seqs, span, width, hidden_width)
    return launch(body, inputs, outputs, scratch, 270, collective)


def back_three_body(n, seqs, span, width, hidden_width, refs):
    me, core = lax.axis_index(SEQ), lax.axis_index(BATCH)
    links, loads = Links(refs), Loads(refs)
    weights = gradient_weights(width, hidden_width, n)
    early, pieces = pieces_of(weights, BACK_THREE_FIRST), pieces_of(weights, BACK_THREE_ORDER)
    given = pieces_of(weights, BACK_TWO_ORDER)
    reducer = Reducer(refs, links, n // 4, weights, early + pieces, given)
    outs = {QKV: refs.qkv_grad, DOWN: refs.down_grad, UP: refs.up_grad, OUT: refs.out_grad}
    stacked = (
        (refs.qkv_all, refs.qkv_grad, refs.qkv_two), (refs.down_all, refs.down_grad, refs.down_two),
        (refs.up_all, refs.up_grad, refs.up_two), (refs.out_all, refs.out_grad, refs.out_two),
    )
    barrier = pltpu.get_barrier_semaphore()
    before, after = (lax.rem(me + n - 1, n), core), (lax.rem(me + 1, n), core)
    greeted = [*reducer.neighbours(), before, after]
    for device in greeted:
        pl.semaphore_signal(barrier, inc=1, device_id=device, device_id_type=MESH)
    tokens = seqs * span
    load_grad = loads.start(refs.grad, refs.grad_in)
    load_out_left = loads.start(refs.gated, refs.out_left)
    load_up_right = loads.start(refs.d_raised, refs.up_right)
    load_up_left = loads.start(refs.normed_two, refs.up_left)
    load_mid = loads.start(refs.mid_in, refs.mid.at[: len(given)])
    load_from_conv = loads.start(refs.from_conv, refs.conv_in)
    load_d_mixer = loads.start(refs.d_mixer, refs.mixer_in)
    load_values = loads.start(refs.values, refs.values_in)
    load_shifted = loads.start(refs.shifted, refs.shifted_in)
    load_keys = loads.start(refs.keys, refs.keys_in)
    load_d_queries = loads.start(refs.d_queries, refs.qkv_right.at[:width, :])
    load_w_qkv = loads.start(refs.w_qkv.at[0], refs.qkv)
    load_normed = loads.start(refs.normed, refs.qkv_left)
    load_tokens = loads.start(refs.tokens, refs.tokens_in)
    pl.semaphore_wait(barrier, len(greeted))
    load_up_left.wait()
    load_up_right.wait()
    reducer.exchange(UP, (refs.up_left, refs.up_left_other), (refs.up_right, refs.up_right_other))
    load_out_left.wait()
    load_grad.wait()
    refs.out_right[...] = refs.grad_in[...].astype(jnp.bfloat16)
    reducer.exchange(
        OUT, (refs.out_left, refs.out_left_other), (refs.out_right, refs.out_right_other)
    )
    load_from_conv.wait()
    load_d_mixer.wait()
    load_values.wait()
    load_shifted.wait()
    valid = valid_positions(refs.lengths, seqs, span, 1)
    conv = jnp.concatenate([refs.conv_in[seq] for seq in range(seqs)], 1).astype(jnp.float32)
    d_carried = (refs.mixer_in[...] * refs.columns[:, 8:9] + conv) * valid
    d_shifted = d_carried * refs.values_in[...]
    refs.d_shifted[...] = d_shifted
    for seq in range(seqs):
        for first in range(0, width, span):
            turned = d_shifted[first : first + span, seq * span : (seq + 1) * span].T
            refs.rim_out[seq, :, first : first + span] = turned[: refs.rim_out.shape[1]]
    refs.qkv_right[2 * width :, :] = (d_carried * refs.shifted_in[...]).astype(jnp.bfloat16)
    halo = links.copy(refs.rim_out, refs.rim_in, before)
    load_mid.wait()
    for piece in given:
        reducer.third(piece)
    for piece in early:
        reducer.first(piece)
    saves = [loads.start(second, whole.at[1]) for whole, _, second in stacked]
    load_keys.wait()
    halo.wait_recv()
    lane = lax.broadcasted_iota(jnp.int32, (width, span), 1)
    there = jnp.where(me == n - 1, 0.0, 1.0)
    rim = refs.rim_in.shape[1]
    tap_sums = [jnp.zeros((width, 1), jnp.float32) for _ in range(TAPS)]
    for seq in range(seqs):
        lanes = slice(seq * span, (seq + 1) * span)
        own = refs.d_shifted[:, lanes]
        keys = refs.keys_in[:, lanes].astype(jnp.float32)
        turned = []
        for first in range(0, width, span):
            piece = refs.rim_in[seq, :, first : first + span] * there
            piece = jnp.concatenate([piece, jnp.zeros((span - rim, span), jnp.float32)], 0)
            turned.append(piece.T)
        following = jnp.concatenate(turned, 0)
        d_keys = jnp.zeros((width, span), jnp.float32)
        for offset in range(TAPS):
            moved = own
            if offset > 0:
                moved = jnp.where(
                    lane < span - offset,
                    pltpu.roll(own, span - offset, 1),
                    pltpu.roll(following, span - offset, 1),
                )
            d_keys = d_keys + refs.columns[:, 4 + offset : 5 + offset] * moved
            tap_sums[offset] = tap_sums[offset] + jnp.sum(moved * keys, 1, keepdims=True)
        refs.qkv_right[width : 2 * width, lanes] = d_keys.astype(jnp.bfloat16)
    load_d_queries.wait()
    load_normed.wait()
    reducer.exchange(QKV, (refs.qkv_left, refs.qkv_left_other), (refs.qkv_right, refs.qkv_right_other))
    load_w_qkv.wait()
    load_tokens.wait()
    d_normed = dot(refs.qkv[...], refs.qkv_right[...])
    for piece in pieces:
        reducer.first(piece)
    flat_in = jnp.concatenate(
        [refs.tokens_in[seq].astype(jnp.float32).T for seq in range(seqs)], 1
    )
    d_inputs, gain_part, bias_part = norm_gradient(flat_in * valid, refs.columns[:, 0:1], d_normed)
    refs.total[...] = (refs.grad_in[...] + d_inputs) * valid
    refs.sums[...] = refs.small_in[...]
    for offset in range(TAPS):
        refs.sums[:, 8 + offset : 9 + offset] = tap_sums[offset]
    refs.sums[:, 0:1] = gain_part
    refs.sums[:, 4:5] = bias_part
    shared = links.copy(refs.sums, refs.sums_other, reducer.sibling)
    for piece in early:
        reducer.second(piece)
    shared.wait_recv()
    rows = width // n
    turned = (refs.sums[...] + refs.sums_other[...]).T[:16]
    for place in range(n):
        start = place * rows // 128 * 128
        window = turned[:, start : min(start + 256, width)]
        away = (window.shape[1] - (place * rows - start)) % window.shape[1]
        refs.slices[place] = pltpu.roll(window, away, 1)[:, :128]
    depth = n // 4
    y, x = reducer.spot
    for outer in range(depth):
        for inner in range(2):
            refs.small_away[outer, inner] = refs.slices[outer * 4 + inner * 2 + 1 - x]
    small = links.copy(refs.small_away, refs.small_one, reducer.across[0])
    for seq in range(seqs):
        for first in range(0, width, span):
            refs.d_tokens[seq, :, first : first + span] = refs.total[
                first : first + span, seq * span : (seq + 1) * span
            ].T
    for piece in early[:2]:
        reducer.third(piece)
    for piece in given:
        reducer.fourth(piece, outs[piece.weight])
    small.wait_recv()
    for outer in range(depth):
        for inner in range(2):
            refs.small_one[outer, inner] += refs.slices[outer * 4 + inner * 2 + x]
    small = links.copy(refs.small_one.at[:, 1 - y], refs.small_two, reducer.across[1])
    for piece in early[2:]:
        reducer.third(piece)
    for piece in pieces:
        reducer.second(piece)
    small.wait_recv()
    for outer in range(depth):
        refs.small_two[outer] += refs.small_one[outer, y]
    smalls = [
        links.copy(refs.small_two.at[other], refs.small_three.at[step], reducer.column[step])
        for step, other in enumerate(reducer.levels)
    ]
    for piece in pieces:
        reducer.third(piece)
    for piece in early + pieces:
        reducer.fourth(piece, outs[piece.weight])
    total = refs.small_two[reducer.level]
    for step, copy in enumerate(smalls):
        copy.wait_recv()
        total = total + refs.small_three[step]
    refs.small_sum[...] = total[:, :rows]
    for piece in given + early + pieces:
        reducer.last(piece)
    saves += [loads.start(mine, whole.at[0]) for whole, mine, _ in stacked]
    for copy in saves:
        copy.wait()
    links.finish()


def back_three(
    from_conv, d_mixer, d_queries, values, shifted, keys, grad, tokens, normed, lengths, columns,
    small, w_qkv, mid, qkv_two, down_two, up_two, out_two, normed_two, d_raised, gated,
    collective,
):
    seqs, width, span = from_conv.shape
    n = normed.shape[0]
    tokens_here = seqs * span
    low, wide = jnp.bfloat16, jnp.float32
    hidden_width = up_two.shape[1]
    weights = gradient_weights(width, hidden_width, n)
    pieces = pieces_of(weights, BACK_THREE_FIRST + BACK_THREE_ORDER)
    inputs = dict(
        from_conv=(from_conv, HBM), d_mixer=(d_mixer, HBM), d_queries=(d_queries, HBM),
        values=(values, HBM), shifted=(shifted, HBM), keys=(keys, HBM), grad=(grad, HBM),
        tokens=(tokens, HBM), normed=(normed, HBM), lengths=(lengths, VMEM), columns=(columns, VMEM),
        small_in=(small, VMEM), w_qkv=(w_qkv, HBM),
        mid_in=(mid, HBM), qkv_two=(qkv_two, VMEM), down_two=(down_two, VMEM), up_two=(up_two, VMEM),
        out_two=(out_two, VMEM), normed_two=(normed_two, HBM), d_raised=(d_raised, HBM),
        gated=(gated, HBM),
    )
    square = (width, tokens_here)
    outputs = dict(
        d_tokens=((seqs, span, width), wide, VMEM),
        qkv_all=((2, *qkv_two.shape), wide, HBM), down_all=((2, *down_two.shape), wide, HBM),
        up_all=((2, *up_two.shape), wide, HBM), out_all=((2, *out_two.shape), wide, HBM),
        small_sum=((16, width // n), wide, VMEM),
    )
    scratch = dict(
        qkv=(w_qkv.shape[1:], low), qkv_left=(normed.shape, low), qkv_right=((3 * width, tokens_here), low),
        conv_in=(from_conv.shape, low), mixer_in=(square, wide), values_in=(square, values.dtype),
        shifted_in=(square, shifted.dtype), keys_in=(square, low), tokens_in=(tokens.shape, low),
        grad_in=(square, wide), d_shifted=(square, wide), total=(square, wide),
        rim_out=((seqs, 8, width), wide), rim_in=((seqs, 8, width), wide),
        sums=((width, 128), wide), sums_other=((width, 128), wide),
        slices=((n, 16, 128), wide),
        qkv_left_other=(normed.shape, low), qkv_right_other=((3 * width // 2, tokens_here), low),
        up_left=(normed_two.shape, low), up_left_other=(normed_two.shape, low),
        up_right=(d_raised.shape, low), up_right_other=((hidden_width // 2, tokens_here), low),
        out_left=(gated.shape, low), out_left_other=(gated.shape, low), out_right=(square, low),
        out_right_other=((width // 2, tokens_here), low),
        qkv_grad=(qkv_two.shape, wide), down_grad=(down_two.shape, wide),
        up_grad=(up_two.shape, wide), out_grad=(out_two.shape, wide),
        small_away=((n // 4, 2, 16, 128), wide), small_one=((n // 4, 2, 16, 128), wide),
        small_two=((n // 4, 16, 128), wide), small_three=((n // 4 - 1, 16, 128), wide),
        **reducer_scratch(weights, pieces, mid.shape[0] + len(pieces), n // 4, tokens_here),
    )
    body = functools.partial(back_three_body, n, seqs, span, width, hidden_width)
    return launch(body, inputs, outputs, scratch, 140, collective)


def earlier_rows(own, before, steps):
    if steps == 0:
        return own
    moved = pltpu.roll(own, steps, 0)
    rim = before.shape[0]
    row = lax.broadcasted_iota(jnp.int32, (rim, own.shape[1]), 0)
    front = jnp.where(row < steps, pltpu.roll(before, steps, 0), moved[:rim])
    return jnp.concatenate([front, moved[rim:]], 0)


def forward_body(n, seqs, groups, span, group_rows, width, hidden_width, refs):
    at = HeadPlaces(n, seqs, groups)
    me, core = at.me, at.core
    channels = width // n
    half, heads = n // 2, group_rows // HEAD
    tokens = seqs * span
    links, loads = Links(refs), Loads(refs)
    peers = [lax.rem(me + step, n) for step in range(1, n)]
    after = (lax.rem(me + 1, n), core)
    barrier = pltpu.get_barrier_semaphore()
    at.signal_all(barrier, [(peer, core) for peer in peers])
    outgoing = []

    def save(source, target):
        outgoing.append(loads.start(source, target))

    load_tokens = loads.start(refs.tokens, refs.tokens_in)
    load_qkv = loads.start(refs.w_qkv.at[0], refs.qkv)
    load_out = loads.start(refs.w_out.at[0], refs.out)
    load_up = loads.start(refs.w_up.at[0], refs.up)
    load_down = loads.start(refs.w_down.at[0], refs.down)

    def normed(value, row, target):
        result = layer_norm(value, refs.gains[row : row + 1], refs.biases[row : row + 1])
        result = result.astype(jnp.bfloat16)
        target[...] = result.T
        return result

    finish_rates = fill_rates(refs, loads, channels)
    valid = valid_positions(refs.lengths, seqs, span, 0)
    refs.columns[...] = jnp.concatenate(
        [refs.gains[...], refs.taps[...], refs.skip[...], jnp.zeros((7, width), jnp.float32)], 0
    ).T
    load_tokens.wait()
    flat_in = jnp.concatenate([refs.tokens_in[seq] for seq in range(seqs)], 0)
    flat_in = flat_in.astype(jnp.float32) * valid
    refs.flat_in[...] = flat_in
    normed_one = normed(flat_in, 0, refs.normed_one_t)
    load_qkv.wait()
    keys = dot(normed_one, refs.qkv[:, width : 2 * width]).astype(jnp.bfloat16)
    refs.keys[...] = keys
    rim = refs.rim_in.shape[1]
    at.wait_all(barrier, n - 1)
    for seq in range(seqs):
        refs.rim_out[seq] = refs.keys[(seq + 1) * span - rim : (seq + 1) * span, :]
    halo = links.copy(refs.rim_out, refs.rim_in, after)
    refs.values[...] = dot(normed_one, refs.qkv[:, 2 * width :])
    refs.queries[...] = dot(normed_one, refs.qkv[:, :width])
    load_qkv = loads.start(refs.w_qkv.at[1], refs.qkv)
    finish_rates()
    fill_tables(0, SHARE, span, refs)
    halo.wait_recv()
    there = jnp.where(me == 0, 0.0, 1.0)
    for seq in range(seqs):
        rows = slice(seq * span, (seq + 1) * span)
        before = refs.rim_in[seq].astype(jnp.float32) * there
        own = refs.keys[rows, :].astype(jnp.float32)
        shifted = jnp.zeros_like(own)
        for offset in range(TAPS):
            shifted = shifted + refs.taps[offset : offset + 1] * earlier_rows(own, before, offset)
        refs.shifted[rows, :] = shifted
        carried = (shifted * refs.values[rows, :] * valid[rows]).astype(jnp.bfloat16)
        refs.carried[rows, :] = carried
        refs.carried_t[seq] = carried.T

    shares = channels // SHARE
    arrive, answered = links.slots(shares * n), links.slots(shares * n)

    def share_rows(device, share):
        return pl.ds(pl.multiple_of(device * channels + share * SHARE, 16), SHARE)

    going, own_copies = [], []
    for share in range(shares):
        within = slice(share * SHARE, (share + 1) * SHARE)
        for step, peer in enumerate(peers):
            going.append(
                links.copy(
                    refs.carried_t.at[:, share_rows(peer, share), :],
                    refs.mixed_in.at[me, :, within, :], (peer, core), arrive + share * n + step,
                )
            )
        own_copies.append(
            loads.start(
                refs.carried_t.at[:, share_rows(me, share), :], refs.mixed_in.at[me, :, within, :]
            )
        )
    fill_tables(SHARE, channels, span, refs)
    for name in table_scratch(channels, span):
        save(getattr(refs, name), getattr(refs, name + KEPT))
    refs.square_t[...] = refs.values[...].T
    save(refs.square_t, refs.values_t)
    refs.square_two_t[...] = refs.shifted[...].T
    save(refs.square_two_t, refs.shifted_t)
    refs.keys_out[...] = refs.keys[...].T
    save(refs.keys_out, refs.keys_t)
    refs.queries_out[...] = refs.queries[...].T
    save(refs.queries_out, refs.queries_t)
    save(refs.normed_one_t, refs.normed_one)
    save(refs.carried_t, refs.carried_out)
    back, back_own = [], []
    for share in range(shares):
        within = slice(share * SHARE, (share + 1) * SHARE)
        own_copies[share].wait()
        for copy in going[share * len(peers) : (share + 1) * len(peers)]:
            copy.wait_recv()
        refs.flat_x[share] = (
            refs.mixed_in[:, :, within, :].astype(jnp.float32).reshape(n * seqs * SHARE, span)
        )

        def one_channel(local, carry):
            mixer_forward_channel(n, seqs, refs, share, local)
            return carry

        lax.fori_loop(0, SHARE, one_channel, 0, unroll=4)
        refs.answer[:, :, within, :] = (
            refs.flat_out[share].reshape(n, seqs, SHARE, span).astype(jnp.bfloat16)
        )
        for step, peer in enumerate(peers):
            back.append(
                links.copy(
                    refs.answer.at[peer, :, within, :],
                    refs.convolved.at[:, share_rows(me, share), :], (peer, core),
                    answered + share * n + step,
                )
            )
        back_own.append(
            loads.start(
                refs.answer.at[me, :, within, :], refs.convolved.at[:, share_rows(me, share), :]
            )
        )
    save(refs.mixed_in, refs.mixed_held)
    for copy in back_own:
        copy.wait()
    for copy in back:
        copy.wait_recv()
    for seq in range(seqs):
        rows = slice(seq * span, (seq + 1) * span)
        convolved = refs.convolved[seq].astype(jnp.float32).T
        mixer = convolved + refs.skip[...] * refs.carried[rows, :].astype(jnp.float32)
        refs.gated[rows, :] = (refs.queries[rows, :] * mixer).astype(jnp.bfloat16)
        refs.mixer_out[:, rows] = mixer.T
    save(refs.mixer_out, refs.mixer_t)
    refs.gated_out[...] = refs.gated[...].T
    save(refs.gated_out, refs.gated_t)
    load_out.wait()
    hidden = refs.flat_in[...] + dot(refs.gated[...], refs.out[...])
    load_out = loads.start(refs.w_out.at[1], refs.out)

    def feed_forward(hidden, row, hidden_out, normed_out, up, down):
        hidden_out[...] = hidden.T
        refs.hidden[...] = hidden
        refs.normed[...] = normed(hidden, row, normed_out)
        up.wait()

        def one_chunk(index, carry):
            columns = pl.ds(pl.multiple_of(index * width, 128), width)
            raised = dot(refs.normed[...], refs.up[:, columns])
            refs.raised[:, columns] = raised
            refs.active[:, columns] = jax.nn.gelu(raised).astype(jnp.bfloat16)
            return carry

        lax.fori_loop(0, hidden_width // width, one_chunk, 0)
        down.wait()
        return refs.hidden[...] + dot(refs.active[...], refs.down[...])

    def turn_hidden(active_out, slope_out):
        def one_chunk(index, carry):
            columns = pl.ds(pl.multiple_of(index * width, 128), width)
            active_out[columns, :] = refs.active[:, columns].T
            slope = gelu_slope(refs.raised[:, columns]).astype(jnp.bfloat16)
            slope_out[columns, :] = slope.T
            return carry

        lax.fori_loop(0, hidden_width // width, one_chunk, 0)

    hidden = feed_forward(
        hidden, 1, refs.hidden_one_t, refs.normed_two_t, load_up, load_down
    )
    load_up = loads.start(refs.w_up.at[1], refs.up)
    load_down = loads.start(refs.w_down.at[1], refs.down)
    refs.hidden[...] = hidden
    refs.normed[...] = normed(hidden, 2, refs.normed_three_t)
    load_qkv.wait()
    for part in range(3):
        columns = dot(refs.normed[...], refs.qkv[:, part * width : (part + 1) * width])
        columns = columns.astype(jnp.bfloat16)
        for seq in range(seqs):
            turned = columns[seq * span : (seq + 1) * span].T
            for head in range(groups * heads):
                refs.spread[head % heads, seq, head // heads, part * HEAD : (part + 1) * HEAD] = (
                    turned[head * HEAD : (head + 1) * HEAD]
                )

    count = len(at.targets)
    arrive, leave = links.slots(heads * half), links.slots(heads * count)
    passing = links.slots(heads * half)
    spread = []
    for head in range(heads):
        for number, (device, seq, group) in enumerate(at.targets):
            sent = (
                refs.spread.at[head, seq, group], refs.held.at[head, me],
                refs.send.at[leave + head * count + number],
                refs.recv.at[arrive + head * half + me // 2], device,
            )
            at.send(*sent)
            spread.append(sent)
    turn_hidden(refs.active_one_t, refs.slope_one_t)
    refs.hidden_two_t[...] = hidden.T
    for source, target in (
        (refs.hidden_one_t, refs.hidden_one_out), (refs.normed_two_t, refs.normed_two),
        (refs.active_one_t, refs.active_one), (refs.slope_one_t, refs.slope_one),
        (refs.hidden_two_t, refs.hidden_two_out), (refs.normed_three_t, refs.normed_three),
    ):
        save(source, target)

    returned, returning = links.slots(heads * count), links.slots(heads * half)
    slot = at.seq * groups + at.group
    going = []

    def gather(head):
        for index, block in enumerate(at.blocks):
            landed = refs.held.at[head, block]
            remote(
                landed, landed, refs.send.at[leave], refs.recv.at[arrive + head * half + index],
                at.sibling,
            ).wait_recv()
            part = refs.held.at[head, block, HEAD : 3 * HEAD]
            links.copy(part, part, at.sibling, passing + head * half + index)
        for index in range(half):
            part = refs.held.at[head, block_of(index, 1 - core), HEAD : 3 * HEAD]
            remote(
                part, part, refs.send.at[leave], refs.recv.at[passing + head * half + index],
                at.sibling,
            ).wait_recv()

    def attend(head):
        fill_head(refs.held, head, 1, n, span, refs.key_rows, None)
        fill_head(refs.held, head, 2, n, span, None, refs.value_columns)
        for index, block in enumerate(at.blocks):
            query = refs.held[head, block, :HEAD, :] * jnp.bfloat16(HEAD**-0.5)
            clear, reach = 2 * index * span, 2 * (index + 1) * span
            edge = dot(refs.key_rows[clear:reach, :], query)
            edge = jnp.where(causal(clear, reach - clear, block * span, span), edge, masked_score)
            top = jnp.max(edge, 0, keepdims=True)
            if index > 0:
                body = dot(refs.key_rows[:clear, :], query)
                top = jnp.maximum(top, jnp.max(body, 0, keepdims=True))
            edge = jnp.exp(edge - top)
            total = jnp.sum(edge, 0, keepdims=True)
            result = dot(refs.value_columns[:, clear:reach], edge.astype(jnp.bfloat16))
            if index > 0:
                body = jnp.exp(body - top)
                total = total + jnp.sum(body, 0, keepdims=True)
                result = result + dot(refs.value_columns[:, :clear], body.astype(jnp.bfloat16))
            refs.outputs[head, index] = (result / total).astype(jnp.bfloat16)
            refs.lse[index, head : head + 1, :] = top + jnp.log(total)
        into = refs.attended_t.at[
            pl.ds(pl.multiple_of(at.group * group_rows + head * HEAD, HEAD), HEAD),
            pl.ds(pl.multiple_of(at.seq * span, span), span),
        ]
        for index, device in enumerate(at.sources):
            sent = (
                refs.outputs.at[head, index], into, refs.send.at[returning + head * half + index],
                refs.recv.at[returned + head * count + slot], device,
            )
            at.send(*sent)
            going.append(sent)

    for head in range(heads):
        gather(head)
        attend(head)
    save(refs.held, refs.held_out)
    for head in range(heads):
        for number, (device, seq, group) in enumerate(at.targets):
            first = group * group_rows + head * HEAD
            landed = refs.attended_t.at[first : first + HEAD, seq * span : (seq + 1) * span]
            remote(
                landed, landed, refs.send.at[leave],
                refs.recv.at[returned + head * count + number], at.sibling,
            ).wait_recv()
    save(refs.attended_t, refs.attended)
    load_out.wait()
    hidden = refs.hidden[...] + dot(refs.attended_t[...].T, refs.out[...])
    hidden = feed_forward(
        hidden, 3, refs.hidden_three_t, refs.normed_four_t, load_up, load_down
    )
    turn_hidden(refs.active_two_t, refs.slope_two_t)
    for source, target in (
        (refs.hidden_three_t, refs.hidden_three_out), (refs.normed_four_t, refs.normed_four),
        (refs.active_two_t, refs.active_two), (refs.slope_two_t, refs.slope_two),
    ):
        save(source, target)
    hidden = (hidden * valid).astype(jnp.bfloat16)
    for seq in range(seqs):
        refs.mixed[seq] = hidden[seq * span : (seq + 1) * span]
    for copy in outgoing:
        copy.wait()
    for sent in spread + going:
        at.wait_sent(*sent)
    links.finish()


def forward(
    tokens, lengths, gains, biases, taps, skip, rates, rate_weights, w_qkv, w_out, w_up, w_down, n,
    groups, collective,
):
    seqs, span, width = tokens.shape
    hidden_width = w_up.shape[2]
    group_rows, channels = width // groups, width // n
    rows = seqs * span
    half, heads = n // 2, group_rows // HEAD
    low, wide = jnp.bfloat16, jnp.float32
    inputs = dict(
        tokens=(tokens, HBM), lengths=(lengths, VMEM), gains=(gains, VMEM), biases=(biases, VMEM),
        taps=(taps, VMEM), skip=(skip, VMEM), all_rates=(rates, HBM), all_weights=(rate_weights, HBM),
        w_qkv=(w_qkv, HBM), w_out=(w_out, HBM), w_up=(w_up, HBM), w_down=(w_down, HBM),
    )
    square, tall, by_head = (width, rows), (hidden_width, rows), (heads, n, 3 * HEAD, span)
    mixed = (n, seqs, channels, span)
    outputs = dict(
        mixed=((seqs, span, width), low, VMEM), columns=((width, 16), wide, VMEM),
        lse=((half, heads, span), wide, VMEM),
        held_out=(by_head, low, HBM), mixed_held=(mixed, low, HBM),
        carried_out=((seqs, width, span), low, HBM),
        values_t=(square, wide, HBM), shifted_t=(square, wide, HBM), keys_t=(square, low, HBM),
        queries_t=(square, wide, HBM), mixer_t=(square, wide, HBM), gated_t=(square, low, HBM),
        attended=(square, low, HBM),
        normed_one=(square, low, HBM), normed_two=(square, low, HBM),
        normed_three=(square, low, HBM), normed_four=(square, low, HBM),
        hidden_one_out=(square, wide, HBM), hidden_two_out=(square, wide, HBM),
        hidden_three_out=(square, wide, HBM),
        active_one=(tall, low, HBM), active_two=(tall, low, HBM),
        slope_one=(tall, low, HBM), slope_two=(tall, low, HBM),
        **{
            name + KEPT: (*shape, HBM) for name, shape in table_scratch(channels, span).items()
        },
    )
    flat = (channels // SHARE, n * seqs * SHARE, span)
    lying = (rows, width)
    scratch = dict(
        qkv=(w_qkv.shape[1:], low), out=(w_out.shape[1:], low), up=(w_up.shape[1:], low),
        down=(w_down.shape[1:], low), tokens_in=(tokens.shape, low), flat_in=(lying, wide),
        keys=(lying, low), values=(lying, wide), queries=(lying, wide), shifted=(lying, wide),
        carried=(lying, low), gated=(lying, low), hidden=(lying, wide), normed=(lying, low),
        active=((rows, hidden_width), low), rim_in=((seqs, 16, width), low),
        rim_out=((seqs, 16, width), low), carried_t=((seqs, width, span), low),
        convolved=((seqs, width, span), low), mixed_in=(mixed, low), answer=(mixed, low),
        flat_x=(flat, wide), flat_out=(flat, wide), **table_scratch(channels, span),
        **rate_scratch(channels), raised=((rows, hidden_width), wide),
        square_t=(square, wide), square_two_t=(square, wide), keys_out=(square, low),
        queries_out=(square, wide), mixer_out=(square, wide), gated_out=(square, low),
        attended_t=(square, low), normed_one_t=(square, low), normed_two_t=(square, low),
        normed_three_t=(square, low), normed_four_t=(square, low), hidden_one_t=(square, wide),
        hidden_two_t=(square, wide), hidden_three_t=(square, wide), active_one_t=(tall, low),
        active_two_t=(tall, low), slope_one_t=(tall, low), slope_two_t=(tall, low),
        spread=((heads, seqs, groups, 3 * HEAD, span), low), held=(by_head, low),
        outputs=((heads, half, HEAD, span), low), key_rows=((n * span, HEAD), low),
        value_columns=((HEAD, n * span), low),
    )
    body = functools.partial(
        forward_body, n, seqs, groups, span, group_rows, width, hidden_width
    )
    return launch(body, inputs, outputs, scratch, 290, collective)


def per_device_by_heads(
    tokens,
    cotangent,
    lengths,
    norm_gain,
    norm_bias,
    w_qkv,
    w_out,
    w_up,
    w_down,
    taps,
    skip,
    ssm_rate,
    ssm_out,
):
    seq_count, span_rows, width = tokens.shape[1:]
    devices = lax.axis_size(SEQ)
    channels = width // devices
    groups = devices // 4
    row_count = seq_count * span_rows
    kept = forward(
        tokens[0], lengths, norm_gain, norm_bias, taps, skip[None], ssm_rate, ssm_out, w_qkv, w_out,
        w_up, w_down, devices, groups, 1,
    )

    def sliced(value):
        return value.reshape(devices, value.shape[0] // devices, row_count)

    back = back_one(
        cotangent[0], lengths, kept.hidden_three_out, kept.slope_two, sliced(kept.normed_four),
        sliced(kept.active_two), sliced(kept.attended), kept.held_out, kept.lse, kept.columns,
        w_out, w_up, w_down, 3,
    )
    tables = {
        name: getattr(kept, name + KEPT) for name in table_scratch(channels, span_rows)
    }
    more = back_two(
        tables, back.mid_out, back.d_qkv.reshape(3 * width, row_count), back.grad_out, kept.hidden_two_out,
        sliced(kept.normed_three), kept.slope_one, sliced(kept.normed_two),
        sliced(kept.active_one), kept.hidden_one_out, kept.queries_t,
        kept.mixer_t, kept.carried_out, kept.mixed_held, kept.columns, back.small, ssm_rate, ssm_out, w_qkv, w_out, w_up,
        w_down, 4,
    )
    end = back_three(
        more.from_conv, more.d_mixer, more.d_queries, kept.values_t, kept.shifted_t, kept.keys_t,
        more.grad_out, tokens[0], sliced(kept.normed_one), lengths, kept.columns, more.small,
        w_qkv, more.mid_out, more.qkv_grad, more.down_grad, more.up_grad,
        more.out_grad, sliced(kept.normed_two), more.d_raised, sliced(kept.gated_t), 5,
    )
    small = end.small_sum
    return (
        kept.mixed[None],
        end.d_tokens[None],
        small[:4],
        small[4:7],
        small[7],
        end.qkv_all,
        end.out_all,
        end.up_all,
        end.down_all,
        small[8 : 8 + TAPS],
        small[8 + TAPS],
        more.rate_sum,
        more.weight_sum,
    )


def fits_by_heads(mesh):
    devices = mesh.shape[SEQ]
    return devices == 16 and mesh.shape[BATCH] == 2


def solution(mesh):
    placed = (
        P(BATCH, None, SEQ, None),
        P(BATCH, None, SEQ, None),
        P(BATCH, None),
        P(),
        P(),
        P(),
        P(),
        P(),
        P(),
        P(),
        P(),
        P(),
        P(),
    )
    return jax.shard_map(
        per_device_by_heads if fits_by_heads(mesh) else per_device,
        mesh=mesh,
        in_specs=placed,
        out_specs=(
            P(BATCH, None, SEQ, None),
            P(BATCH, None, SEQ, None),
            P(None, SEQ),
            P(None, SEQ),
            P(SEQ),
            P(None, SEQ, None),
            P(None, SEQ, None),
            P(None, SEQ, None),
            P(None, SEQ, None),
            P(None, SEQ),
            P(SEQ),
            P(SEQ, None),
            P(SEQ, None),
        ),
        check_vma=False,
    )
```

```python
import functools
import math
import types

import jax
import jax.numpy as jnp
from jax import lax
from jax.experimental import pallas as pl
from jax.experimental.pallas import tpu as pltpu
from jax.sharding import PartitionSpec as P

HEADS = 12
HEAD = 64
TAPS = 4
STATES = 64
KEPT = "_kept"
ONE = "_one"
TWO = "_two"
FIRST = "first"
MESH = pl.DeviceIdType.MESH
SEQ = "seq"
BATCH = "batch"
QKV_MORE = "qkv_more"
QKV_LESS = "qkv_less"
DOWN = "down"
OUT = "out"
UP = "up"
QKV = "qkv"
SMALL = "small"
VMEM_BYTES = 63 * 2**20


norm_eps = 1e-05
highest = lax.Precision.HIGHEST
masked_score = -1e30


def for_sending(array):
    return jax.tree.map(lambda a: a.astype(jnp.bfloat16) if a.dtype == jnp.float32 else a, array)


def passed_along(value, axis, steps):
    count = lax.axis_size(axis)
    initial, last = (max(0, -steps), min(count, count - steps))
    return lax.ppermute(value, axis, [(source, source + steps) for source in range(initial, last)])


def layer_norm(inputs, scale_row, shift_row):
    center = inputs - jnp.mean(inputs, -1, keepdims=True)
    spread = jnp.mean(center * center, -1, keepdims=True)
    return center * lax.rsqrt(spread + norm_eps) * scale_row + shift_row


def dense_product(operand_a, operand_b):
    return jnp.dot(operand_a, operand_b, preferred_element_type=jnp.float32)


def product_left(operand_a, operand_b):
    return lax.dot_general(
        operand_a, operand_b, (((0,), (0,)), ((), ())), preferred_element_type=jnp.float32
    )


def product_right(operand_a, operand_b):
    return lax.dot_general(
        operand_a, operand_b, (((1,), (1,)), ((), ())), preferred_element_type=jnp.float32
    )


def angle_table(count_rows, count_cols, period):
    product_index = (
        jnp.arange(count_rows, dtype=jnp.int32)[:, None]
        * jnp.arange(count_cols, dtype=jnp.int32)[None, :]
        % period
    )
    angles = product_index.astype(jnp.float32) * (2.0 * math.pi / period)
    return (jnp.cos(angles), jnp.sin(angles))


def table_einsum(form, table, data):
    return jnp.einsum(form, table, data, precision=highest)


def forward_spectrum(time_parts):
    count_parts = time_parts.shape[0]
    span_rows = time_parts.shape[2]
    count_freq = 2 * count_parts
    cos_parts, sin_parts = angle_table(count_freq, count_parts, count_freq)
    first_real = table_einsum("fp,pjsc->fjsc", cos_parts, time_parts)
    first_imag = -table_einsum("fp,pjsc->fjsc", sin_parts, time_parts)
    cos_twist, sin_twist = angle_table(count_freq, span_rows, count_freq * span_rows)
    cos_twist = cos_twist[:, None, :, None]
    sin_twist = sin_twist[:, None, :, None]
    twist_real = first_real * cos_twist + first_imag * sin_twist
    twist_imag = first_imag * cos_twist - first_real * sin_twist
    cos_span, sin_span = angle_table(span_rows, span_rows, span_rows)
    out_real = table_einsum("ts,fjsc->fjtc", cos_span, twist_real) + table_einsum(
        "ts,fjsc->fjtc", sin_span, twist_imag
    )
    out_imag = table_einsum("ts,fjsc->fjtc", cos_span, twist_imag) - table_einsum(
        "ts,fjsc->fjtc", sin_span, twist_real
    )
    return (out_real, out_imag)


def inverse_spectrum(freq_real, freq_imag):
    count_freq = freq_real.shape[0]
    span_rows = freq_real.shape[2]
    count_parts = count_freq // 2
    fft_length = count_freq * span_rows
    cos_span, sin_span = angle_table(span_rows, span_rows, span_rows)
    first_real = table_einsum("st,fjtc->fjsc", cos_span, freq_real) - table_einsum(
        "st,fjtc->fjsc", sin_span, freq_imag
    )
    first_imag = table_einsum("st,fjtc->fjsc", cos_span, freq_imag) + table_einsum(
        "st,fjtc->fjsc", sin_span, freq_real
    )
    cos_twist, sin_twist = angle_table(count_freq, span_rows, fft_length)
    cos_twist = cos_twist[:, None, :, None]
    sin_twist = sin_twist[:, None, :, None]
    twist_real = first_real * cos_twist - first_imag * sin_twist
    twist_imag = first_imag * cos_twist + first_real * sin_twist
    cos_parts, sin_parts = angle_table(count_parts, count_freq, count_freq)
    summed = table_einsum("pf,fjsc->pjsc", cos_parts, twist_real) - table_einsum(
        "pf,fjsc->pjsc", sin_parts, twist_imag
    )
    return summed / fft_length


def to_frequency(data_low):
    parts = lax.all_to_all(data_low[None], SEQ, split_axis=3, concat_axis=0, tiled=True)
    return forward_spectrum(parts.astype(jnp.float32))


def from_frequency(freq_real, freq_imag):
    time_parts = inverse_spectrum(freq_real, freq_imag)
    joined = lax.all_to_all(
        for_sending(time_parts), SEQ, split_axis=0, concat_axis=3, tiled=True
    ).astype(time_parts.dtype)
    return joined[0]


def kernel_parts(rate_slice, weight_slice, count_freq, span_rows):
    fft_length = count_freq * span_rows
    length_full = fft_length // 2
    frequency = (
        jnp.arange(count_freq, dtype=jnp.int32)[:, None]
        + count_freq * jnp.arange(span_rows, dtype=jnp.int32)[None, :]
    )
    angles = (frequency.astype(jnp.float32) * (2.0 * math.pi / fft_length))[:, None, :, None, None]
    odd_mask = (frequency % 2 == 1)[:, None, :, None, None]
    channels = rate_slice.shape[0]
    blocks = rate_slice.shape[1] // 8
    rate_blocks = rate_slice.reshape(channels, blocks, 8).transpose(1, 0, 2)
    weight_blocks = weight_slice.reshape(channels, blocks, 8).transpose(1, 0, 2)

    def add_block(running, piece_pair):
        rate_part, weight_part = piece_pair
        decays = jnp.exp(-rate_part)
        half_sine = jnp.sin(angles / 2.0)
        real_den = -jnp.expm1(-rate_part) + decays * 2.0 * half_sine * half_sine
        imag_den = decays * jnp.sin(angles)
        numerator = jnp.where(
            odd_mask, 1.0 + jnp.exp(-rate_part * length_full), -jnp.expm1(-rate_part * length_full)
        )
        factor = weight_part * numerator / (real_den * real_den + imag_den * imag_den)
        return (
            (
                running[0] + jnp.sum(factor * real_den, -1),
                running[1] - jnp.sum(factor * imag_den, -1),
            ),
            None,
        )

    zeros_init = jnp.zeros((count_freq, 1, span_rows, channels), jnp.float32)
    return lax.scan(
        jax.checkpoint(add_block), (zeros_init, zeros_init), (rate_blocks, weight_blocks)
    )[0]


def attention_mask(query_positions, key_count, length_value):
    key_positions = jnp.arange(key_count, dtype=jnp.int32)
    return (key_positions[None, :] <= query_positions[:, None]) & (
        key_positions[None, :] < length_value
    )


def head_slice(matrix, head_index):
    return lax.dynamic_slice_in_dim(matrix, head_index * HEAD, HEAD, 1)


def attend_forward(query_low, keys_low, values_low, length_value, query_positions):
    whole_keys, whole_values = (
        lax.all_gather(keys_low, SEQ, axis=0, tiled=True),
        lax.all_gather(values_low, SEQ, axis=0, tiled=True),
    )
    allowed = attention_mask(query_positions, whole_keys.shape[0], length_value)
    score_scale = HEAD ** (-0.5)

    def head_forward(head_index):
        scores = jnp.where(
            allowed,
            score_scale
            * product_right(head_slice(query_low, head_index), head_slice(whole_keys, head_index)),
            masked_score,
        )
        top_score = jnp.max(scores, -1, keepdims=True)
        expos = jnp.exp(scores - top_score)
        totals = jnp.sum(expos, -1, keepdims=True)
        probs_low = (expos / totals).astype(jnp.bfloat16)
        return (
            dense_product(probs_low, head_slice(whole_values, head_index)),
            (top_score + jnp.log(totals))[:, 0],
        )

    head_outputs, log_totals = lax.map(head_forward, jnp.arange(HEADS, dtype=jnp.int32))
    attended = head_outputs.transpose(1, 0, 2).reshape(query_low.shape[0], HEADS * HEAD)
    return (attended, log_totals, whole_keys, whole_values)


def join_heads(head_rows):
    return head_rows.transpose(1, 0, 2).reshape(head_rows.shape[1], HEADS * HEAD)


def attend_backward(
    query_low, whole_keys, whole_values, log_totals, grad_low, length_value, query_positions
):
    allowed = attention_mask(query_positions, whole_keys.shape[0], length_value)
    score_scale = HEAD ** (-0.5)
    span_rows = query_low.shape[0]

    def query_side(head_index):
        head_query = head_slice(query_low, head_index)
        head_keys = head_slice(whole_keys, head_index)
        head_grad = head_slice(grad_low, head_index)
        scores = jnp.where(
            allowed, score_scale * product_right(head_query, head_keys), masked_score
        )
        weights = jnp.exp(scores - log_totals[head_index][:, None])
        d_weights = product_right(head_grad, head_slice(whole_values, head_index))
        row_term = jnp.sum(weights * d_weights, -1, keepdims=True)
        d_scores = (weights * (d_weights - row_term)).astype(jnp.bfloat16)
        d_query = score_scale * dense_product(d_scores, head_keys)
        return (d_query, row_term[:, 0], d_scores, weights)

    def head_backward(head_index):
        d_query, row_term, d_scores, weights = query_side(head_index)
        head_query = head_slice(query_low, head_index)
        head_grad = head_slice(grad_low, head_index)
        d_keys = score_scale * product_left(d_scores, head_query)
        d_values = product_left(weights.astype(jnp.bfloat16), head_grad)
        return (d_query, d_keys, d_values)

    query_grads, key_grads, value_grads = lax.map(head_backward, jnp.arange(HEADS, dtype=jnp.int32))
    count_rows = span_rows * lax.axis_size(SEQ)
    key_part = (
        lax.slice_in_dim(key_grads, 0, count_rows, axis=1)
        .transpose(1, 0, 2)
        .reshape(count_rows, HEADS * HEAD)
    )
    value_part = (
        lax.slice_in_dim(value_grads, 0, count_rows, axis=1)
        .transpose(1, 0, 2)
        .reshape(count_rows, HEADS * HEAD)
    )
    key_value = lax.psum_scatter(
        jnp.stack([key_part, value_part], 1), SEQ, scatter_dimension=0, tiled=True
    )
    return (join_heads(query_grads), key_value[:, 0], key_value[:, 1])


def per_device(
    tokens,
    cotangent,
    lengths,
    norm_gain,
    norm_bias,
    w_qkv,
    w_out,
    w_up,
    w_down,
    taps,
    skip,
    ssm_rate,
    ssm_out,
):
    seq_count = tokens.shape[1]
    span_rows = tokens.shape[2]
    width = tokens.shape[3]
    devices = lax.axis_size(SEQ)
    place = lax.axis_index(SEQ)
    channels = width // devices
    count_freq = 2 * devices
    fft_length = count_freq * span_rows
    rim = TAPS - 1
    row_count = seq_count * span_rows
    query_positions = place * span_rows + jnp.arange(span_rows, dtype=jnp.int32)
    validity = (query_positions[None, :] < lengths[0][:, None]).astype(jnp.float32)[:, :, None]
    rate_slice = lax.dynamic_slice_in_dim(ssm_rate, place * channels, channels, 0)
    weight_slice = lax.dynamic_slice_in_dim(ssm_out, place * channels, channels, 0)

    def spectrum_of(rate_in, weight_in):
        return kernel_parts(rate_in, weight_in, count_freq, span_rows)

    def feed_forward(inputs, norm_row, layer):
        normed_low = layer_norm(inputs, norm_gain[norm_row], norm_bias[norm_row]).astype(
            jnp.bfloat16
        )
        raised = dense_product(normed_low, w_up[layer])
        active_low = jax.nn.gelu(raised).astype(jnp.bfloat16)
        return (normed_low, raised, active_low, inputs + dense_product(active_low, w_down[layer]))

    def norm_backward(inputs, norm_row, d_normed):
        norm_pull = jax.vjp(layer_norm, inputs, norm_gain[norm_row], norm_bias[norm_row])[1]
        return norm_pull(d_normed)

    def feed_backward(grad_rows, inputs, normed_low, raised, active_low, norm_row, layer):
        branch_low = grad_rows.astype(jnp.bfloat16)
        down_grad = product_left(active_low, branch_low)
        d_active = product_right(branch_low, w_down[layer])
        gelu_pull = jax.vjp(jax.nn.gelu, raised)[1]
        d_raised = gelu_pull(d_active)[0].astype(jnp.bfloat16)
        up_grad = product_left(normed_low, d_raised)
        d_inputs, gain_part, bias_part = norm_backward(
            inputs, norm_row, product_right(d_raised, w_up[layer])
        )
        return (grad_rows + d_inputs, down_grad, up_grad, gain_part, bias_part)

    def forward_pass(token_block):
        masked_in = token_block[0].astype(jnp.float32) * validity
        flat_in = masked_in.reshape(row_count, width)
        normed_one = layer_norm(flat_in, norm_gain[0], norm_bias[0]).astype(jnp.bfloat16)
        qkv_one = dense_product(normed_one, w_qkv[0]).reshape(seq_count, span_rows, 3 * width)
        queries_one = qkv_one[:, :, :width]
        keys_one = qkv_one[:, :, width : 2 * width].astype(jnp.bfloat16)
        values_one = qkv_one[:, :, 2 * width :]
        earlier = passed_along(keys_one[:, span_rows - rim :], SEQ, 1)
        extended = jnp.concatenate([earlier, keys_one], 1)
        shifted = sum(
            (
                taps[offset]
                * extended[:, rim - offset : rim - offset + span_rows].astype(jnp.float32)
                for offset in range(TAPS)
            )
        )
        carried_low = (shifted * values_one * validity).astype(jnp.bfloat16)
        carried_real, carried_imag = to_frequency(carried_low)
        kernel_both, kernel_pull = jax.vjp(spectrum_of, rate_slice, weight_slice)
        kernel_real, kernel_imag = kernel_both
        convolved = from_frequency(
            carried_real * kernel_real - carried_imag * kernel_imag,
            carried_real * kernel_imag + carried_imag * kernel_real,
        )
        carried = carried_low.astype(jnp.float32)
        mixer = convolved + skip * carried
        gated_low = (queries_one * mixer).reshape(row_count, width).astype(jnp.bfloat16)
        hidden_one = flat_in + dense_product(gated_low, w_out[0])
        normed_two, raised_one, active_one, hidden_two = feed_forward(hidden_one, 1, 0)
        normed_three = layer_norm(hidden_two, norm_gain[2], norm_bias[2]).astype(jnp.bfloat16)
        qkv_two = (
            dense_product(normed_three, w_qkv[1])
            .astype(jnp.bfloat16)
            .reshape(seq_count, span_rows, 3 * width)
        )
        attended_list = []
        totals_list = []
        keys_list = []
        values_list = []
        for seq_index in range(seq_count):
            attended, log_totals, whole_keys, whole_values = attend_forward(
                qkv_two[seq_index, :, :width],
                qkv_two[seq_index, :, width : 2 * width],
                qkv_two[seq_index, :, 2 * width :],
                lengths[0, seq_index],
                query_positions,
            )
            attended_list.append(attended)
            totals_list.append(log_totals)
            keys_list.append(whole_keys)
            values_list.append(whole_values)
        attended_low = jnp.concatenate(attended_list, 0).astype(jnp.bfloat16)
        hidden_three = hidden_two + dense_product(attended_low, w_out[1])
        normed_four, raised_two, active_two, hidden_four = feed_forward(hidden_three, 3, 1)
        output = hidden_four.reshape(seq_count, span_rows, width) * validity
        saved = types.SimpleNamespace(
            flat_in=flat_in,
            normed_one=normed_one,
            queries_one=queries_one,
            values_one=values_one,
            extended=extended,
            shifted=shifted,
            carried=carried,
            carried_real=carried_real,
            carried_imag=carried_imag,
            kernel_real=kernel_real,
            kernel_imag=kernel_imag,
            kernel_pull=kernel_pull,
            mixer=mixer,
            gated_low=gated_low,
            hidden_one=hidden_one,
            normed_two=normed_two,
            raised_one=raised_one,
            active_one=active_one,
            hidden_two=hidden_two,
            normed_three=normed_three,
            qkv_two=qkv_two,
            totals_list=totals_list,
            keys_list=keys_list,
            values_list=values_list,
            attended_low=attended_low,
            hidden_three=hidden_three,
            normed_four=normed_four,
            raised_two=raised_two,
            active_two=active_two,
        )
        return (output, saved)

    output = forward_pass(tokens)[0]
    saved = forward_pass(lax.optimization_barrier(tokens))[1]
    grad_rows = (cotangent[0].astype(jnp.float32) * validity).reshape(row_count, width)
    grad_rows, down_two, up_two, gain_four, bias_four = feed_backward(
        grad_rows,
        saved.hidden_three,
        saved.normed_four,
        saved.raised_two,
        saved.active_two,
        3,
        1,
    )
    branch_low = grad_rows.astype(jnp.bfloat16)
    out_two = product_left(saved.attended_low, branch_low)
    d_attended = (
        product_right(branch_low, w_out[1])
        .astype(jnp.bfloat16)
        .reshape(seq_count, span_rows, width)
    )
    qkv_two = saved.qkv_two
    grad_parts = []
    for seq_index in range(seq_count):
        d_query_rows, d_key_rows, d_value_rows = attend_backward(
            qkv_two[seq_index, :, :width],
            saved.keys_list[seq_index],
            saved.values_list[seq_index],
            saved.totals_list[seq_index],
            d_attended[seq_index],
            lengths[0, seq_index],
            query_positions,
        )
        grad_parts.append(jnp.concatenate([d_query_rows, d_key_rows, d_value_rows], -1))
    d_qkv_two = jnp.concatenate(grad_parts, 0).astype(jnp.bfloat16)
    qkv_grad_two = product_left(saved.normed_three, d_qkv_two)
    d_inputs, gain_three, bias_three = norm_backward(
        saved.hidden_two, 2, product_right(d_qkv_two, w_qkv[1])
    )
    grad_rows = grad_rows + d_inputs
    grad_rows, down_one, up_one, gain_two, bias_two = feed_backward(
        grad_rows,
        saved.hidden_one,
        saved.normed_two,
        saved.raised_one,
        saved.active_one,
        1,
        0,
    )
    branch_low = grad_rows.astype(jnp.bfloat16)
    out_one = product_left(saved.gated_low, branch_low)
    d_gated = product_right(branch_low, w_out[0]).reshape(seq_count, span_rows, width)
    d_queries = d_gated * saved.mixer
    d_mixer = d_gated * saved.queries_one
    skip_grad = jnp.sum(d_mixer * saved.carried, (0, 1))
    conv_real, conv_imag = to_frequency(d_mixer.astype(jnp.bfloat16))
    kernel_real = saved.kernel_real
    kernel_imag = saved.kernel_imag
    from_conv = from_frequency(
        kernel_real * conv_real + kernel_imag * conv_imag,
        kernel_real * conv_imag - kernel_imag * conv_real,
    )
    d_carried = d_mixer * skip + from_conv
    carried_real = saved.carried_real
    carried_imag = saved.carried_imag
    cot_real = (
        jnp.sum(carried_real * conv_real + carried_imag * conv_imag, 1, keepdims=True) / fft_length
    )
    cot_imag = (
        jnp.sum(carried_real * conv_imag - carried_imag * conv_real, 1, keepdims=True) / fft_length
    )
    rate_grad, weight_grad = saved.kernel_pull((cot_real, cot_imag))
    d_shifted = d_carried * saved.values_one * validity
    d_values = d_carried * saved.shifted * validity
    extended = saved.extended
    grads_extended = sum(
        (
            jnp.pad(taps[offset] * d_shifted, ((0, 0), (rim - offset, offset), (0, 0)))
            for offset in range(TAPS)
        )
    )
    taps_grad = jnp.stack(
        [
            jnp.sum(
                d_shifted
                * extended[:, rim - offset : rim - offset + span_rows].astype(jnp.float32),
                (0, 1),
            )
            for offset in range(TAPS)
        ]
    )
    later = passed_along(grads_extended[:, :rim], SEQ, -1)
    d_keys = grads_extended[:, rim:] + jnp.pad(later, ((0, 0), (span_rows - rim, 0), (0, 0)))
    d_qkv_one = (
        jnp.concatenate([d_queries, d_keys, d_values], -1)
        .reshape(row_count, 3 * width)
        .astype(jnp.bfloat16)
    )
    qkv_grad_one = product_left(saved.normed_one, d_qkv_one)
    d_inputs, gain_one, bias_one = norm_backward(
        saved.flat_in, 0, product_right(d_qkv_one, w_qkv[0])
    )
    d_tokens = ((grad_rows + d_inputs).reshape(seq_count, span_rows, width) * validity)[None]
    gain_sum, bias_sum, qkv_sum, out_sum, up_sum, down_sum, taps_sum, skip_sum = (
        lax.psum_scatter(
            jnp.stack([gain_one, gain_two, gain_three, gain_four]),
            SEQ,
            scatter_dimension=1,
            tiled=True,
        ),
        lax.psum_scatter(
            jnp.stack([bias_one, bias_two, bias_three, bias_four]),
            SEQ,
            scatter_dimension=1,
            tiled=True,
        ),
        lax.psum_scatter(
            jnp.stack([qkv_grad_one, qkv_grad_two]), SEQ, scatter_dimension=1, tiled=True
        ),
        lax.psum_scatter(jnp.stack([out_one, out_two]), SEQ, scatter_dimension=1, tiled=True),
        lax.psum_scatter(jnp.stack([up_one, up_two]), SEQ, scatter_dimension=1, tiled=True),
        lax.psum_scatter(jnp.stack([down_one, down_two]), SEQ, scatter_dimension=1, tiled=True),
        lax.psum_scatter(taps_grad, SEQ, scatter_dimension=1, tiled=True),
        lax.psum_scatter(skip_grad[None], SEQ, scatter_dimension=1, tiled=True),
    )
    totals = (
        lax.psum(gain_sum.astype(jnp.bfloat16), BATCH).astype(jnp.float32),
        lax.psum(bias_sum.astype(jnp.bfloat16), BATCH).astype(jnp.float32),
        lax.psum(qkv_sum.astype(jnp.bfloat16), BATCH).astype(jnp.float32),
        lax.psum(out_sum.astype(jnp.bfloat16), BATCH).astype(jnp.float32),
        lax.psum(up_sum.astype(jnp.bfloat16), BATCH).astype(jnp.float32),
        lax.psum(down_sum.astype(jnp.bfloat16), BATCH).astype(jnp.float32),
        lax.psum(taps_sum.astype(jnp.bfloat16), BATCH).astype(jnp.float32),
        lax.psum(skip_sum.astype(jnp.bfloat16), BATCH).astype(jnp.float32),
        lax.psum(rate_grad.astype(jnp.bfloat16), BATCH).astype(jnp.float32),
        lax.psum(weight_grad.astype(jnp.bfloat16), BATCH).astype(jnp.float32),
    )
    return (
        output[None].astype(jnp.bfloat16),
        d_tokens,
        totals[0],
        totals[1][:3],
        totals[1][3],
        totals[2],
        totals[3],
        totals[4],
        totals[5],
        totals[6],
        totals[7][0],
        totals[8],
        totals[9],
    )


def other_device(place, core, to_place, to_core):
    return jnp.logical_or(place != to_place, core != to_core)


def greet(devices):
    barrier = pltpu.get_barrier_semaphore()
    for device in devices:
        pl.semaphore_signal(barrier, inc=1, device_id=device, device_id_type=MESH)
    pl.semaphore_wait(barrier, len(devices))


def remote(source, target, send_sem, recv_sem, device):
    return pltpu.make_async_remote_copy(
        src_ref=source,
        dst_ref=target,
        send_sem=send_sem,
        recv_sem=recv_sem,
        device_id=device,
        device_id_type=MESH,
    )


def split_low(value):
    upper = value.astype(jnp.bfloat16)
    return upper, (value - upper.astype(jnp.float32)).astype(jnp.bfloat16)


NN = (((1,), (0,)), ((), ()))
NT = (((1,), (1,)), ((), ()))
TN = (((0,), (0,)), ((), ()))


def dot(left, right, form=NN):
    return lax.dot_general(left, right, form, preferred_element_type=jnp.float32)


def dot_fine(left, right, form=NN):
    left_up, left_low = left
    right_up, right_low = right
    total = dot(left_up, right_up, form) + dot(left_up, right_low, form)
    if left_low is not None:
        total = total + dot(left_low, right_up, form)
    return total


def state_steps(span):
    row = lax.broadcasted_iota(jnp.int32, (span, 2 * STATES), 0)
    lane = lax.broadcasted_iota(jnp.int32, (span, 2 * STATES), 1)
    return jnp.where(lane < STATES, span - 1 - row, row + 1).astype(jnp.float32)


def state_tables(rate_row, weight_row, span):
    steps = state_steps(span)
    table = jnp.exp(-rate_row * steps)
    lane_row = lax.broadcasted_iota(jnp.int32, (8, 2 * STATES), 1)
    lead = jnp.where(lane_row < STATES, 0.0, weight_row * jnp.exp(rate_row))
    response = lax.dot_general(
        lead, table, NT, precision=highest, preferred_element_type=jnp.float32
    )[:1]
    spread = pltpu.roll(
        jnp.broadcast_to(response, (span, span)), 0, 1, stride=1, stride_axis=0
    )
    later = lax.broadcasted_iota(jnp.int32, (span, span), 1)
    earlier = lax.broadcasted_iota(jnp.int32, (span, span), 0)
    toeplitz = jnp.where(later >= earlier, spread, 0.0)
    return table, toeplitz


def shift_rows(value, count):
    if count > 0:
        return jnp.concatenate([jnp.zeros_like(value[:count]), value[:-count]], 0)
    return jnp.concatenate([value[-count:], jnp.zeros_like(value[:-count])], 0)


def scan_states(value, decay, seqs, blocks, direction):
    step = 1
    while step < blocks:
        value = value + shift_rows(value, direction * step * seqs) * jnp.exp(decay * step)
        step *= 2
    return shift_rows(value, direction * seqs)


SHARE = 16


def table_block(refs, kind, channel):
    size = 2 * STATES
    if kind < 3:
        row, column = channel // 2, lax.rem(channel, 2) * 3 + kind
        ref = refs.tables
    else:
        row, column = channel // 8, lax.rem(channel, 8)
        ref = refs.more_tables
    return ref.at[
        pl.ds(pl.multiple_of(row * size, size), size),
        pl.ds(pl.multiple_of(column * size, size), size),
    ]


def table_pair(refs, kind, channel):
    return table_block(refs, kind, channel)[...], table_block(refs, kind + 1, channel)[...]


def fill_tables(first, last, span, refs):
    def one_channel(channel, carry):
        table, toeplitz = state_tables(
            refs.rates[pl.ds(channel, 1), :], refs.rate_weights[pl.ds(channel, 1), :], span
        )
        for kind, value in enumerate((*split_low(toeplitz), *split_low(table))):
            table_block(refs, kind, channel)[...] = value
        return carry

    lax.fori_loop(first, last, one_channel, 0, unroll=4)


def table_shapes(channels, span):
    return (channels // 2 * span, 6 * span), (channels // 8 * span, 8 * span)


def fill_rates(refs, loads, channels, turned):
    copies = [
        loads.start(refs.all_rates, refs.rates_in), loads.start(refs.all_weights, refs.weights_in)
    ]

    def finish():
        rows = pl.ds(pl.multiple_of(lax.axis_index(SEQ) * channels, 8), channels)
        for copy, source, target in zip(
            copies, (refs.rates_in, refs.weights_in), (refs.rates, refs.rate_weights)
        ):
            copy.wait()
            both = jnp.concatenate([source[...]] * 2, 0)
            turned[...] = both.T
            target[...] = turned[rows, :]

    return finish


def rate_scratch(width, channels):
    flat, own = ((STATES, width), jnp.float32), ((channels, 2 * STATES), jnp.float32)
    return dict(
        rates_in=flat, weights_in=flat, rates=own, rate_weights=own,
    )


def valid_positions(lengths, seqs, span, axis):
    shape = (span, 1) if axis == 0 else (1, span)
    position = lax.axis_index(SEQ) * span + lax.broadcasted_iota(jnp.int32, shape, axis)
    parts = [
        jnp.where(position < lengths[0:1, seq : seq + 1], 1.0, 0.0).astype(jnp.float32)
        for seq in range(seqs)
    ]
    return jnp.concatenate(parts, axis)


def mixer_forward_channel(n, seqs, refs, part, local):
    span, channel = refs.flat_x.shape[-1], part * SHARE + local
    rate_row = refs.rates[pl.ds(channel, 1), :]
    weight_row = refs.rate_weights[pl.ds(channel, 1), :]
    rows = pl.ds(local, n * seqs, stride=SHARE)
    data = (refs.flat_x[part, rows, :].astype(jnp.bfloat16), None)
    table_parts = table_pair(refs, 2, channel)
    inner = dot_fine(data, table_pair(refs, 0, channel))
    states = scan_states(dot_fine(data, table_parts), -span * rate_row, seqs, n, 1)
    lane = lax.broadcasted_iota(jnp.int32, states.shape, 1)
    weighted = jnp.where(lane < STATES, 0.0, pltpu.roll(states, STATES, 1) * weight_row)
    refs.flat_out[part, rows, :] = inner + dot_fine(split_low(weighted), table_parts, NT)


def mixer_backward_channel(n, seqs, refs, part, local):
    span, channel = refs.flat_x.shape[-1], part * SHARE + local
    rate_row = refs.rates[pl.ds(channel, 1), :]
    weight_row = refs.rate_weights[pl.ds(channel, 1), :]
    table_parts = table_pair(refs, 2, channel)
    table = table_parts[0].astype(jnp.float32) + table_parts[1].astype(jnp.float32)
    steps = state_steps(span)
    rows = pl.ds(local, n * seqs, stride=SHARE)
    data = refs.flat_x[part, rows, :].astype(jnp.bfloat16)
    grad = refs.flat_d[part, rows, :].astype(jnp.bfloat16)
    stepped_parts = split_low(table * steps)
    both_parts = [jnp.concatenate(pair, 1) for pair in zip(table_parts, stepped_parts)]
    count = n * seqs
    sides = dot_fine((jnp.concatenate([data, grad], 0), None), both_parts)
    lane = lax.broadcasted_iota(jnp.int32, (count, 2 * STATES), 1)
    low_lanes = lane < STATES

    def aligned(value):
        return jnp.where(low_lanes, pltpu.roll(value, STATES, 1), 0.0)

    entering = jnp.where(low_lanes, sides[:count, : 2 * STATES], 0.0)
    entering_steps = jnp.where(low_lanes, sides[:count, 2 * STATES :], 0.0)
    leaving = aligned(sides[count:, : 2 * STATES])
    leaving_steps = aligned(sides[count:, 2 * STATES :])
    decay = -span * rate_row
    states = scan_states(entering, decay, seqs, n, 1)
    states_steps = scan_states(states * jnp.exp(decay), decay, seqs, n, 1)
    returned = scan_states(leaving, decay, seqs, n, -1)
    far_weight = jnp.sum(leaving * states, 0, keepdims=True)
    far_rate = jnp.sum(
        leaving_steps * states + returned * entering_steps + span * (leaving * states_steps),
        0, keepdims=True,
    )
    cross = dot(grad, data, TN)
    later = lax.broadcasted_iota(jnp.int32, (span, span), 0)
    earlier = lax.broadcasted_iota(jnp.int32, (span, span), 1)
    cross = jnp.where(later >= earlier, cross, 0.0)
    met = dot_fine(split_low(cross), both_parts)
    met_plain = pltpu.roll(met[:, : 2 * STATES], STATES, 1)
    met_steps = pltpu.roll(met[:, 2 * STATES :], STATES, 1)
    rise = jnp.exp(span * rate_row)
    near_weight = rise * jnp.sum(table * met_plain, 0, keepdims=True)
    near_rate = rise * jnp.sum(
        table * ((steps - span) * met_plain + met_steps), 0, keepdims=True
    )
    lane_row = lane[:1]
    near_weight = jnp.where(lane_row < STATES, pltpu.roll(near_weight, STATES, 1), 0.0)
    near_rate = jnp.where(lane_row < STATES, pltpu.roll(near_rate, STATES, 1), 0.0)
    refs.weight_grad[pl.ds(channel, 1), :] = near_weight + far_weight
    refs.rate_grad[pl.ds(channel, 1), :] = -weight_row * (near_rate + far_rate)
    inner = dot_fine((grad, None), table_pair(refs, 0, channel), NT)
    weighted = returned * weight_row
    refs.flat_d[part, rows, :] = inner + dot_fine(split_low(weighted), table_parts, NT)


def block_of(index, core):
    return 2 * index + lax.rem(index + core, 2)


def keeper_of(block):
    return lax.rem((block + 1) // 2, 2)


class HeadPlaces:
    def __init__(self, n, seqs, groups):
        self.n, self.seqs, self.groups = n, seqs, groups
        self.me, self.core = lax.axis_index(SEQ), lax.axis_index(BATCH)
        self.group = self.me // (2 * seqs)
        self.seq = lax.rem(self.me // 2, seqs)
        self.batch = lax.rem(self.me, 2)
        self.keeper = keeper_of(self.me)
        self.sibling = (self.me, 1 - self.core)
        self.targets = [
            ((group * 2 * seqs + seq * 2 + self.core, self.keeper), seq, group)
            for seq in range(seqs)
            for group in range(groups)
        ]
        self.blocks = [block_of(index, self.core) for index in range(n // 2)]
        self.sources = [(block, self.batch) for block in self.blocks]

    def is_other(self, device):
        return jnp.logical_or(device[0] != self.me, device[1] != self.core)

    def greet(self):
        barrier = pltpu.get_barrier_semaphore()
        self.signal_all(barrier, [])
        self.wait_all(barrier, 0)

    def signal_all(self, barrier, more):
        for device in [target for target, _, _ in self.targets] + self.sources:

            @pl.when(self.is_other(device))
            def _():
                pl.semaphore_signal(barrier, inc=1, device_id=device, device_id_type=MESH)

        for device in [self.sibling, *more]:
            pl.semaphore_signal(barrier, inc=1, device_id=device, device_id_type=MESH)

    def wait_all(self, barrier, more):
        kept = jnp.logical_and(self.batch == self.core, self.is_kept_here())
        count = len(self.targets) + len(self.sources) + 1 + more
        pl.semaphore_wait(barrier, count - 2 * kept.astype(jnp.int32))

    def is_kept_here(self):
        return self.keeper == self.core

    def send(self, source, target, send_sem, recv_sem, device):
        @pl.when(self.is_other(device))
        def _():
            remote(source, target, send_sem, recv_sem, device).start()

        @pl.when(jnp.logical_not(self.is_other(device)))
        def _():
            pltpu.make_async_copy(source, target, recv_sem).start()

    def wait_sent(self, source, target, send_sem, recv_sem, device):
        @pl.when(self.is_other(device))
        def _():
            remote(source, target, send_sem, recv_sem, device).wait_send()


def fill_head(held, head, part, n, span, rows_out, columns_out):
    for block in range(n):
        piece = held[head, block, part * HEAD : (part + 1) * HEAD, :]
        if rows_out is not None:
            rows_out[block * span : (block + 1) * span, :] = piece.T
        if columns_out is not None:
            columns_out[:, block * span : (block + 1) * span] = piece


def causal(first_key, rows, first_query, span):
    key = first_key + lax.broadcasted_iota(jnp.int32, (rows, span), 0)
    query = first_query + lax.broadcasted_iota(jnp.int32, (rows, span), 1)
    return key <= query


TILE = 384
VMEM, HBM = pltpu.VMEM, pl.ANY


def launch(body, inputs, outputs, scratch, copies, collective):
    names = [*inputs, *outputs, *scratch, "send", "recv", "local"]

    def kernel(*refs):
        body(types.SimpleNamespace(**dict(zip(names, refs))))

    dma = pltpu.SemaphoreType.DMA
    results = pl.pallas_call(
        kernel,
        out_shape=tuple(jax.ShapeDtypeStruct(shape, kind) for shape, kind, _ in outputs.values()),
        in_specs=[pl.BlockSpec(memory_space=space) for _, space in inputs.values()],
        out_specs=tuple(pl.BlockSpec(memory_space=space) for _, _, space in outputs.values()),
        scratch_shapes=[pltpu.VMEM(shape, kind) for shape, kind in scratch.values()]
        + [dma((copies,)), dma((copies,)), dma((LOCAL_COPIES,))],
        compiler_params=pltpu.CompilerParams(
            collective_id=collective, has_side_effects=True, vmem_limit_bytes=VMEM_BYTES
        ),
    )(*(array for array, _ in inputs.values()))
    return types.SimpleNamespace(**dict(zip(outputs, results)))


LOCAL_COPIES = 64


class Loads:
    def __init__(self, refs):
        self.semaphores, self.used = refs.local, 0

    def start(self, source, target):
        copy = pltpu.make_async_copy(source, target, self.semaphores.at[self.used])
        self.used += 1
        copy.start()
        return copy


class Links:
    def __init__(self, refs):
        self.send, self.recv, self.used, self.unsent = refs.send, refs.recv, 0, []

    def slots(self, count):
        self.used += count
        return self.used - count

    def copy(self, source, target, device, slot=None):
        slot = self.slots(1) if slot is None else slot
        made = remote(source, target, self.send.at[slot], self.recv.at[slot], device)
        made.start()
        self.unsent.append(made)
        return made

    def finish(self):
        for made in self.unsent:
            made.wait_send()


class Piece:
    def __init__(self, weight, first_row, first_column, axis):
        self.weight, self.first_row, self.first_column, self.axis = (
            weight, first_row, first_column, axis,
        )


ROWS = 48


def pieces_of(weights, order):
    pieces = []
    for weight, first, last, axes in order:
        rows, half = weights[weight]
        places = [
            (first_row, first_column)
            for first_column in range(0, half, TILE)
            for first_row in range(0, rows, ROWS)
        ]
        for count, place in enumerate(places[first:last]):
            pieces.append(Piece(weight, *place, axes[count % len(axes)]))
    return pieces


class Reducer:
    def __init__(self, refs, links, depth, weights, pieces, given):
        self.refs, self.links, self.depth, self.weights = refs, links, depth, weights
        self.me, self.core = lax.axis_index(SEQ), lax.axis_index(BATCH)
        self.level = self.me // 4
        self.spot = (lax.rem(self.me // 2, 2), lax.rem(self.me, 2))
        base = self.level * 4
        self.across = [
            (base + self.spot[0] * 2 + (1 - self.spot[1]), self.core),
            (base + (1 - self.spot[0]) * 2 + self.spot[1], self.core),
        ]
        self.sibling = (self.me, 1 - self.core)
        self.levels = [lax.rem(self.level + step, depth) for step in range(1, depth)]
        self.column = [
            (other * 4 + self.spot[0] * 2 + self.spot[1], self.core) for other in self.levels
        ]
        self.slots = {piece: slot for slot, piece in enumerate(pieces)}
        self.given = {piece: slot for slot, piece in enumerate(given)}
        self.products = {}
        self.exchanges, self.flights = {}, {}

    def neighbours(self):
        return [self.sibling, *self.across, *self.column]

    def exchange(self, weight, left, right):
        half = self.weights[weight][1]
        theirs = pl.ds(pl.multiple_of((1 - self.core) * half, 16), half)
        self.exchanges[weight] = (
            left, right,
            [
                self.links.copy(left[0], left[1], self.sibling),
                self.links.copy(right[0].at[theirs, :], right[1], self.sibling),
            ],
        )

    def product(self, piece, first):
        left, right, copies = self.exchanges[piece.weight]
        while copies:
            copies.pop().wait_recv()
        places = [
            outer * 4 + (inner * 2 + first if piece.axis == 0 else first * 2 + inner)
            for outer in range(self.depth)
            for inner in range(2)
        ]
        rows = slice(piece.first_row, piece.first_row + ROWS)
        mine, other = (
            jnp.concatenate([side[place, rows, :] for place in places], 0) for side in left
        )
        start = self.core * self.weights[piece.weight][1] + piece.first_column
        own = pl.ds(pl.multiple_of(start, 16), TILE)
        there = slice(piece.first_column, piece.first_column + TILE)
        total = dot(mine, right[0][own, :], NT) + dot(other, right[1][there, :], NT)
        return total.reshape(self.depth, 2, ROWS, TILE)

    def first(self, piece):
        places = self.refs.away.shape[0]
        place = len(self.products)
        if place >= places:
            sent = self.products[place - places]
            sent.wait_send()
            self.links.unsent = [copy for copy in self.links.unsent if copy is not sent]
        away = self.refs.away.at[place % places]
        away[...] = self.product(piece, 1 - self.spot[1 - piece.axis]).astype(jnp.bfloat16)
        self.flights[piece] = self.links.copy(
            away, self.refs.one.at[self.slots[piece]], self.across[piece.axis]
        )
        self.products[place] = self.flights[piece]

    def joined(self, piece, into):
        slot = self.slots[piece]
        self.flights.pop(piece).wait_recv()
        total = self.product(piece, self.spot[1 - piece.axis])
        total = total + self.refs.one[slot].astype(jnp.float32)
        into[...] = total.astype(jnp.bfloat16)

    def resume(self, piece):
        slot = self.slots[piece]
        self.flights[piece] = self.links.copy(
            self.refs.one.at[slot, :, 1 - self.spot[piece.axis]], self.refs.two.at[slot],
            self.across[1 - piece.axis],
        )

    def second(self, piece):
        self.joined(piece, self.refs.one.at[self.slots[piece]])
        self.resume(piece)

    def middle(self, piece, into):
        slot = self.slots[piece]
        self.flights.pop(piece).wait_recv()
        kept = self.refs.one[slot, :, self.spot[piece.axis]].astype(jnp.float32)
        into[...] = (kept + self.refs.two[slot].astype(jnp.float32)).astype(into.dtype)

    def summed(self, piece):
        if piece in self.given:
            slot = self.given[piece]
            return self.refs.mid.at[slot], self.refs.three.at[slot]
        slot = self.slots[piece]
        return self.refs.two.at[slot], self.refs.three.at[len(self.given) + slot]

    def third(self, piece):
        summed, three = self.summed(piece)
        if piece not in self.given:
            self.middle(piece, summed)
        self.flights[piece] = [
            self.links.copy(summed.at[other], three.at[step], self.column[step])
            for step, other in enumerate(self.levels)
        ]

    def fourth(self, piece, out):
        summed, three = self.summed(piece)
        total = summed[self.level].astype(jnp.float32)
        for step, copy in enumerate(self.flights.pop(piece)):
            copy.wait_recv()
            total = total + three[step].astype(jnp.float32)
        start = self.core * self.weights[piece.weight][1] + piece.first_column
        filled = out.at[
            piece.first_row : piece.first_row + ROWS, pl.ds(pl.multiple_of(start, 128), TILE)
        ]
        filled[...] = total
        self.flights[piece] = self.links.copy(filled, filled, self.sibling)

    def last(self, piece):
        self.flights.pop(piece).wait_recv()


def reducer_scratch(products, pieces, given, depth):
    low = jnp.bfloat16
    shapes = dict(
        away=((products, depth, 2, ROWS, TILE), low), one=((pieces, depth, 2, ROWS, TILE), low),
        two=((pieces, depth, ROWS, TILE), low),
    )
    if given > 0:
        shapes.update(
            mid=((given, depth, ROWS, TILE), low),
            three=((given + pieces, depth - 1, ROWS, TILE), low),
        )
    return shapes


def gelu_slope(value):
    scale = math.sqrt(2.0 / math.pi)
    square = value * value
    bent = jnp.tanh(scale * value * (1.0 + 0.044715 * square))
    return 0.5 * (1.0 + bent) + 0.5 * value * (1.0 - bent * bent) * scale * (
        1.0 + 3.0 * 0.044715 * square
    )


def norm_gradient(inputs, gain, grad):
    center = inputs - jnp.mean(inputs, 0, keepdims=True)
    factor = lax.rsqrt(jnp.mean(center * center, 0, keepdims=True) + norm_eps)
    unit = center * factor
    scaled = grad * gain
    result = factor * (
        scaled
        - jnp.mean(scaled, 0, keepdims=True)
        - unit * jnp.mean(scaled * unit, 0, keepdims=True)
    )
    return result, jnp.sum(grad * unit, 1, keepdims=True), jnp.sum(grad, 1, keepdims=True)


def rows_product(matrix, other, out_rows, chunk, store):
    def one_chunk(index, carry):
        rows = pl.ds(pl.multiple_of(index * chunk, 128), chunk)
        store(rows, dot(matrix[rows, :], other))
        return carry

    lax.fori_loop(0, out_rows // chunk, one_chunk, 0)


def back_one_body(n, seqs, groups, span, group_rows, width, hidden_width, refs):
    at = HeadPlaces(n, seqs, groups)
    half = n // 2
    heads = group_rows // HEAD
    tokens = seqs * span
    links, loads = Links(refs), Loads(refs)
    weights = gradient_weights(width, hidden_width, n)
    pieces = pieces_of(weights, BACK_ONE_ORDER)
    reducer = Reducer(refs, links, groups, weights, pieces, [])
    down, up, out = [[piece for piece in pieces if piece.weight == weight] for weight in (DOWN, UP, OUT)]
    barrier = pltpu.get_barrier_semaphore()
    at.signal_all(barrier, reducer.neighbours()[1:])

    load_branch = loads.start(refs.branch, refs.down_right)
    load_active = loads.start(refs.active, refs.down_left)
    load_d_active = loads.start(refs.d_active, refs.d_active_in)
    load_slope = loads.start(refs.slope, refs.slope_in)
    load_w_up = loads.start(refs.w_up.at[1], refs.up)
    load_hidden = loads.start(refs.hidden, refs.hidden_in)
    load_w_out = loads.start(refs.w_out.at[1], refs.out)
    load_normed = loads.start(refs.normed, refs.up_left)
    load_attended = loads.start(refs.attended, refs.out_left)
    load_held = loads.start(refs.held, refs.held_in)

    at.wait_all(barrier, len(reducer.neighbours()) - 1)
    load_active.wait()
    load_branch.wait()
    reducer.exchange(DOWN, (refs.down_left, refs.down_left_other), (refs.down_right, refs.down_right_other))
    load_d_active.wait()
    load_slope.wait()
    refs.up_right[...] = (
        refs.slope_in[...].astype(jnp.float32) * refs.d_active_in[...].astype(jnp.float32)
    ).astype(jnp.bfloat16)
    for piece in down[:2]:
        reducer.first(piece)
    load_w_up.wait()
    load_hidden.wait()
    load_normed.wait()
    reducer.exchange(UP, (refs.up_left, refs.up_left_other), (refs.up_right, refs.up_right_other))
    d_normed = dot(refs.up[...], refs.up_right[...])
    for piece in down[2:]:
        reducer.first(piece)
    d_inputs, gain_part, bias_part = norm_gradient(refs.hidden_in[...], refs.columns[:, 3:4], d_normed)
    refs.small[...] = jnp.zeros_like(refs.small)
    refs.small[:, 3:4] = gain_part
    refs.small[:, 7:8] = bias_part
    grad = refs.down_right[...].astype(jnp.float32) + d_inputs
    refs.grad_out[...] = grad
    refs.out_right[...] = grad.astype(jnp.bfloat16)
    load_w_out.wait()
    load_attended.wait()
    reducer.exchange(OUT, (refs.out_left, refs.out_left_other), (refs.out_right, refs.out_right_other))

    count, lot = len(at.targets), groups * HEAD
    arrive, leave = links.slots(heads * half), links.slots(heads * count)
    spread = []
    for head in range(heads):
        rows = slice(head * lot, (head + 1) * lot)
        refs.d_attended[rows, :] = dot(refs.out[rows, :], refs.out_right[...]).astype(jnp.bfloat16)
        for number, (device, seq, group) in enumerate(at.targets):
            first = head * lot + group * HEAD
            sent = (
                refs.d_attended.at[first : first + HEAD, seq * span : (seq + 1) * span],
                refs.landing.at[head, at.me // 2], refs.send.at[leave + head * count + number],
                refs.recv.at[arrive + head * half + at.me // 2], device,
            )
            at.send(*sent)
            spread.append(sent)
    load_held.wait()
    started = down + up + out
    for piece in up + out:
        reducer.first(piece)

    returned = links.slots(len(at.targets) * heads)
    returning = links.slots(half * heads)
    slot = at.seq * groups + at.group
    going = []
    passed = []

    def send_back(head):
        passed[head].wait_recv()
        for index, device in enumerate(at.sources):
            results = refs.results.at[head, index]
            kept = refs.kept.at[head, index]
            part = refs.partial_recv[head, index].astype(jnp.float32)
            results[1] = (kept[:HEAD] + part[:HEAD]).astype(jnp.bfloat16)
            results[2] = (kept[HEAD:] + part[HEAD:]).astype(jnp.bfloat16)
            into = refs.d_qkv.at[
                :,
                pl.ds(pl.multiple_of(head * lot + at.group * HEAD, HEAD), HEAD),
                pl.ds(pl.multiple_of(at.seq * span, span), span),
            ]
            sent = (
                results, into, refs.send.at[returning + head * half + index],
                refs.recv.at[returned + head * len(at.targets) + slot], device,
            )
            at.send(*sent)
            going.append(sent)

    def attend(head):
        for index in range(half):
            landed = refs.landing.at[head, index]
            remote(
                landed, landed, refs.send.at[leave], refs.recv.at[arrive + head * half + index],
                at.sibling,
            ).wait_recv()
        fill_head(refs.held_in, head, 1, n, span, refs.key_rows, refs.key_columns)
        fill_head(refs.held_in, head, 2, n, span, refs.value_rows, None)
        refs.key_grads[...] = jnp.zeros_like(refs.key_grads)
        refs.value_grads[...] = jnp.zeros_like(refs.value_grads)
        for index, block in enumerate(at.blocks):
            query = refs.held_in[head, block, :HEAD, :] * jnp.bfloat16(HEAD**-0.5)
            grad = refs.landing[head, index]
            log_total = refs.lse[index, head : head + 1, :]
            clear, reach = 2 * index * span, 2 * (index + 1) * span
            pieces = []
            row_term = jnp.zeros((1, span), jnp.float32)
            for first, last in ((0, clear), (clear, reach)):
                if first == last:
                    continue
                scores = dot(refs.key_rows[first:last, :], query)
                if last == reach:
                    scores = jnp.where(
                        causal(clear, reach - clear, block * span, span), scores, masked_score
                    )
                weights = jnp.exp(scores - log_total)
                d_weights = dot(refs.value_rows[first:last, :], grad)
                row_term = row_term + jnp.sum(weights * d_weights, 0, keepdims=True)
                pieces.append((first, last, weights, d_weights))
            d_query = jnp.zeros((HEAD, span), jnp.float32)
            for first, last, weights, d_weights in pieces:
                d_scores = (weights * (d_weights - row_term)).astype(jnp.bfloat16)
                d_query = d_query + dot(refs.key_columns[:, first:last], d_scores)
                refs.key_grads[:, first:last] += dot(query, d_scores, NT)
                refs.value_grads[:, first:last] += dot(grad, weights.astype(jnp.bfloat16), NT)
            refs.results[head, index, 0] = (d_query * HEAD**-0.5).astype(jnp.bfloat16)
        for index in range(half):
            other = pl.ds(pl.multiple_of(block_of(index, 1 - at.core) * span, span), span)
            own = pl.ds(pl.multiple_of(at.blocks[index] * span, span), span)
            refs.partial_send[head, index, :HEAD, :] = refs.key_grads[:, other].astype(jnp.bfloat16)
            refs.partial_send[head, index, HEAD:, :] = refs.value_grads[:, other].astype(jnp.bfloat16)
            refs.kept[head, index, :HEAD, :] = refs.key_grads[:, own]
            refs.kept[head, index, HEAD:, :] = refs.value_grads[:, own]
        passed.append(
            links.copy(refs.partial_send.at[head], refs.partial_recv.at[head], at.sibling)
        )

    waiting = list(started)
    for head in range(heads):
        attend(head)
        if head > 0:
            send_back(head - 1)
        if head < heads - 1:
            for _ in range(2):
                reducer.second(waiting.pop(0))
    reducer.second(waiting.pop(0))
    send_back(heads - 1)
    done = len(started) - LEFT_OVER
    while len(waiting) > LEFT_OVER:
        reducer.second(waiting.pop(0))
    for place, piece in enumerate(started[done:]):
        reducer.joined(piece, refs.half_out.at[place])
    for place, piece in enumerate(started[:done]):
        reducer.middle(piece, refs.mid_out.at[place])
    for head in range(heads):
        for count, (device, seq, group) in enumerate(at.targets):
            landed = refs.d_qkv.at[
                :,
                head * lot + group * HEAD : head * lot + (group + 1) * HEAD,
                seq * span : (seq + 1) * span,
            ]
            remote(
                landed, landed, refs.send.at[leave],
                refs.recv.at[returned + head * len(at.targets) + count], at.sibling,
            ).wait_recv()
    for sent in spread + going:
        at.wait_sent(*sent)
    links.finish()


LEFT_OVER = 4


def gradient_weights(width, hidden_width, n):
    return {
        QKV: (width // n, 3 * width // 2),
        FIRST: (width // n, 3 * width // 2),
        DOWN: (hidden_width // n, width // 2),
        UP: (width // n, hidden_width // 2),
        OUT: (width // n, width // 2),
    }


BACK_ONE_ORDER = ((DOWN, 0, 4, (1, 0)), (UP, 0, 4, (1, 0)), (OUT, 0, 1, (0,)))
BACK_TWO_ORDER = (
    (QKV, 0, 3, (1, 0, 1)), (DOWN, 0, 4, (0, 1)), (UP, 0, 4, (0, 1)), (OUT, 0, 1, (0,)),
    (FIRST, 0, 3, (1, 0, 1)),
)


def back_one(
    branch, d_active, hidden, slope, normed, active, attended, held, lse, columns,
    w_out, w_up, collective,
):
    width, tokens = branch.shape
    heads, n, _, span = held.shape
    seqs = tokens // span
    group_rows = heads * HEAD
    groups = width // group_rows
    hidden_width = w_up.shape[2]
    half = n // 2
    low, wide = jnp.bfloat16, jnp.float32
    weights = gradient_weights(width, hidden_width, n)
    pieces = pieces_of(weights, BACK_ONE_ORDER)
    inputs = dict(
        branch=(branch, HBM), d_active=(d_active, HBM), hidden=(hidden, HBM), slope=(slope, HBM),
        normed=(normed, HBM), active=(active, HBM), attended=(attended, HBM), held=(held, HBM),
        lse=(lse, VMEM), columns=(columns, VMEM), w_out=(w_out, HBM), w_up=(w_up, HBM),
    )
    outputs = dict(
        d_qkv=((3, width, tokens), low, VMEM),
        grad_out=((width, tokens), wide, VMEM),
        small=((width, 128), wide, VMEM),
        mid_out=((len(pieces) - LEFT_OVER, groups, ROWS, TILE), low, VMEM),
        half_out=((LEFT_OVER, groups, 2, ROWS, TILE), low, VMEM),
    )
    scratch = dict(
        up=(w_up.shape[1:], low), out=(w_out.shape[1:], low),
        d_active_in=(d_active.shape, low), hidden_in=((width, tokens), wide),
        slope_in=(slope.shape, low), d_attended=((width, tokens), low),
        down_left=(active.shape, low), down_right=((width, tokens), low),
        up_left=(normed.shape, low), up_right=((hidden_width, tokens), low),
        out_left=(attended.shape, low), out_right=((width, tokens), low),
        held_in=(held.shape, low), landing=((heads, half, HEAD, span), low),
        results=((heads, half, 3, HEAD, span), low), kept=((heads, half, 2 * HEAD, span), wide),
        partial_send=((heads, half, 2 * HEAD, span), low),
        partial_recv=((heads, half, 2 * HEAD, span), low),
        key_grads=((HEAD, n * span), wide), value_grads=((HEAD, n * span), wide),
        key_rows=((n * span, HEAD), low), key_columns=((HEAD, n * span), low),
        value_rows=((n * span, HEAD), low),
        down_left_other=(active.shape, low), down_right_other=((width // 2, tokens), low),
        up_left_other=(normed.shape, low), up_right_other=((hidden_width // 2, tokens), low),
        out_left_other=(attended.shape, low), out_right_other=((width // 2, tokens), low),
        **reducer_scratch(len(pieces), len(pieces), 0, groups),
    )
    body = functools.partial(
        back_one_body, n, seqs, groups, span, group_rows, width, hidden_width
    )
    return launch(body, inputs, outputs, scratch, 160, collective)


def back_two_body(n, seqs, span, width, hidden_width, refs):
    channels = width // n
    me, core = lax.axis_index(SEQ), lax.axis_index(BATCH)
    peers = [lax.rem(me + step, n) for step in range(1, n)]
    before = (lax.rem(me + n - 1, n), core)
    links, loads = Links(refs), Loads(refs)
    weights = gradient_weights(width, hidden_width, n)
    pieces, given = pieces_of(weights, BACK_TWO_ORDER), pieces_of(weights, BACK_ONE_ORDER)
    given, halves = given[:-LEFT_OVER], given[-LEFT_OVER:]
    qkv, down, up, out, last = [
        [piece for piece in pieces if piece.weight == weight]
        for weight in (QKV, DOWN, UP, OUT, FIRST)
    ]
    reducer = Reducer(refs, links, n // 4, weights, halves + pieces, given)
    ends = {FIRST: refs.qkv_one, DOWN: refs.down_one, UP: refs.up_one, OUT: refs.out_one}
    ends_two = {DOWN: refs.down_two, UP: refs.up_two, OUT: refs.out_two}

    def fourth(piece):
        if piece in given or piece in halves:
            reducer.fourth(piece, ends_two[piece.weight])
        else:
            reducer.fourth(piece, refs.qkv_two if piece.weight == QKV else ends[piece.weight])

    barrier = pltpu.get_barrier_semaphore()
    for device in [(peer, core) for peer in peers] + [reducer.sibling]:
        pl.semaphore_signal(barrier, inc=1, device_id=device, device_id_type=MESH)
    load_d_qkv = loads.start(refs.d_qkv, refs.qkv_right)
    load_normed_three = loads.start(refs.normed_three, refs.qkv_left)
    load_half = loads.start(refs.half_in, refs.one.at[:LEFT_OVER])
    load_mid = loads.start(refs.mid_in, refs.mid.at[: len(given)])
    load_small = loads.start(refs.small_in, refs.small)
    load_w_qkv = loads.start(refs.w_qkv.at[1], refs.qkv)
    load_hidden_two = loads.start(refs.hidden_two, refs.hidden_two_in)
    load_grad = loads.start(refs.grad, refs.grad_now)
    load_w_down = loads.start(refs.w_down.at[0], refs.down)
    load_slope = loads.start(refs.slope, refs.slope_in)
    load_w_up = loads.start(refs.w_up.at[0], refs.up)
    load_active = loads.start(refs.active, refs.down_left)
    load_hidden_one = loads.start(refs.hidden_one, refs.hidden_one_in)
    load_normed_two = loads.start(refs.normed_two, refs.up_left)
    load_w_out = loads.start(refs.w_out.at[0], refs.out)
    load_gated = loads.start(refs.gated, refs.out_left)
    load_queries = loads.start(refs.queries, refs.queries_in)
    load_mixer = loads.start(refs.mixer, refs.mixer_in)
    load_carried = loads.start(refs.carried, refs.carried_in)
    finish_rates = fill_rates(refs, loads, channels, refs.small_other)
    load_held = loads.start(refs.held, refs.held_in)

    load_normed_one = loads.start(refs.normed_one, refs.first_left)
    load_tokens = loads.start(refs.tokens, refs.tokens_in)

    load_d_qkv.wait()
    load_normed_three.wait()
    pl.semaphore_wait(barrier, n)
    reducer.exchange(QKV, (refs.qkv_left, refs.qkv_left_other), (refs.qkv_right, refs.qkv_right_other))
    load_half.wait()
    for piece in halves:
        reducer.resume(piece)
    load_mid.wait()
    for piece in given[:2]:
        reducer.third(piece)
    load_w_qkv.wait()
    d_normed = dot(refs.qkv[...], refs.qkv_right[...])
    load_w_qkv = loads.start(refs.w_qkv.at[0], refs.qkv)
    for piece in qkv[:2]:
        reducer.first(piece)
    load_hidden_two.wait()
    load_grad.wait()
    d_inputs, gain_part, bias_part = norm_gradient(
        refs.hidden_two_in[...], refs.columns[:, 2:3], d_normed
    )
    load_small.wait()
    refs.small[:, 2:3] = gain_part
    refs.small[:, 6:7] = bias_part
    grad = refs.grad_now[...] + d_inputs
    refs.grad_now[...] = grad
    refs.down_right[...] = grad.astype(jnp.bfloat16)
    load_w_down.wait()
    load_slope.wait()
    load_active.wait()
    reducer.exchange(DOWN, (refs.down_left, refs.down_left_other), (refs.down_right, refs.down_right_other))

    def store_raised(rows, value):
        slope = refs.slope_in[rows, :].astype(jnp.float32)
        refs.up_right[rows, :] = (slope * value).astype(jnp.bfloat16)

    rows_product(refs.down, refs.down_right[...], hidden_width, 512, store_raised)
    load_w_up.wait()
    load_hidden_one.wait()
    load_normed_two.wait()
    reducer.exchange(UP, (refs.up_left, refs.up_left_other), (refs.up_right, refs.up_right_other))
    d_normed = dot(refs.up[...], refs.up_right[...])
    refs.tables, refs.more_tables = refs.down, refs.up
    load_tables = loads.start(refs.tables_kept, refs.down)
    load_more_tables = loads.start(
        refs.more_tables_kept, refs.up.at[:, : refs.more_tables_kept.shape[1]]
    )
    d_inputs, gain_part, bias_part = norm_gradient(
        refs.hidden_one_in[...], refs.columns[:, 1:2], d_normed
    )
    refs.small[:, 1:2] = gain_part
    refs.small[:, 5:6] = bias_part
    grad = refs.grad_now[...] + d_inputs
    refs.grad_now[...] = grad
    refs.out_right[...] = grad.astype(jnp.bfloat16)
    load_gated.wait()
    reducer.exchange(OUT, (refs.out_left, refs.out_left_other), (refs.out_right, refs.out_right_other))
    load_w_out.wait()
    load_queries.wait()
    load_mixer.wait()
    load_carried.wait()
    d_gated = dot(refs.out[...], refs.out_right[...])
    d_mixer = d_gated * refs.queries_in[...]
    for seq in range(seqs):
        refs.d_conv[seq] = d_mixer[:, seq * span : (seq + 1) * span].astype(jnp.bfloat16)
    shares = channels // SHARE
    arrive, answered = links.slots(shares * n), links.slots(shares * n)

    def share_rows(device, share):
        return pl.ds(pl.multiple_of(device * channels + share * SHARE, 16), SHARE)

    going, own_copies = [], []
    for share in range(shares):
        within = slice(share * SHARE, (share + 1) * SHARE)
        for step, peer in enumerate(peers):
            going.append(
                links.copy(
                    refs.d_conv.at[:, share_rows(peer, share), :],
                    refs.landing.at[me, :, within, :], (peer, core), arrive + share * n + step,
                )
            )
        own_copies.append(
            loads.start(
                refs.d_conv.at[:, share_rows(me, share), :], refs.landing.at[me, :, within, :]
            )
        )
    refs.d_mixer[...] = d_mixer
    refs.first_right[:width, :] = (d_gated * refs.mixer_in[...]).astype(jnp.bfloat16)
    refs.small[:, 12:13] = sum(
        jnp.sum(
            d_mixer[:, seq * span : (seq + 1) * span] * refs.carried_in[seq].astype(jnp.float32), 1,
            keepdims=True,
        )
        for seq in range(seqs)
    )

    load_values = loads.start(refs.values, refs.queries_in)
    load_keys = loads.start(refs.keys, refs.carried_in)
    load_shifted = loads.start(refs.shifted, refs.mixer_in)
    for piece in qkv[2:] + down:
        reducer.first(piece)
    for piece in qkv:
        reducer.second(piece)
    load_held.wait()
    finish_rates()
    load_tables.wait()
    load_more_tables.wait()
    back, back_own = [], []
    for share in range(shares):
        within = slice(share * SHARE, (share + 1) * SHARE)
        own_copies[share].wait()
        for copy in going[share * len(peers) : (share + 1) * len(peers)]:
            copy.wait_recv()
        for flat, source in ((refs.flat_x, refs.held_in), (refs.flat_d, refs.landing)):
            flat[share] = (
                source[:, :, within, :].astype(jnp.float32).reshape(n * seqs * SHARE, span)
            )

        def one_channel(local, carry):
            mixer_backward_channel(n, seqs, refs, share, local)
            return carry

        lax.fori_loop(0, SHARE, one_channel, 0, unroll=4)
        refs.landing[:, :, within, :] = (
            refs.flat_d[share].reshape(n, seqs, SHARE, span).astype(jnp.bfloat16)
        )
        for step, peer in enumerate(peers):
            back.append(
                links.copy(
                    refs.landing.at[peer, :, within, :],
                    refs.from_conv.at[:, share_rows(me, share), :], (peer, core),
                    answered + share * n + step,
                )
            )
        back_own.append(
            loads.start(
                refs.landing.at[me, :, within, :], refs.from_conv.at[:, share_rows(me, share), :]
            )
        )
        reducer.third(given[2 + share])
        reducer.second(down[share])
        if share > 0:
            reducer.first(up[share - 1])
    states = [
        links.copy(refs.rate_grad, refs.rate_other, reducer.sibling),
        links.copy(refs.weight_grad, refs.weight_other, reducer.sibling),
    ]
    reducer.second(down[3])
    for piece in given[:2]:
        fourth(piece)
    for copy in states:
        copy.wait_recv()
    refs.rate_sum[...] = (refs.rate_grad[...] + refs.rate_other[...])[:, :STATES]
    refs.weight_sum[...] = (refs.weight_grad[...] + refs.weight_other[...])[:, :STATES]
    for copy in back_own:
        copy.wait()
    for copy in back:
        copy.wait_recv()
    load_values.wait()
    load_shifted.wait()
    valid = valid_positions(refs.lengths, seqs, span, 1)
    conv = jnp.concatenate([refs.from_conv[seq] for seq in range(seqs)], 1).astype(jnp.float32)
    d_carried = (refs.d_mixer[...] * refs.columns[:, 8:9] + conv) * valid
    d_shifted = d_carried * refs.queries_in[...]
    refs.hidden_one_in[...] = d_shifted
    for seq in range(seqs):
        for first in range(0, width, span):
            turned = d_shifted[first : first + span, seq * span : (seq + 1) * span].T
            refs.rim_out[seq, :, first : first + span] = turned[: refs.rim_out.shape[1]]
    refs.first_right[2 * width :, :] = (d_carried * refs.mixer_in[...]).astype(jnp.bfloat16)
    halo = links.copy(refs.rim_out, refs.rim_in, before)
    for piece in halves:
        reducer.third(piece)
    for piece in up[2:] + out:
        reducer.first(piece)
    for piece in qkv:
        reducer.third(piece)
    load_keys.wait()
    halo.wait_recv()
    lane = lax.broadcasted_iota(jnp.int32, (width, span), 1)
    there = jnp.where(me == n - 1, 0.0, 1.0)
    rim = refs.rim_in.shape[1]
    tap_sums = [jnp.zeros((width, 1), jnp.float32) for _ in range(TAPS)]
    for seq in range(seqs):
        lanes = slice(seq * span, (seq + 1) * span)
        own = refs.hidden_one_in[:, lanes]
        keys = refs.carried_in[seq].astype(jnp.float32)
        turned = []
        for first in range(0, width, span):
            piece = refs.rim_in[seq, :, first : first + span] * there
            piece = jnp.concatenate([piece, jnp.zeros((span - rim, span), jnp.float32)], 0)
            turned.append(piece.T)
        following = jnp.concatenate(turned, 0)
        d_keys = jnp.zeros((width, span), jnp.float32)
        for offset in range(TAPS):
            moved = own
            if offset > 0:
                moved = jnp.where(
                    lane < span - offset,
                    pltpu.roll(own, span - offset, 1),
                    pltpu.roll(following, span - offset, 1),
                )
            d_keys = d_keys + refs.columns[:, 4 + offset : 5 + offset] * moved
            tap_sums[offset] = tap_sums[offset] + jnp.sum(moved * keys, 1, keepdims=True)
        refs.first_right[width : 2 * width, lanes] = d_keys.astype(jnp.bfloat16)
    load_normed_one.wait()
    reducer.exchange(
        FIRST, (refs.first_left, refs.first_left_other), (refs.first_right, refs.first_right_other)
    )
    load_w_qkv.wait()
    load_tokens.wait()
    d_normed = dot(refs.qkv[...], refs.first_right[...])
    for piece in last:
        reducer.first(piece)
    flat_in = jnp.concatenate(
        [refs.tokens_in[seq].astype(jnp.float32).T for seq in range(seqs)], 1
    )
    d_inputs, gain_part, bias_part = norm_gradient(flat_in * valid, refs.columns[:, 0:1], d_normed)
    refs.hidden_two_in[...] = (refs.grad_now[...] + d_inputs) * valid
    for offset in range(TAPS):
        refs.small[:, 8 + offset : 9 + offset] = tap_sums[offset]
    refs.small[:, 0:1] = gain_part
    refs.small[:, 4:5] = bias_part
    shared = links.copy(refs.small, refs.small_other, reducer.sibling)
    for piece in up:
        reducer.second(piece)
    for piece in down:
        reducer.third(piece)
    shared.wait_recv()
    rows = width // n
    turned = (refs.small[...] + refs.small_other[...]).T[:16]
    for place in range(n):
        start = place * rows // 128 * 128
        window = turned[:, start : min(start + 256, width)]
        away = (window.shape[1] - (place * rows - start)) % window.shape[1]
        refs.slices[place] = pltpu.roll(window, away, 1)[:, :128]
    depth = n // 4
    y, x = reducer.spot
    for outer in range(depth):
        for inner in range(2):
            refs.small_away[outer, inner] = refs.slices[outer * 4 + inner * 2 + 1 - x]
    small = links.copy(refs.small_away, refs.small_one, reducer.across[0])
    for seq in range(seqs):
        for first in range(0, width, span):
            refs.d_tokens[seq, :, first : first + span] = refs.hidden_two_in[
                first : first + span, seq * span : (seq + 1) * span
            ].T
    reducer.second(out[0])
    for piece in given[2:] + halves:
        fourth(piece)
    for piece in last:
        reducer.second(piece)
    small.wait_recv()
    for outer in range(depth):
        for inner in range(2):
            refs.small_one[outer, inner] += refs.slices[outer * 4 + inner * 2 + x]
    small = links.copy(refs.small_one.at[:, 1 - y], refs.small_two, reducer.across[1])
    for piece in up + out:
        reducer.third(piece)
    for piece in qkv + down:
        fourth(piece)
    small.wait_recv()
    for outer in range(depth):
        refs.small_two[outer] += refs.small_one[outer, y]
    smalls = [
        links.copy(refs.small_two.at[other], refs.small_three.at[step], reducer.column[step])
        for step, other in enumerate(reducer.levels)
    ]
    for piece in last:
        reducer.third(piece)
    for piece in up + out + last:
        fourth(piece)
    total = refs.small_two[reducer.level]
    for step, copy in enumerate(smalls):
        copy.wait_recv()
        total = total + refs.small_three[step]
    refs.small_sum[...] = total[:, :rows]
    for piece in given + halves + pieces:
        reducer.last(piece)
    links.finish()


def back_two(
    tables, more_tables, mid, half, d_qkv, grad, hidden_two, normed_three, slope, normed_two, active, hidden_one,
    gated, queries, mixer, carried, held, values, shifted, keys, tokens, normed_one, columns, small,
    lengths, rates, rate_weights, w_qkv, w_out, w_up, w_down, collective,
):
    n, seqs, channels, span = held.shape
    width, hidden_width = w_up.shape[1:]
    count = seqs * span
    low, wide = jnp.bfloat16, jnp.float32
    weights = gradient_weights(width, hidden_width, n)
    pieces = pieces_of(weights, BACK_TWO_ORDER)
    inputs = dict(
        tables_kept=(tables, HBM), more_tables_kept=(more_tables, HBM), mid_in=(mid, HBM), half_in=(half, HBM), d_qkv=(d_qkv, HBM), grad=(grad, HBM),
        hidden_two=(hidden_two, HBM), normed_three=(normed_three, HBM), slope=(slope, HBM),
        normed_two=(normed_two, HBM), active=(active, HBM), hidden_one=(hidden_one, HBM),
        gated=(gated, HBM), queries=(queries, HBM), mixer=(mixer, HBM), carried=(carried, HBM),
        held=(held, HBM), values=(values, HBM), shifted=(shifted, HBM), keys=(keys, HBM),
        tokens=(tokens, HBM), normed_one=(normed_one, HBM), columns=(columns, VMEM),
        small_in=(small, HBM), lengths=(lengths, VMEM), all_rates=(rates, HBM),
        all_weights=(rate_weights, HBM), w_qkv=(w_qkv, HBM), w_out=(w_out, HBM), w_up=(w_up, HBM),
        w_down=(w_down, HBM),
    )
    square, state = (width, count), (channels, 2 * STATES)
    rows = width // n
    grads = dict(
        qkv=(rows, 3 * width), down=(hidden_width // n, width), up=(rows, hidden_width),
        out=(rows, width),
    )
    outputs = dict(
        d_tokens=((seqs, span, width), wide, VMEM),
        rate_sum=((channels, STATES), wide, VMEM),
        weight_sum=((channels, STATES), wide, VMEM),
        small_sum=((16, rows), wide, VMEM),
        **{name + ONE: (shape, wide, VMEM) for name, shape in grads.items()},
        **{name + TWO: (shape, wide, VMEM) for name, shape in grads.items()},
    )
    flat = (channels // SHARE, n * seqs * SHARE, span)
    rim, lot = ((seqs, 8, width), wide), (n // 4, 2, 16, 128)
    scratch = dict(
        qkv=(w_qkv.shape[1:], low), down=(w_down.shape[1:], low), up=(w_up.shape[1:], low),
        out=(w_out.shape[1:], low),
        qkv_left=(normed_three.shape, low), qkv_right=((3 * width, count), low),
        first_left=(normed_one.shape, low), first_right=((3 * width, count), low),
        down_left=(active.shape, low), down_right=(square, low),
        up_left=(normed_two.shape, low), up_right=((hidden_width, count), low),
        out_left=(gated.shape, low), out_right=(square, low),
        hidden_two_in=(square, wide), hidden_one_in=(square, wide), grad_now=(square, wide),
        slope_in=(slope.shape, low), queries_in=(square, wide), mixer_in=(square, wide),
        carried_in=(carried.shape, low), held_in=(held.shape, low), d_mixer=(square, wide),
        from_conv=((seqs, width, span), low), d_conv=((seqs, width, span), low),
        landing=(held.shape, low), flat_x=(flat, wide),
        flat_d=(flat, wide), **rate_scratch(width, channels),
        rate_grad=(state, wide), weight_grad=(state, wide), rate_other=(state, wide),
        weight_other=(state, wide), tokens_in=(tokens.shape, low),
        rim_out=rim, rim_in=rim, small=((width, 128), wide), small_other=((width, 128), wide),
        slices=((n, 16, 128), wide), small_away=(lot, wide), small_one=(lot, wide),
        small_two=((n // 4, 16, 128), wide), small_three=((n // 4 - 1, 16, 128), wide),
        qkv_left_other=(normed_three.shape, low), qkv_right_other=((3 * width // 2, count), low),
        first_left_other=(normed_one.shape, low),
        first_right_other=((3 * width // 2, count), low),
        down_left_other=(active.shape, low), down_right_other=((width // 2, count), low),
        up_left_other=(normed_two.shape, low), up_right_other=((hidden_width // 2, count), low),
        out_left_other=(gated.shape, low), out_right_other=((width // 2, count), low),
        **reducer_scratch(6, LEFT_OVER + len(pieces), mid.shape[0], n // 4),
    )
    body = functools.partial(back_two_body, n, seqs, span, width, hidden_width)
    return launch(body, inputs, outputs, scratch, 420, collective)


def earlier_rows(own, before, steps):
    if steps == 0:
        return own
    moved = pltpu.roll(own, steps, 0)
    rim = before.shape[0]
    row = lax.broadcasted_iota(jnp.int32, (rim, own.shape[1]), 0)
    front = jnp.where(row < steps, pltpu.roll(before, steps, 0), moved[:rim])
    return jnp.concatenate([front, moved[rim:]], 0)


def forward_body(n, seqs, groups, span, group_rows, width, hidden_width, refs):
    at = HeadPlaces(n, seqs, groups)
    me, core = at.me, at.core
    channels = width // n
    half, heads = n // 2, group_rows // HEAD
    tokens = seqs * span
    links, loads = Links(refs), Loads(refs)
    peers = [lax.rem(me + step, n) for step in range(1, n)]
    after = (lax.rem(me + 1, n), core)
    barrier = pltpu.get_barrier_semaphore()
    at.signal_all(barrier, [(peer, core) for peer in peers])
    outgoing = []

    def save(source, target):
        outgoing.append(loads.start(source, target))

    load_tokens = loads.start(refs.tokens, refs.tokens_in)
    load_qkv = loads.start(refs.w_qkv.at[0], refs.qkv)
    load_cotangent = loads.start(refs.cotangent, refs.cot)
    load_out = loads.start(refs.w_out.at[0], refs.out)
    load_up = loads.start(refs.w_up.at[0], refs.up)
    load_down = loads.start(refs.w_down.at[0], refs.down)

    def normed(value, row, target):
        result = layer_norm(value, refs.gains[row : row + 1], refs.biases[row : row + 1])
        result = result.astype(jnp.bfloat16)
        target[...] = result.T
        return result

    finish_rates = fill_rates(refs, loads, channels, refs.turned_rates)
    valid = valid_positions(refs.lengths, seqs, span, 0)
    refs.columns[...] = jnp.concatenate(
        [refs.gains[...], refs.taps[...], refs.skip[...].reshape(1, width), jnp.zeros((7, width), jnp.float32)], 0
    ).T
    load_tokens.wait()
    flat_in = jnp.concatenate([refs.tokens_in[seq] for seq in range(seqs)], 0)
    flat_in = flat_in.astype(jnp.float32) * valid
    refs.flat_in[...] = flat_in
    normed_one = normed(flat_in, 0, refs.normed_one_t)
    load_qkv.wait()
    keys = dot(normed_one, refs.qkv[:, width : 2 * width]).astype(jnp.bfloat16)
    refs.keys[...] = keys
    rim = refs.rim_in.shape[1]
    at.wait_all(barrier, n - 1)
    for seq in range(seqs):
        refs.rim_out[seq] = refs.keys[(seq + 1) * span - rim : (seq + 1) * span, :]
    halo = links.copy(refs.rim_out, refs.rim_in, after)
    refs.values[...] = dot(normed_one, refs.qkv[:, 2 * width :])
    refs.queries[...] = dot(normed_one, refs.qkv[:, :width])
    load_qkv = loads.start(refs.w_qkv.at[1], refs.qkv)
    finish_rates()
    fill_tables(0, SHARE, span, refs)
    halo.wait_recv()
    there = jnp.where(me == 0, 0.0, 1.0)
    for seq in range(seqs):
        rows = slice(seq * span, (seq + 1) * span)
        before = refs.rim_in[seq].astype(jnp.float32) * there
        own = refs.keys[rows, :].astype(jnp.float32)
        shifted = jnp.zeros_like(own)
        for offset in range(TAPS):
            shifted = shifted + refs.taps[offset : offset + 1] * earlier_rows(own, before, offset)
        refs.shifted[rows, :] = shifted
        carried = (shifted * refs.values[rows, :] * valid[rows]).astype(jnp.bfloat16)
        refs.carried[rows, :] = carried
        refs.carried_t[seq] = carried.T

    shares = channels // SHARE
    arrive, answered = links.slots(shares * n), links.slots(shares * n)

    def share_rows(device, share):
        return pl.ds(pl.multiple_of(device * channels + share * SHARE, 16), SHARE)

    going, own_copies = [], []
    for share in range(shares):
        within = slice(share * SHARE, (share + 1) * SHARE)
        for step, peer in enumerate(peers):
            going.append(
                links.copy(
                    refs.carried_t.at[:, share_rows(peer, share), :],
                    refs.mixed_in.at[me, :, within, :], (peer, core), arrive + share * n + step,
                )
            )
        own_copies.append(
            loads.start(
                refs.carried_t.at[:, share_rows(me, share), :], refs.mixed_in.at[me, :, within, :]
            )
        )
    fill_tables(SHARE, channels, span, refs)
    save(refs.tables, refs.tables_kept)
    save(refs.more_tables, refs.more_tables_kept)
    refs.square_t[...] = refs.values[...].T
    save(refs.square_t, refs.values_t)
    refs.square_two_t[...] = refs.shifted[...].T
    save(refs.square_two_t, refs.shifted_t)
    for seq in range(seqs):
        refs.keys_out[seq] = refs.keys[seq * span : (seq + 1) * span, :].T
    save(refs.keys_out, refs.keys_t)
    refs.queries_out[...] = refs.queries[...].T
    save(refs.queries_out, refs.queries_t)
    save(refs.normed_one_t, refs.normed_one)
    save(refs.carried_t, refs.carried_out)
    back, back_own = [], []
    for share in range(shares):
        within = slice(share * SHARE, (share + 1) * SHARE)
        own_copies[share].wait()
        for copy in going[share * len(peers) : (share + 1) * len(peers)]:
            copy.wait_recv()
        refs.flat_x[share] = (
            refs.mixed_in[:, :, within, :].astype(jnp.float32).reshape(n * seqs * SHARE, span)
        )

        def one_channel(local, carry):
            mixer_forward_channel(n, seqs, refs, share, local)
            return carry

        lax.fori_loop(0, SHARE, one_channel, 0, unroll=4)
        refs.answer[:, :, within, :] = (
            refs.flat_out[share].reshape(n, seqs, SHARE, span).astype(jnp.bfloat16)
        )
        for step, peer in enumerate(peers):
            back.append(
                links.copy(
                    refs.answer.at[peer, :, within, :],
                    refs.convolved.at[:, share_rows(me, share), :], (peer, core),
                    answered + share * n + step,
                )
            )
        back_own.append(
            loads.start(
                refs.answer.at[me, :, within, :], refs.convolved.at[:, share_rows(me, share), :]
            )
        )
    save(refs.mixed_in, refs.mixed_held)
    for copy in back_own:
        copy.wait()
    for copy in back:
        copy.wait_recv()
    for seq in range(seqs):
        rows = slice(seq * span, (seq + 1) * span)
        convolved = refs.convolved[seq].astype(jnp.float32).T
        mixer = convolved + refs.skip[...].reshape(1, width) * refs.carried[rows, :].astype(jnp.float32)
        refs.gated[rows, :] = (refs.queries[rows, :] * mixer).astype(jnp.bfloat16)
        refs.mixer_out[:, rows] = mixer.T
    save(refs.mixer_out, refs.mixer_t)
    refs.gated_out[...] = refs.gated[...].T
    save(refs.gated_out, refs.gated_t)
    load_out.wait()
    hidden = refs.flat_in[...] + dot(refs.gated[...], refs.out[...])
    load_out = loads.start(refs.w_out.at[1], refs.out)

    def feed_forward(hidden, row, hidden_out, normed_out, up, down):
        hidden_out[...] = hidden.T
        refs.hidden[...] = hidden
        refs.normed[...] = normed(hidden, row, normed_out)
        up.wait()

        def one_chunk(index, carry):
            columns = pl.ds(pl.multiple_of(index * width, 128), width)
            raised = dot(refs.normed[...], refs.up[:, columns])
            refs.raised[:, columns] = raised
            refs.active[:, columns] = jax.nn.gelu(raised).astype(jnp.bfloat16)
            return carry

        lax.fori_loop(0, hidden_width // width, one_chunk, 0)
        if down is not None:
            down.wait()
        return refs.hidden[...] + dot(refs.active[...], refs.down[...])

    def turn_hidden(active_out, slope_out):
        def one_chunk(index, carry):
            columns = pl.ds(pl.multiple_of(index * width, 128), width)
            active_out[columns, :] = refs.active[:, columns].T
            slope = gelu_slope(refs.raised[:, columns]).astype(jnp.bfloat16)
            slope_out[columns, :] = slope.T
            return carry

        lax.fori_loop(0, hidden_width // width, one_chunk, 0)

    hidden = feed_forward(
        hidden, 1, refs.hidden_one_t, refs.normed_two_t, load_up, load_down
    )
    load_up = loads.start(refs.w_up.at[1], refs.up)
    load_down = loads.start(refs.w_down.at[1], refs.down)
    refs.hidden[...] = hidden
    refs.normed[...] = normed(hidden, 2, refs.normed_three_t)
    load_qkv.wait()
    count = len(at.targets)
    arrive, leave = links.slots(heads * half), links.slots(heads * count)
    passing = links.slots(heads * half)
    spread = []
    lot = groups * HEAD
    for head in range(heads):
        for part in range(3):
            first = part * width + head * lot
            columns = dot(refs.normed[...], refs.qkv[:, first : first + lot]).astype(jnp.bfloat16)
            for seq in range(seqs):
                refs.spread[head, seq, :, part * HEAD : (part + 1) * HEAD] = columns[
                    seq * span : (seq + 1) * span
                ].T.reshape(groups, HEAD, span)
        for number, (device, seq, group) in enumerate(at.targets):
            sent = (
                refs.spread.at[head, seq, group], refs.held.at[head, me],
                refs.send.at[leave + head * count + number],
                refs.recv.at[arrive + head * half + me // 2], device,
            )
            at.send(*sent)
            spread.append(sent)
    turn_hidden(refs.active_one_t, refs.slope_one_t)
    load_cotangent.wait()
    valid_row = valid_positions(refs.lengths, seqs, span, 1)
    for seq in range(seqs):
        lanes = slice(seq * span, (seq + 1) * span)
        turned = refs.cot[seq].astype(jnp.float32).T * valid_row[:, lanes]
        refs.branch_t[:, lanes] = turned.astype(jnp.bfloat16)
    save(refs.branch_t, refs.branch)
    load_down.wait()

    def store_active(rows, value):
        refs.d_active_t[rows, :] = value.astype(jnp.bfloat16)

    rows_product(refs.down, refs.branch_t[...], hidden_width, 512, store_active)
    save(refs.d_active_t, refs.d_active)
    refs.hidden_two_t[...] = hidden.T
    for source, target in (
        (refs.hidden_one_t, refs.hidden_one_out), (refs.normed_two_t, refs.normed_two),
        (refs.active_one_t, refs.active_one), (refs.slope_one_t, refs.slope_one),
        (refs.hidden_two_t, refs.hidden_two_out), (refs.normed_three_t, refs.normed_three),
    ):
        save(source, target)

    returned, returning = links.slots(heads * count), links.slots(heads * half)
    slot = at.seq * groups + at.group
    going = []

    def gather(head):
        for index, block in enumerate(at.blocks):
            landed = refs.held.at[head, block]
            remote(
                landed, landed, refs.send.at[leave], refs.recv.at[arrive + head * half + index],
                at.sibling,
            ).wait_recv()
            part = refs.held.at[head, block, HEAD : 3 * HEAD]
            links.copy(part, part, at.sibling, passing + head * half + index)
        for index in range(half):
            part = refs.held.at[head, block_of(index, 1 - core), HEAD : 3 * HEAD]
            remote(
                part, part, refs.send.at[leave], refs.recv.at[passing + head * half + index],
                at.sibling,
            ).wait_recv()

    def attend(head):
        fill_head(refs.held, head, 1, n, span, refs.key_rows, None)
        fill_head(refs.held, head, 2, n, span, None, refs.value_columns)
        for index, block in enumerate(at.blocks):
            query = refs.held[head, block, :HEAD, :] * jnp.bfloat16(HEAD**-0.5)
            clear, reach = 2 * index * span, 2 * (index + 1) * span
            edge = dot(refs.key_rows[clear:reach, :], query)
            edge = jnp.where(causal(clear, reach - clear, block * span, span), edge, masked_score)
            top = jnp.max(edge, 0, keepdims=True)
            if index > 0:
                body = dot(refs.key_rows[:clear, :], query)
                top = jnp.maximum(top, jnp.max(body, 0, keepdims=True))
            edge = jnp.exp(edge - top)
            total = jnp.sum(edge, 0, keepdims=True)
            result = dot(refs.value_columns[:, clear:reach], edge.astype(jnp.bfloat16))
            if index > 0:
                body = jnp.exp(body - top)
                total = total + jnp.sum(body, 0, keepdims=True)
                result = result + dot(refs.value_columns[:, :clear], body.astype(jnp.bfloat16))
            refs.outputs[head, index] = (result / total).astype(jnp.bfloat16)
            refs.lse[index, head : head + 1, :] = top + jnp.log(total)
        into = refs.attended_t.at[
            pl.ds(pl.multiple_of(head * lot + at.group * HEAD, HEAD), HEAD),
            pl.ds(pl.multiple_of(at.seq * span, span), span),
        ]
        for index, device in enumerate(at.sources):
            sent = (
                refs.outputs.at[head, index], into, refs.send.at[returning + head * half + index],
                refs.recv.at[returned + head * count + slot], device,
            )
            at.send(*sent)
            going.append(sent)

    for head in range(heads):
        gather(head)
        attend(head)
    save(refs.held, refs.held_out)
    for head in range(heads):
        for number, (device, seq, group) in enumerate(at.targets):
            first = head * lot + group * HEAD
            landed = refs.attended_t.at[first : first + HEAD, seq * span : (seq + 1) * span]
            remote(
                landed, landed, refs.send.at[leave],
                refs.recv.at[returned + head * count + number], at.sibling,
            ).wait_recv()
    save(refs.attended_t, refs.attended)
    load_out.wait()
    hidden = refs.hidden[...] + dot(refs.attended_t[...].T, refs.out[...])
    hidden = feed_forward(
        hidden, 3, refs.hidden_three_t, refs.normed_four_t, load_up, None
    )
    turn_hidden(refs.active_two_t, refs.slope_two_t)
    for source, target in (
        (refs.hidden_three_t, refs.hidden_three_out), (refs.normed_four_t, refs.normed_four),
        (refs.active_two_t, refs.active_two), (refs.slope_two_t, refs.slope_two),
    ):
        save(source, target)
    hidden = (hidden * valid).astype(jnp.bfloat16)
    for seq in range(seqs):
        refs.mixed[seq] = hidden[seq * span : (seq + 1) * span]
    for copy in outgoing:
        copy.wait()
    for sent in spread + going:
        at.wait_sent(*sent)
    links.finish()


def forward(
    tokens, cotangent, lengths, gains, biases, taps, skip, rates, rate_weights, w_qkv, w_out, w_up, w_down, n,
    groups, collective,
):
    seqs, span, width = tokens.shape
    hidden_width = w_up.shape[2]
    group_rows, channels = width // groups, width // n
    rows = seqs * span
    half, heads = n // 2, group_rows // HEAD
    low, wide = jnp.bfloat16, jnp.float32
    inputs = dict(
        tokens=(tokens, HBM), cotangent=(cotangent, HBM), lengths=(lengths, VMEM), gains=(gains, VMEM), biases=(biases, VMEM),
        taps=(taps, VMEM), skip=(skip, VMEM), all_rates=(rates, HBM), all_weights=(rate_weights, HBM),
        w_qkv=(w_qkv, HBM), w_out=(w_out, HBM), w_up=(w_up, HBM), w_down=(w_down, HBM),
    )
    square, tall, by_head = (width, rows), (hidden_width, rows), (heads, n, 3 * HEAD, span)
    mixed = (n, seqs, channels, span)
    tables, more_tables = table_shapes(channels, span)
    outputs = dict(
        mixed=((seqs, span, width), low, VMEM), columns=((width, 16), wide, VMEM),
        lse=((half, heads, span), wide, VMEM),
        held_out=(by_head, low, HBM), mixed_held=(mixed, low, HBM),
        carried_out=((seqs, width, span), low, HBM),
        values_t=(square, wide, HBM), shifted_t=(square, wide, HBM), keys_t=((seqs, width, span), low, HBM),
        queries_t=(square, wide, HBM), mixer_t=(square, wide, HBM), gated_t=(square, low, HBM),
        attended=(square, low, HBM), branch=(square, low, HBM), d_active=(tall, low, HBM),
        normed_one=(square, low, HBM), normed_two=(square, low, HBM),
        normed_three=(square, low, HBM), normed_four=(square, low, HBM),
        hidden_one_out=(square, wide, HBM), hidden_two_out=(square, wide, HBM),
        hidden_three_out=(square, wide, HBM),
        active_one=(tall, low, HBM), active_two=(tall, low, HBM),
        slope_one=(tall, low, HBM), slope_two=(tall, low, HBM),
        tables_kept=(tables, low, HBM), more_tables_kept=(more_tables, low, HBM),
    )
    flat = (channels // SHARE, n * seqs * SHARE, span)
    lying = (rows, width)
    scratch = dict(
        qkv=(w_qkv.shape[1:], low), out=(w_out.shape[1:], low), up=(w_up.shape[1:], low),
        down=(w_down.shape[1:], low), tokens_in=(tokens.shape, low), flat_in=(lying, wide),
        keys=(lying, low), values=(lying, wide), queries=(lying, wide), shifted=(lying, wide),
        carried=(lying, low), gated=(lying, low), hidden=(lying, wide), normed=(lying, low),
        active=((rows, hidden_width), low), rim_in=((seqs, 16, width), low),
        rim_out=((seqs, 16, width), low), carried_t=((seqs, width, span), low),
        convolved=((seqs, width, span), low), mixed_in=(mixed, low), answer=(mixed, low),
        flat_x=(flat, wide), flat_out=(flat, wide), tables=(tables, low), more_tables=(more_tables, low),
        turned_rates=((width, 2 * STATES), wide),
        **rate_scratch(width, channels), raised=((rows, hidden_width), wide),
        cot=(tokens.shape, low), branch_t=(square, low), d_active_t=(tall, low),
        square_t=(square, wide), square_two_t=(square, wide), keys_out=((seqs, width, span), low),
        queries_out=(square, wide), mixer_out=(square, wide), gated_out=(square, low),
        attended_t=(square, low), normed_one_t=(square, low), normed_two_t=(square, low),
        normed_three_t=(square, low), normed_four_t=(square, low), hidden_one_t=(square, wide),
        hidden_two_t=(square, wide), hidden_three_t=(square, wide), active_one_t=(tall, low),
        active_two_t=(tall, low), slope_one_t=(tall, low), slope_two_t=(tall, low),
        spread=((heads, seqs, groups, 3 * HEAD, span), low), held=(by_head, low),
        outputs=((heads, half, HEAD, span), low), key_rows=((n * span, HEAD), low),
        value_columns=((HEAD, n * span), low),
    )
    body = functools.partial(
        forward_body, n, seqs, groups, span, group_rows, width, hidden_width
    )
    return launch(body, inputs, outputs, scratch, 290, collective)


def per_device_by_heads(
    tokens,
    cotangent,
    lengths,
    norm_gain,
    norm_bias,
    w_qkv,
    w_out,
    w_up,
    w_down,
    taps,
    skip,
    ssm_rate,
    ssm_out,
):
    seq_count, span_rows, width = tokens.shape[1:]
    devices = lax.axis_size(SEQ)
    channels = width // devices
    groups = devices // 4
    row_count = seq_count * span_rows
    rates, weights = ssm_rate.T, ssm_out.T
    kept = forward(
        tokens[0], cotangent[0], lengths, norm_gain, norm_bias, taps, skip, rates, weights, w_qkv, w_out,
        w_up, w_down, devices, groups, 1,
    )

    def sliced(value):
        return value.reshape(devices, value.shape[0] // devices, row_count)

    back = back_one(
        kept.branch, kept.d_active, kept.hidden_three_out, kept.slope_two, sliced(kept.normed_four),
        sliced(kept.active_two), sliced(kept.attended), kept.held_out, kept.lse, kept.columns,
        w_out, w_up, 3,
    )
    end = back_two(
        kept.tables_kept, kept.more_tables_kept, back.mid_out, back.half_out, back.d_qkv.reshape(3 * width, row_count),
        back.grad_out, kept.hidden_two_out, sliced(kept.normed_three), kept.slope_one,
        sliced(kept.normed_two), sliced(kept.active_one), kept.hidden_one_out,
        sliced(kept.gated_t), kept.queries_t, kept.mixer_t, kept.carried_out, kept.mixed_held,
        kept.values_t, kept.shifted_t, kept.keys_t, tokens[0], sliced(kept.normed_one),
        kept.columns, back.small, lengths, rates, weights, w_qkv, w_out, w_up, w_down, 4,
    )
    return collected(kept, end, norm_gain.shape[0])


def collected(kept, end, layers):
    pairs = [
        (end.qkv_one, end.qkv_two), (end.out_one, end.out_two), (end.up_one, end.up_two),
        (end.down_one, end.down_two),
    ]
    alone = [kept.mixed, end.d_tokens, end.rate_sum, end.weight_sum]
    rows = end.small_sum.shape[1]
    small = [(layers, rows), (layers - 1, rows), (rows,), (TAPS, rows), (rows,)]
    wide = jnp.float32

    def body(*refs):
        refs = list(refs)
        pair_refs = [(refs.pop(0), refs.pop(0)) for _ in pairs]
        alone_refs = [refs.pop(0) for _ in alone]
        sums = refs.pop(0)
        for first, second in pair_refs:
            out = refs.pop(0)
            out[0] = first[...]
            out[1] = second[...]
        for source in alone_refs:
            refs.pop(0)[...] = source[...]
        gain, bias, last, taps, skip = refs
        gain[...] = sums[:layers, :]
        bias[...] = sums[layers : 2 * layers - 1, :]
        last[...] = sums[2 * layers - 1, :]
        taps[...] = sums[2 * layers : 2 * layers + TAPS, :]
        skip[...] = sums[2 * layers + TAPS, :]

    arrays = [array for pair in pairs for array in pair] + alone + [end.small_sum]
    shapes = [jax.ShapeDtypeStruct((2, *first.shape), wide) for first, _ in pairs]
    shapes += [jax.ShapeDtypeStruct(array.shape, array.dtype) for array in alone]
    shapes += [jax.ShapeDtypeStruct(shape, wide) for shape in small]
    vmem = pl.BlockSpec(memory_space=VMEM)
    outs = pl.pallas_call(
        body,
        out_shape=tuple(shapes),
        in_specs=[vmem] * len(arrays),
        out_specs=(vmem,) * len(shapes),
        compiler_params=pltpu.CompilerParams(vmem_limit_bytes=VMEM_BYTES),
    )(*arrays)
    qkv, out, up, down, mixed, d_tokens, rate, weight, gain, bias, last, taps, skip = outs
    return (
        mixed[None], d_tokens[None], gain, bias, last, qkv, out, up, down, taps, skip, rate, weight,
    )


def fits_by_heads(mesh):
    devices = mesh.shape[SEQ]
    return devices == 16 and mesh.shape[BATCH] == 2


def solution(mesh):
    placed = (
        P(BATCH, None, SEQ, None),
        P(BATCH, None, SEQ, None),
        P(BATCH, None),
        P(),
        P(),
        P(),
        P(),
        P(),
        P(),
        P(),
        P(),
        P(),
        P(),
    )
    return jax.shard_map(
        per_device_by_heads if fits_by_heads(mesh) else per_device,
        mesh=mesh,
        in_specs=placed,
        out_specs=(
            P(BATCH, None, SEQ, None),
            P(BATCH, None, SEQ, None),
            P(None, SEQ),
            P(None, SEQ),
            P(SEQ),
            P(None, SEQ, None),
            P(None, SEQ, None),
            P(None, SEQ, None),
            P(None, SEQ, None),
            P(None, SEQ),
            P(SEQ),
            P(SEQ, None),
            P(SEQ, None),
        ),
        check_vma=False,
    )
```

```python
import functools
import math
import types

import jax
import jax.numpy as jnp
from jax import lax
from jax.experimental import pallas as pl
from jax.experimental.pallas import tpu as pltpu
from jax.sharding import PartitionSpec as P

HEADS = 12
HEAD = 64
TAPS = 4
STATES = 64
KEPT = "_kept"
ONE = "_one"
TWO = "_two"
FIRST = "first"
MESH = pl.DeviceIdType.MESH
SEQ = "seq"
BATCH = "batch"
QKV_MORE = "qkv_more"
QKV_LESS = "qkv_less"
DOWN = "down"
OUT = "out"
UP = "up"
QKV = "qkv"
SMALL = "small"
VMEM_BYTES = 63 * 2**20


norm_eps = 1e-05
highest = lax.Precision.HIGHEST
masked_score = -1e30


def for_sending(array):
    return jax.tree.map(lambda a: a.astype(jnp.bfloat16) if a.dtype == jnp.float32 else a, array)


def passed_along(value, axis, steps):
    count = lax.axis_size(axis)
    initial, last = (max(0, -steps), min(count, count - steps))
    return lax.ppermute(value, axis, [(source, source + steps) for source in range(initial, last)])


def layer_norm(inputs, scale_row, shift_row):
    center = inputs - jnp.mean(inputs, -1, keepdims=True)
    spread = jnp.mean(center * center, -1, keepdims=True)
    return center * lax.rsqrt(spread + norm_eps) * scale_row + shift_row


def dense_product(operand_a, operand_b):
    return jnp.dot(operand_a, operand_b, preferred_element_type=jnp.float32)


def product_left(operand_a, operand_b):
    return lax.dot_general(
        operand_a, operand_b, (((0,), (0,)), ((), ())), preferred_element_type=jnp.float32
    )


def product_right(operand_a, operand_b):
    return lax.dot_general(
        operand_a, operand_b, (((1,), (1,)), ((), ())), preferred_element_type=jnp.float32
    )


def angle_table(count_rows, count_cols, period):
    product_index = (
        jnp.arange(count_rows, dtype=jnp.int32)[:, None]
        * jnp.arange(count_cols, dtype=jnp.int32)[None, :]
        % period
    )
    angles = product_index.astype(jnp.float32) * (2.0 * math.pi / period)
    return (jnp.cos(angles), jnp.sin(angles))


def table_einsum(form, table, data):
    return jnp.einsum(form, table, data, precision=highest)


def forward_spectrum(time_parts):
    count_parts = time_parts.shape[0]
    span_rows = time_parts.shape[2]
    count_freq = 2 * count_parts
    cos_parts, sin_parts = angle_table(count_freq, count_parts, count_freq)
    first_real = table_einsum("fp,pjsc->fjsc", cos_parts, time_parts)
    first_imag = -table_einsum("fp,pjsc->fjsc", sin_parts, time_parts)
    cos_twist, sin_twist = angle_table(count_freq, span_rows, count_freq * span_rows)
    cos_twist = cos_twist[:, None, :, None]
    sin_twist = sin_twist[:, None, :, None]
    twist_real = first_real * cos_twist + first_imag * sin_twist
    twist_imag = first_imag * cos_twist - first_real * sin_twist
    cos_span, sin_span = angle_table(span_rows, span_rows, span_rows)
    out_real = table_einsum("ts,fjsc->fjtc", cos_span, twist_real) + table_einsum(
        "ts,fjsc->fjtc", sin_span, twist_imag
    )
    out_imag = table_einsum("ts,fjsc->fjtc", cos_span, twist_imag) - table_einsum(
        "ts,fjsc->fjtc", sin_span, twist_real
    )
    return (out_real, out_imag)


def inverse_spectrum(freq_real, freq_imag):
    count_freq = freq_real.shape[0]
    span_rows = freq_real.shape[2]
    count_parts = count_freq // 2
    fft_length = count_freq * span_rows
    cos_span, sin_span = angle_table(span_rows, span_rows, span_rows)
    first_real = table_einsum("st,fjtc->fjsc", cos_span, freq_real) - table_einsum(
        "st,fjtc->fjsc", sin_span, freq_imag
    )
    first_imag = table_einsum("st,fjtc->fjsc", cos_span, freq_imag) + table_einsum(
        "st,fjtc->fjsc", sin_span, freq_real
    )
    cos_twist, sin_twist = angle_table(count_freq, span_rows, fft_length)
    cos_twist = cos_twist[:, None, :, None]
    sin_twist = sin_twist[:, None, :, None]
    twist_real = first_real * cos_twist - first_imag * sin_twist
    twist_imag = first_imag * cos_twist + first_real * sin_twist
    cos_parts, sin_parts = angle_table(count_parts, count_freq, count_freq)
    summed = table_einsum("pf,fjsc->pjsc", cos_parts, twist_real) - table_einsum(
        "pf,fjsc->pjsc", sin_parts, twist_imag
    )
    return summed / fft_length


def to_frequency(data_low):
    parts = lax.all_to_all(data_low[None], SEQ, split_axis=3, concat_axis=0, tiled=True)
    return forward_spectrum(parts.astype(jnp.float32))


def from_frequency(freq_real, freq_imag):
    time_parts = inverse_spectrum(freq_real, freq_imag)
    joined = lax.all_to_all(
        for_sending(time_parts), SEQ, split_axis=0, concat_axis=3, tiled=True
    ).astype(time_parts.dtype)
    return joined[0]


def kernel_parts(rate_slice, weight_slice, count_freq, span_rows):
    fft_length = count_freq * span_rows
    length_full = fft_length // 2
    frequency = (
        jnp.arange(count_freq, dtype=jnp.int32)[:, None]
        + count_freq * jnp.arange(span_rows, dtype=jnp.int32)[None, :]
    )
    angles = (frequency.astype(jnp.float32) * (2.0 * math.pi / fft_length))[:, None, :, None, None]
    odd_mask = (frequency % 2 == 1)[:, None, :, None, None]
    channels = rate_slice.shape[0]
    blocks = rate_slice.shape[1] // 8
    rate_blocks = rate_slice.reshape(channels, blocks, 8).transpose(1, 0, 2)
    weight_blocks = weight_slice.reshape(channels, blocks, 8).transpose(1, 0, 2)

    def add_block(running, piece_pair):
        rate_part, weight_part = piece_pair
        decays = jnp.exp(-rate_part)
        half_sine = jnp.sin(angles / 2.0)
        real_den = -jnp.expm1(-rate_part) + decays * 2.0 * half_sine * half_sine
        imag_den = decays * jnp.sin(angles)
        numerator = jnp.where(
            odd_mask, 1.0 + jnp.exp(-rate_part * length_full), -jnp.expm1(-rate_part * length_full)
        )
        factor = weight_part * numerator / (real_den * real_den + imag_den * imag_den)
        return (
            (
                running[0] + jnp.sum(factor * real_den, -1),
                running[1] - jnp.sum(factor * imag_den, -1),
            ),
            None,
        )

    zeros_init = jnp.zeros((count_freq, 1, span_rows, channels), jnp.float32)
    return lax.scan(
        jax.checkpoint(add_block), (zeros_init, zeros_init), (rate_blocks, weight_blocks)
    )[0]


def attention_mask(query_positions, key_count, length_value):
    key_positions = jnp.arange(key_count, dtype=jnp.int32)
    return (key_positions[None, :] <= query_positions[:, None]) & (
        key_positions[None, :] < length_value
    )


def head_slice(matrix, head_index):
    return lax.dynamic_slice_in_dim(matrix, head_index * HEAD, HEAD, 1)


def attend_forward(query_low, keys_low, values_low, length_value, query_positions):
    whole_keys, whole_values = (
        lax.all_gather(keys_low, SEQ, axis=0, tiled=True),
        lax.all_gather(values_low, SEQ, axis=0, tiled=True),
    )
    allowed = attention_mask(query_positions, whole_keys.shape[0], length_value)
    score_scale = HEAD ** (-0.5)

    def head_forward(head_index):
        scores = jnp.where(
            allowed,
            score_scale
            * product_right(head_slice(query_low, head_index), head_slice(whole_keys, head_index)),
            masked_score,
        )
        top_score = jnp.max(scores, -1, keepdims=True)
        expos = jnp.exp(scores - top_score)
        totals = jnp.sum(expos, -1, keepdims=True)
        probs_low = (expos / totals).astype(jnp.bfloat16)
        return (
            dense_product(probs_low, head_slice(whole_values, head_index)),
            (top_score + jnp.log(totals))[:, 0],
        )

    head_outputs, log_totals = lax.map(head_forward, jnp.arange(HEADS, dtype=jnp.int32))
    attended = head_outputs.transpose(1, 0, 2).reshape(query_low.shape[0], HEADS * HEAD)
    return (attended, log_totals, whole_keys, whole_values)


def join_heads(head_rows):
    return head_rows.transpose(1, 0, 2).reshape(head_rows.shape[1], HEADS * HEAD)


def attend_backward(
    query_low, whole_keys, whole_values, log_totals, grad_low, length_value, query_positions
):
    allowed = attention_mask(query_positions, whole_keys.shape[0], length_value)
    score_scale = HEAD ** (-0.5)
    span_rows = query_low.shape[0]

    def query_side(head_index):
        head_query = head_slice(query_low, head_index)
        head_keys = head_slice(whole_keys, head_index)
        head_grad = head_slice(grad_low, head_index)
        scores = jnp.where(
            allowed, score_scale * product_right(head_query, head_keys), masked_score
        )
        weights = jnp.exp(scores - log_totals[head_index][:, None])
        d_weights = product_right(head_grad, head_slice(whole_values, head_index))
        row_term = jnp.sum(weights * d_weights, -1, keepdims=True)
        d_scores = (weights * (d_weights - row_term)).astype(jnp.bfloat16)
        d_query = score_scale * dense_product(d_scores, head_keys)
        return (d_query, row_term[:, 0], d_scores, weights)

    def head_backward(head_index):
        d_query, row_term, d_scores, weights = query_side(head_index)
        head_query = head_slice(query_low, head_index)
        head_grad = head_slice(grad_low, head_index)
        d_keys = score_scale * product_left(d_scores, head_query)
        d_values = product_left(weights.astype(jnp.bfloat16), head_grad)
        return (d_query, d_keys, d_values)

    query_grads, key_grads, value_grads = lax.map(head_backward, jnp.arange(HEADS, dtype=jnp.int32))
    count_rows = span_rows * lax.axis_size(SEQ)
    key_part = (
        lax.slice_in_dim(key_grads, 0, count_rows, axis=1)
        .transpose(1, 0, 2)
        .reshape(count_rows, HEADS * HEAD)
    )
    value_part = (
        lax.slice_in_dim(value_grads, 0, count_rows, axis=1)
        .transpose(1, 0, 2)
        .reshape(count_rows, HEADS * HEAD)
    )
    key_value = lax.psum_scatter(
        jnp.stack([key_part, value_part], 1), SEQ, scatter_dimension=0, tiled=True
    )
    return (join_heads(query_grads), key_value[:, 0], key_value[:, 1])


def per_device(
    tokens,
    cotangent,
    lengths,
    norm_gain,
    norm_bias,
    w_qkv,
    w_out,
    w_up,
    w_down,
    taps,
    skip,
    ssm_rate,
    ssm_out,
):
    seq_count = tokens.shape[1]
    span_rows = tokens.shape[2]
    width = tokens.shape[3]
    devices = lax.axis_size(SEQ)
    place = lax.axis_index(SEQ)
    channels = width // devices
    count_freq = 2 * devices
    fft_length = count_freq * span_rows
    rim = TAPS - 1
    row_count = seq_count * span_rows
    query_positions = place * span_rows + jnp.arange(span_rows, dtype=jnp.int32)
    validity = (query_positions[None, :] < lengths[0][:, None]).astype(jnp.float32)[:, :, None]
    rate_slice = lax.dynamic_slice_in_dim(ssm_rate, place * channels, channels, 0)
    weight_slice = lax.dynamic_slice_in_dim(ssm_out, place * channels, channels, 0)

    def spectrum_of(rate_in, weight_in):
        return kernel_parts(rate_in, weight_in, count_freq, span_rows)

    def feed_forward(inputs, norm_row, layer):
        normed_low = layer_norm(inputs, norm_gain[norm_row], norm_bias[norm_row]).astype(
            jnp.bfloat16
        )
        raised = dense_product(normed_low, w_up[layer])
        active_low = jax.nn.gelu(raised).astype(jnp.bfloat16)
        return (normed_low, raised, active_low, inputs + dense_product(active_low, w_down[layer]))

    def norm_backward(inputs, norm_row, d_normed):
        norm_pull = jax.vjp(layer_norm, inputs, norm_gain[norm_row], norm_bias[norm_row])[1]
        return norm_pull(d_normed)

    def feed_backward(grad_rows, inputs, normed_low, raised, active_low, norm_row, layer):
        branch_low = grad_rows.astype(jnp.bfloat16)
        down_grad = product_left(active_low, branch_low)
        d_active = product_right(branch_low, w_down[layer])
        gelu_pull = jax.vjp(jax.nn.gelu, raised)[1]
        d_raised = gelu_pull(d_active)[0].astype(jnp.bfloat16)
        up_grad = product_left(normed_low, d_raised)
        d_inputs, gain_part, bias_part = norm_backward(
            inputs, norm_row, product_right(d_raised, w_up[layer])
        )
        return (grad_rows + d_inputs, down_grad, up_grad, gain_part, bias_part)

    def forward_pass(token_block):
        masked_in = token_block[0].astype(jnp.float32) * validity
        flat_in = masked_in.reshape(row_count, width)
        normed_one = layer_norm(flat_in, norm_gain[0], norm_bias[0]).astype(jnp.bfloat16)
        qkv_one = dense_product(normed_one, w_qkv[0]).reshape(seq_count, span_rows, 3 * width)
        queries_one = qkv_one[:, :, :width]
        keys_one = qkv_one[:, :, width : 2 * width].astype(jnp.bfloat16)
        values_one = qkv_one[:, :, 2 * width :]
        earlier = passed_along(keys_one[:, span_rows - rim :], SEQ, 1)
        extended = jnp.concatenate([earlier, keys_one], 1)
        shifted = sum(
            (
                taps[offset]
                * extended[:, rim - offset : rim - offset + span_rows].astype(jnp.float32)
                for offset in range(TAPS)
            )
        )
        carried_low = (shifted * values_one * validity).astype(jnp.bfloat16)
        carried_real, carried_imag = to_frequency(carried_low)
        kernel_both, kernel_pull = jax.vjp(spectrum_of, rate_slice, weight_slice)
        kernel_real, kernel_imag = kernel_both
        convolved = from_frequency(
            carried_real * kernel_real - carried_imag * kernel_imag,
            carried_real * kernel_imag + carried_imag * kernel_real,
        )
        carried = carried_low.astype(jnp.float32)
        mixer = convolved + skip * carried
        gated_low = (queries_one * mixer).reshape(row_count, width).astype(jnp.bfloat16)
        hidden_one = flat_in + dense_product(gated_low, w_out[0])
        normed_two, raised_one, active_one, hidden_two = feed_forward(hidden_one, 1, 0)
        normed_three = layer_norm(hidden_two, norm_gain[2], norm_bias[2]).astype(jnp.bfloat16)
        qkv_two = (
            dense_product(normed_three, w_qkv[1])
            .astype(jnp.bfloat16)
            .reshape(seq_count, span_rows, 3 * width)
        )
        attended_list = []
        totals_list = []
        keys_list = []
        values_list = []
        for seq_index in range(seq_count):
            attended, log_totals, whole_keys, whole_values = attend_forward(
                qkv_two[seq_index, :, :width],
                qkv_two[seq_index, :, width : 2 * width],
                qkv_two[seq_index, :, 2 * width :],
                lengths[0, seq_index],
                query_positions,
            )
            attended_list.append(attended)
            totals_list.append(log_totals)
            keys_list.append(whole_keys)
            values_list.append(whole_values)
        attended_low = jnp.concatenate(attended_list, 0).astype(jnp.bfloat16)
        hidden_three = hidden_two + dense_product(attended_low, w_out[1])
        normed_four, raised_two, active_two, hidden_four = feed_forward(hidden_three, 3, 1)
        output = hidden_four.reshape(seq_count, span_rows, width) * validity
        saved = types.SimpleNamespace(
            flat_in=flat_in,
            normed_one=normed_one,
            queries_one=queries_one,
            values_one=values_one,
            extended=extended,
            shifted=shifted,
            carried=carried,
            carried_real=carried_real,
            carried_imag=carried_imag,
            kernel_real=kernel_real,
            kernel_imag=kernel_imag,
            kernel_pull=kernel_pull,
            mixer=mixer,
            gated_low=gated_low,
            hidden_one=hidden_one,
            normed_two=normed_two,
            raised_one=raised_one,
            active_one=active_one,
            hidden_two=hidden_two,
            normed_three=normed_three,
            qkv_two=qkv_two,
            totals_list=totals_list,
            keys_list=keys_list,
            values_list=values_list,
            attended_low=attended_low,
            hidden_three=hidden_three,
            normed_four=normed_four,
            raised_two=raised_two,
            active_two=active_two,
        )
        return (output, saved)

    output = forward_pass(tokens)[0]
    saved = forward_pass(lax.optimization_barrier(tokens))[1]
    grad_rows = (cotangent[0].astype(jnp.float32) * validity).reshape(row_count, width)
    grad_rows, down_two, up_two, gain_four, bias_four = feed_backward(
        grad_rows,
        saved.hidden_three,
        saved.normed_four,
        saved.raised_two,
        saved.active_two,
        3,
        1,
    )
    branch_low = grad_rows.astype(jnp.bfloat16)
    out_two = product_left(saved.attended_low, branch_low)
    d_attended = (
        product_right(branch_low, w_out[1])
        .astype(jnp.bfloat16)
        .reshape(seq_count, span_rows, width)
    )
    qkv_two = saved.qkv_two
    grad_parts = []
    for seq_index in range(seq_count):
        d_query_rows, d_key_rows, d_value_rows = attend_backward(
            qkv_two[seq_index, :, :width],
            saved.keys_list[seq_index],
            saved.values_list[seq_index],
            saved.totals_list[seq_index],
            d_attended[seq_index],
            lengths[0, seq_index],
            query_positions,
        )
        grad_parts.append(jnp.concatenate([d_query_rows, d_key_rows, d_value_rows], -1))
    d_qkv_two = jnp.concatenate(grad_parts, 0).astype(jnp.bfloat16)
    qkv_grad_two = product_left(saved.normed_three, d_qkv_two)
    d_inputs, gain_three, bias_three = norm_backward(
        saved.hidden_two, 2, product_right(d_qkv_two, w_qkv[1])
    )
    grad_rows = grad_rows + d_inputs
    grad_rows, down_one, up_one, gain_two, bias_two = feed_backward(
        grad_rows,
        saved.hidden_one,
        saved.normed_two,
        saved.raised_one,
        saved.active_one,
        1,
        0,
    )
    branch_low = grad_rows.astype(jnp.bfloat16)
    out_one = product_left(saved.gated_low, branch_low)
    d_gated = product_right(branch_low, w_out[0]).reshape(seq_count, span_rows, width)
    d_queries = d_gated * saved.mixer
    d_mixer = d_gated * saved.queries_one
    skip_grad = jnp.sum(d_mixer * saved.carried, (0, 1))
    conv_real, conv_imag = to_frequency(d_mixer.astype(jnp.bfloat16))
    kernel_real = saved.kernel_real
    kernel_imag = saved.kernel_imag
    from_conv = from_frequency(
        kernel_real * conv_real + kernel_imag * conv_imag,
        kernel_real * conv_imag - kernel_imag * conv_real,
    )
    d_carried = d_mixer * skip + from_conv
    carried_real = saved.carried_real
    carried_imag = saved.carried_imag
    cot_real = (
        jnp.sum(carried_real * conv_real + carried_imag * conv_imag, 1, keepdims=True) / fft_length
    )
    cot_imag = (
        jnp.sum(carried_real * conv_imag - carried_imag * conv_real, 1, keepdims=True) / fft_length
    )
    rate_grad, weight_grad = saved.kernel_pull((cot_real, cot_imag))
    d_shifted = d_carried * saved.values_one * validity
    d_values = d_carried * saved.shifted * validity
    extended = saved.extended
    grads_extended = sum(
        (
            jnp.pad(taps[offset] * d_shifted, ((0, 0), (rim - offset, offset), (0, 0)))
            for offset in range(TAPS)
        )
    )
    taps_grad = jnp.stack(
        [
            jnp.sum(
                d_shifted
                * extended[:, rim - offset : rim - offset + span_rows].astype(jnp.float32),
                (0, 1),
            )
            for offset in range(TAPS)
        ]
    )
    later = passed_along(grads_extended[:, :rim], SEQ, -1)
    d_keys = grads_extended[:, rim:] + jnp.pad(later, ((0, 0), (span_rows - rim, 0), (0, 0)))
    d_qkv_one = (
        jnp.concatenate([d_queries, d_keys, d_values], -1)
        .reshape(row_count, 3 * width)
        .astype(jnp.bfloat16)
    )
    qkv_grad_one = product_left(saved.normed_one, d_qkv_one)
    d_inputs, gain_one, bias_one = norm_backward(
        saved.flat_in, 0, product_right(d_qkv_one, w_qkv[0])
    )
    d_tokens = ((grad_rows + d_inputs).reshape(seq_count, span_rows, width) * validity)[None]
    gain_sum, bias_sum, qkv_sum, out_sum, up_sum, down_sum, taps_sum, skip_sum = (
        lax.psum_scatter(
            jnp.stack([gain_one, gain_two, gain_three, gain_four]),
            SEQ,
            scatter_dimension=1,
            tiled=True,
        ),
        lax.psum_scatter(
            jnp.stack([bias_one, bias_two, bias_three, bias_four]),
            SEQ,
            scatter_dimension=1,
            tiled=True,
        ),
        lax.psum_scatter(
            jnp.stack([qkv_grad_one, qkv_grad_two]), SEQ, scatter_dimension=1, tiled=True
        ),
        lax.psum_scatter(jnp.stack([out_one, out_two]), SEQ, scatter_dimension=1, tiled=True),
        lax.psum_scatter(jnp.stack([up_one, up_two]), SEQ, scatter_dimension=1, tiled=True),
        lax.psum_scatter(jnp.stack([down_one, down_two]), SEQ, scatter_dimension=1, tiled=True),
        lax.psum_scatter(taps_grad, SEQ, scatter_dimension=1, tiled=True),
        lax.psum_scatter(skip_grad[None], SEQ, scatter_dimension=1, tiled=True),
    )
    totals = (
        lax.psum(gain_sum.astype(jnp.bfloat16), BATCH).astype(jnp.float32),
        lax.psum(bias_sum.astype(jnp.bfloat16), BATCH).astype(jnp.float32),
        lax.psum(qkv_sum.astype(jnp.bfloat16), BATCH).astype(jnp.float32),
        lax.psum(out_sum.astype(jnp.bfloat16), BATCH).astype(jnp.float32),
        lax.psum(up_sum.astype(jnp.bfloat16), BATCH).astype(jnp.float32),
        lax.psum(down_sum.astype(jnp.bfloat16), BATCH).astype(jnp.float32),
        lax.psum(taps_sum.astype(jnp.bfloat16), BATCH).astype(jnp.float32),
        lax.psum(skip_sum.astype(jnp.bfloat16), BATCH).astype(jnp.float32),
        lax.psum(rate_grad.astype(jnp.bfloat16), BATCH).astype(jnp.float32),
        lax.psum(weight_grad.astype(jnp.bfloat16), BATCH).astype(jnp.float32),
    )
    return (
        output[None].astype(jnp.bfloat16),
        d_tokens,
        totals[0],
        totals[1][:3],
        totals[1][3],
        totals[2],
        totals[3],
        totals[4],
        totals[5],
        totals[6],
        totals[7][0],
        totals[8],
        totals[9],
    )


def other_device(place, core, to_place, to_core):
    return jnp.logical_or(place != to_place, core != to_core)


def greet(devices):
    barrier = pltpu.get_barrier_semaphore()
    for device in devices:
        pl.semaphore_signal(barrier, inc=1, device_id=device, device_id_type=MESH)
    pl.semaphore_wait(barrier, len(devices))


def remote(source, target, send_sem, recv_sem, device):
    return pltpu.make_async_remote_copy(
        src_ref=source,
        dst_ref=target,
        send_sem=send_sem,
        recv_sem=recv_sem,
        device_id=device,
        device_id_type=MESH,
    )


def split_low(value):
    upper = value.astype(jnp.bfloat16)
    return upper, (value - upper.astype(jnp.float32)).astype(jnp.bfloat16)


NN = (((1,), (0,)), ((), ()))
NT = (((1,), (1,)), ((), ()))
TN = (((0,), (0,)), ((), ()))


def dot(left, right, form=NN):
    return lax.dot_general(left, right, form, preferred_element_type=jnp.float32)


def dot_fine(left, right, form=NN):
    left_up, left_low = left
    right_up, right_low = right
    total = dot(left_up, right_up, form) + dot(left_up, right_low, form)
    if left_low is not None:
        total = total + dot(left_low, right_up, form)
    return total


def state_steps(span):
    row = lax.broadcasted_iota(jnp.int32, (span, 2 * STATES), 0)
    lane = lax.broadcasted_iota(jnp.int32, (span, 2 * STATES), 1)
    return jnp.where(lane < STATES, span - 1 - row, row + 1).astype(jnp.float32)


def state_tables(rate_row, weight_row, span):
    steps = state_steps(span)
    table = jnp.exp(-rate_row * steps)
    lane_row = lax.broadcasted_iota(jnp.int32, (8, 2 * STATES), 1)
    lead = jnp.where(lane_row < STATES, 0.0, weight_row * jnp.exp(rate_row))
    response = lax.dot_general(
        lead, table, NT, precision=highest, preferred_element_type=jnp.float32
    )[:1]
    spread = pltpu.roll(
        jnp.broadcast_to(response, (span, span)), 0, 1, stride=1, stride_axis=0
    )
    later = lax.broadcasted_iota(jnp.int32, (span, span), 1)
    earlier = lax.broadcasted_iota(jnp.int32, (span, span), 0)
    toeplitz = jnp.where(later >= earlier, spread, 0.0)
    return table, toeplitz


def shift_rows(value, count):
    if count > 0:
        return jnp.concatenate([jnp.zeros_like(value[:count]), value[:-count]], 0)
    return jnp.concatenate([value[-count:], jnp.zeros_like(value[:-count])], 0)


def scan_states(value, decay, seqs, blocks, direction):
    step = 1
    while step < blocks:
        value = value + shift_rows(value, direction * step * seqs) * jnp.exp(decay * step)
        step *= 2
    return shift_rows(value, direction * seqs)


SHARE = 16


def table_block(refs, kind, channel):
    size = 2 * STATES
    if kind < 3:
        row, column = channel // 2, lax.rem(channel, 2) * 3 + kind
        ref = refs.tables
    else:
        row, column = channel // 8, lax.rem(channel, 8)
        ref = refs.more_tables
    return ref.at[
        pl.ds(pl.multiple_of(row * size, size), size),
        pl.ds(pl.multiple_of(column * size, size), size),
    ]


def table_pair(refs, kind, channel):
    return table_block(refs, kind, channel)[...], table_block(refs, kind + 1, channel)[...]


def fill_tables(first, last, span, refs):
    def one_channel(channel, carry):
        table, toeplitz = state_tables(
            refs.rates[pl.ds(channel, 1), :], refs.rate_weights[pl.ds(channel, 1), :], span
        )
        for kind, value in enumerate((*split_low(toeplitz), *split_low(table))):
            table_block(refs, kind, channel)[...] = value
        return carry

    lax.fori_loop(first, last, one_channel, 0, unroll=4)


def table_shapes(channels, span):
    return (channels // 2 * span, 6 * span), (channels // 8 * span, 8 * span)


def fill_rates(refs, loads, channels, turned):
    copies = [
        loads.start(refs.all_rates, refs.rates_in), loads.start(refs.all_weights, refs.weights_in)
    ]

    def finish():
        rows = pl.ds(pl.multiple_of(lax.axis_index(SEQ) * channels, 8), channels)
        for copy, source, target in zip(
            copies, (refs.rates_in, refs.weights_in), (refs.rates, refs.rate_weights)
        ):
            copy.wait()
            both = jnp.concatenate([source[...]] * 2, 0)
            turned[...] = both.T
            target[...] = turned[rows, :]

    return finish


def rate_scratch(width, channels):
    flat, own = ((STATES, width), jnp.float32), ((channels, 2 * STATES), jnp.float32)
    return dict(
        rates_in=flat, weights_in=flat, rates=own, rate_weights=own,
    )


def valid_positions(lengths, seqs, span, axis):
    shape = (span, 1) if axis == 0 else (1, span)
    position = lax.axis_index(SEQ) * span + lax.broadcasted_iota(jnp.int32, shape, axis)
    parts = [
        jnp.where(position < lengths[0:1, seq : seq + 1], 1.0, 0.0).astype(jnp.float32)
        for seq in range(seqs)
    ]
    return jnp.concatenate(parts, axis)


def mixer_forward_channel(n, seqs, refs, part, local):
    span, channel = refs.flat_x.shape[-1], part * SHARE + local
    rate_row = refs.rates[pl.ds(channel, 1), :]
    weight_row = refs.rate_weights[pl.ds(channel, 1), :]
    rows = pl.ds(local, n * seqs, stride=SHARE)
    data = (refs.flat_x[part, rows, :].astype(jnp.bfloat16), None)
    table_parts = table_pair(refs, 2, channel)
    inner = dot_fine(data, table_pair(refs, 0, channel))
    states = scan_states(dot_fine(data, table_parts), -span * rate_row, seqs, n, 1)
    lane = lax.broadcasted_iota(jnp.int32, states.shape, 1)
    weighted = jnp.where(lane < STATES, 0.0, pltpu.roll(states, STATES, 1) * weight_row)
    refs.flat_out[part, rows, :] = inner + dot_fine(split_low(weighted), table_parts, NT)


def mixer_backward_channel(n, seqs, refs, part, local):
    span, channel = refs.flat_x.shape[-1], part * SHARE + local
    rate_row = refs.rates[pl.ds(channel, 1), :]
    weight_row = refs.rate_weights[pl.ds(channel, 1), :]
    table_parts = table_pair(refs, 2, channel)
    table = table_parts[0].astype(jnp.float32) + table_parts[1].astype(jnp.float32)
    steps = state_steps(span)
    rows = pl.ds(local, n * seqs, stride=SHARE)
    data = refs.flat_x[part, rows, :].astype(jnp.bfloat16)
    grad = refs.flat_d[part, rows, :].astype(jnp.bfloat16)
    stepped_parts = split_low(table * steps)
    both_parts = [jnp.concatenate(pair, 1) for pair in zip(table_parts, stepped_parts)]
    count = n * seqs
    sides = dot_fine((jnp.concatenate([data, grad], 0), None), both_parts)
    lane = lax.broadcasted_iota(jnp.int32, (count, 2 * STATES), 1)
    low_lanes = lane < STATES

    def aligned(value):
        return jnp.where(low_lanes, pltpu.roll(value, STATES, 1), 0.0)

    entering = jnp.where(low_lanes, sides[:count, : 2 * STATES], 0.0)
    entering_steps = jnp.where(low_lanes, sides[:count, 2 * STATES :], 0.0)
    leaving = aligned(sides[count:, : 2 * STATES])
    leaving_steps = aligned(sides[count:, 2 * STATES :])
    decay = -span * rate_row
    states = scan_states(entering, decay, seqs, n, 1)
    states_steps = scan_states(states * jnp.exp(decay), decay, seqs, n, 1)
    returned = scan_states(leaving, decay, seqs, n, -1)
    far_weight = jnp.sum(leaving * states, 0, keepdims=True)
    far_rate = jnp.sum(
        leaving_steps * states + returned * entering_steps + span * (leaving * states_steps),
        0, keepdims=True,
    )
    cross = dot(grad, data, TN)
    later = lax.broadcasted_iota(jnp.int32, (span, span), 0)
    earlier = lax.broadcasted_iota(jnp.int32, (span, span), 1)
    cross = jnp.where(later >= earlier, cross, 0.0)
    met = dot_fine(split_low(cross), both_parts)
    met_plain = pltpu.roll(met[:, : 2 * STATES], STATES, 1)
    met_steps = pltpu.roll(met[:, 2 * STATES :], STATES, 1)
    rise = jnp.exp(span * rate_row)
    near_weight = rise * jnp.sum(table * met_plain, 0, keepdims=True)
    near_rate = rise * jnp.sum(
        table * ((steps - span) * met_plain + met_steps), 0, keepdims=True
    )
    lane_row = lane[:1]
    near_weight = jnp.where(lane_row < STATES, pltpu.roll(near_weight, STATES, 1), 0.0)
    near_rate = jnp.where(lane_row < STATES, pltpu.roll(near_rate, STATES, 1), 0.0)
    refs.weight_grad[pl.ds(channel, 1), :] = near_weight + far_weight
    refs.rate_grad[pl.ds(channel, 1), :] = -weight_row * (near_rate + far_rate)
    inner = dot_fine((grad, None), table_pair(refs, 0, channel), NT)
    weighted = returned * weight_row
    refs.flat_d[part, rows, :] = inner + dot_fine(split_low(weighted), table_parts, NT)


def block_of(index, core):
    return 2 * index + lax.rem(index + core, 2)


def keeper_of(block):
    return lax.rem((block + 1) // 2, 2)


class HeadPlaces:
    def __init__(self, n, seqs, groups):
        self.n, self.seqs, self.groups = n, seqs, groups
        self.me, self.core = lax.axis_index(SEQ), lax.axis_index(BATCH)
        self.group = self.me // (2 * seqs)
        self.seq = lax.rem(self.me // 2, seqs)
        self.batch = lax.rem(self.me, 2)
        self.keeper = keeper_of(self.me)
        self.sibling = (self.me, 1 - self.core)
        self.targets = [
            ((group * 2 * seqs + seq * 2 + self.core, self.keeper), seq, group)
            for seq in range(seqs)
            for group in range(groups)
        ]
        self.blocks = [block_of(index, self.core) for index in range(n // 2)]
        self.sources = [(block, self.batch) for block in self.blocks]

    def is_other(self, device):
        return jnp.logical_or(device[0] != self.me, device[1] != self.core)

    def greet(self):
        barrier = pltpu.get_barrier_semaphore()
        self.signal_all(barrier, [])
        self.wait_all(barrier, 0)

    def signal_all(self, barrier, more):
        for device in [target for target, _, _ in self.targets] + self.sources:

            @pl.when(self.is_other(device))
            def _():
                pl.semaphore_signal(barrier, inc=1, device_id=device, device_id_type=MESH)

        for device in [self.sibling, *more]:
            pl.semaphore_signal(barrier, inc=1, device_id=device, device_id_type=MESH)

    def wait_all(self, barrier, more):
        kept = jnp.logical_and(self.batch == self.core, self.is_kept_here())
        count = len(self.targets) + len(self.sources) + 1 + more
        pl.semaphore_wait(barrier, count - 2 * kept.astype(jnp.int32))

    def is_kept_here(self):
        return self.keeper == self.core

    def send(self, source, target, send_sem, recv_sem, device):
        @pl.when(self.is_other(device))
        def _():
            remote(source, target, send_sem, recv_sem, device).start()

        @pl.when(jnp.logical_not(self.is_other(device)))
        def _():
            pltpu.make_async_copy(source, target, recv_sem).start()

    def wait_sent(self, source, target, send_sem, recv_sem, device):
        @pl.when(self.is_other(device))
        def _():
            remote(source, target, send_sem, recv_sem, device).wait_send()


def fill_head(held, head, part, n, span, rows_out, columns_out):
    for block in range(n):
        piece = held[head, block, part * HEAD : (part + 1) * HEAD, :]
        if rows_out is not None:
            rows_out[block * span : (block + 1) * span, :] = piece.T
        if columns_out is not None:
            columns_out[:, block * span : (block + 1) * span] = piece


def causal(first_key, rows, first_query, span):
    key = first_key + lax.broadcasted_iota(jnp.int32, (rows, span), 0)
    query = first_query + lax.broadcasted_iota(jnp.int32, (rows, span), 1)
    return key <= query


TILE = 384
VMEM, HBM = pltpu.VMEM, pl.ANY


def launch(body, inputs, outputs, scratch, copies, collective):
    names = [*inputs, *outputs, *scratch, "send", "recv", "local"]

    def kernel(*refs):
        body(types.SimpleNamespace(**dict(zip(names, refs))))

    dma = pltpu.SemaphoreType.DMA
    results = pl.pallas_call(
        kernel,
        out_shape=tuple(jax.ShapeDtypeStruct(shape, kind) for shape, kind, _ in outputs.values()),
        in_specs=[pl.BlockSpec(memory_space=space) for _, space in inputs.values()],
        out_specs=tuple(pl.BlockSpec(memory_space=space) for _, _, space in outputs.values()),
        scratch_shapes=[pltpu.VMEM(shape, kind) for shape, kind in scratch.values()]
        + [dma((copies,)), dma((copies,)), dma((LOCAL_COPIES,))],
        compiler_params=pltpu.CompilerParams(
            collective_id=collective, has_side_effects=True, vmem_limit_bytes=VMEM_BYTES
        ),
    )(*(array for array, _ in inputs.values()))
    return types.SimpleNamespace(**dict(zip(outputs, results)))


LOCAL_COPIES = 64


class Loads:
    def __init__(self, refs):
        self.semaphores, self.used = refs.local, 0

    def start(self, source, target):
        copy = pltpu.make_async_copy(source, target, self.semaphores.at[self.used])
        self.used += 1
        copy.start()
        return copy


class Links:
    def __init__(self, refs):
        self.send, self.recv, self.used, self.unsent = refs.send, refs.recv, 0, []

    def slots(self, count):
        self.used += count
        return self.used - count

    def copy(self, source, target, device, slot=None):
        slot = self.slots(1) if slot is None else slot
        made = remote(source, target, self.send.at[slot], self.recv.at[slot], device)
        made.start()
        self.unsent.append(made)
        return made

    def finish(self):
        for made in self.unsent:
            made.wait_send()


class Piece:
    def __init__(self, weight, first_row, first_column, axis):
        self.weight, self.first_row, self.first_column, self.axis = (
            weight, first_row, first_column, axis,
        )


ROWS = 48


def pieces_of(weights, order):
    pieces = []
    for weight, first, last, axes in order:
        rows, half = weights[weight]
        places = [
            (first_row, first_column)
            for first_column in range(0, half, TILE)
            for first_row in range(0, rows, ROWS)
        ]
        for count, place in enumerate(places[first:last]):
            pieces.append(Piece(weight, *place, axes[count % len(axes)]))
    return pieces


class Reducer:
    def __init__(self, refs, links, depth, weights, pieces, given):
        self.refs, self.links, self.depth, self.weights = refs, links, depth, weights
        self.me, self.core = lax.axis_index(SEQ), lax.axis_index(BATCH)
        self.level = self.me // 4
        self.spot = (lax.rem(self.me // 2, 2), lax.rem(self.me, 2))
        base = self.level * 4
        self.across = [
            (base + self.spot[0] * 2 + (1 - self.spot[1]), self.core),
            (base + (1 - self.spot[0]) * 2 + self.spot[1], self.core),
        ]
        self.sibling = (self.me, 1 - self.core)
        self.levels = [lax.rem(self.level + step, depth) for step in range(1, depth)]
        self.column = [
            (other * 4 + self.spot[0] * 2 + self.spot[1], self.core) for other in self.levels
        ]
        place = self.spot[0] * 2 + self.spot[1]
        beside = self.level + 1 - 2 * lax.rem(self.level, 2)
        self.beside = (beside * 4 + place, self.core)
        self.beyond = (lax.rem(self.level + 2, depth) * 4 + place, self.core)
        self.slots = {piece: slot for slot, piece in enumerate(pieces)}
        self.given = {piece: slot for slot, piece in enumerate(given)}
        self.products = {}
        self.exchanges, self.flights = {}, {}

    def neighbours(self):
        return [self.sibling, *self.across, *self.column]

    def exchange(self, weight, left, right, blocks=None):
        if weight not in self.exchanges:
            sent = self.links.copy(left[0], left[1], self.sibling)
            self.exchanges[weight] = (left, right, {None: sent})
        for block in range(self.weights[weight][1] // TILE) if blocks is None else blocks:
            theirs = (2 * block + 1 - self.core) * TILE
            self.exchanges[weight][2][block] = self.links.copy(
                right[0].at[pl.ds(pl.multiple_of(theirs, TILE), TILE), :],
                right[1].at[block * TILE : (block + 1) * TILE, :], self.sibling,
            )

    def own_columns(self, piece):
        start = (2 * (piece.first_column // TILE) + self.core) * TILE
        return pl.ds(pl.multiple_of(start, TILE), TILE)

    def product(self, piece, first):
        left, right, copies = self.exchanges[piece.weight]
        for key in (None, piece.first_column // TILE):
            if key in copies:
                copies.pop(key).wait_recv()
        places = [
            outer * 4 + (inner * 2 + first if piece.axis == 0 else first * 2 + inner)
            for outer in range(self.depth)
            for inner in range(2)
        ]
        rows = slice(piece.first_row, piece.first_row + ROWS)
        mine, other = (
            jnp.concatenate([side[place, rows, :] for place in places], 0) for side in left
        )
        own = self.own_columns(piece)
        there = slice(piece.first_column, piece.first_column + TILE)
        total = dot(mine, right[0][own, :], NT) + dot(other, right[1][there, :], NT)
        return total.reshape(self.depth, 2, ROWS, TILE)

    def first(self, piece):
        places = self.refs.away.shape[0]
        place = len(self.products)
        if place >= places:
            sent = self.products[place - places]
            sent.wait_send()
            self.links.unsent = [copy for copy in self.links.unsent if copy is not sent]
        away = self.refs.away.at[place % places]
        away[...] = self.product(piece, 1 - self.spot[1 - piece.axis]).astype(jnp.bfloat16)
        self.flights[piece] = self.links.copy(
            away, self.refs.one.at[self.slots[piece]], self.across[piece.axis]
        )
        self.products[place] = self.flights[piece]

    def joined(self, piece, into):
        slot = self.slots[piece]
        self.flights.pop(piece).wait_recv()
        total = self.product(piece, self.spot[1 - piece.axis])
        total = total + self.refs.one[slot].astype(jnp.float32)
        into[...] = total.astype(jnp.bfloat16)

    def resume(self, piece):
        slot = self.slots[piece]
        self.flights[piece] = self.links.copy(
            self.refs.one.at[slot, :, 1 - self.spot[piece.axis]], self.refs.two.at[slot],
            self.across[1 - piece.axis],
        )

    def second(self, piece):
        self.joined(piece, self.refs.one.at[self.slots[piece]])
        self.resume(piece)

    def middle(self, piece, into):
        slot = self.slots[piece]
        self.flights.pop(piece).wait_recv()
        kept = self.refs.one[slot, :, self.spot[piece.axis]].astype(jnp.float32)
        total = (kept + self.refs.two[slot].astype(jnp.float32)).astype(into.dtype)
        for outer in range(self.depth):
            into[outer % 2 * 2 + outer // 2] = total[outer]

    def summed(self, piece):
        if piece in self.given:
            slot = self.given[piece]
            return self.refs.mid.at[slot], self.refs.three.at[slot]
        slot = self.slots[piece]
        return self.refs.two.at[slot], self.refs.three.at[len(self.given) + slot]

    def third(self, piece):
        summed, three = self.summed(piece)
        if piece not in self.given:
            self.middle(piece, summed)
        theirs = 2 * (1 - lax.rem(self.level, 2))
        self.flights[piece] = self.links.copy(
            summed.at[pl.ds(theirs, 2)], three.at[:2], self.beside
        )

    def fold(self, piece):
        summed, three = self.summed(piece)
        self.flights.pop(piece).wait_recv()
        mine = 2 * lax.rem(self.level, 2)
        for pair in range(2):
            summed[mine + pair] = (
                summed[mine + pair].astype(jnp.float32) + three[pair].astype(jnp.float32)
            ).astype(summed.dtype)
        self.flights[piece] = self.links.copy(
            summed.at[mine + 1 - self.level // 2], three.at[2], self.beyond
        )

    def fourth(self, piece, out):
        summed, three = self.summed(piece)
        self.flights.pop(piece).wait_recv()
        total = summed[2 * lax.rem(self.level, 2) + self.level // 2].astype(jnp.float32)
        total = total + three[2].astype(jnp.float32)
        filled = out.at[piece.first_row : piece.first_row + ROWS, self.own_columns(piece)]
        filled[...] = total
        self.flights[piece] = self.links.copy(filled, filled, self.sibling)

    def last(self, piece):
        self.flights.pop(piece).wait_recv()


def reducer_scratch(products, pieces, given, depth):
    low = jnp.bfloat16
    shapes = dict(
        away=((products, depth, 2, ROWS, TILE), low), one=((pieces, depth, 2, ROWS, TILE), low),
        two=((pieces, depth, ROWS, TILE), low),
    )
    if given > 0:
        shapes.update(
            mid=((given, depth, ROWS, TILE), low),
            three=((given + pieces, depth - 1, ROWS, TILE), low),
        )
    return shapes


def gelu_slope(value):
    scale = math.sqrt(2.0 / math.pi)
    square = value * value
    bent = jnp.tanh(scale * value * (1.0 + 0.044715 * square))
    return 0.5 * (1.0 + bent) + 0.5 * value * (1.0 - bent * bent) * scale * (
        1.0 + 3.0 * 0.044715 * square
    )


def norm_gradient(inputs, gain, grad):
    center = inputs - jnp.mean(inputs, 0, keepdims=True)
    factor = lax.rsqrt(jnp.mean(center * center, 0, keepdims=True) + norm_eps)
    unit = center * factor
    scaled = grad * gain
    result = factor * (
        scaled
        - jnp.mean(scaled, 0, keepdims=True)
        - unit * jnp.mean(scaled * unit, 0, keepdims=True)
    )
    return result, jnp.sum(grad * unit, 1, keepdims=True), jnp.sum(grad, 1, keepdims=True)


def rows_product(matrix, other, out_rows, chunk, store):
    def one_chunk(index, carry):
        rows = pl.ds(pl.multiple_of(index * chunk, 128), chunk)
        store(rows, dot(matrix[rows, :], other))
        return carry

    lax.fori_loop(0, out_rows // chunk, one_chunk, 0)


def back_one_body(n, seqs, groups, span, group_rows, width, hidden_width, refs):
    at = HeadPlaces(n, seqs, groups)
    half = n // 2
    heads = group_rows // HEAD
    tokens = seqs * span
    links, loads = Links(refs), Loads(refs)
    weights = gradient_weights(width, hidden_width, n)
    pieces = pieces_of(weights, BACK_ONE_ORDER)
    reducer = Reducer(refs, links, groups, weights, pieces, [])
    down, up, out = [[piece for piece in pieces if piece.weight == weight] for weight in (DOWN, UP, OUT)]
    barrier = pltpu.get_barrier_semaphore()
    at.signal_all(barrier, reducer.neighbours()[1:])

    load_branch = loads.start(refs.branch, refs.down_right)
    load_active = loads.start(refs.active, refs.down_left)
    load_d_active = loads.start(refs.d_active, refs.d_active_in)
    load_slope = loads.start(refs.slope, refs.slope_in)
    load_w_up = loads.start(refs.w_up.at[1], refs.up)
    load_hidden = loads.start(refs.hidden, refs.hidden_in)
    load_w_out = loads.start(refs.w_out.at[1], refs.out)
    load_normed = loads.start(refs.normed, refs.up_left)
    load_attended = loads.start(refs.attended, refs.out_left)
    load_held = loads.start(refs.held, refs.held_in)

    at.wait_all(barrier, len(reducer.neighbours()) - 1)
    load_active.wait()
    load_branch.wait()
    reducer.exchange(DOWN, (refs.down_left, refs.down_left_other), (refs.down_right, refs.down_right_other))
    load_d_active.wait()
    load_slope.wait()
    refs.up_right[...] = (
        refs.slope_in[...].astype(jnp.float32) * refs.d_active_in[...].astype(jnp.float32)
    ).astype(jnp.bfloat16)
    for piece in down[:2]:
        reducer.first(piece)
    load_w_up.wait()
    load_hidden.wait()
    load_normed.wait()
    reducer.exchange(UP, (refs.up_left, refs.up_left_other), (refs.up_right, refs.up_right_other))
    d_normed = dot(refs.up[...], refs.up_right[...])
    for piece in down[2:]:
        reducer.first(piece)
    d_inputs, gain_part, bias_part = norm_gradient(refs.hidden_in[...], refs.columns[:, 3:4], d_normed)
    refs.small[...] = jnp.zeros_like(refs.small)
    refs.small[:, 3:4] = gain_part
    refs.small[:, 7:8] = bias_part
    grad = refs.down_right[...].astype(jnp.float32) + d_inputs
    refs.grad_out[...] = grad
    refs.out_right[...] = grad.astype(jnp.bfloat16)
    load_w_out.wait()
    load_attended.wait()
    reducer.exchange(OUT, (refs.out_left, refs.out_left_other), (refs.out_right, refs.out_right_other))

    count, lot = len(at.targets), groups * HEAD
    arrive, leave = links.slots(heads * half), links.slots(heads * count)
    spread = []
    for head in range(heads):
        rows = slice(head * lot, (head + 1) * lot)
        refs.d_attended[rows, :] = dot(refs.out[rows, :], refs.out_right[...]).astype(jnp.bfloat16)
        for number, (device, seq, group) in enumerate(at.targets):
            first = head * lot + group * HEAD
            sent = (
                refs.d_attended.at[first : first + HEAD, seq * span : (seq + 1) * span],
                refs.landing.at[head, at.me // 2], refs.send.at[leave + head * count + number],
                refs.recv.at[arrive + head * half + at.me // 2], device,
            )
            at.send(*sent)
            spread.append(sent)
    load_held.wait()
    started = down + up + out
    for piece in up + out:
        reducer.first(piece)

    returned = links.slots(len(at.targets) * heads)
    returning = links.slots(half * heads)
    slot = at.seq * groups + at.group
    going = []
    passed = []

    def send_back(head):
        passed[head].wait_recv()
        for index, device in enumerate(at.sources):
            results = refs.results.at[head, index]
            kept = refs.kept.at[head, index]
            part = refs.partial_recv[head, index].astype(jnp.float32)
            results[1] = (kept[:HEAD] + part[:HEAD]).astype(jnp.bfloat16)
            results[2] = (kept[HEAD:] + part[HEAD:]).astype(jnp.bfloat16)
            into = refs.d_qkv.at[
                :,
                pl.ds(pl.multiple_of(head * lot + at.group * HEAD, HEAD), HEAD),
                pl.ds(pl.multiple_of(at.seq * span, span), span),
            ]
            sent = (
                results, into, refs.send.at[returning + head * half + index],
                refs.recv.at[returned + head * len(at.targets) + slot], device,
            )
            at.send(*sent)
            going.append(sent)

    def attend(head):
        for index in range(half):
            landed = refs.landing.at[head, index]
            remote(
                landed, landed, refs.send.at[leave], refs.recv.at[arrive + head * half + index],
                at.sibling,
            ).wait_recv()
        fill_head(refs.held_in, head, 1, n, span, refs.key_rows, refs.key_columns)
        fill_head(refs.held_in, head, 2, n, span, refs.value_rows, None)
        refs.key_grads[...] = jnp.zeros_like(refs.key_grads)
        refs.value_grads[...] = jnp.zeros_like(refs.value_grads)
        for index, block in enumerate(at.blocks):
            query = refs.held_in[head, block, :HEAD, :] * jnp.bfloat16(HEAD**-0.5)
            grad = refs.landing[head, index]
            log_total = refs.lse[index, head : head + 1, :]
            clear, reach = 2 * index * span, 2 * (index + 1) * span
            pieces = []
            row_term = jnp.zeros((1, span), jnp.float32)
            for first, last in ((0, clear), (clear, reach)):
                if first == last:
                    continue
                scores = dot(refs.key_rows[first:last, :], query)
                if last == reach:
                    scores = jnp.where(
                        causal(clear, reach - clear, block * span, span), scores, masked_score
                    )
                weights = jnp.exp(scores - log_total)
                d_weights = dot(refs.value_rows[first:last, :], grad)
                row_term = row_term + jnp.sum(weights * d_weights, 0, keepdims=True)
                pieces.append((first, last, weights, d_weights))
            d_query = jnp.zeros((HEAD, span), jnp.float32)
            for first, last, weights, d_weights in pieces:
                d_scores = (weights * (d_weights - row_term)).astype(jnp.bfloat16)
                d_query = d_query + dot(refs.key_columns[:, first:last], d_scores)
                refs.key_grads[:, first:last] += dot(query, d_scores, NT)
                refs.value_grads[:, first:last] += dot(grad, weights.astype(jnp.bfloat16), NT)
            refs.results[head, index, 0] = (d_query * HEAD**-0.5).astype(jnp.bfloat16)
        for index in range(half):
            other = pl.ds(pl.multiple_of(block_of(index, 1 - at.core) * span, span), span)
            own = pl.ds(pl.multiple_of(at.blocks[index] * span, span), span)
            refs.partial_send[head, index, :HEAD, :] = refs.key_grads[:, other].astype(jnp.bfloat16)
            refs.partial_send[head, index, HEAD:, :] = refs.value_grads[:, other].astype(jnp.bfloat16)
            refs.kept[head, index, :HEAD, :] = refs.key_grads[:, own]
            refs.kept[head, index, HEAD:, :] = refs.value_grads[:, own]
        passed.append(
            links.copy(refs.partial_send.at[head], refs.partial_recv.at[head], at.sibling)
        )

    waiting = list(started)
    for head in range(heads):
        attend(head)
        if head > 0:
            send_back(head - 1)
        if head < heads - 1:
            for _ in range(2):
                reducer.second(waiting.pop(0))
    reducer.second(waiting.pop(0))
    send_back(heads - 1)
    done = len(started) - LEFT_OVER
    while len(waiting) > LEFT_OVER:
        reducer.second(waiting.pop(0))
    for place, piece in enumerate(started[done:]):
        reducer.joined(piece, refs.half_out.at[place])
    for place, piece in enumerate(started[:done]):
        reducer.middle(piece, refs.mid_out.at[place])
    for head in range(heads):
        for count, (device, seq, group) in enumerate(at.targets):
            landed = refs.d_qkv.at[
                :,
                head * lot + group * HEAD : head * lot + (group + 1) * HEAD,
                seq * span : (seq + 1) * span,
            ]
            remote(
                landed, landed, refs.send.at[leave],
                refs.recv.at[returned + head * len(at.targets) + count], at.sibling,
            ).wait_recv()
    for sent in spread + going:
        at.wait_sent(*sent)
    links.finish()


LEFT_OVER = 4


def gradient_weights(width, hidden_width, n):
    return {
        QKV: (width // n, 3 * width // 2),
        FIRST: (width // n, 3 * width // 2),
        DOWN: (hidden_width // n, width // 2),
        UP: (width // n, hidden_width // 2),
        OUT: (width // n, width // 2),
    }


BACK_ONE_ORDER = ((DOWN, 0, 4, (1, 0)), (UP, 0, 4, (0, 1)), (OUT, 0, 1, (0,)))
BACK_TWO_ORDER = (
    (QKV, 0, 3, (1, 0, 1)), (DOWN, 0, 4, (0, 1)), (UP, 0, 4, (0, 1)), (OUT, 0, 1, (0,)),
    (FIRST, 0, 3, (1, 0, 1)),
)


def back_one(
    branch, d_active, hidden, slope, normed, active, attended, held, lse, columns,
    w_out, w_up, collective,
):
    width, tokens = branch.shape
    heads, n, _, span = held.shape
    seqs = tokens // span
    group_rows = heads * HEAD
    groups = width // group_rows
    hidden_width = w_up.shape[2]
    half = n // 2
    low, wide = jnp.bfloat16, jnp.float32
    weights = gradient_weights(width, hidden_width, n)
    pieces = pieces_of(weights, BACK_ONE_ORDER)
    inputs = dict(
        branch=(branch, HBM), d_active=(d_active, HBM), hidden=(hidden, HBM), slope=(slope, HBM),
        normed=(normed, HBM), active=(active, HBM), attended=(attended, HBM), held=(held, HBM),
        lse=(lse, VMEM), columns=(columns, VMEM), w_out=(w_out, HBM), w_up=(w_up, HBM),
    )
    outputs = dict(
        d_qkv=((3, width, tokens), low, VMEM),
        grad_out=((width, tokens), wide, VMEM),
        small=((width, 128), wide, VMEM),
        mid_out=((len(pieces) - LEFT_OVER, groups, ROWS, TILE), low, VMEM),
        half_out=((LEFT_OVER, groups, 2, ROWS, TILE), low, VMEM),
    )
    scratch = dict(
        up=(w_up.shape[1:], low), out=(w_out.shape[1:], low),
        d_active_in=(d_active.shape, low), hidden_in=((width, tokens), wide),
        slope_in=(slope.shape, low), d_attended=((width, tokens), low),
        down_left=(active.shape, low), down_right=((width, tokens), low),
        up_left=(normed.shape, low), up_right=((hidden_width, tokens), low),
        out_left=(attended.shape, low), out_right=((width, tokens), low),
        held_in=(held.shape, low), landing=((heads, half, HEAD, span), low),
        results=((heads, half, 3, HEAD, span), low), kept=((heads, half, 2 * HEAD, span), wide),
        partial_send=((heads, half, 2 * HEAD, span), low),
        partial_recv=((heads, half, 2 * HEAD, span), low),
        key_grads=((HEAD, n * span), wide), value_grads=((HEAD, n * span), wide),
        key_rows=((n * span, HEAD), low), key_columns=((HEAD, n * span), low),
        value_rows=((n * span, HEAD), low),
        down_left_other=(active.shape, low), down_right_other=((width // 2, tokens), low),
        up_left_other=(normed.shape, low), up_right_other=((hidden_width // 2, tokens), low),
        out_left_other=(attended.shape, low), out_right_other=((width // 2, tokens), low),
        **reducer_scratch(len(pieces), len(pieces), 0, groups),
    )
    body = functools.partial(
        back_one_body, n, seqs, groups, span, group_rows, width, hidden_width
    )
    return launch(body, inputs, outputs, scratch, 160, collective)


def back_two_body(n, seqs, span, width, hidden_width, refs):
    channels = width // n
    me, core = lax.axis_index(SEQ), lax.axis_index(BATCH)
    peers = [lax.rem(me + step, n) for step in range(1, n)]
    before = (lax.rem(me + n - 1, n), core)
    links, loads = Links(refs), Loads(refs)
    weights = gradient_weights(width, hidden_width, n)
    pieces, given = pieces_of(weights, BACK_TWO_ORDER), pieces_of(weights, BACK_ONE_ORDER)
    given, halves = given[:-LEFT_OVER], given[-LEFT_OVER:]
    qkv, down, up, out, last = [
        [piece for piece in pieces if piece.weight == weight]
        for weight in (QKV, DOWN, UP, OUT, FIRST)
    ]
    reducer = Reducer(refs, links, n // 4, weights, halves + pieces, given)
    ends = {FIRST: refs.qkv_one, DOWN: refs.down_one, UP: refs.up_one, OUT: refs.out_one}
    ends_two = {DOWN: refs.down_two, UP: refs.up_two, OUT: refs.out_two}

    def fourth(piece):
        if piece in given or piece in halves:
            reducer.fourth(piece, ends_two[piece.weight])
        else:
            reducer.fourth(piece, refs.qkv_two if piece.weight == QKV else ends[piece.weight])

    barrier = pltpu.get_barrier_semaphore()
    for device in [(peer, core) for peer in peers] + [reducer.sibling]:
        pl.semaphore_signal(barrier, inc=1, device_id=device, device_id_type=MESH)
    load_d_qkv = loads.start(refs.d_qkv, refs.qkv_right)
    load_normed_three = loads.start(refs.normed_three, refs.qkv_left)
    load_half = loads.start(refs.half_in, refs.one.at[:LEFT_OVER])
    load_mid = loads.start(refs.mid_in, refs.mid.at[: len(given)])
    load_small = loads.start(refs.small_in, refs.small)
    load_w_qkv = loads.start(refs.w_qkv.at[1], refs.qkv)
    load_hidden_two = loads.start(refs.hidden_two, refs.hidden_two_in)
    load_grad = loads.start(refs.grad, refs.grad_now)
    load_w_down = loads.start(refs.w_down.at[0], refs.down)
    load_slope = loads.start(refs.slope, refs.slope_in)
    load_w_up = loads.start(refs.w_up.at[0], refs.up)
    load_active = loads.start(refs.active, refs.down_left)
    load_hidden_one = loads.start(refs.hidden_one, refs.hidden_one_in)
    load_normed_two = loads.start(refs.normed_two, refs.up_left)
    load_w_out = loads.start(refs.w_out.at[0], refs.out)
    load_gated = loads.start(refs.gated, refs.out_left)
    load_queries = loads.start(refs.queries, refs.queries_in)
    load_mixer = loads.start(refs.mixer, refs.mixer_in)
    load_carried = loads.start(refs.carried, refs.carried_in)
    finish_rates = fill_rates(refs, loads, channels, refs.small_other)
    load_held = loads.start(refs.held, refs.held_in)

    load_normed_one = loads.start(refs.normed_one, refs.first_left)
    load_tokens = loads.start(refs.tokens, refs.tokens_in)

    load_d_qkv.wait()
    load_normed_three.wait()
    pl.semaphore_wait(barrier, n)
    reducer.exchange(QKV, (refs.qkv_left, refs.qkv_left_other), (refs.qkv_right, refs.qkv_right_other))
    load_half.wait()
    for piece in halves:
        reducer.resume(piece)
    load_mid.wait()
    for piece in given[:3]:
        reducer.third(piece)
    load_w_qkv.wait()
    d_normed = dot(refs.qkv[...], refs.qkv_right[...])
    load_w_qkv = loads.start(refs.w_qkv.at[0], refs.qkv)
    for piece in qkv[:2]:
        reducer.first(piece)
    load_hidden_two.wait()
    load_grad.wait()
    d_inputs, gain_part, bias_part = norm_gradient(
        refs.hidden_two_in[...], refs.columns[:, 2:3], d_normed
    )
    load_small.wait()
    refs.small[:, 2:3] = gain_part
    refs.small[:, 6:7] = bias_part
    grad = refs.grad_now[...] + d_inputs
    refs.grad_now[...] = grad
    refs.down_right[...] = grad.astype(jnp.bfloat16)
    load_w_down.wait()
    load_slope.wait()
    load_active.wait()
    reducer.exchange(DOWN, (refs.down_left, refs.down_left_other), (refs.down_right, refs.down_right_other))

    def store_raised(rows, value):
        slope = refs.slope_in[rows, :].astype(jnp.float32)
        refs.up_right[rows, :] = (slope * value).astype(jnp.bfloat16)

    rows_product(refs.down, refs.down_right[...], hidden_width, 512, store_raised)
    load_w_up.wait()
    load_hidden_one.wait()
    load_normed_two.wait()
    reducer.exchange(UP, (refs.up_left, refs.up_left_other), (refs.up_right, refs.up_right_other))
    d_normed = dot(refs.up[...], refs.up_right[...])
    refs.tables, refs.more_tables = refs.down, refs.up
    load_tables = loads.start(refs.tables_kept, refs.down)
    load_more_tables = loads.start(
        refs.more_tables_kept, refs.up.at[:, : refs.more_tables_kept.shape[1]]
    )
    d_inputs, gain_part, bias_part = norm_gradient(
        refs.hidden_one_in[...], refs.columns[:, 1:2], d_normed
    )
    refs.small[:, 1:2] = gain_part
    refs.small[:, 5:6] = bias_part
    grad = refs.grad_now[...] + d_inputs
    refs.grad_now[...] = grad
    refs.out_right[...] = grad.astype(jnp.bfloat16)
    load_gated.wait()
    reducer.exchange(OUT, (refs.out_left, refs.out_left_other), (refs.out_right, refs.out_right_other))
    load_w_out.wait()
    load_queries.wait()
    load_mixer.wait()
    load_carried.wait()
    d_gated = dot(refs.out[...], refs.out_right[...])
    d_mixer = d_gated * refs.queries_in[...]
    for seq in range(seqs):
        refs.d_conv[seq] = d_mixer[:, seq * span : (seq + 1) * span].astype(jnp.bfloat16)
    shares = channels // SHARE
    arrive, answered = links.slots(shares * n), links.slots(shares * n)

    def share_rows(device, share):
        return pl.ds(pl.multiple_of(device * channels + share * SHARE, 16), SHARE)

    going, own_copies = [], []
    for share in range(shares):
        within = slice(share * SHARE, (share + 1) * SHARE)
        for step, peer in enumerate(peers):
            going.append(
                links.copy(
                    refs.d_conv.at[:, share_rows(peer, share), :],
                    refs.landing.at[me, :, within, :], (peer, core), arrive + share * n + step,
                )
            )
        own_copies.append(
            loads.start(
                refs.d_conv.at[:, share_rows(me, share), :], refs.landing.at[me, :, within, :]
            )
        )
    refs.d_mixer[...] = d_mixer
    refs.first_right[:width, :] = (d_gated * refs.mixer_in[...]).astype(jnp.bfloat16)
    refs.small[:, 12:13] = sum(
        jnp.sum(
            d_mixer[:, seq * span : (seq + 1) * span] * refs.carried_in[seq].astype(jnp.float32), 1,
            keepdims=True,
        )
        for seq in range(seqs)
    )

    first_left = (refs.first_left, refs.first_left_other)
    first_right = (refs.first_right, refs.first_right_other)
    load_normed_one.wait()
    reducer.exchange(FIRST, first_left, first_right, (0,))
    load_values = loads.start(refs.values, refs.queries_in)
    load_keys = loads.start(refs.keys, refs.carried_in)
    load_shifted = loads.start(refs.shifted, refs.mixer_in)
    for piece in given[:3]:
        reducer.fold(piece)
    for piece in down[:2] + qkv[2:] + down[2:]:
        reducer.first(piece)
    for piece in given[3:]:
        reducer.third(piece)
    load_held.wait()
    finish_rates()
    load_tables.wait()
    load_more_tables.wait()
    back, back_own = [], []
    for share in range(shares):
        within = slice(share * SHARE, (share + 1) * SHARE)
        own_copies[share].wait()
        for copy in going[share * len(peers) : (share + 1) * len(peers)]:
            copy.wait_recv()
        for flat, source in ((refs.flat_x, refs.held_in), (refs.flat_d, refs.landing)):
            flat[share] = (
                source[:, :, within, :].astype(jnp.float32).reshape(n * seqs * SHARE, span)
            )

        def one_channel(local, carry):
            mixer_backward_channel(n, seqs, refs, share, local)
            return carry

        lax.fori_loop(0, SHARE, one_channel, 0, unroll=4)
        refs.landing[:, :, within, :] = (
            refs.flat_d[share].reshape(n, seqs, SHARE, span).astype(jnp.bfloat16)
        )
        for step, peer in enumerate(peers):
            back.append(
                links.copy(
                    refs.landing.at[peer, :, within, :],
                    refs.from_conv.at[:, share_rows(me, share), :], (peer, core),
                    answered + share * n + step,
                )
            )
        back_own.append(
            loads.start(
                refs.landing.at[me, :, within, :], refs.from_conv.at[:, share_rows(me, share), :]
            )
        )
        for piece in (qkv[:2], down[:2], [qkv[2], down[2]])[share]:
            reducer.second(piece)
        if share == 0:
            for piece in given[3:]:
                reducer.fold(piece)
        else:
            reducer.first(up[share - 1])
    for piece in halves:
        reducer.third(piece)
    states = [
        links.copy(refs.rate_grad, refs.rate_other, reducer.sibling),
        links.copy(refs.weight_grad, refs.weight_other, reducer.sibling),
    ]
    reducer.second(down[3])
    for piece in qkv[:2]:
        reducer.third(piece)
    for piece in halves:
        reducer.fold(piece)
    for piece in given:
        fourth(piece)
    for copy in states:
        copy.wait_recv()
    refs.rate_sum[...] = (refs.rate_grad[...] + refs.rate_other[...])[:, :STATES]
    refs.weight_sum[...] = (refs.weight_grad[...] + refs.weight_other[...])[:, :STATES]
    for copy in back_own:
        copy.wait()
    for copy in back:
        copy.wait_recv()
    load_values.wait()
    load_shifted.wait()
    valid = valid_positions(refs.lengths, seqs, span, 1)
    conv = jnp.concatenate([refs.from_conv[seq] for seq in range(seqs)], 1).astype(jnp.float32)
    d_carried = (refs.d_mixer[...] * refs.columns[:, 8:9] + conv) * valid
    d_shifted = d_carried * refs.queries_in[...]
    refs.hidden_one_in[...] = d_shifted
    for seq in range(seqs):
        for first in range(0, width, span):
            turned = d_shifted[first : first + span, seq * span : (seq + 1) * span].T
            refs.rim_out[seq, :, first : first + span] = turned[: refs.rim_out.shape[1]]
    refs.first_right[2 * width :, :] = (d_carried * refs.mixer_in[...]).astype(jnp.bfloat16)
    halo = links.copy(refs.rim_out, refs.rim_in, before)
    reducer.exchange(FIRST, first_left, first_right, (2,))
    for piece in up[2:] + out:
        reducer.first(piece)
    for piece in up[:2]:
        reducer.second(piece)
    for piece in qkv[2:] + down[:2]:
        reducer.third(piece)
    load_keys.wait()
    halo.wait_recv()
    lane = lax.broadcasted_iota(jnp.int32, (width, span), 1)
    there = jnp.where(me == n - 1, 0.0, 1.0)
    rim = refs.rim_in.shape[1]
    tap_sums = [jnp.zeros((width, 1), jnp.float32) for _ in range(TAPS)]
    for seq in range(seqs):
        lanes = slice(seq * span, (seq + 1) * span)
        own = refs.hidden_one_in[:, lanes]
        keys = refs.carried_in[seq].astype(jnp.float32)
        turned = []
        for first in range(0, width, span):
            piece = refs.rim_in[seq, :, first : first + span] * there
            piece = jnp.concatenate([piece, jnp.zeros((span - rim, span), jnp.float32)], 0)
            turned.append(piece.T)
        following = jnp.concatenate(turned, 0)
        d_keys = jnp.zeros((width, span), jnp.float32)
        for offset in range(TAPS):
            moved = own
            if offset > 0:
                moved = jnp.where(
                    lane < span - offset,
                    pltpu.roll(own, span - offset, 1),
                    pltpu.roll(following, span - offset, 1),
                )
            d_keys = d_keys + refs.columns[:, 4 + offset : 5 + offset] * moved
            tap_sums[offset] = tap_sums[offset] + jnp.sum(moved * keys, 1, keepdims=True)
        refs.first_right[width : 2 * width, lanes] = d_keys.astype(jnp.bfloat16)
    reducer.exchange(FIRST, first_left, first_right, (1,))
    load_w_qkv.wait()
    load_tokens.wait()
    d_normed = dot(refs.qkv[...], refs.first_right[...])
    flat_in = jnp.concatenate(
        [refs.tokens_in[seq].astype(jnp.float32).T for seq in range(seqs)], 1
    )
    d_inputs, gain_part, bias_part = norm_gradient(flat_in * valid, refs.columns[:, 0:1], d_normed)
    refs.hidden_two_in[...] = (refs.grad_now[...] + d_inputs) * valid
    for offset in range(TAPS):
        refs.small[:, 8 + offset : 9 + offset] = tap_sums[offset]
    refs.small[:, 0:1] = gain_part
    refs.small[:, 4:5] = bias_part
    shared = links.copy(refs.small, refs.small_other, reducer.sibling)
    for piece in last:
        reducer.first(piece)
    for piece in up[2:]:
        reducer.second(piece)
    for piece in qkv + down[:2]:
        reducer.fold(piece)
    for piece in down[2:]:
        reducer.third(piece)
    shared.wait_recv()
    rows = width // n
    turned = (refs.small[...] + refs.small_other[...]).T[:16]
    for place in range(n):
        start = place * rows // 128 * 128
        window = turned[:, start : min(start + 256, width)]
        away = (window.shape[1] - (place * rows - start)) % window.shape[1]
        refs.slices[place] = pltpu.roll(window, away, 1)[:, :128]
    depth = n // 4
    y, x = reducer.spot
    for outer in range(depth):
        for inner in range(2):
            refs.small_away[outer, inner] = refs.slices[outer * 4 + inner * 2 + 1 - x]
    small = links.copy(refs.small_away, refs.small_one, reducer.across[0])
    for seq in range(seqs):
        for first in range(0, width, span):
            refs.d_tokens[seq, :, first : first + span] = refs.hidden_two_in[
                first : first + span, seq * span : (seq + 1) * span
            ].T
    reducer.second(out[0])
    for piece in up[:2]:
        reducer.third(piece)
    for piece in halves + qkv:
        fourth(piece)
    for piece in down[2:]:
        reducer.fold(piece)
    small.wait_recv()
    for outer in range(depth):
        for inner in range(2):
            refs.small_one[outer, inner] += refs.slices[outer * 4 + inner * 2 + x]
    small = links.copy(refs.small_one.at[:, 1 - y], refs.small_two, reducer.across[1])
    reducer.second(last[2])
    for piece in up[2:]:
        reducer.third(piece)
    for piece in up[:2]:
        reducer.fold(piece)
    for piece in last[:2]:
        reducer.second(piece)
    reducer.third(out[0])
    for piece in down:
        fourth(piece)
    for piece in up[2:]:
        reducer.fold(piece)
    small.wait_recv()
    for outer in range(depth):
        refs.small_two[outer] += refs.small_one[outer, y]
    smalls = [
        links.copy(refs.small_two.at[other], refs.small_three.at[step], reducer.column[step])
        for step, other in enumerate(reducer.levels)
    ]
    reducer.fold(out[0])
    for piece in last:
        reducer.third(piece)
    for piece in up:
        fourth(piece)
    for piece in last:
        reducer.fold(piece)
    for piece in out + last:
        fourth(piece)
    total = refs.small_two[reducer.level]
    for step, copy in enumerate(smalls):
        copy.wait_recv()
        total = total + refs.small_three[step]
    refs.small_sum[...] = total[:, :rows]
    for piece in given + halves + pieces:
        reducer.last(piece)
    links.finish()


def back_two(
    tables, more_tables, mid, half, d_qkv, grad, hidden_two, normed_three, slope, normed_two, active, hidden_one,
    gated, queries, mixer, carried, held, values, shifted, keys, tokens, normed_one, columns, small,
    lengths, rates, rate_weights, w_qkv, w_out, w_up, w_down, collective,
):
    n, seqs, channels, span = held.shape
    width, hidden_width = w_up.shape[1:]
    count = seqs * span
    low, wide = jnp.bfloat16, jnp.float32
    weights = gradient_weights(width, hidden_width, n)
    pieces = pieces_of(weights, BACK_TWO_ORDER)
    inputs = dict(
        tables_kept=(tables, HBM), more_tables_kept=(more_tables, HBM), mid_in=(mid, HBM), half_in=(half, HBM), d_qkv=(d_qkv, HBM), grad=(grad, HBM),
        hidden_two=(hidden_two, HBM), normed_three=(normed_three, HBM), slope=(slope, HBM),
        normed_two=(normed_two, HBM), active=(active, HBM), hidden_one=(hidden_one, HBM),
        gated=(gated, HBM), queries=(queries, HBM), mixer=(mixer, HBM), carried=(carried, HBM),
        held=(held, HBM), values=(values, HBM), shifted=(shifted, HBM), keys=(keys, HBM),
        tokens=(tokens, HBM), normed_one=(normed_one, HBM), columns=(columns, VMEM),
        small_in=(small, HBM), lengths=(lengths, VMEM), all_rates=(rates, HBM),
        all_weights=(rate_weights, HBM), w_qkv=(w_qkv, HBM), w_out=(w_out, HBM), w_up=(w_up, HBM),
        w_down=(w_down, HBM),
    )
    square, state = (width, count), (channels, 2 * STATES)
    rows = width // n
    grads = dict(
        qkv=(rows, 3 * width), down=(hidden_width // n, width), up=(rows, hidden_width),
        out=(rows, width),
    )
    outputs = dict(
        d_tokens=((seqs, span, width), wide, VMEM),
        rate_sum=((channels, STATES), wide, VMEM),
        weight_sum=((channels, STATES), wide, VMEM),
        small_sum=((16, rows), wide, VMEM),
        **{name + ONE: (shape, wide, VMEM) for name, shape in grads.items()},
        **{name + TWO: (shape, wide, VMEM) for name, shape in grads.items()},
    )
    flat = (channels // SHARE, n * seqs * SHARE, span)
    rim, lot = ((seqs, 8, width), wide), (n // 4, 2, 16, 128)
    scratch = dict(
        qkv=(w_qkv.shape[1:], low), down=(w_down.shape[1:], low), up=(w_up.shape[1:], low),
        out=(w_out.shape[1:], low),
        qkv_left=(normed_three.shape, low), qkv_right=((3 * width, count), low),
        first_left=(normed_one.shape, low), first_right=((3 * width, count), low),
        down_left=(active.shape, low), down_right=(square, low),
        up_left=(normed_two.shape, low), up_right=((hidden_width, count), low),
        out_left=(gated.shape, low), out_right=(square, low),
        hidden_two_in=(square, wide), hidden_one_in=(square, wide), grad_now=(square, wide),
        slope_in=(slope.shape, low), queries_in=(square, wide), mixer_in=(square, wide),
        carried_in=(carried.shape, low), held_in=(held.shape, low), d_mixer=(square, wide),
        from_conv=((seqs, width, span), low), d_conv=((seqs, width, span), low),
        landing=(held.shape, low), flat_x=(flat, wide),
        flat_d=(flat, wide), **rate_scratch(width, channels),
        rate_grad=(state, wide), weight_grad=(state, wide), rate_other=(state, wide),
        weight_other=(state, wide), tokens_in=(tokens.shape, low),
        rim_out=rim, rim_in=rim, small=((width, 128), wide), small_other=((width, 128), wide),
        slices=((n, 16, 128), wide), small_away=(lot, wide), small_one=(lot, wide),
        small_two=((n // 4, 16, 128), wide), small_three=((n // 4 - 1, 16, 128), wide),
        qkv_left_other=(normed_three.shape, low), qkv_right_other=((3 * width // 2, count), low),
        first_left_other=(normed_one.shape, low),
        first_right_other=((3 * width // 2, count), low),
        down_left_other=(active.shape, low), down_right_other=((width // 2, count), low),
        up_left_other=(normed_two.shape, low), up_right_other=((hidden_width // 2, count), low),
        out_left_other=(gated.shape, low), out_right_other=((width // 2, count), low),
        **reducer_scratch(6, LEFT_OVER + len(pieces), mid.shape[0], n // 4),
    )
    body = functools.partial(back_two_body, n, seqs, span, width, hidden_width)
    return launch(body, inputs, outputs, scratch, 420, collective)


def earlier_rows(own, before, steps):
    if steps == 0:
        return own
    moved = pltpu.roll(own, steps, 0)
    rim = before.shape[0]
    row = lax.broadcasted_iota(jnp.int32, (rim, own.shape[1]), 0)
    front = jnp.where(row < steps, pltpu.roll(before, steps, 0), moved[:rim])
    return jnp.concatenate([front, moved[rim:]], 0)


def forward_body(n, seqs, groups, span, group_rows, width, hidden_width, refs):
    at = HeadPlaces(n, seqs, groups)
    me, core = at.me, at.core
    channels = width // n
    half, heads = n // 2, group_rows // HEAD
    tokens = seqs * span
    links, loads = Links(refs), Loads(refs)
    peers = [lax.rem(me + step, n) for step in range(1, n)]
    after = (lax.rem(me + 1, n), core)
    barrier = pltpu.get_barrier_semaphore()
    at.signal_all(barrier, [(peer, core) for peer in peers])
    outgoing = []

    def save(source, target):
        outgoing.append(loads.start(source, target))

    load_tokens = loads.start(refs.tokens, refs.tokens_in)
    load_qkv = loads.start(refs.w_qkv.at[0], refs.qkv)
    load_cotangent = loads.start(refs.cotangent, refs.cot)
    load_out = loads.start(refs.w_out.at[0], refs.out)
    load_up = loads.start(refs.w_up.at[0], refs.up)
    load_down = loads.start(refs.w_down.at[0], refs.down)

    def normed(value, row, target):
        result = layer_norm(value, refs.gains[row : row + 1], refs.biases[row : row + 1])
        result = result.astype(jnp.bfloat16)
        target[...] = result.T
        return result

    finish_rates = fill_rates(refs, loads, channels, refs.turned_rates)
    valid = valid_positions(refs.lengths, seqs, span, 0)
    refs.columns[...] = jnp.concatenate(
        [refs.gains[...], refs.taps[...], refs.skip[...].reshape(1, width), jnp.zeros((7, width), jnp.float32)], 0
    ).T
    load_tokens.wait()
    flat_in = jnp.concatenate([refs.tokens_in[seq] for seq in range(seqs)], 0)
    flat_in = flat_in.astype(jnp.float32) * valid
    refs.flat_in[...] = flat_in
    normed_one = normed(flat_in, 0, refs.normed_one_t)
    load_qkv.wait()
    keys = dot(normed_one, refs.qkv[:, width : 2 * width]).astype(jnp.bfloat16)
    refs.keys[...] = keys
    rim = refs.rim_in.shape[1]
    at.wait_all(barrier, n - 1)
    for seq in range(seqs):
        refs.rim_out[seq] = refs.keys[(seq + 1) * span - rim : (seq + 1) * span, :]
    halo = links.copy(refs.rim_out, refs.rim_in, after)
    refs.values[...] = dot(normed_one, refs.qkv[:, 2 * width :])
    refs.queries[...] = dot(normed_one, refs.qkv[:, :width])
    load_qkv = loads.start(refs.w_qkv.at[1], refs.qkv)
    finish_rates()
    fill_tables(0, SHARE, span, refs)
    halo.wait_recv()
    there = jnp.where(me == 0, 0.0, 1.0)
    for seq in range(seqs):
        rows = slice(seq * span, (seq + 1) * span)
        before = refs.rim_in[seq].astype(jnp.float32) * there
        own = refs.keys[rows, :].astype(jnp.float32)
        shifted = jnp.zeros_like(own)
        for offset in range(TAPS):
            shifted = shifted + refs.taps[offset : offset + 1] * earlier_rows(own, before, offset)
        refs.shifted[rows, :] = shifted
        carried = (shifted * refs.values[rows, :] * valid[rows]).astype(jnp.bfloat16)
        refs.carried[rows, :] = carried
        refs.carried_t[seq] = carried.T

    shares = channels // SHARE
    arrive, answered = links.slots(shares * n), links.slots(shares * n)

    def share_rows(device, share):
        return pl.ds(pl.multiple_of(device * channels + share * SHARE, 16), SHARE)

    going, own_copies = [], []
    for share in range(shares):
        within = slice(share * SHARE, (share + 1) * SHARE)
        for step, peer in enumerate(peers):
            going.append(
                links.copy(
                    refs.carried_t.at[:, share_rows(peer, share), :],
                    refs.mixed_in.at[me, :, within, :], (peer, core), arrive + share * n + step,
                )
            )
        own_copies.append(
            loads.start(
                refs.carried_t.at[:, share_rows(me, share), :], refs.mixed_in.at[me, :, within, :]
            )
        )
    fill_tables(SHARE, channels, span, refs)
    save(refs.tables, refs.tables_kept)
    save(refs.more_tables, refs.more_tables_kept)
    refs.square_t[...] = refs.values[...].T
    save(refs.square_t, refs.values_t)
    refs.square_two_t[...] = refs.shifted[...].T
    save(refs.square_two_t, refs.shifted_t)
    for seq in range(seqs):
        refs.keys_out[seq] = refs.keys[seq * span : (seq + 1) * span, :].T
    save(refs.keys_out, refs.keys_t)
    refs.queries_out[...] = refs.queries[...].T
    save(refs.queries_out, refs.queries_t)
    save(refs.normed_one_t, refs.normed_one)
    save(refs.carried_t, refs.carried_out)
    back, back_own = [], []
    for share in range(shares):
        within = slice(share * SHARE, (share + 1) * SHARE)
        own_copies[share].wait()
        for copy in going[share * len(peers) : (share + 1) * len(peers)]:
            copy.wait_recv()
        refs.flat_x[share] = (
            refs.mixed_in[:, :, within, :].astype(jnp.float32).reshape(n * seqs * SHARE, span)
        )

        def one_channel(local, carry):
            mixer_forward_channel(n, seqs, refs, share, local)
            return carry

        lax.fori_loop(0, SHARE, one_channel, 0, unroll=4)
        refs.answer[:, :, within, :] = (
            refs.flat_out[share].reshape(n, seqs, SHARE, span).astype(jnp.bfloat16)
        )
        for step, peer in enumerate(peers):
            back.append(
                links.copy(
                    refs.answer.at[peer, :, within, :],
                    refs.convolved.at[:, share_rows(me, share), :], (peer, core),
                    answered + share * n + step,
                )
            )
        back_own.append(
            loads.start(
                refs.answer.at[me, :, within, :], refs.convolved.at[:, share_rows(me, share), :]
            )
        )
    save(refs.mixed_in, refs.mixed_held)
    for copy in back_own:
        copy.wait()
    for copy in back:
        copy.wait_recv()
    for seq in range(seqs):
        rows = slice(seq * span, (seq + 1) * span)
        convolved = refs.convolved[seq].astype(jnp.float32).T
        mixer = convolved + refs.skip[...].reshape(1, width) * refs.carried[rows, :].astype(jnp.float32)
        refs.gated[rows, :] = (refs.queries[rows, :] * mixer).astype(jnp.bfloat16)
        refs.mixer_out[:, rows] = mixer.T
    save(refs.mixer_out, refs.mixer_t)
    refs.gated_out[...] = refs.gated[...].T
    save(refs.gated_out, refs.gated_t)
    load_out.wait()
    hidden = refs.flat_in[...] + dot(refs.gated[...], refs.out[...])
    load_out = loads.start(refs.w_out.at[1], refs.out)

    def feed_forward(hidden, row, hidden_out, normed_out, up, down):
        hidden_out[...] = hidden.T
        refs.hidden[...] = hidden
        refs.normed[...] = normed(hidden, row, normed_out)
        up.wait()

        def one_chunk(index, carry):
            columns = pl.ds(pl.multiple_of(index * width, 128), width)
            raised = dot(refs.normed[...], refs.up[:, columns])
            refs.raised[:, columns] = raised
            refs.active[:, columns] = jax.nn.gelu(raised).astype(jnp.bfloat16)
            return carry

        lax.fori_loop(0, hidden_width // width, one_chunk, 0, unroll=4)
        if down is not None:
            down.wait()
        return refs.hidden[...] + dot(refs.active[...], refs.down[...])

    def turn_hidden(active_out, slope_out):
        def one_chunk(index, carry):
            columns = pl.ds(pl.multiple_of(index * width, 128), width)
            active_out[columns, :] = refs.active[:, columns].T
            slope = gelu_slope(refs.raised[:, columns]).astype(jnp.bfloat16)
            slope_out[columns, :] = slope.T
            return carry

        lax.fori_loop(0, hidden_width // width, one_chunk, 0, unroll=4)

    hidden = feed_forward(
        hidden, 1, refs.hidden_one_t, refs.normed_two_t, load_up, load_down
    )
    load_up = loads.start(refs.w_up.at[1], refs.up)
    load_down = loads.start(refs.w_down.at[1], refs.down)
    refs.hidden[...] = hidden
    refs.normed[...] = normed(hidden, 2, refs.normed_three_t)
    load_qkv.wait()
    count = len(at.targets)
    arrive, leave = links.slots(heads * half), links.slots(heads * count)
    passing = links.slots(heads * half)
    spread = []
    lot = groups * HEAD
    for head in range(heads):
        for part in range(3):
            first = part * width + head * lot
            columns = dot(refs.normed[...], refs.qkv[:, first : first + lot]).astype(jnp.bfloat16)
            for seq in range(seqs):
                refs.spread[head, seq, :, part * HEAD : (part + 1) * HEAD] = columns[
                    seq * span : (seq + 1) * span
                ].T.reshape(groups, HEAD, span)
        for number, (device, seq, group) in enumerate(at.targets):
            sent = (
                refs.spread.at[head, seq, group], refs.held.at[head, me],
                refs.send.at[leave + head * count + number],
                refs.recv.at[arrive + head * half + me // 2], device,
            )
            at.send(*sent)
            spread.append(sent)
    turn_hidden(refs.active_one_t, refs.slope_one_t)
    load_cotangent.wait()
    valid_row = valid_positions(refs.lengths, seqs, span, 1)
    for seq in range(seqs):
        lanes = slice(seq * span, (seq + 1) * span)
        turned = refs.cot[seq].astype(jnp.float32).T * valid_row[:, lanes]
        refs.branch_t[:, lanes] = turned.astype(jnp.bfloat16)
    save(refs.branch_t, refs.branch)
    load_down.wait()

    def store_active(rows, value):
        refs.d_active_t[rows, :] = value.astype(jnp.bfloat16)

    rows_product(refs.down, refs.branch_t[...], hidden_width, 512, store_active)
    save(refs.d_active_t, refs.d_active)
    refs.hidden_two_t[...] = hidden.T
    for source, target in (
        (refs.hidden_one_t, refs.hidden_one_out), (refs.normed_two_t, refs.normed_two),
        (refs.active_one_t, refs.active_one), (refs.slope_one_t, refs.slope_one),
        (refs.hidden_two_t, refs.hidden_two_out), (refs.normed_three_t, refs.normed_three),
    ):
        save(source, target)

    returned, returning = links.slots(heads * count), links.slots(heads * half)
    slot = at.seq * groups + at.group
    going = []

    def gather(head):
        for index, block in enumerate(at.blocks):
            landed = refs.held.at[head, block]
            remote(
                landed, landed, refs.send.at[leave], refs.recv.at[arrive + head * half + index],
                at.sibling,
            ).wait_recv()
            part = refs.held.at[head, block, HEAD : 3 * HEAD]
            links.copy(part, part, at.sibling, passing + head * half + index)
        for index in range(half):
            part = refs.held.at[head, block_of(index, 1 - core), HEAD : 3 * HEAD]
            remote(
                part, part, refs.send.at[leave], refs.recv.at[passing + head * half + index],
                at.sibling,
            ).wait_recv()

    def attend(head):
        fill_head(refs.held, head, 1, n, span, refs.key_rows, None)
        fill_head(refs.held, head, 2, n, span, None, refs.value_columns)
        for index, block in enumerate(at.blocks):
            query = refs.held[head, block, :HEAD, :] * jnp.bfloat16(HEAD**-0.5)
            clear, reach = 2 * index * span, 2 * (index + 1) * span
            edge = dot(refs.key_rows[clear:reach, :], query)
            edge = jnp.where(causal(clear, reach - clear, block * span, span), edge, masked_score)
            top = jnp.max(edge, 0, keepdims=True)
            if index > 0:
                body = dot(refs.key_rows[:clear, :], query)
                top = jnp.maximum(top, jnp.max(body, 0, keepdims=True))
            edge = jnp.exp(edge - top)
            total = jnp.sum(edge, 0, keepdims=True)
            result = dot(refs.value_columns[:, clear:reach], edge.astype(jnp.bfloat16))
            if index > 0:
                body = jnp.exp(body - top)
                total = total + jnp.sum(body, 0, keepdims=True)
                result = result + dot(refs.value_columns[:, :clear], body.astype(jnp.bfloat16))
            refs.outputs[head, index] = (result / total).astype(jnp.bfloat16)
            refs.lse[index, head : head + 1, :] = top + jnp.log(total)
        into = refs.attended_t.at[
            pl.ds(pl.multiple_of(head * lot + at.group * HEAD, HEAD), HEAD),
            pl.ds(pl.multiple_of(at.seq * span, span), span),
        ]
        for index, device in enumerate(at.sources):
            sent = (
                refs.outputs.at[head, index], into, refs.send.at[returning + head * half + index],
                refs.recv.at[returned + head * count + slot], device,
            )
            at.send(*sent)
            going.append(sent)

    for head in range(heads):
        gather(head)
        attend(head)
    save(refs.held, refs.held_out)
    for head in range(heads):
        for number, (device, seq, group) in enumerate(at.targets):
            first = head * lot + group * HEAD
            landed = refs.attended_t.at[first : first + HEAD, seq * span : (seq + 1) * span]
            remote(
                landed, landed, refs.send.at[leave],
                refs.recv.at[returned + head * count + number], at.sibling,
            ).wait_recv()
    save(refs.attended_t, refs.attended)
    load_out.wait()
    hidden = refs.hidden[...] + dot(refs.attended_t[...].T, refs.out[...])
    hidden = feed_forward(
        hidden, 3, refs.hidden_three_t, refs.normed_four_t, load_up, None
    )
    turn_hidden(refs.active_two_t, refs.slope_two_t)
    for source, target in (
        (refs.hidden_three_t, refs.hidden_three_out), (refs.normed_four_t, refs.normed_four),
        (refs.active_two_t, refs.active_two), (refs.slope_two_t, refs.slope_two),
    ):
        save(source, target)
    hidden = (hidden * valid).astype(jnp.bfloat16)
    for seq in range(seqs):
        refs.mixed[seq] = hidden[seq * span : (seq + 1) * span]
    for copy in outgoing:
        copy.wait()
    for sent in spread + going:
        at.wait_sent(*sent)
    links.finish()


def forward(
    tokens, cotangent, lengths, gains, biases, taps, skip, rates, rate_weights, w_qkv, w_out, w_up, w_down, n,
    groups, collective,
):
    seqs, span, width = tokens.shape
    hidden_width = w_up.shape[2]
    group_rows, channels = width // groups, width // n
    rows = seqs * span
    half, heads = n // 2, group_rows // HEAD
    low, wide = jnp.bfloat16, jnp.float32
    inputs = dict(
        tokens=(tokens, HBM), cotangent=(cotangent, HBM), lengths=(lengths, VMEM), gains=(gains, VMEM), biases=(biases, VMEM),
        taps=(taps, VMEM), skip=(skip, VMEM), all_rates=(rates, HBM), all_weights=(rate_weights, HBM),
        w_qkv=(w_qkv, HBM), w_out=(w_out, HBM), w_up=(w_up, HBM), w_down=(w_down, HBM),
    )
    square, tall, by_head = (width, rows), (hidden_width, rows), (heads, n, 3 * HEAD, span)
    mixed = (n, seqs, channels, span)
    tables, more_tables = table_shapes(channels, span)
    outputs = dict(
        mixed=((seqs, span, width), low, VMEM), columns=((width, 16), wide, VMEM),
        lse=((half, heads, span), wide, VMEM),
        held_out=(by_head, low, HBM), mixed_held=(mixed, low, HBM),
        carried_out=((seqs, width, span), low, HBM),
        values_t=(square, wide, HBM), shifted_t=(square, wide, HBM), keys_t=((seqs, width, span), low, HBM),
        queries_t=(square, wide, HBM), mixer_t=(square, wide, HBM), gated_t=(square, low, HBM),
        attended=(square, low, HBM), branch=(square, low, HBM), d_active=(tall, low, HBM),
        normed_one=(square, low, HBM), normed_two=(square, low, HBM),
        normed_three=(square, low, HBM), normed_four=(square, low, HBM),
        hidden_one_out=(square, wide, HBM), hidden_two_out=(square, wide, HBM),
        hidden_three_out=(square, wide, HBM),
        active_one=(tall, low, HBM), active_two=(tall, low, HBM),
        slope_one=(tall, low, HBM), slope_two=(tall, low, HBM),
        tables_kept=(tables, low, HBM), more_tables_kept=(more_tables, low, HBM),
    )
    flat = (channels // SHARE, n * seqs * SHARE, span)
    lying = (rows, width)
    scratch = dict(
        qkv=(w_qkv.shape[1:], low), out=(w_out.shape[1:], low), up=(w_up.shape[1:], low),
        down=(w_down.shape[1:], low), tokens_in=(tokens.shape, low), flat_in=(lying, wide),
        keys=(lying, low), values=(lying, wide), queries=(lying, wide), shifted=(lying, wide),
        carried=(lying, low), gated=(lying, low), hidden=(lying, wide), normed=(lying, low),
        active=((rows, hidden_width), low), rim_in=((seqs, 16, width), low),
        rim_out=((seqs, 16, width), low), carried_t=((seqs, width, span), low),
        convolved=((seqs, width, span), low), mixed_in=(mixed, low), answer=(mixed, low),
        flat_x=(flat, wide), flat_out=(flat, wide), tables=(tables, low), more_tables=(more_tables, low),
        turned_rates=((width, 2 * STATES), wide),
        **rate_scratch(width, channels), raised=((rows, hidden_width), wide),
        cot=(tokens.shape, low), branch_t=(square, low), d_active_t=(tall, low),
        square_t=(square, wide), square_two_t=(square, wide), keys_out=((seqs, width, span), low),
        queries_out=(square, wide), mixer_out=(square, wide), gated_out=(square, low),
        attended_t=(square, low), normed_one_t=(square, low), normed_two_t=(square, low),
        normed_three_t=(square, low), normed_four_t=(square, low), hidden_one_t=(square, wide),
        hidden_two_t=(square, wide), hidden_three_t=(square, wide), active_one_t=(tall, low),
        active_two_t=(tall, low), slope_one_t=(tall, low), slope_two_t=(tall, low),
        spread=((heads, seqs, groups, 3 * HEAD, span), low), held=(by_head, low),
        outputs=((heads, half, HEAD, span), low), key_rows=((n * span, HEAD), low),
        value_columns=((HEAD, n * span), low),
    )
    body = functools.partial(
        forward_body, n, seqs, groups, span, group_rows, width, hidden_width
    )
    return launch(body, inputs, outputs, scratch, 290, collective)


def per_device_by_heads(
    tokens,
    cotangent,
    lengths,
    norm_gain,
    norm_bias,
    w_qkv,
    w_out,
    w_up,
    w_down,
    taps,
    skip,
    ssm_rate,
    ssm_out,
):
    seq_count, span_rows, width = tokens.shape[1:]
    devices = lax.axis_size(SEQ)
    channels = width // devices
    groups = devices // 4
    row_count = seq_count * span_rows
    rates, weights = ssm_rate.T, ssm_out.T
    kept = forward(
        tokens[0], cotangent[0], lengths, norm_gain, norm_bias, taps, skip, rates, weights, w_qkv, w_out,
        w_up, w_down, devices, groups, 1,
    )

    def sliced(value):
        return value.reshape(devices, value.shape[0] // devices, row_count)

    back = back_one(
        kept.branch, kept.d_active, kept.hidden_three_out, kept.slope_two, sliced(kept.normed_four),
        sliced(kept.active_two), sliced(kept.attended), kept.held_out, kept.lse, kept.columns,
        w_out, w_up, 3,
    )
    end = back_two(
        kept.tables_kept, kept.more_tables_kept, back.mid_out, back.half_out, back.d_qkv.reshape(3 * width, row_count),
        back.grad_out, kept.hidden_two_out, sliced(kept.normed_three), kept.slope_one,
        sliced(kept.normed_two), sliced(kept.active_one), kept.hidden_one_out,
        sliced(kept.gated_t), kept.queries_t, kept.mixer_t, kept.carried_out, kept.mixed_held,
        kept.values_t, kept.shifted_t, kept.keys_t, tokens[0], sliced(kept.normed_one),
        kept.columns, back.small, lengths, rates, weights, w_qkv, w_out, w_up, w_down, 4,
    )
    return collected(kept, end, norm_gain.shape[0])


def collected(kept, end, layers):
    pairs = [
        (end.qkv_one, end.qkv_two), (end.out_one, end.out_two), (end.up_one, end.up_two),
        (end.down_one, end.down_two),
    ]
    alone = [kept.mixed, end.d_tokens, end.rate_sum, end.weight_sum]
    rows = end.small_sum.shape[1]
    small = [(layers, rows), (layers - 1, rows), (rows,), (TAPS, rows), (rows,)]
    wide = jnp.float32

    def body(*refs):
        refs = list(refs)
        pair_refs = [(refs.pop(0), refs.pop(0)) for _ in pairs]
        alone_refs = [refs.pop(0) for _ in alone]
        sums = refs.pop(0)
        for first, second in pair_refs:
            out = refs.pop(0)
            out[0] = first[...]
            out[1] = second[...]
        for source in alone_refs:
            refs.pop(0)[...] = source[...]
        gain, bias, last, taps, skip = refs
        gain[...] = sums[:layers, :]
        bias[...] = sums[layers : 2 * layers - 1, :]
        last[...] = sums[2 * layers - 1, :]
        taps[...] = sums[2 * layers : 2 * layers + TAPS, :]
        skip[...] = sums[2 * layers + TAPS, :]

    arrays = [array for pair in pairs for array in pair] + alone + [end.small_sum]
    shapes = [jax.ShapeDtypeStruct((2, *first.shape), wide) for first, _ in pairs]
    shapes += [jax.ShapeDtypeStruct(array.shape, array.dtype) for array in alone]
    shapes += [jax.ShapeDtypeStruct(shape, wide) for shape in small]
    vmem = pl.BlockSpec(memory_space=VMEM)
    outs = pl.pallas_call(
        body,
        out_shape=tuple(shapes),
        in_specs=[vmem] * len(arrays),
        out_specs=(vmem,) * len(shapes),
        compiler_params=pltpu.CompilerParams(vmem_limit_bytes=VMEM_BYTES),
    )(*arrays)
    qkv, out, up, down, mixed, d_tokens, rate, weight, gain, bias, last, taps, skip = outs
    return (
        mixed[None], d_tokens[None], gain, bias, last, qkv, out, up, down, taps, skip, rate, weight,
    )


def fits_by_heads(mesh):
    devices = mesh.shape[SEQ]
    return devices == 16 and mesh.shape[BATCH] == 2


def solution(mesh):
    placed = (
        P(BATCH, None, SEQ, None),
        P(BATCH, None, SEQ, None),
        P(BATCH, None),
        P(),
        P(),
        P(),
        P(),
        P(),
        P(),
        P(),
        P(),
        P(),
        P(),
    )
    return jax.shard_map(
        per_device_by_heads if fits_by_heads(mesh) else per_device,
        mesh=mesh,
        in_specs=placed,
        out_specs=(
            P(BATCH, None, SEQ, None),
            P(BATCH, None, SEQ, None),
            P(None, SEQ),
            P(None, SEQ),
            P(SEQ),
            P(None, SEQ, None),
            P(None, SEQ, None),
            P(None, SEQ, None),
            P(None, SEQ, None),
            P(None, SEQ),
            P(SEQ),
            P(SEQ, None),
            P(SEQ, None),
        ),
        check_vma=False,
    )
```

```python
import functools
import math
import types

import jax
import jax.numpy as jnp
from jax import lax
from jax.experimental import pallas as pl
from jax.experimental.pallas import tpu as pltpu
from jax.sharding import PartitionSpec as P

HEADS = 12
HEAD = 64
TAPS = 4
STATES = 64
KEPT = "_kept"
ONE = "_one"
TWO = "_two"
FIRST = "first"
MESH = pl.DeviceIdType.MESH
SEQ = "seq"
BATCH = "batch"
QKV_MORE = "qkv_more"
QKV_LESS = "qkv_less"
DOWN = "down"
OUT = "out"
UP = "up"
QKV = "qkv"
SMALL = "small"
VMEM_BYTES = 63 * 2**20


norm_eps = 1e-05
highest = lax.Precision.HIGHEST
masked_score = -1e30


def for_sending(array):
    return jax.tree.map(lambda a: a.astype(jnp.bfloat16) if a.dtype == jnp.float32 else a, array)


def passed_along(value, axis, steps):
    count = lax.axis_size(axis)
    initial, last = (max(0, -steps), min(count, count - steps))
    return lax.ppermute(value, axis, [(source, source + steps) for source in range(initial, last)])


def layer_norm(inputs, scale_row, shift_row):
    center = inputs - jnp.mean(inputs, -1, keepdims=True)
    spread = jnp.mean(center * center, -1, keepdims=True)
    return center * lax.rsqrt(spread + norm_eps) * scale_row + shift_row


def dense_product(operand_a, operand_b):
    return jnp.dot(operand_a, operand_b, preferred_element_type=jnp.float32)


def product_left(operand_a, operand_b):
    return lax.dot_general(
        operand_a, operand_b, (((0,), (0,)), ((), ())), preferred_element_type=jnp.float32
    )


def product_right(operand_a, operand_b):
    return lax.dot_general(
        operand_a, operand_b, (((1,), (1,)), ((), ())), preferred_element_type=jnp.float32
    )


def angle_table(count_rows, count_cols, period):
    product_index = (
        jnp.arange(count_rows, dtype=jnp.int32)[:, None]
        * jnp.arange(count_cols, dtype=jnp.int32)[None, :]
        % period
    )
    angles = product_index.astype(jnp.float32) * (2.0 * math.pi / period)
    return (jnp.cos(angles), jnp.sin(angles))


def table_einsum(form, table, data):
    return jnp.einsum(form, table, data, precision=highest)


def forward_spectrum(time_parts):
    count_parts = time_parts.shape[0]
    span_rows = time_parts.shape[2]
    count_freq = 2 * count_parts
    cos_parts, sin_parts = angle_table(count_freq, count_parts, count_freq)
    first_real = table_einsum("fp,pjsc->fjsc", cos_parts, time_parts)
    first_imag = -table_einsum("fp,pjsc->fjsc", sin_parts, time_parts)
    cos_twist, sin_twist = angle_table(count_freq, span_rows, count_freq * span_rows)
    cos_twist = cos_twist[:, None, :, None]
    sin_twist = sin_twist[:, None, :, None]
    twist_real = first_real * cos_twist + first_imag * sin_twist
    twist_imag = first_imag * cos_twist - first_real * sin_twist
    cos_span, sin_span = angle_table(span_rows, span_rows, span_rows)
    out_real = table_einsum("ts,fjsc->fjtc", cos_span, twist_real) + table_einsum(
        "ts,fjsc->fjtc", sin_span, twist_imag
    )
    out_imag = table_einsum("ts,fjsc->fjtc", cos_span, twist_imag) - table_einsum(
        "ts,fjsc->fjtc", sin_span, twist_real
    )
    return (out_real, out_imag)


def inverse_spectrum(freq_real, freq_imag):
    count_freq = freq_real.shape[0]
    span_rows = freq_real.shape[2]
    count_parts = count_freq // 2
    fft_length = count_freq * span_rows
    cos_span, sin_span = angle_table(span_rows, span_rows, span_rows)
    first_real = table_einsum("st,fjtc->fjsc", cos_span, freq_real) - table_einsum(
        "st,fjtc->fjsc", sin_span, freq_imag
    )
    first_imag = table_einsum("st,fjtc->fjsc", cos_span, freq_imag) + table_einsum(
        "st,fjtc->fjsc", sin_span, freq_real
    )
    cos_twist, sin_twist = angle_table(count_freq, span_rows, fft_length)
    cos_twist = cos_twist[:, None, :, None]
    sin_twist = sin_twist[:, None, :, None]
    twist_real = first_real * cos_twist - first_imag * sin_twist
    twist_imag = first_imag * cos_twist + first_real * sin_twist
    cos_parts, sin_parts = angle_table(count_parts, count_freq, count_freq)
    summed = table_einsum("pf,fjsc->pjsc", cos_parts, twist_real) - table_einsum(
        "pf,fjsc->pjsc", sin_parts, twist_imag
    )
    return summed / fft_length


def to_frequency(data_low):
    parts = lax.all_to_all(data_low[None], SEQ, split_axis=3, concat_axis=0, tiled=True)
    return forward_spectrum(parts.astype(jnp.float32))


def from_frequency(freq_real, freq_imag):
    time_parts = inverse_spectrum(freq_real, freq_imag)
    joined = lax.all_to_all(
        for_sending(time_parts), SEQ, split_axis=0, concat_axis=3, tiled=True
    ).astype(time_parts.dtype)
    return joined[0]


def kernel_parts(rate_slice, weight_slice, count_freq, span_rows):
    fft_length = count_freq * span_rows
    length_full = fft_length // 2
    frequency = (
        jnp.arange(count_freq, dtype=jnp.int32)[:, None]
        + count_freq * jnp.arange(span_rows, dtype=jnp.int32)[None, :]
    )
    angles = (frequency.astype(jnp.float32) * (2.0 * math.pi / fft_length))[:, None, :, None, None]
    odd_mask = (frequency % 2 == 1)[:, None, :, None, None]
    channels = rate_slice.shape[0]
    blocks = rate_slice.shape[1] // 8
    rate_blocks = rate_slice.reshape(channels, blocks, 8).transpose(1, 0, 2)
    weight_blocks = weight_slice.reshape(channels, blocks, 8).transpose(1, 0, 2)

    def add_block(running, piece_pair):
        rate_part, weight_part = piece_pair
        decays = jnp.exp(-rate_part)
        half_sine = jnp.sin(angles / 2.0)
        real_den = -jnp.expm1(-rate_part) + decays * 2.0 * half_sine * half_sine
        imag_den = decays * jnp.sin(angles)
        numerator = jnp.where(
            odd_mask, 1.0 + jnp.exp(-rate_part * length_full), -jnp.expm1(-rate_part * length_full)
        )
        factor = weight_part * numerator / (real_den * real_den + imag_den * imag_den)
        return (
            (
                running[0] + jnp.sum(factor * real_den, -1),
                running[1] - jnp.sum(factor * imag_den, -1),
            ),
            None,
        )

    zeros_init = jnp.zeros((count_freq, 1, span_rows, channels), jnp.float32)
    return lax.scan(
        jax.checkpoint(add_block), (zeros_init, zeros_init), (rate_blocks, weight_blocks)
    )[0]


def attention_mask(query_positions, key_count, length_value):
    key_positions = jnp.arange(key_count, dtype=jnp.int32)
    return (key_positions[None, :] <= query_positions[:, None]) & (
        key_positions[None, :] < length_value
    )


def head_slice(matrix, head_index):
    return lax.dynamic_slice_in_dim(matrix, head_index * HEAD, HEAD, 1)


def attend_forward(query_low, keys_low, values_low, length_value, query_positions):
    whole_keys, whole_values = (
        lax.all_gather(keys_low, SEQ, axis=0, tiled=True),
        lax.all_gather(values_low, SEQ, axis=0, tiled=True),
    )
    allowed = attention_mask(query_positions, whole_keys.shape[0], length_value)
    score_scale = HEAD ** (-0.5)

    def head_forward(head_index):
        scores = jnp.where(
            allowed,
            score_scale
            * product_right(head_slice(query_low, head_index), head_slice(whole_keys, head_index)),
            masked_score,
        )
        top_score = jnp.max(scores, -1, keepdims=True)
        expos = jnp.exp(scores - top_score)
        totals = jnp.sum(expos, -1, keepdims=True)
        probs_low = (expos / totals).astype(jnp.bfloat16)
        return (
            dense_product(probs_low, head_slice(whole_values, head_index)),
            (top_score + jnp.log(totals))[:, 0],
        )

    head_outputs, log_totals = lax.map(head_forward, jnp.arange(HEADS, dtype=jnp.int32))
    attended = head_outputs.transpose(1, 0, 2).reshape(query_low.shape[0], HEADS * HEAD)
    return (attended, log_totals, whole_keys, whole_values)


def join_heads(head_rows):
    return head_rows.transpose(1, 0, 2).reshape(head_rows.shape[1], HEADS * HEAD)


def attend_backward(
    query_low, whole_keys, whole_values, log_totals, grad_low, length_value, query_positions
):
    allowed = attention_mask(query_positions, whole_keys.shape[0], length_value)
    score_scale = HEAD ** (-0.5)
    span_rows = query_low.shape[0]

    def query_side(head_index):
        head_query = head_slice(query_low, head_index)
        head_keys = head_slice(whole_keys, head_index)
        head_grad = head_slice(grad_low, head_index)
        scores = jnp.where(
            allowed, score_scale * product_right(head_query, head_keys), masked_score
        )
        weights = jnp.exp(scores - log_totals[head_index][:, None])
        d_weights = product_right(head_grad, head_slice(whole_values, head_index))
        row_term = jnp.sum(weights * d_weights, -1, keepdims=True)
        d_scores = (weights * (d_weights - row_term)).astype(jnp.bfloat16)
        d_query = score_scale * dense_product(d_scores, head_keys)
        return (d_query, row_term[:, 0], d_scores, weights)

    def head_backward(head_index):
        d_query, row_term, d_scores, weights = query_side(head_index)
        head_query = head_slice(query_low, head_index)
        head_grad = head_slice(grad_low, head_index)
        d_keys = score_scale * product_left(d_scores, head_query)
        d_values = product_left(weights.astype(jnp.bfloat16), head_grad)
        return (d_query, d_keys, d_values)

    query_grads, key_grads, value_grads = lax.map(head_backward, jnp.arange(HEADS, dtype=jnp.int32))
    count_rows = span_rows * lax.axis_size(SEQ)
    key_part = (
        lax.slice_in_dim(key_grads, 0, count_rows, axis=1)
        .transpose(1, 0, 2)
        .reshape(count_rows, HEADS * HEAD)
    )
    value_part = (
        lax.slice_in_dim(value_grads, 0, count_rows, axis=1)
        .transpose(1, 0, 2)
        .reshape(count_rows, HEADS * HEAD)
    )
    key_value = lax.psum_scatter(
        jnp.stack([key_part, value_part], 1), SEQ, scatter_dimension=0, tiled=True
    )
    return (join_heads(query_grads), key_value[:, 0], key_value[:, 1])


def per_device(
    tokens,
    cotangent,
    lengths,
    norm_gain,
    norm_bias,
    w_qkv,
    w_out,
    w_up,
    w_down,
    taps,
    skip,
    ssm_rate,
    ssm_out,
):
    seq_count = tokens.shape[1]
    span_rows = tokens.shape[2]
    width = tokens.shape[3]
    devices = lax.axis_size(SEQ)
    place = lax.axis_index(SEQ)
    channels = width // devices
    count_freq = 2 * devices
    fft_length = count_freq * span_rows
    rim = TAPS - 1
    row_count = seq_count * span_rows
    query_positions = place * span_rows + jnp.arange(span_rows, dtype=jnp.int32)
    validity = (query_positions[None, :] < lengths[0][:, None]).astype(jnp.float32)[:, :, None]
    rate_slice = lax.dynamic_slice_in_dim(ssm_rate, place * channels, channels, 0)
    weight_slice = lax.dynamic_slice_in_dim(ssm_out, place * channels, channels, 0)

    def spectrum_of(rate_in, weight_in):
        return kernel_parts(rate_in, weight_in, count_freq, span_rows)

    def feed_forward(inputs, norm_row, layer):
        normed_low = layer_norm(inputs, norm_gain[norm_row], norm_bias[norm_row]).astype(
            jnp.bfloat16
        )
        raised = dense_product(normed_low, w_up[layer])
        active_low = jax.nn.gelu(raised).astype(jnp.bfloat16)
        return (normed_low, raised, active_low, inputs + dense_product(active_low, w_down[layer]))

    def norm_backward(inputs, norm_row, d_normed):
        norm_pull = jax.vjp(layer_norm, inputs, norm_gain[norm_row], norm_bias[norm_row])[1]
        return norm_pull(d_normed)

    def feed_backward(grad_rows, inputs, normed_low, raised, active_low, norm_row, layer):
        branch_low = grad_rows.astype(jnp.bfloat16)
        down_grad = product_left(active_low, branch_low)
        d_active = product_right(branch_low, w_down[layer])
        gelu_pull = jax.vjp(jax.nn.gelu, raised)[1]
        d_raised = gelu_pull(d_active)[0].astype(jnp.bfloat16)
        up_grad = product_left(normed_low, d_raised)
        d_inputs, gain_part, bias_part = norm_backward(
            inputs, norm_row, product_right(d_raised, w_up[layer])
        )
        return (grad_rows + d_inputs, down_grad, up_grad, gain_part, bias_part)

    def forward_pass(token_block):
        masked_in = token_block[0].astype(jnp.float32) * validity
        flat_in = masked_in.reshape(row_count, width)
        normed_one = layer_norm(flat_in, norm_gain[0], norm_bias[0]).astype(jnp.bfloat16)
        qkv_one = dense_product(normed_one, w_qkv[0]).reshape(seq_count, span_rows, 3 * width)
        queries_one = qkv_one[:, :, :width]
        keys_one = qkv_one[:, :, width : 2 * width].astype(jnp.bfloat16)
        values_one = qkv_one[:, :, 2 * width :]
        earlier = passed_along(keys_one[:, span_rows - rim :], SEQ, 1)
        extended = jnp.concatenate([earlier, keys_one], 1)
        shifted = sum(
            (
                taps[offset]
                * extended[:, rim - offset : rim - offset + span_rows].astype(jnp.float32)
                for offset in range(TAPS)
            )
        )
        carried_low = (shifted * values_one * validity).astype(jnp.bfloat16)
        carried_real, carried_imag = to_frequency(carried_low)
        kernel_both, kernel_pull = jax.vjp(spectrum_of, rate_slice, weight_slice)
        kernel_real, kernel_imag = kernel_both
        convolved = from_frequency(
            carried_real * kernel_real - carried_imag * kernel_imag,
            carried_real * kernel_imag + carried_imag * kernel_real,
        )
        carried = carried_low.astype(jnp.float32)
        mixer = convolved + skip * carried
        gated_low = (queries_one * mixer).reshape(row_count, width).astype(jnp.bfloat16)
        hidden_one = flat_in + dense_product(gated_low, w_out[0])
        normed_two, raised_one, active_one, hidden_two = feed_forward(hidden_one, 1, 0)
        normed_three = layer_norm(hidden_two, norm_gain[2], norm_bias[2]).astype(jnp.bfloat16)
        qkv_two = (
            dense_product(normed_three, w_qkv[1])
            .astype(jnp.bfloat16)
            .reshape(seq_count, span_rows, 3 * width)
        )
        attended_list = []
        totals_list = []
        keys_list = []
        values_list = []
        for seq_index in range(seq_count):
            attended, log_totals, whole_keys, whole_values = attend_forward(
                qkv_two[seq_index, :, :width],
                qkv_two[seq_index, :, width : 2 * width],
                qkv_two[seq_index, :, 2 * width :],
                lengths[0, seq_index],
                query_positions,
            )
            attended_list.append(attended)
            totals_list.append(log_totals)
            keys_list.append(whole_keys)
            values_list.append(whole_values)
        attended_low = jnp.concatenate(attended_list, 0).astype(jnp.bfloat16)
        hidden_three = hidden_two + dense_product(attended_low, w_out[1])
        normed_four, raised_two, active_two, hidden_four = feed_forward(hidden_three, 3, 1)
        output = hidden_four.reshape(seq_count, span_rows, width) * validity
        saved = types.SimpleNamespace(
            flat_in=flat_in,
            normed_one=normed_one,
            queries_one=queries_one,
            values_one=values_one,
            extended=extended,
            shifted=shifted,
            carried=carried,
            carried_real=carried_real,
            carried_imag=carried_imag,
            kernel_real=kernel_real,
            kernel_imag=kernel_imag,
            kernel_pull=kernel_pull,
            mixer=mixer,
            gated_low=gated_low,
            hidden_one=hidden_one,
            normed_two=normed_two,
            raised_one=raised_one,
            active_one=active_one,
            hidden_two=hidden_two,
            normed_three=normed_three,
            qkv_two=qkv_two,
            totals_list=totals_list,
            keys_list=keys_list,
            values_list=values_list,
            attended_low=attended_low,
            hidden_three=hidden_three,
            normed_four=normed_four,
            raised_two=raised_two,
            active_two=active_two,
        )
        return (output, saved)

    output = forward_pass(tokens)[0]
    saved = forward_pass(lax.optimization_barrier(tokens))[1]
    grad_rows = (cotangent[0].astype(jnp.float32) * validity).reshape(row_count, width)
    grad_rows, down_two, up_two, gain_four, bias_four = feed_backward(
        grad_rows,
        saved.hidden_three,
        saved.normed_four,
        saved.raised_two,
        saved.active_two,
        3,
        1,
    )
    branch_low = grad_rows.astype(jnp.bfloat16)
    out_two = product_left(saved.attended_low, branch_low)
    d_attended = (
        product_right(branch_low, w_out[1])
        .astype(jnp.bfloat16)
        .reshape(seq_count, span_rows, width)
    )
    qkv_two = saved.qkv_two
    grad_parts = []
    for seq_index in range(seq_count):
        d_query_rows, d_key_rows, d_value_rows = attend_backward(
            qkv_two[seq_index, :, :width],
            saved.keys_list[seq_index],
            saved.values_list[seq_index],
            saved.totals_list[seq_index],
            d_attended[seq_index],
            lengths[0, seq_index],
            query_positions,
        )
        grad_parts.append(jnp.concatenate([d_query_rows, d_key_rows, d_value_rows], -1))
    d_qkv_two = jnp.concatenate(grad_parts, 0).astype(jnp.bfloat16)
    qkv_grad_two = product_left(saved.normed_three, d_qkv_two)
    d_inputs, gain_three, bias_three = norm_backward(
        saved.hidden_two, 2, product_right(d_qkv_two, w_qkv[1])
    )
    grad_rows = grad_rows + d_inputs
    grad_rows, down_one, up_one, gain_two, bias_two = feed_backward(
        grad_rows,
        saved.hidden_one,
        saved.normed_two,
        saved.raised_one,
        saved.active_one,
        1,
        0,
    )
    branch_low = grad_rows.astype(jnp.bfloat16)
    out_one = product_left(saved.gated_low, branch_low)
    d_gated = product_right(branch_low, w_out[0]).reshape(seq_count, span_rows, width)
    d_queries = d_gated * saved.mixer
    d_mixer = d_gated * saved.queries_one
    skip_grad = jnp.sum(d_mixer * saved.carried, (0, 1))
    conv_real, conv_imag = to_frequency(d_mixer.astype(jnp.bfloat16))
    kernel_real = saved.kernel_real
    kernel_imag = saved.kernel_imag
    from_conv = from_frequency(
        kernel_real * conv_real + kernel_imag * conv_imag,
        kernel_real * conv_imag - kernel_imag * conv_real,
    )
    d_carried = d_mixer * skip + from_conv
    carried_real = saved.carried_real
    carried_imag = saved.carried_imag
    cot_real = (
        jnp.sum(carried_real * conv_real + carried_imag * conv_imag, 1, keepdims=True) / fft_length
    )
    cot_imag = (
        jnp.sum(carried_real * conv_imag - carried_imag * conv_real, 1, keepdims=True) / fft_length
    )
    rate_grad, weight_grad = saved.kernel_pull((cot_real, cot_imag))
    d_shifted = d_carried * saved.values_one * validity
    d_values = d_carried * saved.shifted * validity
    extended = saved.extended
    grads_extended = sum(
        (
            jnp.pad(taps[offset] * d_shifted, ((0, 0), (rim - offset, offset), (0, 0)))
            for offset in range(TAPS)
        )
    )
    taps_grad = jnp.stack(
        [
            jnp.sum(
                d_shifted
                * extended[:, rim - offset : rim - offset + span_rows].astype(jnp.float32),
                (0, 1),
            )
            for offset in range(TAPS)
        ]
    )
    later = passed_along(grads_extended[:, :rim], SEQ, -1)
    d_keys = grads_extended[:, rim:] + jnp.pad(later, ((0, 0), (span_rows - rim, 0), (0, 0)))
    d_qkv_one = (
        jnp.concatenate([d_queries, d_keys, d_values], -1)
        .reshape(row_count, 3 * width)
        .astype(jnp.bfloat16)
    )
    qkv_grad_one = product_left(saved.normed_one, d_qkv_one)
    d_inputs, gain_one, bias_one = norm_backward(
        saved.flat_in, 0, product_right(d_qkv_one, w_qkv[0])
    )
    d_tokens = ((grad_rows + d_inputs).reshape(seq_count, span_rows, width) * validity)[None]
    gain_sum, bias_sum, qkv_sum, out_sum, up_sum, down_sum, taps_sum, skip_sum = (
        lax.psum_scatter(
            jnp.stack([gain_one, gain_two, gain_three, gain_four]),
            SEQ,
            scatter_dimension=1,
            tiled=True,
        ),
        lax.psum_scatter(
            jnp.stack([bias_one, bias_two, bias_three, bias_four]),
            SEQ,
            scatter_dimension=1,
            tiled=True,
        ),
        lax.psum_scatter(
            jnp.stack([qkv_grad_one, qkv_grad_two]), SEQ, scatter_dimension=1, tiled=True
        ),
        lax.psum_scatter(jnp.stack([out_one, out_two]), SEQ, scatter_dimension=1, tiled=True),
        lax.psum_scatter(jnp.stack([up_one, up_two]), SEQ, scatter_dimension=1, tiled=True),
        lax.psum_scatter(jnp.stack([down_one, down_two]), SEQ, scatter_dimension=1, tiled=True),
        lax.psum_scatter(taps_grad, SEQ, scatter_dimension=1, tiled=True),
        lax.psum_scatter(skip_grad[None], SEQ, scatter_dimension=1, tiled=True),
    )
    totals = (
        lax.psum(gain_sum.astype(jnp.bfloat16), BATCH).astype(jnp.float32),
        lax.psum(bias_sum.astype(jnp.bfloat16), BATCH).astype(jnp.float32),
        lax.psum(qkv_sum.astype(jnp.bfloat16), BATCH).astype(jnp.float32),
        lax.psum(out_sum.astype(jnp.bfloat16), BATCH).astype(jnp.float32),
        lax.psum(up_sum.astype(jnp.bfloat16), BATCH).astype(jnp.float32),
        lax.psum(down_sum.astype(jnp.bfloat16), BATCH).astype(jnp.float32),
        lax.psum(taps_sum.astype(jnp.bfloat16), BATCH).astype(jnp.float32),
        lax.psum(skip_sum.astype(jnp.bfloat16), BATCH).astype(jnp.float32),
        lax.psum(rate_grad.astype(jnp.bfloat16), BATCH).astype(jnp.float32),
        lax.psum(weight_grad.astype(jnp.bfloat16), BATCH).astype(jnp.float32),
    )
    return (
        output[None].astype(jnp.bfloat16),
        d_tokens,
        totals[0],
        totals[1][:3],
        totals[1][3],
        totals[2],
        totals[3],
        totals[4],
        totals[5],
        totals[6],
        totals[7][0],
        totals[8],
        totals[9],
    )


def other_device(place, core, to_place, to_core):
    return jnp.logical_or(place != to_place, core != to_core)


def greet(devices):
    barrier = pltpu.get_barrier_semaphore()
    for device in devices:
        pl.semaphore_signal(barrier, inc=1, device_id=device, device_id_type=MESH)
    pl.semaphore_wait(barrier, len(devices))


def remote(source, target, send_sem, recv_sem, device):
    return pltpu.make_async_remote_copy(
        src_ref=source,
        dst_ref=target,
        send_sem=send_sem,
        recv_sem=recv_sem,
        device_id=device,
        device_id_type=MESH,
    )


def split_low(value):
    upper = value.astype(jnp.bfloat16)
    return upper, (value - upper.astype(jnp.float32)).astype(jnp.bfloat16)


NN = (((1,), (0,)), ((), ()))
NT = (((1,), (1,)), ((), ()))
TN = (((0,), (0,)), ((), ()))


def dot(left, right, form=NN):
    return lax.dot_general(left, right, form, preferred_element_type=jnp.float32)


def dot_fine(left, right, form=NN):
    left_up, left_low = left
    right_up, right_low = right
    total = dot(left_up, right_up, form) + dot(left_up, right_low, form)
    if left_low is not None:
        total = total + dot(left_low, right_up, form)
    return total


def state_steps(span):
    row = lax.broadcasted_iota(jnp.int32, (span, 2 * STATES), 0)
    lane = lax.broadcasted_iota(jnp.int32, (span, 2 * STATES), 1)
    return jnp.where(lane < STATES, span - 1 - row, row + 1).astype(jnp.float32)


def state_tables(rate_row, weight_row, span):
    steps = state_steps(span)
    table = jnp.exp(-rate_row * steps)
    lane_row = lax.broadcasted_iota(jnp.int32, (8, 2 * STATES), 1)
    lead = jnp.where(lane_row < STATES, 0.0, weight_row * jnp.exp(rate_row))
    response = lax.dot_general(
        lead, table, NT, precision=highest, preferred_element_type=jnp.float32
    )[:1]
    spread = pltpu.roll(
        jnp.broadcast_to(response, (span, span)), 0, 1, stride=1, stride_axis=0
    )
    later = lax.broadcasted_iota(jnp.int32, (span, span), 1)
    earlier = lax.broadcasted_iota(jnp.int32, (span, span), 0)
    toeplitz = jnp.where(later >= earlier, spread, 0.0)
    return table, toeplitz


def shift_rows(value, count):
    if count > 0:
        return jnp.concatenate([jnp.zeros_like(value[:count]), value[:-count]], 0)
    return jnp.concatenate([value[-count:], jnp.zeros_like(value[:-count])], 0)


def scan_states(value, decay, seqs, blocks, direction):
    step = 1
    while step < blocks:
        value = value + shift_rows(value, direction * step * seqs) * jnp.exp(decay * step)
        step *= 2
    return shift_rows(value, direction * seqs)


SHARE = 16


def table_block(refs, kind, channel):
    size = 2 * STATES
    if kind < 3:
        row, column = channel // 2, lax.rem(channel, 2) * 3 + kind
        ref = refs.tables
    else:
        row, column = channel // 8, lax.rem(channel, 8)
        ref = refs.more_tables
    return ref.at[
        pl.ds(pl.multiple_of(row * size, size), size),
        pl.ds(pl.multiple_of(column * size, size), size),
    ]


def table_pair(refs, kind, channel):
    return table_block(refs, kind, channel)[...], table_block(refs, kind + 1, channel)[...]


def fill_tables(first, last, span, refs):
    def one_channel(channel, carry):
        table, toeplitz = state_tables(
            refs.rates[pl.ds(channel, 1), :], refs.rate_weights[pl.ds(channel, 1), :], span
        )
        for kind, value in enumerate((*split_low(toeplitz), *split_low(table))):
            table_block(refs, kind, channel)[...] = value
        return carry

    lax.fori_loop(first, last, one_channel, 0, unroll=4)


def table_shapes(channels, span):
    return (channels // 2 * span, 6 * span), (channels // 8 * span, 8 * span)


def fill_rates(refs, loads, channels, turned):
    copies = [
        loads.start(refs.all_rates, refs.rates_in), loads.start(refs.all_weights, refs.weights_in)
    ]

    def finish():
        rows = pl.ds(pl.multiple_of(lax.axis_index(SEQ) * channels, 8), channels)
        for copy, source, target in zip(
            copies, (refs.rates_in, refs.weights_in), (refs.rates, refs.rate_weights)
        ):
            copy.wait()
            both = jnp.concatenate([source[...]] * 2, 0)
            turned[...] = both.T
            target[...] = turned[rows, :]

    return finish


def rate_scratch(width, channels):
    flat, own = ((STATES, width), jnp.float32), ((channels, 2 * STATES), jnp.float32)
    return dict(
        rates_in=flat, weights_in=flat, rates=own, rate_weights=own,
    )


def valid_positions(lengths, seqs, span, axis):
    shape = (span, 1) if axis == 0 else (1, span)
    position = lax.axis_index(SEQ) * span + lax.broadcasted_iota(jnp.int32, shape, axis)
    parts = [
        jnp.where(position < lengths[0:1, seq : seq + 1], 1.0, 0.0).astype(jnp.float32)
        for seq in range(seqs)
    ]
    return jnp.concatenate(parts, axis)


def mixer_forward_channel(n, seqs, refs, part, local):
    span, channel = refs.flat_x.shape[-1], part * SHARE + local
    rate_row = refs.rates[pl.ds(channel, 1), :]
    weight_row = refs.rate_weights[pl.ds(channel, 1), :]
    rows = pl.ds(local, n * seqs, stride=SHARE)
    data = (refs.flat_x[part, rows, :].astype(jnp.bfloat16), None)
    table_parts = table_pair(refs, 2, channel)
    inner = dot_fine(data, table_pair(refs, 0, channel))
    states = scan_states(dot_fine(data, table_parts), -span * rate_row, seqs, n, 1)
    lane = lax.broadcasted_iota(jnp.int32, states.shape, 1)
    weighted = jnp.where(lane < STATES, 0.0, pltpu.roll(states, STATES, 1) * weight_row)
    refs.flat_out[part, rows, :] = inner + dot_fine(split_low(weighted), table_parts, NT)


def mixer_backward_channel(n, seqs, refs, part, local):
    span, channel = refs.flat_x.shape[-1], part * SHARE + local
    rate_row = refs.rates[pl.ds(channel, 1), :]
    weight_row = refs.rate_weights[pl.ds(channel, 1), :]
    table_parts = table_pair(refs, 2, channel)
    table = table_parts[0].astype(jnp.float32) + table_parts[1].astype(jnp.float32)
    steps = state_steps(span)
    rows = pl.ds(local, n * seqs, stride=SHARE)
    data = refs.flat_x[part, rows, :].astype(jnp.bfloat16)
    grad = refs.flat_d[part, rows, :].astype(jnp.bfloat16)
    stepped_parts = split_low(table * steps)
    both_parts = [jnp.concatenate(pair, 1) for pair in zip(table_parts, stepped_parts)]
    count = n * seqs
    sides = dot_fine((jnp.concatenate([data, grad], 0), None), both_parts)
    lane = lax.broadcasted_iota(jnp.int32, (count, 2 * STATES), 1)
    low_lanes = lane < STATES

    def aligned(value):
        return jnp.where(low_lanes, pltpu.roll(value, STATES, 1), 0.0)

    entering = jnp.where(low_lanes, sides[:count, : 2 * STATES], 0.0)
    entering_steps = jnp.where(low_lanes, sides[:count, 2 * STATES :], 0.0)
    leaving = aligned(sides[count:, : 2 * STATES])
    leaving_steps = aligned(sides[count:, 2 * STATES :])
    decay = -span * rate_row
    states = scan_states(entering, decay, seqs, n, 1)
    states_steps = scan_states(states * jnp.exp(decay), decay, seqs, n, 1)
    returned = scan_states(leaving, decay, seqs, n, -1)
    far_weight = jnp.sum(leaving * states, 0, keepdims=True)
    far_rate = jnp.sum(
        leaving_steps * states + returned * entering_steps + span * (leaving * states_steps),
        0, keepdims=True,
    )
    cross = dot(grad, data, TN)
    later = lax.broadcasted_iota(jnp.int32, (span, span), 0)
    earlier = lax.broadcasted_iota(jnp.int32, (span, span), 1)
    cross = jnp.where(later >= earlier, cross, 0.0)
    met = dot_fine(split_low(cross), both_parts)
    met_plain = pltpu.roll(met[:, : 2 * STATES], STATES, 1)
    met_steps = pltpu.roll(met[:, 2 * STATES :], STATES, 1)
    rise = jnp.exp(span * rate_row)
    near_weight = rise * jnp.sum(table * met_plain, 0, keepdims=True)
    near_rate = rise * jnp.sum(
        table * ((steps - span) * met_plain + met_steps), 0, keepdims=True
    )
    lane_row = lane[:1]
    near_weight = jnp.where(lane_row < STATES, pltpu.roll(near_weight, STATES, 1), 0.0)
    near_rate = jnp.where(lane_row < STATES, pltpu.roll(near_rate, STATES, 1), 0.0)
    refs.weight_grad[pl.ds(channel, 1), :] = near_weight + far_weight
    refs.rate_grad[pl.ds(channel, 1), :] = -weight_row * (near_rate + far_rate)
    inner = dot_fine((grad, None), table_pair(refs, 0, channel), NT)
    weighted = returned * weight_row
    refs.flat_d[part, rows, :] = inner + dot_fine(split_low(weighted), table_parts, NT)


def block_of(index, core):
    return 2 * index + lax.rem(index + core, 2)


def keeper_of(block):
    return lax.rem((block + 1) // 2, 2)


class HeadPlaces:
    def __init__(self, n, seqs, groups):
        self.n, self.seqs, self.groups = n, seqs, groups
        self.me, self.core = lax.axis_index(SEQ), lax.axis_index(BATCH)
        self.group = self.me // (2 * seqs)
        self.seq = lax.rem(self.me // 2, seqs)
        self.batch = lax.rem(self.me, 2)
        self.keeper = keeper_of(self.me)
        self.sibling = (self.me, 1 - self.core)
        self.targets = [
            ((group * 2 * seqs + seq * 2 + self.core, self.keeper), seq, group)
            for seq in range(seqs)
            for group in range(groups)
        ]
        self.blocks = [block_of(index, self.core) for index in range(n // 2)]
        self.sources = [(block, self.batch) for block in self.blocks]

    def is_other(self, device):
        return jnp.logical_or(device[0] != self.me, device[1] != self.core)

    def greet(self):
        barrier = pltpu.get_barrier_semaphore()
        self.signal_all(barrier, [])
        self.wait_all(barrier, 0)

    def signal_all(self, barrier, more):
        for device in [target for target, _, _ in self.targets] + self.sources:

            @pl.when(self.is_other(device))
            def _():
                pl.semaphore_signal(barrier, inc=1, device_id=device, device_id_type=MESH)

        for device in [self.sibling, *more]:
            pl.semaphore_signal(barrier, inc=1, device_id=device, device_id_type=MESH)

    def wait_all(self, barrier, more):
        kept = jnp.logical_and(self.batch == self.core, self.is_kept_here())
        count = len(self.targets) + len(self.sources) + 1 + more
        pl.semaphore_wait(barrier, count - 2 * kept.astype(jnp.int32))

    def is_kept_here(self):
        return self.keeper == self.core

    def send(self, source, target, send_sem, recv_sem, device):
        @pl.when(self.is_other(device))
        def _():
            remote(source, target, send_sem, recv_sem, device).start()

        @pl.when(jnp.logical_not(self.is_other(device)))
        def _():
            pltpu.make_async_copy(source, target, recv_sem).start()

    def wait_sent(self, source, target, send_sem, recv_sem, device):
        @pl.when(self.is_other(device))
        def _():
            remote(source, target, send_sem, recv_sem, device).wait_send()


def fill_head(held, head, part, n, span, rows_out, columns_out):
    for block in range(n):
        piece = held[head, block, part * HEAD : (part + 1) * HEAD, :]
        if rows_out is not None:
            rows_out[block * span : (block + 1) * span, :] = piece.T
        if columns_out is not None:
            columns_out[:, block * span : (block + 1) * span] = piece


def causal(first_key, rows, first_query, span):
    key = first_key + lax.broadcasted_iota(jnp.int32, (rows, span), 0)
    query = first_query + lax.broadcasted_iota(jnp.int32, (rows, span), 1)
    return key <= query


TILE = 384
VMEM, HBM = pltpu.VMEM, pl.ANY


def launch(body, inputs, outputs, scratch, copies, collective):
    names = [*inputs, *outputs, *scratch, "send", "recv", "local"]

    def kernel(*refs):
        body(types.SimpleNamespace(**dict(zip(names, refs))))

    dma = pltpu.SemaphoreType.DMA
    results = pl.pallas_call(
        kernel,
        out_shape=tuple(jax.ShapeDtypeStruct(shape, kind) for shape, kind, _ in outputs.values()),
        in_specs=[pl.BlockSpec(memory_space=space) for _, space in inputs.values()],
        out_specs=tuple(pl.BlockSpec(memory_space=space) for _, _, space in outputs.values()),
        scratch_shapes=[pltpu.VMEM(shape, kind) for shape, kind in scratch.values()]
        + [dma((copies,)), dma((copies,)), dma((LOCAL_COPIES,))],
        compiler_params=pltpu.CompilerParams(
            collective_id=collective, has_side_effects=True, vmem_limit_bytes=VMEM_BYTES
        ),
    )(*(array for array, _ in inputs.values()))
    return types.SimpleNamespace(**dict(zip(outputs, results)))


LOCAL_COPIES = 64


class Loads:
    def __init__(self, refs):
        self.semaphores, self.used = refs.local, 0

    def start(self, source, target):
        copy = pltpu.make_async_copy(source, target, self.semaphores.at[self.used])
        self.used += 1
        copy.start()
        return copy


class Links:
    def __init__(self, refs):
        self.send, self.recv, self.used, self.unsent = refs.send, refs.recv, 0, []

    def slots(self, count):
        self.used += count
        return self.used - count

    def copy(self, source, target, device, slot=None):
        slot = self.slots(1) if slot is None else slot
        made = remote(source, target, self.send.at[slot], self.recv.at[slot], device)
        made.start()
        self.unsent.append(made)
        return made

    def finish(self):
        for made in self.unsent:
            made.wait_send()


class Piece:
    def __init__(self, weight, first_row, first_column, axis):
        self.weight, self.first_row, self.first_column, self.axis = (
            weight, first_row, first_column, axis,
        )


ROWS = 48


def pieces_of(weights, order):
    pieces = []
    for weight, first, last, axes in order:
        rows, half = weights[weight]
        places = [
            (first_row, first_column)
            for first_column in range(0, half, TILE)
            for first_row in range(0, rows, ROWS)
        ]
        for count, place in enumerate(places[first:last]):
            pieces.append(Piece(weight, *place, axes[count % len(axes)]))
    return pieces


class Reducer:
    def __init__(self, refs, links, depth, weights, pieces, given):
        self.refs, self.links, self.depth, self.weights = refs, links, depth, weights
        self.me, self.core = lax.axis_index(SEQ), lax.axis_index(BATCH)
        self.level = self.me // 4
        self.spot = (lax.rem(self.me // 2, 2), lax.rem(self.me, 2))
        base = self.level * 4
        self.across = [
            (base + self.spot[0] * 2 + (1 - self.spot[1]), self.core),
            (base + (1 - self.spot[0]) * 2 + self.spot[1], self.core),
        ]
        self.sibling = (self.me, 1 - self.core)
        self.levels = [lax.rem(self.level + step, depth) for step in range(1, depth)]
        self.column = [
            (other * 4 + self.spot[0] * 2 + self.spot[1], self.core) for other in self.levels
        ]
        place = self.spot[0] * 2 + self.spot[1]
        beside = self.level + 1 - 2 * lax.rem(self.level, 2)
        self.beside = (beside * 4 + place, self.core)
        self.beyond = (lax.rem(self.level + 2, depth) * 4 + place, self.core)
        self.slots = {piece: slot for slot, piece in enumerate(pieces)}
        self.given = {piece: slot for slot, piece in enumerate(given)}
        self.products = {}
        self.exchanges, self.flights = {}, {}

    def neighbours(self):
        return [self.sibling, *self.across, *self.column]

    def exchange(self, weight, left, right, blocks=None):
        if weight not in self.exchanges:
            sent = self.links.copy(left[0], left[1], self.sibling)
            self.exchanges[weight] = (left, right, {None: sent})
        for block in range(self.weights[weight][1] // TILE) if blocks is None else blocks:
            theirs = (2 * block + 1 - self.core) * TILE
            self.exchanges[weight][2][block] = self.links.copy(
                right[0].at[pl.ds(pl.multiple_of(theirs, TILE), TILE), :],
                right[1].at[block * TILE : (block + 1) * TILE, :], self.sibling,
            )

    def own_columns(self, piece):
        start = (2 * (piece.first_column // TILE) + self.core) * TILE
        return pl.ds(pl.multiple_of(start, TILE), TILE)

    def product(self, piece, first):
        left, right, copies = self.exchanges[piece.weight]
        for key in (None, piece.first_column // TILE):
            if key in copies:
                copies.pop(key).wait_recv()
        places = [
            outer * 4 + (inner * 2 + first if piece.axis == 0 else first * 2 + inner)
            for outer in range(self.depth)
            for inner in range(2)
        ]
        rows = slice(piece.first_row, piece.first_row + ROWS)
        mine, other = (
            jnp.concatenate([side[place, rows, :] for place in places], 0) for side in left
        )
        own = self.own_columns(piece)
        there = slice(piece.first_column, piece.first_column + TILE)
        total = dot(mine, right[0][own, :], NT) + dot(other, right[1][there, :], NT)
        return total.reshape(self.depth, 2, ROWS, TILE)

    def first(self, piece):
        places = self.refs.away.shape[0]
        place = len(self.products)
        if place >= places:
            sent = self.products[place - places]
            sent.wait_send()
            self.links.unsent = [copy for copy in self.links.unsent if copy is not sent]
        away = self.refs.away.at[place % places]
        away[...] = self.product(piece, 1 - self.spot[1 - piece.axis]).astype(jnp.bfloat16)
        self.flights[piece] = self.links.copy(
            away, self.refs.one.at[self.slots[piece]], self.across[piece.axis]
        )
        self.products[place] = self.flights[piece]

    def joined(self, piece, into):
        slot = self.slots[piece]
        self.flights.pop(piece).wait_recv()
        total = self.product(piece, self.spot[1 - piece.axis])
        total = total + self.refs.one[slot].astype(jnp.float32)
        into[...] = total.astype(jnp.bfloat16)

    def resume(self, piece):
        slot = self.slots[piece]
        self.flights[piece] = self.links.copy(
            self.refs.one.at[slot, :, 1 - self.spot[piece.axis]], self.refs.two.at[slot],
            self.across[1 - piece.axis],
        )

    def second(self, piece):
        self.joined(piece, self.refs.one.at[self.slots[piece]])
        self.resume(piece)

    def middle(self, piece, into):
        slot = self.slots[piece]
        self.flights.pop(piece).wait_recv()
        kept = self.refs.one[slot, :, self.spot[piece.axis]].astype(jnp.float32)
        total = (kept + self.refs.two[slot].astype(jnp.float32)).astype(into.dtype)
        for outer in range(self.depth):
            into[outer % 2 * 2 + outer // 2] = total[outer]

    def summed(self, piece):
        if piece in self.given:
            slot = self.given[piece]
            return self.refs.mid.at[slot], self.refs.three.at[slot]
        slot = self.slots[piece]
        return self.refs.two.at[slot], self.refs.three.at[len(self.given) + slot]

    def third(self, piece):
        summed, three = self.summed(piece)
        if piece not in self.given:
            self.middle(piece, summed)
        theirs = 2 * (1 - lax.rem(self.level, 2))
        self.flights[piece] = self.links.copy(
            summed.at[pl.ds(theirs, 2)], three.at[:2], self.beside
        )

    def fold(self, piece):
        summed, three = self.summed(piece)
        self.flights.pop(piece).wait_recv()
        mine = 2 * lax.rem(self.level, 2)
        for pair in range(2):
            summed[mine + pair] = (
                summed[mine + pair].astype(jnp.float32) + three[pair].astype(jnp.float32)
            ).astype(summed.dtype)
        self.flights[piece] = self.links.copy(
            summed.at[mine + 1 - self.level // 2], three.at[2], self.beyond
        )

    def fourth(self, piece, out):
        summed, three = self.summed(piece)
        self.flights.pop(piece).wait_recv()
        total = summed[2 * lax.rem(self.level, 2) + self.level // 2].astype(jnp.float32)
        total = total + three[2].astype(jnp.float32)
        filled = out.at[piece.first_row : piece.first_row + ROWS, self.own_columns(piece)]
        filled[...] = total
        self.flights[piece] = self.links.copy(filled, filled, self.sibling)

    def last(self, piece):
        self.flights.pop(piece).wait_recv()


def reducer_scratch(products, pieces, given, depth):
    low = jnp.bfloat16
    shapes = dict(
        away=((products, depth, 2, ROWS, TILE), low), one=((pieces, depth, 2, ROWS, TILE), low),
        two=((pieces, depth, ROWS, TILE), low),
    )
    if given > 0:
        shapes.update(
            mid=((given, depth, ROWS, TILE), low),
            three=((given + pieces, depth - 1, ROWS, TILE), low),
        )
    return shapes


def gelu_slope(value):
    scale = math.sqrt(2.0 / math.pi)
    square = value * value
    bent = jnp.tanh(scale * value * (1.0 + 0.044715 * square))
    return 0.5 * (1.0 + bent) + 0.5 * value * (1.0 - bent * bent) * scale * (
        1.0 + 3.0 * 0.044715 * square
    )


def norm_gradient(inputs, gain, grad):
    center = inputs - jnp.mean(inputs, 0, keepdims=True)
    factor = lax.rsqrt(jnp.mean(center * center, 0, keepdims=True) + norm_eps)
    unit = center * factor
    scaled = grad * gain
    result = factor * (
        scaled
        - jnp.mean(scaled, 0, keepdims=True)
        - unit * jnp.mean(scaled * unit, 0, keepdims=True)
    )
    return result, jnp.sum(grad * unit, 1, keepdims=True), jnp.sum(grad, 1, keepdims=True)


def rows_product(matrix, other, out_rows, chunk, store):
    def one_chunk(index, carry):
        rows = pl.ds(pl.multiple_of(index * chunk, 128), chunk)
        store(rows, dot(matrix[rows, :], other))
        return carry

    lax.fori_loop(0, out_rows // chunk, one_chunk, 0)


def back_one_body(n, seqs, groups, span, group_rows, width, hidden_width, refs):
    at = HeadPlaces(n, seqs, groups)
    half = n // 2
    heads = group_rows // HEAD
    tokens = seqs * span
    links, loads = Links(refs), Loads(refs)
    weights = gradient_weights(width, hidden_width, n)
    pieces = pieces_of(weights, BACK_ONE_ORDER)
    reducer = Reducer(refs, links, groups, weights, pieces, [])
    down, up, out = [[piece for piece in pieces if piece.weight == weight] for weight in (DOWN, UP, OUT)]
    barrier = pltpu.get_barrier_semaphore()
    at.signal_all(barrier, reducer.neighbours()[1:])

    load_branch = loads.start(refs.branch, refs.down_right)
    load_active = loads.start(refs.active, refs.down_left)
    load_d_active = loads.start(refs.d_active, refs.d_active_in)
    load_slope = loads.start(refs.slope, refs.slope_in)
    load_w_up = loads.start(refs.w_up.at[1], refs.up)
    load_hidden = loads.start(refs.hidden, refs.hidden_in)
    load_w_out = loads.start(refs.w_out.at[1], refs.out)
    load_normed = loads.start(refs.normed, refs.up_left)
    load_attended = loads.start(refs.attended, refs.out_left)
    load_held = loads.start(refs.held, refs.held_in)

    at.wait_all(barrier, len(reducer.neighbours()) - 1)
    load_active.wait()
    load_branch.wait()
    reducer.exchange(DOWN, (refs.down_left, refs.down_left_other), (refs.down_right, refs.down_right_other))
    load_d_active.wait()
    load_slope.wait()
    refs.up_right[...] = (
        refs.slope_in[...].astype(jnp.float32) * refs.d_active_in[...].astype(jnp.float32)
    ).astype(jnp.bfloat16)
    for piece in down[:2]:
        reducer.first(piece)
    load_w_up.wait()
    load_hidden.wait()
    load_normed.wait()
    reducer.exchange(UP, (refs.up_left, refs.up_left_other), (refs.up_right, refs.up_right_other))
    d_normed = dot(refs.up[...], refs.up_right[...])
    for piece in down[2:]:
        reducer.first(piece)
    d_inputs, gain_part, bias_part = norm_gradient(refs.hidden_in[...], refs.columns[:, 3:4], d_normed)
    refs.small[...] = jnp.zeros_like(refs.small)
    refs.small[:, 3:4] = gain_part
    refs.small[:, 7:8] = bias_part
    grad = refs.down_right[...].astype(jnp.float32) + d_inputs
    refs.grad_out[...] = grad
    refs.out_right[...] = grad.astype(jnp.bfloat16)
    load_w_out.wait()
    load_attended.wait()
    reducer.exchange(OUT, (refs.out_left, refs.out_left_other), (refs.out_right, refs.out_right_other))

    count, lot = len(at.targets), groups * HEAD
    arrive, leave = links.slots(heads * half), links.slots(heads * count)
    spread = []
    for head in range(heads):
        rows = slice(head * lot, (head + 1) * lot)
        refs.d_attended[rows, :] = dot(refs.out[rows, :], refs.out_right[...]).astype(jnp.bfloat16)
        for number, (device, seq, group) in enumerate(at.targets):
            first = head * lot + group * HEAD
            sent = (
                refs.d_attended.at[first : first + HEAD, seq * span : (seq + 1) * span],
                refs.landing.at[head, at.me // 2], refs.send.at[leave + head * count + number],
                refs.recv.at[arrive + head * half + at.me // 2], device,
            )
            at.send(*sent)
            spread.append(sent)
    load_held.wait()
    started = down + up + out
    for piece in up + out:
        reducer.first(piece)

    returned = links.slots(len(at.targets) * heads)
    returning = links.slots(half * heads)
    slot = at.seq * groups + at.group
    going = []
    passed = []

    def send_back(head):
        passed[head].wait_recv()
        for index, device in enumerate(at.sources):
            results = refs.results.at[head, index]
            kept = refs.kept.at[head, index]
            part = refs.partial_recv[head, index].astype(jnp.float32)
            results[1] = (kept[:HEAD] + part[:HEAD]).astype(jnp.bfloat16)
            results[2] = (kept[HEAD:] + part[HEAD:]).astype(jnp.bfloat16)
            into = refs.d_qkv.at[
                :,
                pl.ds(pl.multiple_of(head * lot + at.group * HEAD, HEAD), HEAD),
                pl.ds(pl.multiple_of(at.seq * span, span), span),
            ]
            sent = (
                results, into, refs.send.at[returning + head * half + index],
                refs.recv.at[returned + head * len(at.targets) + slot], device,
            )
            at.send(*sent)
            going.append(sent)

    def attend(head):
        for index in range(half):
            landed = refs.landing.at[head, index]
            remote(
                landed, landed, refs.send.at[leave], refs.recv.at[arrive + head * half + index],
                at.sibling,
            ).wait_recv()
        fill_head(refs.held_in, head, 1, n, span, refs.key_rows, refs.key_columns)
        fill_head(refs.held_in, head, 2, n, span, refs.value_rows, None)
        refs.key_grads[...] = jnp.zeros_like(refs.key_grads)
        refs.value_grads[...] = jnp.zeros_like(refs.value_grads)
        for index, block in enumerate(at.blocks):
            query = refs.held_in[head, block, :HEAD, :] * jnp.bfloat16(HEAD**-0.5)
            grad = refs.landing[head, index]
            log_total = refs.lse[index, head : head + 1, :]
            clear, reach = 2 * index * span, 2 * (index + 1) * span
            pieces = []
            row_term = jnp.zeros((1, span), jnp.float32)
            for first, last in ((0, clear), (clear, reach)):
                if first == last:
                    continue
                scores = dot(refs.key_rows[first:last, :], query)
                if last == reach:
                    scores = jnp.where(
                        causal(clear, reach - clear, block * span, span), scores, masked_score
                    )
                weights = jnp.exp(scores - log_total)
                d_weights = dot(refs.value_rows[first:last, :], grad)
                row_term = row_term + jnp.sum(weights * d_weights, 0, keepdims=True)
                pieces.append((first, last, weights, d_weights))
            d_query = jnp.zeros((HEAD, span), jnp.float32)
            for first, last, weights, d_weights in pieces:
                d_scores = (weights * (d_weights - row_term)).astype(jnp.bfloat16)
                d_query = d_query + dot(refs.key_columns[:, first:last], d_scores)
                refs.key_grads[:, first:last] += dot(query, d_scores, NT)
                refs.value_grads[:, first:last] += dot(grad, weights.astype(jnp.bfloat16), NT)
            refs.results[head, index, 0] = (d_query * HEAD**-0.5).astype(jnp.bfloat16)
        for index in range(half):
            other = pl.ds(pl.multiple_of(block_of(index, 1 - at.core) * span, span), span)
            own = pl.ds(pl.multiple_of(at.blocks[index] * span, span), span)
            refs.partial_send[head, index, :HEAD, :] = refs.key_grads[:, other].astype(jnp.bfloat16)
            refs.partial_send[head, index, HEAD:, :] = refs.value_grads[:, other].astype(jnp.bfloat16)
            refs.kept[head, index, :HEAD, :] = refs.key_grads[:, own]
            refs.kept[head, index, HEAD:, :] = refs.value_grads[:, own]
        passed.append(
            links.copy(refs.partial_send.at[head], refs.partial_recv.at[head], at.sibling)
        )

    waiting = list(started)
    for head in range(heads):
        attend(head)
        if head > 0:
            send_back(head - 1)
        if head < heads - 1:
            for _ in range(2):
                reducer.second(waiting.pop(0))
    reducer.second(waiting.pop(0))
    send_back(heads - 1)
    done = len(started) - LEFT_OVER
    while len(waiting) > LEFT_OVER:
        reducer.second(waiting.pop(0))
    for place, piece in enumerate(started[done:]):
        reducer.joined(piece, refs.half_out.at[place])
    for place, piece in enumerate(started[:done]):
        reducer.middle(piece, refs.mid_out.at[place])
    for head in range(heads):
        for count, (device, seq, group) in enumerate(at.targets):
            landed = refs.d_qkv.at[
                :,
                head * lot + group * HEAD : head * lot + (group + 1) * HEAD,
                seq * span : (seq + 1) * span,
            ]
            remote(
                landed, landed, refs.send.at[leave],
                refs.recv.at[returned + head * len(at.targets) + count], at.sibling,
            ).wait_recv()
    for sent in spread + going:
        at.wait_sent(*sent)
    links.finish()


LEFT_OVER = 4


def gradient_weights(width, hidden_width, n):
    return {
        QKV: (width // n, 3 * width // 2),
        FIRST: (width // n, 3 * width // 2),
        DOWN: (hidden_width // n, width // 2),
        UP: (width // n, hidden_width // 2),
        OUT: (width // n, width // 2),
    }


BACK_ONE_ORDER = ((DOWN, 0, 4, (1, 0)), (UP, 0, 4, (0, 1)), (OUT, 0, 1, (0,)))
BACK_TWO_ORDER = (
    (QKV, 0, 3, (1, 0, 1)), (DOWN, 0, 4, (0, 1)), (UP, 0, 4, (0, 1)), (OUT, 0, 1, (0,)),
    (FIRST, 0, 3, (1, 0, 1)),
)


def back_one(
    branch, d_active, hidden, slope, normed, active, attended, held, lse, columns,
    w_out, w_up, collective,
):
    width, tokens = branch.shape
    heads, n, _, span = held.shape
    seqs = tokens // span
    group_rows = heads * HEAD
    groups = width // group_rows
    hidden_width = w_up.shape[2]
    half = n // 2
    low, wide = jnp.bfloat16, jnp.float32
    weights = gradient_weights(width, hidden_width, n)
    pieces = pieces_of(weights, BACK_ONE_ORDER)
    inputs = dict(
        branch=(branch, HBM), d_active=(d_active, HBM), hidden=(hidden, HBM), slope=(slope, HBM),
        normed=(normed, HBM), active=(active, HBM), attended=(attended, HBM), held=(held, HBM),
        lse=(lse, VMEM), columns=(columns, VMEM), w_out=(w_out, HBM), w_up=(w_up, HBM),
    )
    outputs = dict(
        d_qkv=((3, width, tokens), low, VMEM),
        grad_out=((width, tokens), wide, VMEM),
        small=((width, 128), wide, VMEM),
        mid_out=((len(pieces) - LEFT_OVER, groups, ROWS, TILE), low, VMEM),
        half_out=((LEFT_OVER, groups, 2, ROWS, TILE), low, VMEM),
    )
    scratch = dict(
        up=(w_up.shape[1:], low), out=(w_out.shape[1:], low),
        d_active_in=(d_active.shape, low), hidden_in=((width, tokens), wide),
        slope_in=(slope.shape, low), d_attended=((width, tokens), low),
        down_left=(active.shape, low), down_right=((width, tokens), low),
        up_left=(normed.shape, low), up_right=((hidden_width, tokens), low),
        out_left=(attended.shape, low), out_right=((width, tokens), low),
        held_in=(held.shape, low), landing=((heads, half, HEAD, span), low),
        results=((heads, half, 3, HEAD, span), low), kept=((heads, half, 2 * HEAD, span), wide),
        partial_send=((heads, half, 2 * HEAD, span), low),
        partial_recv=((heads, half, 2 * HEAD, span), low),
        key_grads=((HEAD, n * span), wide), value_grads=((HEAD, n * span), wide),
        key_rows=((n * span, HEAD), low), key_columns=((HEAD, n * span), low),
        value_rows=((n * span, HEAD), low),
        down_left_other=(active.shape, low), down_right_other=((width // 2, tokens), low),
        up_left_other=(normed.shape, low), up_right_other=((hidden_width // 2, tokens), low),
        out_left_other=(attended.shape, low), out_right_other=((width // 2, tokens), low),
        **reducer_scratch(len(pieces), len(pieces), 0, groups),
    )
    body = functools.partial(
        back_one_body, n, seqs, groups, span, group_rows, width, hidden_width
    )
    return launch(body, inputs, outputs, scratch, 160, collective)


def back_two_body(n, seqs, span, width, hidden_width, refs):
    channels = width // n
    me, core = lax.axis_index(SEQ), lax.axis_index(BATCH)
    peers = [lax.rem(me + step, n) for step in range(1, n)]
    before = (lax.rem(me + n - 1, n), core)
    links, loads = Links(refs), Loads(refs)
    weights = gradient_weights(width, hidden_width, n)
    pieces, given = pieces_of(weights, BACK_TWO_ORDER), pieces_of(weights, BACK_ONE_ORDER)
    given, halves = given[:-LEFT_OVER], given[-LEFT_OVER:]
    qkv, down, up, out, last = [
        [piece for piece in pieces if piece.weight == weight]
        for weight in (QKV, DOWN, UP, OUT, FIRST)
    ]
    reducer = Reducer(refs, links, n // 4, weights, halves + pieces, given)
    ends = {FIRST: refs.qkv_one, DOWN: refs.down_one, UP: refs.up_one, OUT: refs.out_one}
    ends_two = {DOWN: refs.down_two, UP: refs.up_two, OUT: refs.out_two}

    def fourth(piece):
        if piece in given or piece in halves:
            reducer.fourth(piece, ends_two[piece.weight])
        else:
            reducer.fourth(piece, refs.qkv_two if piece.weight == QKV else ends[piece.weight])

    barrier = pltpu.get_barrier_semaphore()
    for device in [(peer, core) for peer in peers] + [reducer.sibling]:
        pl.semaphore_signal(barrier, inc=1, device_id=device, device_id_type=MESH)
    load_d_qkv = loads.start(refs.d_qkv, refs.qkv_right)
    load_normed_three = loads.start(refs.normed_three, refs.qkv_left)
    load_half = loads.start(refs.half_in, refs.one.at[:LEFT_OVER])
    load_mid = loads.start(refs.mid_in, refs.mid.at[: len(given)])
    load_small = loads.start(refs.small_in, refs.small)
    load_w_qkv = loads.start(refs.w_qkv.at[1], refs.qkv)
    load_hidden_two = loads.start(refs.hidden_two, refs.hidden_two_in)
    load_grad = loads.start(refs.grad, refs.grad_now)
    load_w_down = loads.start(refs.w_down.at[0], refs.down)
    load_slope = loads.start(refs.slope, refs.slope_in)
    load_w_up = loads.start(refs.w_up.at[0], refs.up)
    load_active = loads.start(refs.active, refs.down_left)
    load_hidden_one = loads.start(refs.hidden_one, refs.hidden_one_in)
    load_normed_two = loads.start(refs.normed_two, refs.up_left)
    load_w_out = loads.start(refs.w_out.at[0], refs.out)
    load_gated = loads.start(refs.gated, refs.out_left)
    load_queries = loads.start(refs.queries, refs.queries_in)
    load_mixer = loads.start(refs.mixer, refs.mixer_in)
    load_carried = loads.start(refs.carried, refs.carried_in)
    finish_rates = fill_rates(refs, loads, channels, refs.small_other)
    load_held = loads.start(refs.held, refs.held_in)

    load_normed_one = loads.start(refs.normed_one, refs.first_left)
    load_tokens = loads.start(refs.tokens, refs.tokens_in)

    load_d_qkv.wait()
    load_normed_three.wait()
    pl.semaphore_wait(barrier, n)
    reducer.exchange(QKV, (refs.qkv_left, refs.qkv_left_other), (refs.qkv_right, refs.qkv_right_other))
    load_half.wait()
    for piece in halves:
        reducer.resume(piece)
    load_mid.wait()
    for piece in given[:3]:
        reducer.third(piece)
    load_w_qkv.wait()
    d_normed = dot(refs.qkv[...], refs.qkv_right[...])
    load_w_qkv = loads.start(refs.w_qkv.at[0], refs.qkv)
    for piece in qkv[:2]:
        reducer.first(piece)
    load_hidden_two.wait()
    load_grad.wait()
    d_inputs, gain_part, bias_part = norm_gradient(
        refs.hidden_two_in[...], refs.columns[:, 2:3], d_normed
    )
    load_small.wait()
    refs.small[:, 2:3] = gain_part
    refs.small[:, 6:7] = bias_part
    grad = refs.grad_now[...] + d_inputs
    refs.grad_now[...] = grad
    refs.down_right[...] = grad.astype(jnp.bfloat16)
    load_w_down.wait()
    load_slope.wait()
    load_active.wait()
    reducer.exchange(DOWN, (refs.down_left, refs.down_left_other), (refs.down_right, refs.down_right_other))

    def store_raised(rows, value):
        slope = refs.slope_in[rows, :].astype(jnp.float32)
        refs.up_right[rows, :] = (slope * value).astype(jnp.bfloat16)

    rows_product(refs.down, refs.down_right[...], hidden_width, 512, store_raised)
    load_w_up.wait()
    load_hidden_one.wait()
    load_normed_two.wait()
    reducer.exchange(UP, (refs.up_left, refs.up_left_other), (refs.up_right, refs.up_right_other))
    d_normed = dot(refs.up[...], refs.up_right[...])
    refs.tables, refs.more_tables = refs.down, refs.up
    load_tables = loads.start(refs.tables_kept, refs.down)
    load_more_tables = loads.start(
        refs.more_tables_kept, refs.up.at[:, : refs.more_tables_kept.shape[1]]
    )
    d_inputs, gain_part, bias_part = norm_gradient(
        refs.hidden_one_in[...], refs.columns[:, 1:2], d_normed
    )
    refs.small[:, 1:2] = gain_part
    refs.small[:, 5:6] = bias_part
    grad = refs.grad_now[...] + d_inputs
    refs.grad_now[...] = grad
    refs.out_right[...] = grad.astype(jnp.bfloat16)
    load_gated.wait()
    reducer.exchange(OUT, (refs.out_left, refs.out_left_other), (refs.out_right, refs.out_right_other))
    load_w_out.wait()
    load_queries.wait()
    load_mixer.wait()
    load_carried.wait()
    d_gated = dot(refs.out[...], refs.out_right[...])
    d_mixer = d_gated * refs.queries_in[...]
    for seq in range(seqs):
        refs.d_conv[seq] = d_mixer[:, seq * span : (seq + 1) * span].astype(jnp.bfloat16)
    shares = channels // SHARE
    arrive, answered = links.slots(shares * n), links.slots(shares * n)

    def share_rows(device, share):
        return pl.ds(pl.multiple_of(device * channels + share * SHARE, 16), SHARE)

    going, own_copies = [], []
    for share in range(shares):
        within = slice(share * SHARE, (share + 1) * SHARE)
        for step, peer in enumerate(peers):
            going.append(
                links.copy(
                    refs.d_conv.at[:, share_rows(peer, share), :],
                    refs.landing.at[me, :, within, :], (peer, core), arrive + share * n + step,
                )
            )
        own_copies.append(
            loads.start(
                refs.d_conv.at[:, share_rows(me, share), :], refs.landing.at[me, :, within, :]
            )
        )
    refs.d_mixer[...] = d_mixer
    refs.first_right[:width, :] = (d_gated * refs.mixer_in[...]).astype(jnp.bfloat16)
    refs.small[:, 12:13] = sum(
        jnp.sum(
            d_mixer[:, seq * span : (seq + 1) * span] * refs.carried_in[seq].astype(jnp.float32), 1,
            keepdims=True,
        )
        for seq in range(seqs)
    )

    first_left = (refs.first_left, refs.first_left_other)
    first_right = (refs.first_right, refs.first_right_other)
    load_normed_one.wait()
    reducer.exchange(FIRST, first_left, first_right, (0,))
    load_values = loads.start(refs.values, refs.queries_in)
    load_keys = loads.start(refs.keys, refs.carried_in)
    load_shifted = loads.start(refs.shifted, refs.mixer_in)
    for piece in given[:3]:
        reducer.fold(piece)
    for piece in down[:2] + qkv[2:] + down[2:]:
        reducer.first(piece)
    for piece in given[3:]:
        reducer.third(piece)
    load_held.wait()
    finish_rates()
    load_tables.wait()
    load_more_tables.wait()
    back, back_own = [], []
    for share in range(shares):
        within = slice(share * SHARE, (share + 1) * SHARE)
        own_copies[share].wait()
        for copy in going[share * len(peers) : (share + 1) * len(peers)]:
            copy.wait_recv()
        for flat, source in ((refs.flat_x, refs.held_in), (refs.flat_d, refs.landing)):
            flat[share, : n * seqs * SHARE, :] = (
                source[:, :, within, :].astype(jnp.float32).reshape(n * seqs * SHARE, span)
            )

        def one_channel(local, carry):
            mixer_backward_channel(n, seqs, refs, share, local)
            return carry

        lax.fori_loop(0, SHARE, one_channel, 0, unroll=4)
        refs.landing[:, :, within, :] = (
            refs.flat_d[share, : n * seqs * SHARE, :].reshape(n, seqs, SHARE, span).astype(jnp.bfloat16)
        )
        for step, peer in enumerate(peers):
            back.append(
                links.copy(
                    refs.landing.at[peer, :, within, :],
                    refs.from_conv.at[:, share_rows(me, share), :], (peer, core),
                    answered + share * n + step,
                )
            )
        back_own.append(
            loads.start(
                refs.landing.at[me, :, within, :], refs.from_conv.at[:, share_rows(me, share), :]
            )
        )
        for piece in (qkv[:2], down[:2], [qkv[2], down[2]])[share]:
            reducer.second(piece)
        if share == 0:
            for piece in given[3:]:
                reducer.fold(piece)
        else:
            reducer.first(up[share - 1])
    for piece in halves:
        reducer.third(piece)
    states = [
        links.copy(refs.rate_grad, refs.rate_other, reducer.sibling),
        links.copy(refs.weight_grad, refs.weight_other, reducer.sibling),
    ]
    reducer.second(down[3])
    for piece in qkv[:2]:
        reducer.third(piece)
    for piece in halves:
        reducer.fold(piece)
    for piece in given:
        fourth(piece)
    for copy in states:
        copy.wait_recv()
    refs.rate_sum[...] = (refs.rate_grad[...] + refs.rate_other[...])[:, :STATES]
    refs.weight_sum[...] = (refs.weight_grad[...] + refs.weight_other[...])[:, :STATES]
    for copy in back_own:
        copy.wait()
    for copy in back:
        copy.wait_recv()
    load_values.wait()
    load_shifted.wait()
    valid = valid_positions(refs.lengths, seqs, span, 1)
    conv = jnp.concatenate([refs.from_conv[seq] for seq in range(seqs)], 1).astype(jnp.float32)
    d_carried = (refs.d_mixer[...] * refs.columns[:, 8:9] + conv) * valid
    d_shifted = d_carried * refs.queries_in[...]
    refs.hidden_one_in[...] = d_shifted
    for seq in range(seqs):
        for first in range(0, width, span):
            turned = d_shifted[first : first + span, seq * span : (seq + 1) * span].T
            refs.rim_out[seq, :, first : first + span] = turned[: refs.rim_out.shape[1]]
    refs.first_right[2 * width :, :] = (d_carried * refs.mixer_in[...]).astype(jnp.bfloat16)
    halo = links.copy(refs.rim_out, refs.rim_in, before)
    reducer.exchange(FIRST, first_left, first_right, (2,))
    for piece in up[2:] + out:
        reducer.first(piece)
    for piece in up[:2]:
        reducer.second(piece)
    for piece in qkv[2:] + down[:2]:
        reducer.third(piece)
    load_keys.wait()
    halo.wait_recv()
    lane = lax.broadcasted_iota(jnp.int32, (width, span), 1)
    there = jnp.where(me == n - 1, 0.0, 1.0)
    rim = refs.rim_in.shape[1]
    tap_sums = [jnp.zeros((width, 1), jnp.float32) for _ in range(TAPS)]
    for seq in range(seqs):
        lanes = slice(seq * span, (seq + 1) * span)
        own = refs.hidden_one_in[:, lanes]
        keys = refs.carried_in[seq].astype(jnp.float32)
        turned = []
        for first in range(0, width, span):
            piece = refs.rim_in[seq, :, first : first + span] * there
            piece = jnp.concatenate([piece, jnp.zeros((span - rim, span), jnp.float32)], 0)
            turned.append(piece.T)
        following = jnp.concatenate(turned, 0)
        d_keys = jnp.zeros((width, span), jnp.float32)
        for offset in range(TAPS):
            moved = own
            if offset > 0:
                moved = jnp.where(
                    lane < span - offset,
                    pltpu.roll(own, span - offset, 1),
                    pltpu.roll(following, span - offset, 1),
                )
            d_keys = d_keys + refs.columns[:, 4 + offset : 5 + offset] * moved
            tap_sums[offset] = tap_sums[offset] + jnp.sum(moved * keys, 1, keepdims=True)
        refs.first_right[width : 2 * width, lanes] = d_keys.astype(jnp.bfloat16)
    reducer.exchange(FIRST, first_left, first_right, (1,))
    load_w_qkv.wait()
    load_tokens.wait()
    d_normed = dot(refs.qkv[...], refs.first_right[...])
    flat_in = jnp.concatenate(
        [refs.tokens_in[seq].astype(jnp.float32).T for seq in range(seqs)], 1
    )
    d_inputs, gain_part, bias_part = norm_gradient(flat_in * valid, refs.columns[:, 0:1], d_normed)
    refs.hidden_two_in[...] = (refs.grad_now[...] + d_inputs) * valid
    for offset in range(TAPS):
        refs.small[:, 8 + offset : 9 + offset] = tap_sums[offset]
    refs.small[:, 0:1] = gain_part
    refs.small[:, 4:5] = bias_part
    shared = links.copy(refs.small, refs.small_other, reducer.sibling)
    for piece in last:
        reducer.first(piece)
    for piece in up[2:]:
        reducer.second(piece)
    for piece in qkv + down[:2]:
        reducer.fold(piece)
    for piece in down[2:]:
        reducer.third(piece)
    shared.wait_recv()
    rows = width // n
    turned = (refs.small[...] + refs.small_other[...]).T[:16]
    for place in range(n):
        start = place * rows // 128 * 128
        window = turned[:, start : min(start + 256, width)]
        away = (window.shape[1] - (place * rows - start)) % window.shape[1]
        refs.slices[place] = pltpu.roll(window, away, 1)[:, :128]
    depth = n // 4
    y, x = reducer.spot
    for outer in range(depth):
        for inner in range(2):
            refs.small_away[outer, inner] = refs.slices[outer * 4 + inner * 2 + 1 - x]
    small = links.copy(refs.small_away, refs.small_one, reducer.across[0])
    for seq in range(seqs):
        for first in range(0, width, span):
            refs.d_tokens[seq, :, first : first + span] = refs.hidden_two_in[
                first : first + span, seq * span : (seq + 1) * span
            ].T
    reducer.second(out[0])
    for piece in up[:2]:
        reducer.third(piece)
    for piece in halves + qkv:
        fourth(piece)
    for piece in down[2:]:
        reducer.fold(piece)
    small.wait_recv()
    for outer in range(depth):
        for inner in range(2):
            refs.small_one[outer, inner] += refs.slices[outer * 4 + inner * 2 + x]
    small = links.copy(refs.small_one.at[:, 1 - y], refs.small_two, reducer.across[1])
    reducer.second(last[2])
    for piece in up[2:]:
        reducer.third(piece)
    for piece in up[:2]:
        reducer.fold(piece)
    for piece in last[:2]:
        reducer.second(piece)
    reducer.third(out[0])
    for piece in down:
        fourth(piece)
    for piece in up[2:]:
        reducer.fold(piece)
    small.wait_recv()
    for outer in range(depth):
        refs.small_two[outer] += refs.small_one[outer, y]
    smalls = [
        links.copy(refs.small_two.at[other], refs.small_three.at[step], reducer.column[step])
        for step, other in enumerate(reducer.levels)
    ]
    reducer.fold(out[0])
    for piece in last:
        reducer.third(piece)
    for piece in up:
        fourth(piece)
    for piece in last:
        reducer.fold(piece)
    for piece in out + last:
        fourth(piece)
    total = refs.small_two[reducer.level]
    for step, copy in enumerate(smalls):
        copy.wait_recv()
        total = total + refs.small_three[step]
    refs.small_sum[...] = total[:, :rows]
    for piece in given + halves + pieces:
        reducer.last(piece)
    links.finish()


def back_two(
    tables, more_tables, mid, half, d_qkv, grad, hidden_two, normed_three, slope, normed_two, active, hidden_one,
    gated, queries, mixer, carried, held, values, shifted, keys, tokens, normed_one, columns, small,
    lengths, rates, rate_weights, w_qkv, w_out, w_up, w_down, collective,
):
    n, seqs, channels, span = held.shape
    width, hidden_width = w_up.shape[1:]
    count = seqs * span
    low, wide = jnp.bfloat16, jnp.float32
    weights = gradient_weights(width, hidden_width, n)
    pieces = pieces_of(weights, BACK_TWO_ORDER)
    inputs = dict(
        tables_kept=(tables, HBM), more_tables_kept=(more_tables, HBM), mid_in=(mid, HBM), half_in=(half, HBM), d_qkv=(d_qkv, HBM), grad=(grad, HBM),
        hidden_two=(hidden_two, HBM), normed_three=(normed_three, HBM), slope=(slope, HBM),
        normed_two=(normed_two, HBM), active=(active, HBM), hidden_one=(hidden_one, HBM),
        gated=(gated, HBM), queries=(queries, HBM), mixer=(mixer, HBM), carried=(carried, HBM),
        held=(held, HBM), values=(values, HBM), shifted=(shifted, HBM), keys=(keys, HBM),
        tokens=(tokens, HBM), normed_one=(normed_one, HBM), columns=(columns, VMEM),
        small_in=(small, HBM), lengths=(lengths, VMEM), all_rates=(rates, HBM),
        all_weights=(rate_weights, HBM), w_qkv=(w_qkv, HBM), w_out=(w_out, HBM), w_up=(w_up, HBM),
        w_down=(w_down, HBM),
    )
    square, state = (width, count), (channels, 2 * STATES)
    rows = width // n
    grads = dict(
        qkv=(rows, 3 * width), down=(hidden_width // n, width), up=(rows, hidden_width),
        out=(rows, width),
    )
    outputs = dict(
        d_tokens=((seqs, span, width), wide, VMEM),
        rate_sum=((channels, STATES), wide, VMEM),
        weight_sum=((channels, STATES), wide, VMEM),
        small_sum=((16, rows), wide, VMEM),
        **{name + ONE: (shape, wide, VMEM) for name, shape in grads.items()},
        **{name + TWO: (shape, wide, VMEM) for name, shape in grads.items()},
    )
    flat = (channels // SHARE, n * seqs * SHARE + SHARE, span)
    rim, lot = ((seqs, 8, width), wide), (n // 4, 2, 16, 128)
    scratch = dict(
        qkv=(w_qkv.shape[1:], low), down=(w_down.shape[1:], low), up=(w_up.shape[1:], low),
        out=(w_out.shape[1:], low),
        qkv_left=(normed_three.shape, low), qkv_right=((3 * width, count), low),
        first_left=(normed_one.shape, low), first_right=((3 * width, count), low),
        down_left=(active.shape, low), down_right=(square, low),
        up_left=(normed_two.shape, low), up_right=((hidden_width, count), low),
        out_left=(gated.shape, low), out_right=(square, low),
        hidden_two_in=(square, wide), hidden_one_in=(square, wide), grad_now=(square, wide),
        slope_in=(slope.shape, low), queries_in=(square, wide), mixer_in=(square, wide),
        carried_in=(carried.shape, low), held_in=(held.shape, low), d_mixer=(square, wide),
        from_conv=((seqs, width, span), low), d_conv=((seqs, width, span), low),
        landing=(held.shape, low), flat_x=(flat, wide),
        flat_d=(flat, wide), **rate_scratch(width, channels),
        rate_grad=(state, wide), weight_grad=(state, wide), rate_other=(state, wide),
        weight_other=(state, wide), tokens_in=(tokens.shape, low),
        rim_out=rim, rim_in=rim, small=((width, 128), wide), small_other=((width, 128), wide),
        slices=((n, 16, 128), wide), small_away=(lot, wide), small_one=(lot, wide),
        small_two=((n // 4, 16, 128), wide), small_three=((n // 4 - 1, 16, 128), wide),
        qkv_left_other=(normed_three.shape, low), qkv_right_other=((3 * width // 2, count), low),
        first_left_other=(normed_one.shape, low),
        first_right_other=((3 * width // 2, count), low),
        down_left_other=(active.shape, low), down_right_other=((width // 2, count), low),
        up_left_other=(normed_two.shape, low), up_right_other=((hidden_width // 2, count), low),
        out_left_other=(gated.shape, low), out_right_other=((width // 2, count), low),
        **reducer_scratch(6, LEFT_OVER + len(pieces), mid.shape[0], n // 4),
    )
    body = functools.partial(back_two_body, n, seqs, span, width, hidden_width)
    return launch(body, inputs, outputs, scratch, 420, collective)


def earlier_rows(own, before, steps):
    if steps == 0:
        return own
    moved = pltpu.roll(own, steps, 0)
    rim = before.shape[0]
    row = lax.broadcasted_iota(jnp.int32, (rim, own.shape[1]), 0)
    front = jnp.where(row < steps, pltpu.roll(before, steps, 0), moved[:rim])
    return jnp.concatenate([front, moved[rim:]], 0)


def forward_body(n, seqs, groups, span, group_rows, width, hidden_width, refs):
    at = HeadPlaces(n, seqs, groups)
    me, core = at.me, at.core
    channels = width // n
    half, heads = n // 2, group_rows // HEAD
    tokens = seqs * span
    links, loads = Links(refs), Loads(refs)
    peers = [lax.rem(me + step, n) for step in range(1, n)]
    after = (lax.rem(me + 1, n), core)
    barrier = pltpu.get_barrier_semaphore()
    at.signal_all(barrier, [(peer, core) for peer in peers])
    outgoing = []

    def save(source, target):
        outgoing.append(loads.start(source, target))

    load_tokens = loads.start(refs.tokens, refs.tokens_in)
    load_qkv = loads.start(refs.w_qkv.at[0], refs.qkv)
    load_cotangent = loads.start(refs.cotangent, refs.cot)
    load_out = loads.start(refs.w_out.at[0], refs.out)
    load_up = loads.start(refs.w_up.at[0], refs.up)
    load_down = loads.start(refs.w_down.at[0], refs.down)

    def normed(value, row, target):
        result = layer_norm(value, refs.gains[row : row + 1], refs.biases[row : row + 1])
        result = result.astype(jnp.bfloat16)
        target[...] = result.T
        return result

    finish_rates = fill_rates(refs, loads, channels, refs.turned_rates)
    valid = valid_positions(refs.lengths, seqs, span, 0)
    refs.columns[...] = jnp.concatenate(
        [refs.gains[...], refs.taps[...], refs.skip[...].reshape(1, width), jnp.zeros((7, width), jnp.float32)], 0
    ).T
    load_tokens.wait()
    flat_in = jnp.concatenate([refs.tokens_in[seq] for seq in range(seqs)], 0)
    flat_in = flat_in.astype(jnp.float32) * valid
    refs.flat_in[...] = flat_in
    normed_one = normed(flat_in, 0, refs.normed_one_t)
    load_qkv.wait()
    keys = dot(normed_one, refs.qkv[:, width : 2 * width]).astype(jnp.bfloat16)
    refs.keys[...] = keys
    rim = refs.rim_in.shape[1]
    at.wait_all(barrier, n - 1)
    for seq in range(seqs):
        refs.rim_out[seq] = refs.keys[(seq + 1) * span - rim : (seq + 1) * span, :]
    halo = links.copy(refs.rim_out, refs.rim_in, after)
    refs.values[...] = dot(normed_one, refs.qkv[:, 2 * width :])
    refs.queries[...] = dot(normed_one, refs.qkv[:, :width])
    load_qkv = loads.start(refs.w_qkv.at[1], refs.qkv)
    finish_rates()
    fill_tables(0, SHARE, span, refs)
    halo.wait_recv()
    there = jnp.where(me == 0, 0.0, 1.0)
    for seq in range(seqs):
        rows = slice(seq * span, (seq + 1) * span)
        before = refs.rim_in[seq].astype(jnp.float32) * there
        own = refs.keys[rows, :].astype(jnp.float32)
        shifted = jnp.zeros_like(own)
        for offset in range(TAPS):
            shifted = shifted + refs.taps[offset : offset + 1] * earlier_rows(own, before, offset)
        refs.shifted[rows, :] = shifted
        carried = (shifted * refs.values[rows, :] * valid[rows]).astype(jnp.bfloat16)
        refs.carried[rows, :] = carried
        refs.carried_t[seq] = carried.T

    shares = channels // SHARE
    arrive, answered = links.slots(shares * n), links.slots(shares * n)

    def share_rows(device, share):
        return pl.ds(pl.multiple_of(device * channels + share * SHARE, 16), SHARE)

    going, own_copies = [], []
    for share in range(shares):
        within = slice(share * SHARE, (share + 1) * SHARE)
        for step, peer in enumerate(peers):
            going.append(
                links.copy(
                    refs.carried_t.at[:, share_rows(peer, share), :],
                    refs.mixed_in.at[me, :, within, :], (peer, core), arrive + share * n + step,
                )
            )
        own_copies.append(
            loads.start(
                refs.carried_t.at[:, share_rows(me, share), :], refs.mixed_in.at[me, :, within, :]
            )
        )
    fill_tables(SHARE, channels, span, refs)
    save(refs.tables, refs.tables_kept)
    save(refs.more_tables, refs.more_tables_kept)
    refs.square_t[...] = refs.values[...].T
    save(refs.square_t, refs.values_t)
    refs.square_two_t[...] = refs.shifted[...].T
    save(refs.square_two_t, refs.shifted_t)
    for seq in range(seqs):
        refs.keys_out[seq] = refs.keys[seq * span : (seq + 1) * span, :].T
    save(refs.keys_out, refs.keys_t)
    refs.queries_out[...] = refs.queries[...].T
    save(refs.queries_out, refs.queries_t)
    save(refs.normed_one_t, refs.normed_one)
    save(refs.carried_t, refs.carried_out)
    back, back_own = [], []
    for share in range(shares):
        within = slice(share * SHARE, (share + 1) * SHARE)
        own_copies[share].wait()
        for copy in going[share * len(peers) : (share + 1) * len(peers)]:
            copy.wait_recv()
        refs.flat_x[share, : n * seqs * SHARE, :] = (
            refs.mixed_in[:, :, within, :].astype(jnp.float32).reshape(n * seqs * SHARE, span)
        )

        def one_channel(local, carry):
            mixer_forward_channel(n, seqs, refs, share, local)
            return carry

        lax.fori_loop(0, SHARE, one_channel, 0, unroll=4)
        refs.answer[:, :, within, :] = (
            refs.flat_out[share, : n * seqs * SHARE, :].reshape(n, seqs, SHARE, span).astype(jnp.bfloat16)
        )
        for step, peer in enumerate(peers):
            back.append(
                links.copy(
                    refs.answer.at[peer, :, within, :],
                    refs.convolved.at[:, share_rows(me, share), :], (peer, core),
                    answered + share * n + step,
                )
            )
        back_own.append(
            loads.start(
                refs.answer.at[me, :, within, :], refs.convolved.at[:, share_rows(me, share), :]
            )
        )
    save(refs.mixed_in, refs.mixed_held)
    for copy in back_own:
        copy.wait()
    for copy in back:
        copy.wait_recv()
    for seq in range(seqs):
        rows = slice(seq * span, (seq + 1) * span)
        convolved = refs.convolved[seq].astype(jnp.float32).T
        mixer = convolved + refs.skip[...].reshape(1, width) * refs.carried[rows, :].astype(jnp.float32)
        refs.gated[rows, :] = (refs.queries[rows, :] * mixer).astype(jnp.bfloat16)
        refs.mixer_out[:, rows] = mixer.T
    save(refs.mixer_out, refs.mixer_t)
    refs.gated_out[...] = refs.gated[...].T
    save(refs.gated_out, refs.gated_t)
    load_out.wait()
    hidden = refs.flat_in[...] + dot(refs.gated[...], refs.out[...])
    load_out = loads.start(refs.w_out.at[1], refs.out)

    def feed_forward(hidden, row, hidden_out, normed_out, up, down):
        hidden_out[...] = hidden.T
        refs.hidden[...] = hidden
        refs.normed[...] = normed(hidden, row, normed_out)
        up.wait()

        def one_chunk(index, carry):
            columns = pl.ds(pl.multiple_of(index * width, 128), width)
            raised = dot(refs.normed[...], refs.up[:, columns])
            refs.raised[:, columns] = raised
            refs.active[:, columns] = jax.nn.gelu(raised).astype(jnp.bfloat16)
            return carry

        lax.fori_loop(0, hidden_width // width, one_chunk, 0, unroll=4)
        if down is not None:
            down.wait()
        return refs.hidden[...] + dot(refs.active[...], refs.down[...])

    def turn_hidden(active_out, slope_out):
        def one_chunk(index, carry):
            columns = pl.ds(pl.multiple_of(index * width, 128), width)
            active_out[columns, :] = refs.active[:, columns].T
            slope = gelu_slope(refs.raised[:, columns]).astype(jnp.bfloat16)
            slope_out[columns, :] = slope.T
            return carry

        lax.fori_loop(0, hidden_width // width, one_chunk, 0, unroll=4)

    hidden = feed_forward(
        hidden, 1, refs.hidden_one_t, refs.normed_two_t, load_up, load_down
    )
    load_up = loads.start(refs.w_up.at[1], refs.up)
    load_down = loads.start(refs.w_down.at[1], refs.down)
    refs.hidden[...] = hidden
    refs.normed[...] = normed(hidden, 2, refs.normed_three_t)
    load_qkv.wait()
    count = len(at.targets)
    arrive, leave = links.slots(heads * half), links.slots(heads * count)
    passing = links.slots(heads * half)
    spread = []
    lot = groups * HEAD
    for head in range(heads):
        for part in range(3):
            first = part * width + head * lot
            columns = dot(refs.normed[...], refs.qkv[:, first : first + lot]).astype(jnp.bfloat16)
            for seq in range(seqs):
                refs.spread[head, seq, :, part * HEAD : (part + 1) * HEAD] = columns[
                    seq * span : (seq + 1) * span
                ].T.reshape(groups, HEAD, span)
        for number, (device, seq, group) in enumerate(at.targets):
            sent = (
                refs.spread.at[head, seq, group], refs.held.at[head, me],
                refs.send.at[leave + head * count + number],
                refs.recv.at[arrive + head * half + me // 2], device,
            )
            at.send(*sent)
            spread.append(sent)
    turn_hidden(refs.active_one_t, refs.slope_one_t)
    load_cotangent.wait()
    valid_row = valid_positions(refs.lengths, seqs, span, 1)
    for seq in range(seqs):
        lanes = slice(seq * span, (seq + 1) * span)
        turned = refs.cot[seq].astype(jnp.float32).T * valid_row[:, lanes]
        refs.branch_t[:, lanes] = turned.astype(jnp.bfloat16)
    save(refs.branch_t, refs.branch)
    load_down.wait()

    def store_active(rows, value):
        refs.d_active_t[rows, :] = value.astype(jnp.bfloat16)

    rows_product(refs.down, refs.branch_t[...], hidden_width, 512, store_active)
    save(refs.d_active_t, refs.d_active)
    refs.hidden_two_t[...] = hidden.T
    for source, target in (
        (refs.hidden_one_t, refs.hidden_one_out), (refs.normed_two_t, refs.normed_two),
        (refs.active_one_t, refs.active_one), (refs.slope_one_t, refs.slope_one),
        (refs.hidden_two_t, refs.hidden_two_out), (refs.normed_three_t, refs.normed_three),
    ):
        save(source, target)

    returned, returning = links.slots(heads * count), links.slots(heads * half)
    slot = at.seq * groups + at.group
    going = []

    def gather(head):
        for index, block in enumerate(at.blocks):
            landed = refs.held.at[head, block]
            remote(
                landed, landed, refs.send.at[leave], refs.recv.at[arrive + head * half + index],
                at.sibling,
            ).wait_recv()
            part = refs.held.at[head, block, HEAD : 3 * HEAD]
            links.copy(part, part, at.sibling, passing + head * half + index)
        for index in range(half):
            part = refs.held.at[head, block_of(index, 1 - core), HEAD : 3 * HEAD]
            remote(
                part, part, refs.send.at[leave], refs.recv.at[passing + head * half + index],
                at.sibling,
            ).wait_recv()

    def attend(head):
        fill_head(refs.held, head, 1, n, span, refs.key_rows, None)
        fill_head(refs.held, head, 2, n, span, None, refs.value_columns)
        for index, block in enumerate(at.blocks):
            query = refs.held[head, block, :HEAD, :] * jnp.bfloat16(HEAD**-0.5)
            clear, reach = 2 * index * span, 2 * (index + 1) * span
            edge = dot(refs.key_rows[clear:reach, :], query)
            edge = jnp.where(causal(clear, reach - clear, block * span, span), edge, masked_score)
            top = jnp.max(edge, 0, keepdims=True)
            if index > 0:
                body = dot(refs.key_rows[:clear, :], query)
                top = jnp.maximum(top, jnp.max(body, 0, keepdims=True))
            edge = jnp.exp(edge - top)
            total = jnp.sum(edge, 0, keepdims=True)
            result = dot(refs.value_columns[:, clear:reach], edge.astype(jnp.bfloat16))
            if index > 0:
                body = jnp.exp(body - top)
                total = total + jnp.sum(body, 0, keepdims=True)
                result = result + dot(refs.value_columns[:, :clear], body.astype(jnp.bfloat16))
            refs.outputs[head, index] = (result / total).astype(jnp.bfloat16)
            refs.lse[index, head : head + 1, :] = top + jnp.log(total)
        into = refs.attended_t.at[
            pl.ds(pl.multiple_of(head * lot + at.group * HEAD, HEAD), HEAD),
            pl.ds(pl.multiple_of(at.seq * span, span), span),
        ]
        for index, device in enumerate(at.sources):
            sent = (
                refs.outputs.at[head, index], into, refs.send.at[returning + head * half + index],
                refs.recv.at[returned + head * count + slot], device,
            )
            at.send(*sent)
            going.append(sent)

    for head in range(heads):
        gather(head)
        attend(head)
    save(refs.held, refs.held_out)
    for head in range(heads):
        for number, (device, seq, group) in enumerate(at.targets):
            first = head * lot + group * HEAD
            landed = refs.attended_t.at[first : first + HEAD, seq * span : (seq + 1) * span]
            remote(
                landed, landed, refs.send.at[leave],
                refs.recv.at[returned + head * count + number], at.sibling,
            ).wait_recv()
    save(refs.attended_t, refs.attended)
    load_out.wait()
    hidden = refs.hidden[...] + dot(refs.attended_t[...].T, refs.out[...])
    hidden = feed_forward(
        hidden, 3, refs.hidden_three_t, refs.normed_four_t, load_up, None
    )
    turn_hidden(refs.active_two_t, refs.slope_two_t)
    for source, target in (
        (refs.hidden_three_t, refs.hidden_three_out), (refs.normed_four_t, refs.normed_four),
        (refs.active_two_t, refs.active_two), (refs.slope_two_t, refs.slope_two),
    ):
        save(source, target)
    hidden = (hidden * valid).astype(jnp.bfloat16)
    for seq in range(seqs):
        refs.mixed[seq] = hidden[seq * span : (seq + 1) * span]
    for copy in outgoing:
        copy.wait()
    for sent in spread + going:
        at.wait_sent(*sent)
    links.finish()


def forward(
    tokens, cotangent, lengths, gains, biases, taps, skip, rates, rate_weights, w_qkv, w_out, w_up, w_down, n,
    groups, collective,
):
    seqs, span, width = tokens.shape
    hidden_width = w_up.shape[2]
    group_rows, channels = width // groups, width // n
    rows = seqs * span
    half, heads = n // 2, group_rows // HEAD
    low, wide = jnp.bfloat16, jnp.float32
    inputs = dict(
        tokens=(tokens, HBM), cotangent=(cotangent, HBM), lengths=(lengths, VMEM), gains=(gains, VMEM), biases=(biases, VMEM),
        taps=(taps, VMEM), skip=(skip, VMEM), all_rates=(rates, HBM), all_weights=(rate_weights, HBM),
        w_qkv=(w_qkv, HBM), w_out=(w_out, HBM), w_up=(w_up, HBM), w_down=(w_down, HBM),
    )
    square, tall, by_head = (width, rows), (hidden_width, rows), (heads, n, 3 * HEAD, span)
    mixed = (n, seqs, channels, span)
    tables, more_tables = table_shapes(channels, span)
    outputs = dict(
        mixed=((seqs, span, width), low, VMEM), columns=((width, 16), wide, VMEM),
        lse=((half, heads, span), wide, VMEM),
        held_out=(by_head, low, HBM), mixed_held=(mixed, low, HBM),
        carried_out=((seqs, width, span), low, HBM),
        values_t=(square, wide, HBM), shifted_t=(square, wide, HBM), keys_t=((seqs, width, span), low, HBM),
        queries_t=(square, wide, HBM), mixer_t=(square, wide, HBM), gated_t=(square, low, HBM),
        attended=(square, low, HBM), branch=(square, low, HBM), d_active=(tall, low, HBM),
        normed_one=(square, low, HBM), normed_two=(square, low, HBM),
        normed_three=(square, low, HBM), normed_four=(square, low, HBM),
        hidden_one_out=(square, wide, HBM), hidden_two_out=(square, wide, HBM),
        hidden_three_out=(square, wide, HBM),
        active_one=(tall, low, HBM), active_two=(tall, low, HBM),
        slope_one=(tall, low, HBM), slope_two=(tall, low, HBM),
        tables_kept=(tables, low, HBM), more_tables_kept=(more_tables, low, HBM),
    )
    flat = (channels // SHARE, n * seqs * SHARE + SHARE, span)
    lying = (rows, width)
    scratch = dict(
        qkv=(w_qkv.shape[1:], low), out=(w_out.shape[1:], low), up=(w_up.shape[1:], low),
        down=(w_down.shape[1:], low), tokens_in=(tokens.shape, low), flat_in=(lying, wide),
        keys=(lying, low), values=(lying, wide), queries=(lying, wide), shifted=(lying, wide),
        carried=(lying, low), gated=(lying, low), hidden=(lying, wide), normed=(lying, low),
        active=((rows, hidden_width), low), rim_in=((seqs, 16, width), low),
        rim_out=((seqs, 16, width), low), carried_t=((seqs, width, span), low),
        convolved=((seqs, width, span), low), mixed_in=(mixed, low), answer=(mixed, low),
        flat_x=(flat, wide), flat_out=(flat, wide), tables=(tables, low), more_tables=(more_tables, low),
        turned_rates=((width, 2 * STATES), wide),
        **rate_scratch(width, channels), raised=((rows, hidden_width), wide),
        cot=(tokens.shape, low), branch_t=(square, low), d_active_t=(tall, low),
        square_t=(square, wide), square_two_t=(square, wide), keys_out=((seqs, width, span), low),
        queries_out=(square, wide), mixer_out=(square, wide), gated_out=(square, low),
        attended_t=(square, low), normed_one_t=(square, low), normed_two_t=(square, low),
        normed_three_t=(square, low), normed_four_t=(square, low), hidden_one_t=(square, wide),
        hidden_two_t=(square, wide), hidden_three_t=(square, wide), active_one_t=(tall, low),
        active_two_t=(tall, low), slope_one_t=(tall, low), slope_two_t=(tall, low),
        spread=((heads, seqs, groups, 3 * HEAD, span), low), held=(by_head, low),
        outputs=((heads, half, HEAD, span), low), key_rows=((n * span, HEAD), low),
        value_columns=((HEAD, n * span), low),
    )
    body = functools.partial(
        forward_body, n, seqs, groups, span, group_rows, width, hidden_width
    )
    return launch(body, inputs, outputs, scratch, 290, collective)


def per_device_by_heads(
    tokens,
    cotangent,
    lengths,
    norm_gain,
    norm_bias,
    w_qkv,
    w_out,
    w_up,
    w_down,
    taps,
    skip,
    ssm_rate,
    ssm_out,
):
    seq_count, span_rows, width = tokens.shape[1:]
    devices = lax.axis_size(SEQ)
    channels = width // devices
    groups = devices // 4
    row_count = seq_count * span_rows
    rates, weights = ssm_rate.T, ssm_out.T
    kept = forward(
        tokens[0], cotangent[0], lengths, norm_gain, norm_bias, taps, skip, rates, weights, w_qkv, w_out,
        w_up, w_down, devices, groups, 1,
    )

    def sliced(value):
        return value.reshape(devices, value.shape[0] // devices, row_count)

    back = back_one(
        kept.branch, kept.d_active, kept.hidden_three_out, kept.slope_two, sliced(kept.normed_four),
        sliced(kept.active_two), sliced(kept.attended), kept.held_out, kept.lse, kept.columns,
        w_out, w_up, 3,
    )
    end = back_two(
        kept.tables_kept, kept.more_tables_kept, back.mid_out, back.half_out, back.d_qkv.reshape(3 * width, row_count),
        back.grad_out, kept.hidden_two_out, sliced(kept.normed_three), kept.slope_one,
        sliced(kept.normed_two), sliced(kept.active_one), kept.hidden_one_out,
        sliced(kept.gated_t), kept.queries_t, kept.mixer_t, kept.carried_out, kept.mixed_held,
        kept.values_t, kept.shifted_t, kept.keys_t, tokens[0], sliced(kept.normed_one),
        kept.columns, back.small, lengths, rates, weights, w_qkv, w_out, w_up, w_down, 4,
    )
    return collected(kept, end, norm_gain.shape[0])


def collected(kept, end, layers):
    pairs = [
        (end.qkv_one, end.qkv_two), (end.out_one, end.out_two), (end.up_one, end.up_two),
        (end.down_one, end.down_two),
    ]
    alone = [kept.mixed, end.d_tokens, end.rate_sum, end.weight_sum]
    rows = end.small_sum.shape[1]
    small = [(layers, rows), (layers - 1, rows), (rows,), (TAPS, rows), (rows,)]
    wide = jnp.float32

    def body(*refs):
        refs = list(refs)
        pair_refs = [(refs.pop(0), refs.pop(0)) for _ in pairs]
        alone_refs = [refs.pop(0) for _ in alone]
        sums = refs.pop(0)
        for first, second in pair_refs:
            out = refs.pop(0)
            out[0] = first[...]
            out[1] = second[...]
        for source in alone_refs:
            refs.pop(0)[...] = source[...]
        gain, bias, last, taps, skip = refs
        gain[...] = sums[:layers, :]
        bias[...] = sums[layers : 2 * layers - 1, :]
        last[...] = sums[2 * layers - 1, :]
        taps[...] = sums[2 * layers : 2 * layers + TAPS, :]
        skip[...] = sums[2 * layers + TAPS, :]

    arrays = [array for pair in pairs for array in pair] + alone + [end.small_sum]
    shapes = [jax.ShapeDtypeStruct((2, *first.shape), wide) for first, _ in pairs]
    shapes += [jax.ShapeDtypeStruct(array.shape, array.dtype) for array in alone]
    shapes += [jax.ShapeDtypeStruct(shape, wide) for shape in small]
    vmem = pl.BlockSpec(memory_space=VMEM)
    outs = pl.pallas_call(
        body,
        out_shape=tuple(shapes),
        in_specs=[vmem] * len(arrays),
        out_specs=(vmem,) * len(shapes),
        compiler_params=pltpu.CompilerParams(vmem_limit_bytes=VMEM_BYTES),
    )(*arrays)
    qkv, out, up, down, mixed, d_tokens, rate, weight, gain, bias, last, taps, skip = outs
    return (
        mixed[None], d_tokens[None], gain, bias, last, qkv, out, up, down, taps, skip, rate, weight,
    )


def fits_by_heads(mesh):
    devices = mesh.shape[SEQ]
    return devices == 16 and mesh.shape[BATCH] == 2


def solution(mesh):
    placed = (
        P(BATCH, None, SEQ, None),
        P(BATCH, None, SEQ, None),
        P(BATCH, None),
        P(),
        P(),
        P(),
        P(),
        P(),
        P(),
        P(),
        P(),
        P(),
        P(),
    )
    return jax.shard_map(
        per_device_by_heads if fits_by_heads(mesh) else per_device,
        mesh=mesh,
        in_specs=placed,
        out_specs=(
            P(BATCH, None, SEQ, None),
            P(BATCH, None, SEQ, None),
            P(None, SEQ),
            P(None, SEQ),
            P(SEQ),
            P(None, SEQ, None),
            P(None, SEQ, None),
            P(None, SEQ, None),
            P(None, SEQ, None),
            P(None, SEQ),
            P(SEQ),
            P(SEQ, None),
            P(SEQ, None),
        ),
        check_vma=False,
    )
```
